32 devices in a mesh: expert: 8 (over y, x, core), hidden: 4 (over z).
Axes of the slice: x: 2, y: 2, z: 4, core: 2. Of those that a mesh axis runs over, the one named last changes fastest.
Arguments:
- tokens: bfloat16 [16384, 1024], P(('expert', 'hidden')), may hold values from -6 to 6
- gain_one: float32 [1024], replicated, may hold values from 0.5 to 1.5
- w_query: bfloat16 [1024, 1024], replicated, may hold values from -0.1875 to 0.1875
- w_key: bfloat16 [1024, 1024], replicated, may hold values from -0.1875 to 0.1875
- w_value: bfloat16 [1024, 1024], replicated, may hold values from -0.1875 to 0.1875
- w_out: bfloat16 [1024, 1024], replicated, may hold values from -1.5 to 1.5
- bias_table: float32 [32, 16], replicated, may hold values from -4 to 4
- gain_two: float32 [1024], replicated, may hold values from 0.5 to 1.5
- w_router: float32 [1024, 16], replicated, may hold values from -0.1875 to 0.1875
- w_gate: bfloat16 [16, 1024, 2816], P('expert', None, 'hidden'), may hold values from -0.1875 to 0.1875
- w_up: bfloat16 [16, 1024, 2816], P('expert', None, 'hidden'), may hold values from -0.1875 to 0.1875
- w_down: bfloat16 [16, 2816, 1024], P('expert', 'hidden'), may hold values from -0.109375 to 0.109375
- routes: int32 [16384, 2], P(('expert', 'hidden')), may hold values from 0 to 15, all different within a row; in each aligned block of 256 rows (0 to 255, 256 to 511, ...) at most 40 rows name the same one
- cotangent: bfloat16 [16384, 1024], P(('expert', 'hidden')), may hold values from -6 to 6
Outputs:
- block_out: bfloat16 [16384, 1024], P(('expert', 'hidden'))
- tokens_grad: float32 [16384, 1024], P(('expert', 'hidden'))
- gain_one_grad: float32 [1024], replicated
- query_grad: float32 [1024, 1024], replicated
- key_grad: float32 [1024, 1024], replicated
- value_grad: float32 [1024, 1024], replicated
- w_out_grad: float32 [1024, 1024], replicated
- bias_table_grad: float32 [32, 16], replicated
- gain_two_grad: float32 [1024], replicated
- router_grad: float32 [1024, 16], replicated
- gate_grad: float32 [16, 1024, 2816], P('expert', None, 'hidden')
- up_grad: float32 [16, 1024, 2816], P('expert', None, 'hidden')
- down_grad: float32 [16, 2816, 1024], P('expert', 'hidden')
The draws below stay inside these ranges and needn't reach their ends.
Inputs may be any that keep to these rules, and one draw needn't show every extreme that they name: `routes`: each row names two different experts; in each aligned block of 256 rows (one micro-batch of one device) no expert is named by more than 40 rows, a bound that some block reaches.
All inputs are finite; a program needn't handle non-finite values.
Results may differ from the reference program's by a relative error of at most 0.015.
Values may be sent and summed in bfloat16 or wider, within the bound.
A program may use at most 384 MiB of HBM per device.

```python
import math
import jax
import jax.numpy as jnp
import numpy as np
from jax import lax

D = 1024
FF = 2816
HEADS = 16
HEAD_DIM = 64
BUCKETS = 32
LEN = 512
MB_TOK = 256
EXPERTS = 16
CAP = 40
TOKENS = 16384
DEVICES = 32


def level_of(own_key, shape, shards, smallest, high):
    def one(axis_at, parts):
        heights = jax.random.uniform(jax.random.fold_in(jax.random.fold_in(own_key, 6), axis_at), (parts,), jnp.float32, smallest / len(shards), high / len(shards))
        return jnp.repeat(jnp.exp(heights), shape[axis_at] // parts).reshape((-1,) + (1,) * (len(shape) - axis_at - 1))

    level = one(*shards[0])
    for cut in shards[1:]:
        level = level * one(*cut)
    return level


def routed_block(stream_key, own, number, rows, amount, top, bound, slope):
    ranking = jax.random.permutation(stream_key, amount)
    crowded, ordinary = shares(amount, rows * top, bound, slope, True), shares(amount, rows * top, bound, slope, False)
    places = jnp.arange(amount)

    def named(lengths, turn):
        used = int((lengths > 0).sum())
        fixed = max(1, used // 4)
        shifted = fixed + (places - fixed + turn * (used - fixed)) % max(1, amount - fixed)
        return jnp.zeros((amount,), jnp.int32).at[ranking[jnp.where(places < fixed, places, shifted)]].set(jnp.asarray(lengths, jnp.int32))

    lengths = jnp.where(number % 4 == 0, named(crowded, number // 4), named(ordinary, number - number // 4 - 1))
    mixed = jax.random.permutation(jax.random.fold_in(own, 3), amount)
    giver, receiver = mixed[0:amount // 2 * 2:2], mixed[1:amount // 2 * 2:2]
    slack = jnp.minimum(lengths[giver] - 1, bound - lengths[receiver]) // 2
    slack = jnp.where((giver == ranking[0]) | (receiver == ranking[0]) | (lengths[receiver] == 0), 0, jnp.maximum(slack, 0))
    shifted = jax.random.randint(jax.random.fold_in(own, 4), (amount // 2,), 0, 1 << 20) % (slack + 1)
    lengths = lengths.at[giver].add(-shifted).at[receiver].add(shifted)
    items = jnp.searchsorted(jnp.cumsum(lengths), jnp.arange(rows * top), side="right").astype(jnp.int32)
    grid = items.reshape(top, rows).T
    grid = grid[jax.random.permutation(jax.random.fold_in(own, 1), rows)]
    turn = jax.random.randint(jax.random.fold_in(own, 2), (rows, 1), 0, top)
    return jnp.take_along_axis(grid, (jnp.arange(top)[None, :] + turn) % top, axis=1)


def shares(number_of, total, most, slope, full):
    weights = [(1 << 20) // math.isqrt(grade ** slope) + 1 for grade in range(1, number_of + 1)]
    largest = most if full else min(most, max(-(-total // number_of), total * weights[0] // sum(weights)))
    least = 1 if total - largest >= number_of - 1 else 0
    counts, rest = [largest] + [least] * (number_of - 1), total - largest - least * (number_of - 1)
    while rest > 0:
        free = [i for i in range(1, number_of) if counts[i] < largest] or [i for i in range(1, number_of) if counts[i] < most]
        whole, left = sum([weights[i] for i in free]), rest
        for i in free:
            more = min(most - counts[i], max(1, left * weights[i] // whole), rest)
            counts[i] = counts[i] + more
            rest = rest - more
    return np.array(counts)


def normal_values(own_key, dims, width, bound, cuts=(), kind=jnp.bfloat16):
    drawn = width * jax.random.normal(own_key, dims, jnp.float32)
    if cuts:
        drawn = drawn * level_of(own_key, dims, cuts, -0.22, 0.18)
    return jnp.clip(drawn, -bound, bound).astype(kind)


def setup_inputs(seed: int = 0) -> dict:
    key_list = jax.random.split(jax.random.key(seed), 15)
    tokens = normal_values(key_list[0], (TOKENS, D), 1.0, 6.0, ((0, 32),))
    gain_one = jnp.clip(1.0 + 0.1 * jax.random.normal(key_list[1], (D,), jnp.float32), 0.5, 1.5)
    w_query = normal_values(key_list[2], (D, D), D ** -0.5, 0.1875)
    w_key = normal_values(key_list[3], (D, D), D ** -0.5, 0.1875)
    w_value = normal_values(key_list[4], (D, D), D ** -0.5, 0.1875)
    w_out = normal_values(key_list[5], (D, D), (D // 64) ** -0.5, 1.5)
    bias_table = normal_values(key_list[6], (BUCKETS, HEADS), 1.0, 4.0, (), jnp.float32)
    gain_two = jnp.clip(1.0 + 0.1 * jax.random.normal(key_list[7], (D,), jnp.float32), 0.5, 1.5)
    w_router = normal_values(key_list[8], (D, EXPERTS), D ** -0.5, 0.1875, (), jnp.float32)
    w_gate = normal_values(key_list[9], (EXPERTS, D, FF), D ** -0.5, 0.1875, ((0, 8), (2, 4)))
    w_up = normal_values(key_list[10], (EXPERTS, D, FF), D ** -0.5, 0.1875, ((0, 8), (2, 4)))
    w_down = normal_values(key_list[11], (EXPERTS, FF, D), FF ** -0.5, 0.109375, ((0, 8), (1, 4)))
    routes_keys = jax.random.split(jax.random.fold_in(key_list[12], 1), TOKENS // MB_TOK)
    routes_turns = jax.random.permutation(jax.random.fold_in(key_list[12], 3), TOKENS // MB_TOK)
    routes = jax.vmap(lambda own, number: routed_block(jax.random.fold_in(key_list[12], 2), own, number, MB_TOK, EXPERTS, 2, CAP, 1))(routes_keys, routes_turns).reshape((TOKENS, 2))
    cotangent = normal_values(key_list[13], (TOKENS, D), 1.0, 6.0, ((0, 32),))
    return {"tokens": tokens, "gain_one": gain_one, "w_query": w_query, "w_key": w_key, "w_value": w_value, "w_out": w_out, "bias_table": bias_table, "gain_two": gain_two, "w_router": w_router, "w_gate": w_gate, "w_up": w_up, "w_down": w_down, "routes": routes, "cotangent": cotangent}


eps = 1e-06
precise = lax.Precision.HIGHEST
thresholds = (12, 16, 23, 32, 46, 64, 91)

@jax.custom_vjp
def low(v):
    return lax.optimization_barrier(v.astype(jnp.bfloat16)).astype(jnp.float32)

@jax.custom_vjp
def low_back(v):
    return v

def low_keep(v):
    return (low(v), None)

def low_pass(kept, grad):
    return (grad,)

def back_keep(v):
    return (v, None)

def back_low(kept, grad):
    return (low(grad),)
low.defvjp(low_keep, low_pass)
low_back.defvjp(back_keep, back_low)

def bucket_ids(length):
    position = jnp.arange(length, dtype=jnp.int32)
    offset = position[None, :] - position[:, None]
    distance = jnp.abs(offset)
    far_bucket = 8 + sum(((distance >= threshold).astype(jnp.int32) for threshold in thresholds))
    near_bucket = jnp.where(distance < 8, distance, far_bucket)
    return near_bucket + 16 * (offset > 0).astype(jnp.int32)

def rms_norm(values, gain):
    return values * lax.rsqrt(lax.optimization_barrier(jnp.mean(values * values, axis=-1, keepdims=True)) + eps) * gain

def attend_one(sequence, gain_one, w_query, w_key, w_value, w_out, bias_table, slots):
    normed = low(rms_norm(sequence, gain_one))

    def project(weight):
        return low_back(low(jnp.dot(normed, weight, precision=precise)))
    query_heads = project(w_query).reshape(LEN, HEADS, HEAD_DIM)
    key_heads = project(w_key).reshape(LEN, HEADS, HEAD_DIM)
    value_heads = project(w_value).reshape(LEN, HEADS, HEAD_DIM)
    bias_rows = jnp.transpose(bias_table[slots], (2, 0, 1))
    scores = jnp.einsum('qhd,khd->hqk', query_heads, key_heads, precision=precise) * HEAD_DIM ** (-0.5)
    scores = low_back(scores + bias_rows)
    soft = jax.nn.softmax(scores, axis=-1)
    mixed_rows = jnp.einsum('hqk,khd->qhd', low(soft), value_heads, precision=precise).reshape(LEN, D)
    mixed_rows = low_back(low(mixed_rows))
    return low_back(jnp.dot(mixed_rows, w_out, precision=precise))

def place_rows(routes):
    blocks = TOKENS // MB_TOK
    flat_routes = routes.reshape(blocks, MB_TOK * 2)
    route_hits = (flat_routes[:, :, None] == jnp.arange(EXPERTS, dtype=jnp.int32)).astype(jnp.int32)
    slot_rank = lax.optimization_barrier(jnp.sum((jnp.cumsum(route_hits, axis=1) - 1) * route_hits, axis=-1))
    block_ids = jnp.arange(blocks, dtype=jnp.int32)[:, None]
    position = (block_ids * CAP + slot_rank).reshape(-1).astype(jnp.int32)
    chosen_expert = routes.reshape(-1).astype(jnp.int32)
    row_ids = jnp.arange(TOKENS * 2, dtype=jnp.int32)
    index_table = jnp.zeros((EXPERTS, blocks * CAP), jnp.int32).at[chosen_expert, position].set(row_ids)
    filled = jnp.zeros((EXPERTS, blocks * CAP), jnp.float32).at[chosen_expert, position].set(1.0)
    back_index = (chosen_expert * (blocks * CAP) + position).astype(jnp.int32)
    return (index_table, filled, back_index)

def expert_outputs(sent, w_gate, w_up, w_down, routes):
    index_table, filled, back_index = place_rows(routes)
    copies = jnp.repeat(sent, 2, axis=0)

    def one_expert(pieces):
        row_ids, live, gate_weight, up_weight, down_weight = pieces
        taken = low_back(copies[row_ids] * live[:, None])
        gate_pre = low_back(jnp.dot(taken, gate_weight, precision=precise))
        up_pre = low_back(jnp.dot(taken, up_weight, precision=precise))
        activation = low(jax.nn.gelu(gate_pre, approximate=True) * up_pre)
        result = low_back(low(jnp.dot(activation, down_weight, precision=precise)))
        return result * live[:, None]
    results = lax.map(jax.checkpoint(one_expert), (index_table, filled, w_gate, w_up, w_down))
    return results.reshape(-1, D)[back_index].reshape(TOKENS, 2, D)

def forward(tokens, gain_one, w_query, w_key, w_value, w_out, bias_table, gain_two, w_router, w_gate, w_up, w_down, routes):
    slots = bucket_ids(LEN)

    def per_sequence(sequence):
        return attend_one(sequence, gain_one, w_query, w_key, w_value, w_out, bias_table, slots)
    attended = lax.map(jax.checkpoint(per_sequence), tokens.reshape(DEVICES, LEN, D)).reshape(TOKENS, D)
    hidden = tokens + attended
    normed_two = rms_norm(hidden, gain_two)
    sent = low(normed_two)
    logits = jnp.dot(normed_two, w_router, precision=precise)
    route_hot = (routes[:, :, None] == jnp.arange(EXPERTS, dtype=jnp.int32)).astype(jnp.float32)
    chosen = lax.optimization_barrier(jnp.sum(route_hot * logits[:, None, :], axis=-1))
    gate_values = jax.nn.softmax(chosen, axis=-1)
    returned = expert_outputs(sent, w_gate, w_up, w_down, routes)
    return hidden + lax.optimization_barrier(jnp.sum(gate_values[:, :, None] * returned, axis=1))

def reference(tokens, gain_one, w_query, w_key, w_value, w_out, bias_table, gain_two, w_router, w_gate, w_up, w_down, routes, cotangent):
    floats = tuple((item.astype(jnp.float32) for item in (tokens, gain_one, w_query, w_key, w_value, w_out, bias_table, gain_two, w_router, w_gate, w_up, w_down)))

    def closed(*params):
        return forward(*params, routes)
    result, pullback = jax.vjp(closed, *floats)
    grads = pullback(cotangent.astype(jnp.float32))
    return (result.astype(jnp.bfloat16), grads[0], grads[1], grads[2], grads[3], grads[4], grads[5], grads[6], grads[7], grads[8], grads[9], grads[10], grads[11])
```

```python
import functools

import jax
import jax.numpy as jnp
from jax import lax
from jax.experimental import pallas as pl
from jax.experimental.pallas import tpu as pltpu
from jax.sharding import PartitionSpec as P

D = 1024
HEADS = 16
HEAD_DIM = 64
BUCKETS = 32
LEN = 512
MICRO = 2
MB_TOK = 256
VMEM = 62 * 1024 * 1024
MESH = pl.DeviceIdType.MESH


eps = 1e-06
precise = lax.Precision.HIGHEST
thresholds = (12, 16, 23, 32, 46, 64, 91)


def bucket_ids(length):
    position = jnp.arange(length, dtype=jnp.int32)
    offset = position[None, :] - position[:, None]
    distance = jnp.abs(offset)
    far_bucket = 8 + sum(((distance >= threshold).astype(jnp.int32) for threshold in thresholds))
    near_bucket = jnp.where(distance < 8, distance, far_bucket)
    return near_bucket + 16 * (offset > 0).astype(jnp.int32)


def contract_last(matrix_a, matrix_b, mode=None):
    return lax.dot_general(
        matrix_a,
        matrix_b,
        (((1,), (1,)), ((), ())),
        precision=mode,
        preferred_element_type=jnp.float32,
    )


def contract_first(matrix_a, matrix_b, mode=None):
    return lax.dot_general(
        matrix_a,
        matrix_b,
        (((0,), (0,)), ((), ())),
        precision=mode,
        preferred_element_type=jnp.float32,
    )


def dot(matrix_a, matrix_b):
    return jnp.dot(matrix_a, matrix_b, preferred_element_type=jnp.float32)


def slot_targets(routes, experts_all, capacity, stride):
    pairs = 2 * MB_TOK
    flat = routes.reshape(-1, pairs)
    hits = (flat[:, :, None] == jnp.arange(experts_all, dtype=jnp.int32)).astype(jnp.bfloat16)
    lower = (
        jnp.arange(pairs, dtype=jnp.int32)[:, None] > jnp.arange(pairs, dtype=jnp.int32)[None, :]
    ).astype(jnp.bfloat16)
    earlier = jnp.einsum("pq,bqe->bpe", lower, hits, preferred_element_type=jnp.float32)
    rank = jnp.sum(earlier * hits.astype(jnp.float32), axis=-1).astype(jnp.int32)
    block = jnp.arange(flat.shape[0], dtype=jnp.int32)[:, None]
    target = flat * stride + block * capacity + rank
    return target.reshape(-1, 2).T


class Plan:
    def __init__(self, n_e, n_h, experts_all, width):
        self.n_e, self.n_h, self.width = n_e, n_h, width
        self.capacity = 10 * MB_TOK // (4 * experts_all)
        self.stride = -(-MICRO * self.capacity // 16) * 16
        self.span = 2 * self.stride
        self.rows = n_e * self.stride
        self.total = n_h * self.rows

    def place(self):
        return lax.axis_index("expert"), lax.axis_index("hidden")


def across(here, mask):
    there, bit = here, 1
    while bit <= mask:
        if mask & bit:
            there = there + bit * (1 - 2 * lax.rem(lax.div(here, bit), 2))
        bit *= 2
    return there


def remote(src, dst, send_sem, recv_sem, device):
    return pltpu.make_async_remote_copy(
        src_ref=src,
        dst_ref=dst,
        send_sem=send_sem,
        recv_sem=recv_sem,
        device_id=device,
        device_id_type=MESH,
    )


def greet(plan):
    e, z = plan.place()
    barrier = pltpu.get_barrier_semaphore()
    for mask in range(1, plan.n_e):
        pl.semaphore_signal(barrier, inc=1, device_id=(across(e, mask), z), device_id_type=MESH)
    for shift in range(1, plan.n_h):
        pl.semaphore_signal(
            barrier, inc=1, device_id=(e, lax.rem(z + shift, plan.n_h)), device_id_type=MESH
        )
    pl.semaphore_wait(barrier, plan.n_e + plan.n_h - 2)


def slot_hits(plan, base, target):
    slots = lax.broadcasted_iota(jnp.int32, (plan.stride, LEN), 0).astype(jnp.float32) + base
    return jnp.where((slots == target[0:1, :]) | (slots == target[1:2, :]), 1.0, 0.0).astype(
        jnp.bfloat16
    )


def slot_base(plan, device, j):
    return (device * plan.span + j * plan.stride).astype(jnp.float32)


class Dispatch:
    def __init__(self, plan, rows, meta, land, out, meta_out, rows_v, meta_v, stage, sems):
        self.plan = plan
        self.rows, self.meta, self.land = rows, meta, land
        self.out, self.meta_out = out, meta_out
        self.rows_v, self.meta_v, self.stage = rows_v, meta_v, stage
        (
            self.z_send,
            self.z_recv,
            self.zm_send,
            self.zm_recv,
            self.a_send,
            self.a_recv,
            self.m_send,
            self.m_recv,
            self.local,
        ) = sems

    @staticmethod
    def sem_shapes(plan):
        dma = pltpu.SemaphoreType.DMA
        n_h, n_e = plan.n_h, plan.n_e
        return [
            dma((n_h,)),
            dma((n_h,)),
            dma((n_h,)),
            dma((n_h,)),
            dma((2, n_e)),
            dma((n_h, n_e)),
            dma((n_h, n_e)),
            dma((n_h, n_e)),
            dma((3,)),
        ]

    def along_z(self, shift):
        e, z = self.plan.place()
        peer = (e, lax.rem(z + self.plan.n_h - shift, self.plan.n_h))
        return (
            remote(
                self.meta,
                self.meta_v.at[shift],
                self.zm_send.at[shift],
                self.zm_recv.at[shift],
                peer,
            ),
            remote(
                self.rows,
                self.land.at[shift],
                self.z_send.at[shift],
                self.z_recv.at[shift],
                peer,
            ),
        )

    def begin(self):
        for shift in range(1, self.plan.n_h):
            for copy in self.along_z(shift):
                copy.start()
        copy = pltpu.make_async_copy(self.meta, self.meta_v.at[0], self.local.at[1])
        copy.start()
        copy.wait()

    def in_plane(self, chunk, mask):
        plan = self.plan
        e, z = plan.place()
        buffer = lax.rem(chunk, 2)
        at = pl.multiple_of((chunk * plan.n_e + mask) * plan.stride, 16)
        return remote(
            self.stage.at[buffer, :, pl.ds(mask * plan.stride, plan.stride), :],
            self.out.at[:, pl.ds(at, plan.stride), :],
            self.a_send.at[buffer, mask],
            self.a_recv.at[chunk, mask],
            (across(e, mask), z),
        )

    def meta_copy(self, chunk, mask):
        e, z = self.plan.place()
        return remote(
            self.meta_v.at[chunk],
            self.meta_out.at[chunk, mask],
            self.m_send.at[chunk, mask],
            self.m_recv.at[chunk, mask],
            (across(e, mask), z),
        )

    def chunk(self, chunk, target_of):
        plan = self.plan
        e, _ = plan.place()
        buffer = lax.rem(chunk, 2)

        @pl.when(chunk == 0)
        def _():
            copy = pltpu.make_async_copy(self.rows, self.rows_v.at[buffer], self.local.at[0])
            copy.start()
            copy.wait()

        @pl.when(chunk > 0)
        def _():
            for copy in self.along_z(chunk):
                copy.wait_recv()
            copy = pltpu.make_async_copy(
                self.land.at[chunk], self.rows_v.at[buffer], self.local.at[0]
            )
            copy.start()
            copy.wait()

        for mask in range(1, plan.n_e):
            self.meta_copy(chunk, mask).start()
        own_meta = pltpu.make_async_copy(
            self.meta_v.at[chunk], self.meta_out.at[chunk, 0], self.local.at[1]
        )
        own_meta.start()

        @pl.when(chunk >= 2)
        def _():
            for mask in range(1, plan.n_e):
                self.in_plane(chunk - 2, mask).wait_send()

        target = target_of(chunk)
        group = min(4, plan.n_e)
        for start in range(0, plan.n_e, group):
            for j in range(2):
                hot = jnp.concatenate(
                    [
                        slot_hits(plan, slot_base(plan, across(e, start + i), j), target)
                        for i in range(group)
                    ],
                    axis=0,
                )
                picked = dot(hot, self.rows_v[buffer]).astype(jnp.bfloat16)
                self.stage[
                    buffer, j, start * plan.stride : (start + group) * plan.stride, :
                ] = picked
            for mask in range(max(start, 1), start + group):
                self.in_plane(chunk, mask).start()
        at = pl.multiple_of(chunk * plan.rows, 16)
        own = pltpu.make_async_copy(
            self.stage.at[buffer, :, pl.ds(0, plan.stride), :],
            self.out.at[:, pl.ds(at, plan.stride), :],
            self.local.at[2],
        )
        own.start()
        own.wait()
        own_meta.wait()

    def arrived(self, chunk):
        for mask in range(1, self.plan.n_e):
            self.meta_copy(chunk, mask).wait_recv()
            self.in_plane(chunk, mask).wait_recv()

    def finish(self):
        plan = self.plan
        for chunk in range(max(0, plan.n_h - 2), plan.n_h):
            for mask in range(1, plan.n_e):
                self.in_plane(chunk, mask).wait_send()
        for shift in range(1, plan.n_h):
            for copy in self.along_z(shift):
                copy.wait_send()
        for chunk in range(plan.n_h):
            for mask in range(1, plan.n_e):
                self.meta_copy(chunk, mask).wait_send()


class Return:
    def __init__(self, plan, back, land, out, stage, rows_v, total, sems):
        self.plan = plan
        self.back, self.land, self.out = back, land, out
        self.stage, self.rows_v, self.total = stage, rows_v, total
        (self.b_send, self.b_recv, self.s_send, self.s_recv, self.local, self.own) = sems

    @staticmethod
    def sem_shapes(plan):
        dma = pltpu.SemaphoreType.DMA
        n_h, n_e = plan.n_h, plan.n_e
        return [
            dma((n_h, n_e)),
            dma((n_h, n_e)),
            dma((n_h,)),
            dma((n_h,)),
            dma((2,)),
            dma((n_h,)),
        ]

    def source(self, chunk, mask):
        raise NotImplementedError

    def in_plane(self, chunk, mask):
        plan = self.plan
        e, z = plan.place()
        return remote(
            self.source(chunk, mask),
            self.back.at[chunk, :, pl.ds(mask * plan.stride, plan.stride), :],
            self.b_send.at[chunk, mask],
            self.b_recv.at[chunk, mask],
            (across(e, mask), z),
        )

    def own_copy(self, chunk):
        plan = self.plan
        return pltpu.make_async_copy(
            self.source(chunk, 0),
            self.back.at[chunk, :, pl.ds(0, plan.stride), :],
            self.own.at[chunk],
        )

    def send(self, chunk):
        for mask in range(1, self.plan.n_e):
            self.in_plane(chunk, mask).start()
        self.own_copy(chunk).start()

    def along_z(self, chunk):
        e, z = self.plan.place()
        return remote(
            self.rows_v.at[lax.rem(chunk, 2)],
            self.land.at[chunk],
            self.s_send.at[chunk],
            self.s_recv.at[chunk],
            (e, lax.rem(z + chunk, self.plan.n_h)),
        )

    def combine(self, chunk, target):
        plan = self.plan
        e, _ = plan.place()
        buffer = lax.rem(chunk, 2)
        for mask in range(1, plan.n_e):
            self.in_plane(chunk, mask).wait_recv()
        self.own_copy(chunk).wait()
        copy = pltpu.make_async_copy(self.back.at[chunk], self.stage.at[buffer], self.local.at[0])
        copy.start()
        hot = [
            jnp.concatenate(
                [
                    slot_hits(plan, slot_base(plan, across(e, mask), j), target)
                    for mask in range(plan.n_e)
                ],
                axis=0,
            )
            for j in range(2)
        ]
        copy.wait()

        @pl.when(chunk >= 3)
        def _():
            self.along_z(chunk - 2).wait_send()

        part = contract_first(hot[0], self.stage[buffer, 0]) + contract_first(
            hot[1], self.stage[buffer, 1]
        )

        @pl.when(chunk == 0)
        def _():
            self.total[...] = part

        @pl.when(chunk > 0)
        def _():
            self.rows_v[buffer] = part.astype(jnp.bfloat16)
            self.along_z(chunk).start()

    def finish(self):
        plan = self.plan
        for chunk in range(max(1, plan.n_h - 2), plan.n_h):
            self.along_z(chunk).wait_send()
        for chunk in range(1, plan.n_h):
            self.along_z(chunk).wait_recv()
            copy = pltpu.make_async_copy(
                self.land.at[chunk], self.rows_v.at[chunk % 2], self.local.at[0]
            )
            copy.start()
            copy.wait()
            self.total[...] += self.rows_v[chunk % 2].astype(jnp.float32)
        copy = pltpu.make_async_copy(self.total, self.out, self.local.at[0])
        copy.start()
        copy.wait()


class ReturnHeld(Return):
    def __init__(self, plan, given, *rest):
        super().__init__(plan, *rest)
        self.given = given

    def source(self, chunk, mask):
        plan = self.plan
        at = pl.multiple_of((chunk * plan.n_e + mask) * plan.stride, 16)
        return self.given.at[:, pl.ds(at, plan.stride), :]

    def sent(self):
        for chunk in range(self.plan.n_h):
            for mask in range(1, self.plan.n_e):
                self.in_plane(chunk, mask).wait_send()


class ReturnMade(Return):
    def __init__(self, plan, made, *rest):
        super().__init__(plan, *rest)
        self.made = made
        self.ring = made.shape[0]

    def source(self, chunk, mask):
        plan = self.plan
        return self.made.at[
            lax.rem(chunk, self.ring), :, pl.ds(mask * plan.stride, plan.stride), :
        ]

    def free(self, chunk):
        if self.plan.n_h > self.ring:

            @pl.when(chunk >= self.ring)
            def _():
                self.wait_sent(chunk - self.ring)
                self.own_copy(chunk - self.ring).wait()

    def wait_sent(self, chunk):
        for mask in range(1, self.plan.n_e):
            self.in_plane(chunk, mask).wait_send()

    def sent(self):
        for chunk in range(max(0, self.plan.n_h - self.ring), self.plan.n_h):
            self.wait_sent(chunk)


ANY = pl.BlockSpec(memory_space=pl.ANY)


def send_body(plan, rows, meta, out, meta_out, land, rows_v, meta_v, stage, *sems):
    greet(plan)
    work = Dispatch(plan, rows, meta, land, out, meta_out, rows_v, meta_v, stage, sems)
    work.begin()
    pl.loop(0, plan.n_h)(lambda chunk: work.chunk(chunk, lambda at: meta_v[at]))
    for chunk in range(plan.n_h):
        work.arrived(chunk)
    work.finish()


def send_rows(plan, rows, meta):
    n_h, n_e = plan.n_h, plan.n_e
    out = pl.pallas_call(
        functools.partial(send_body, plan),
        in_specs=[ANY, ANY],
        out_specs=[ANY, ANY, ANY],
        out_shape=[
            jax.ShapeDtypeStruct((2, plan.total, D), jnp.bfloat16),
            jax.ShapeDtypeStruct((n_h, n_e, 8, LEN), jnp.float32),
            jax.ShapeDtypeStruct((n_h, LEN, D), jnp.bfloat16),
        ],
        scratch_shapes=[
            pltpu.VMEM((2, LEN, D), jnp.bfloat16),
            pltpu.VMEM((n_h, 8, LEN), jnp.float32),
            pltpu.VMEM((2, 2, plan.rows, D), jnp.bfloat16),
        ]
        + Dispatch.sem_shapes(plan),
        compiler_params=pltpu.CompilerParams(
            collective_id=1, has_side_effects=True, vmem_limit_bytes=VMEM
        ),
        name="send_rows",
    )(rows, meta)
    return out[0], out[1]


def expert_body(plan, halves, n_d, *refs):
    (
        sent,
        gates,
        grads,
        targets,
        w_gate,
        w_up,
        w_down,
        total_out,
        gg_out,
        rows_out,
        y_out,
        dgate_out,
        dup_out,
        act_out,
        meta_out,
        land,
        back,
        land_back,
        rows_v,
        meta_v,
        stage,
        wg_v,
        wu_v,
        wd_v,
        target_v,
        gate_v,
        x_v,
        g_v,
        dx_v,
        y_v,
        dgate_v,
        dup_v,
        act_v,
        gg_v,
        gg_back,
        gg_part,
        gg_land,
        total,
        w_sem,
        t_sem,
        x_sem,
        o_sem,
        gg_send,
        gg_recv,
        ggs_send,
        ggs_recv,
        *sems,
    ) = refs
    n_e, n_h = plan.n_e, plan.n_h
    e, z = plan.place()
    loads = [
        pltpu.make_async_copy(source, held, w_sem.at[i])
        for i, (source, held) in enumerate(((w_gate, wg_v), (w_up, wu_v), (w_down, wd_v)))
    ]
    for load in loads:
        load.start()
    targets_in = pltpu.make_async_copy(targets, target_v, t_sem.at[0])
    targets_in.start()
    greet(plan)
    work = Dispatch(
        plan, sent, gates, land, rows_out, meta_out, rows_v, meta_v, stage, sems[:n_d]
    )
    give = ReturnMade(
        plan, dx_v, back, land_back, total_out, stage, rows_v, total, sems[n_d:]
    )
    work.begin()
    targets_in.wait()
    ahead = min(3, n_h)
    pl.loop(0, ahead)(lambda chunk: work.chunk(chunk, lambda at: target_v[at, 0]))
    for load in loads:
        load.wait()

    def gg_copy(chunk, mask):
        return remote(
            gg_v.at[chunk, mask],
            gg_back.at[chunk, mask],
            gg_send.at[chunk, mask],
            gg_recv.at[chunk, mask],
            (across(e, mask), z),
        )

    def gg_along(chunk):
        return remote(
            gg_part.at[chunk],
            gg_land.at[chunk],
            ggs_send.at[chunk],
            ggs_recv.at[chunk],
            (e, lax.rem(z + chunk, n_h)),
        )

    def outs(chunk, j):
        at = pl.multiple_of(chunk * plan.rows, 16)
        return [
            pltpu.make_async_copy(held.at[j], out.at[j, pl.ds(at, plan.rows), :], o_sem.at[i, j])
            for i, (held, out) in enumerate(
                ((y_v, y_out), (dgate_v, dgate_out), (dup_v, dup_out), (act_v, act_out))
            )
        ]

    masks = n_e // halves
    piece = masks * plan.stride

    def step(chunk, index):
        j, half = lax.div(index, halves), lax.rem(index, halves)
        at = pl.ds(pl.multiple_of(half * piece, 16), piece)
        rows, grads_in = x_v[j, at, :], g_v[j, at, :]
        gate_pre = dot(rows, wg_v[j])
        up_pre = dot(rows, wu_v[j])
        raw = contract_last(grads_in, wd_v[j])
        slots = lax.broadcasted_iota(jnp.int32, (plan.stride, LEN), 0).astype(
            jnp.float32
        ) + slot_base(plan, e, j)
        columns = []
        for i in range(masks):
            mask = half * masks + i
            aim, weight = target_v[chunk, mask], gate_v[mask]
            hit = jnp.where(slots == aim[0:1, :], weight[0:1, :], 0.0)
            hit = hit + jnp.where(slots == aim[1:2, :], weight[1:2, :], 0.0)
            columns.append(jnp.sum(hit, axis=1, keepdims=True))
        gate = jnp.concatenate(columns, axis=0)
        square = gate_pre * gate_pre
        tanh = jnp.tanh(0.7978845608028654 * gate_pre * (1.0 + 0.044715 * square))
        side = 0.5 * (1.0 + tanh)
        gelu = gate_pre * side
        slope = side + 0.5 * gate_pre * (1.0 - tanh * tanh) * (
            0.7978845608028654 * (1.0 + 0.134145 * square)
        )
        act = gelu * up_pre
        act_low = act.astype(jnp.bfloat16)
        dots = jnp.sum(act_low.astype(jnp.float32) * raw, axis=1, keepdims=True)
        for i in range(masks):
            mask = half * masks + i
            aim, part = target_v[chunk, mask], dots[i * plan.stride : (i + 1) * plan.stride]
            for k in range(2):
                line = jnp.sum(
                    jnp.where(slots == aim[k : k + 1, :], part, 0.0), axis=0, keepdims=True
                )
                gg_v[chunk, mask, k : k + 1, :] += line
        grad_act = gate * raw
        grad_gate = (grad_act * up_pre * slope).astype(jnp.bfloat16)
        grad_up = (grad_act * gelu).astype(jnp.bfloat16)
        dgate_v[j, at, :] = grad_gate
        dup_v[j, at, :] = grad_up
        act_v[j, at, :] = (act * gate).astype(jnp.bfloat16)
        dx_v[lax.rem(chunk, dx_v.shape[0]), j, at, :] = (
            contract_last(grad_gate, wg_v[j]) + contract_last(grad_up, wu_v[j])
        ).astype(jnp.bfloat16)
        y_v[j, at, :] = (dot(act_low, wd_v[j]) * gate).astype(jnp.bfloat16)

    gg_v[...] = jnp.zeros_like(gg_v)

    @pl.loop(0, n_h)
    def _(chunk):
        work.arrived(chunk)
        at = pl.multiple_of(chunk * plan.rows, 16)
        gate_in = pltpu.make_async_copy(meta_out.at[chunk], gate_v, t_sem.at[0])
        gate_in.start()
        ins = [
            pltpu.make_async_copy(source.at[:, pl.ds(at, plan.rows), :], held, x_sem.at[i])
            for i, (source, held) in enumerate(((rows_out, x_v), (grads, g_v)))
        ]
        for copy in ins:
            copy.start()
        give.free(chunk)

        @pl.when(chunk > 0)
        def _():
            for j in range(2):
                for copy in outs(chunk - 1, j):
                    copy.wait()

        gate_in.wait()
        for copy in ins:
            copy.wait()
        pl.loop(0, 2 * halves)(lambda index: step(chunk, index))
        for mask in range(1, n_e):
            gg_copy(chunk, mask).start()
        give.send(chunk)
        for j in range(2):
            for copy in outs(chunk, j):
                copy.start()

        @pl.when(chunk + ahead < n_h)
        def _():
            work.chunk(chunk + ahead, lambda at: target_v[at, 0])

    work.finish()
    for j in range(2):
        for copy in outs(n_h - 1, j):
            copy.wait()

    @pl.loop(0, n_h)
    def _(chunk):
        part = gg_v[chunk, 0]
        for mask in range(1, n_e):
            gg_copy(chunk, mask).wait_recv()
            part = part + gg_back[chunk, mask]
        gg_part[chunk] = part

        @pl.when(chunk > 0)
        def _():
            gg_along(chunk).start()

        give.combine(chunk, target_v[chunk, 0])

    give.sent()
    for chunk in range(n_h):
        for mask in range(1, n_e):
            gg_copy(chunk, mask).wait_send()
    sum_gg = gg_part[0]
    for chunk in range(1, n_h):
        gg_along(chunk).wait_recv()
        sum_gg = sum_gg + gg_land[chunk]
    gg_out[...] = sum_gg
    for chunk in range(1, n_h):
        gg_along(chunk).wait_send()
    give.finish()


def run_experts(plan, sent, gates, grads, targets, w_gate, w_up, w_down):
    n_h, n_e, width = plan.n_h, plan.n_e, plan.width
    bf16, f32 = jnp.bfloat16, jnp.float32
    shape = jax.ShapeDtypeStruct
    dma = pltpu.SemaphoreType.DMA
    ring = min(4, n_h)
    d_sems, r_sems = Dispatch.sem_shapes(plan), Return.sem_shapes(plan)
    halves = 2 if plan.rows <= 640 else 4
    return pl.pallas_call(
        functools.partial(expert_body, plan, halves, len(d_sems)),
        in_specs=[ANY] * 7,
        out_specs=[ANY, pl.BlockSpec(memory_space=pltpu.VMEM)] + [ANY] * 9,
        out_shape=[
            shape((LEN, D), f32),
            shape((8, LEN), f32),
            shape((2, plan.total, D), bf16),
            shape((2, plan.total, D), bf16),
            shape((2, plan.total, width), bf16),
            shape((2, plan.total, width), bf16),
            shape((2, plan.total, width), bf16),
            shape((n_h, n_e, 8, LEN), f32),
            shape((n_h, LEN, D), bf16),
            shape((n_h, 2, plan.rows, D), bf16),
            shape((n_h, LEN, D), bf16),
        ],
        scratch_shapes=[
            pltpu.VMEM((2, LEN, D), bf16),
            pltpu.VMEM((n_h, 8, LEN), f32),
            pltpu.VMEM((2, 2, plan.rows, D), bf16),
            pltpu.VMEM((2, D, width), bf16),
            pltpu.VMEM((2, D, width), bf16),
            pltpu.VMEM((2, width, D), bf16),
            pltpu.VMEM((n_h, n_e, 8, LEN), f32),
            pltpu.VMEM((n_e, 8, LEN), f32),
            pltpu.VMEM((2, plan.rows, D), bf16),
            pltpu.VMEM((2, plan.rows, D), bf16),
            pltpu.VMEM((ring, 2, plan.rows, D), bf16),
            pltpu.VMEM((2, plan.rows, D), bf16),
            pltpu.VMEM((2, plan.rows, width), bf16),
            pltpu.VMEM((2, plan.rows, width), bf16),
            pltpu.VMEM((2, plan.rows, width), bf16),
            pltpu.VMEM((n_h, n_e, 8, LEN), f32),
            pltpu.VMEM((n_h, n_e, 8, LEN), f32),
            pltpu.VMEM((n_h, 8, LEN), f32),
            pltpu.VMEM((n_h, 8, LEN), f32),
            pltpu.VMEM((LEN, D), f32),
            dma((3,)),
            dma((1,)),
            dma((2,)),
            dma((4, 2)),
            dma((n_h, n_e)),
            dma((n_h, n_e)),
            dma((n_h,)),
            dma((n_h,)),
        ]
        + d_sems
        + r_sems,
        compiler_params=pltpu.CompilerParams(
            collective_id=2, has_side_effects=True, vmem_limit_bytes=VMEM
        ),
        name="run_experts",
    )(sent, gates, grads, targets, w_gate, w_up, w_down)


def back_body(plan, given, targets, out, back, land, rows_v, stage, target_v, total, t_sem, *sems):
    targets_in = pltpu.make_async_copy(targets, target_v, t_sem.at[0])
    targets_in.start()
    greet(plan)
    give = ReturnHeld(plan, given, back, land, out, stage, rows_v, total, sems)
    for chunk in range(plan.n_h):
        give.send(chunk)
    targets_in.wait()
    pl.loop(0, plan.n_h)(lambda chunk: give.combine(chunk, target_v[chunk, 0]))
    give.sent()
    give.finish()


def bring_back(plan, given, targets):
    n_h, n_e = plan.n_h, plan.n_e
    bf16, f32 = jnp.bfloat16, jnp.float32
    shape = jax.ShapeDtypeStruct
    return pl.pallas_call(
        functools.partial(back_body, plan),
        in_specs=[ANY, ANY],
        out_specs=[ANY] * 3,
        out_shape=[
            shape((LEN, D), f32),
            shape((n_h, 2, plan.rows, D), bf16),
            shape((n_h, LEN, D), bf16),
        ],
        scratch_shapes=[
            pltpu.VMEM((2, LEN, D), bf16),
            pltpu.VMEM((2, 2, plan.rows, D), bf16),
            pltpu.VMEM((n_h, n_e, 8, LEN), f32),
            pltpu.VMEM((LEN, D), f32),
            pltpu.SemaphoreType.DMA((1,)),
        ]
        + Return.sem_shapes(plan),
        compiler_params=pltpu.CompilerParams(
            collective_id=3, has_side_effects=True, vmem_limit_bytes=VMEM
        ),
        name="bring_back",
    )(given, targets)[0]


def per_device(
    n_e,
    n_h,
    tokens,
    gain_one,
    w_query,
    w_key,
    w_value,
    w_out,
    bias_table,
    gain_two,
    w_router,
    w_gate,
    w_up,
    w_down,
    routes,
    cotangent,
):
    experts_all = w_router.shape[1]
    plan = Plan(n_e, n_h, experts_all, w_gate.shape[2])
    both = ("expert", "hidden")

    def small(array):
        return jnp.pad(array.astype(jnp.float32), ((0, 6), (0, 0)))

    targets = small(slot_targets(routes, experts_all, plan.capacity, plan.stride))
    grads_in, targets_all = send_rows(plan, cotangent, targets)
    scaling = HEAD_DIM ** (-0.5)
    bucket_hot = (bucket_ids(LEN)[:, :, None] == jnp.arange(BUCKETS, dtype=jnp.int32)).astype(
        jnp.float32
    )
    inputs = tokens.astype(jnp.float32)
    inv_one = lax.rsqrt(jnp.mean(inputs * inputs, axis=-1, keepdims=True) + eps)
    normed_one = (inputs * inv_one * gain_one).astype(jnp.bfloat16)
    query_rows = jnp.dot(normed_one, w_query, preferred_element_type=jnp.float32).astype(
        jnp.bfloat16
    )
    key_rows = jnp.dot(normed_one, w_key, preferred_element_type=jnp.float32).astype(jnp.bfloat16)
    value_rows = jnp.dot(normed_one, w_value, preferred_element_type=jnp.float32).astype(
        jnp.bfloat16
    )
    query_heads = query_rows.reshape(LEN, HEADS, HEAD_DIM)
    key_heads = key_rows.reshape(LEN, HEADS, HEAD_DIM)
    value_heads = value_rows.reshape(LEN, HEADS, HEAD_DIM)
    bias_rows = jnp.einsum("ijb,bh->hij", bucket_hot, bias_table, precision=precise)

    def score_of():
        raw = jnp.einsum("qhd,khd->hqk", query_heads, key_heads, preferred_element_type=jnp.float32)
        return raw * scaling + bias_rows

    scores = score_of()
    row_peak = jnp.max(scores, axis=-1, keepdims=True)
    exp_terms = jnp.exp(scores - row_peak)
    row_total = jnp.sum(exp_terms, axis=-1, keepdims=True)
    log_total = row_peak + jnp.log(row_total)
    soft_low = (exp_terms / row_total).astype(jnp.bfloat16)
    mixed_rows = jnp.einsum(
        "hqk,khd->qhd", soft_low, value_heads, preferred_element_type=jnp.float32
    )
    mixed_rows = mixed_rows.reshape(LEN, D).astype(jnp.bfloat16)
    hidden = inputs + jnp.dot(mixed_rows, w_out, preferred_element_type=jnp.float32)
    inv_two = lax.rsqrt(jnp.mean(hidden * hidden, axis=-1, keepdims=True) + eps)
    normed_two = hidden * inv_two * gain_two
    sent = normed_two.astype(jnp.bfloat16)
    logits = jnp.dot(normed_two, w_router, precision=precise)
    route_hot = (routes[:, :, None] == jnp.arange(experts_all, dtype=jnp.int32)).astype(jnp.float32)
    chosen = jnp.sum(route_hot * logits[:, None, :], axis=-1)
    gate_values = jax.nn.softmax(chosen, axis=-1)
    grad_sent, grad_gates, rows_in, y_rows, gate_rows, up_rows, act_rows = run_experts(
        plan, sent, small(gate_values.T), grads_in, targets_all, w_gate, w_up, w_down
    )[:7]
    branch = bring_back(plan, y_rows, targets_all)
    grad_gates = grad_gates[:2].T
    block_out = (hidden + branch).astype(jnp.bfloat16)
    down_grad = jnp.einsum("xrf,xrd->xfd", act_rows, grads_in, preferred_element_type=jnp.float32)
    gate_grad = jnp.einsum("xrd,xrf->xdf", rows_in, gate_rows, preferred_element_type=jnp.float32)
    up_grad = jnp.einsum("xrd,xrf->xdf", rows_in, up_rows, preferred_element_type=jnp.float32)
    grad_out = cotangent.astype(jnp.float32)
    grad_chosen = gate_values * (
        grad_gates - jnp.sum(gate_values * grad_gates, axis=-1, keepdims=True)
    )
    grad_logits = jnp.sum(route_hot * grad_chosen[:, :, None], axis=1)
    router_grad = contract_first(normed_two, grad_logits, precise)
    grad_normed_two = contract_last(grad_logits, w_router, precise)
    grad_normed_two = grad_normed_two + grad_sent.astype(jnp.float32)
    gain_two_grad = jnp.sum(grad_normed_two * hidden * inv_two, axis=0)
    scaled_two = grad_normed_two * gain_two
    grad_hidden = (
        grad_out
        + inv_two * scaled_two
        - hidden * inv_two**3 * jnp.mean(scaled_two * hidden, axis=-1, keepdims=True)
    )
    grad_branch = grad_hidden.astype(jnp.bfloat16)
    w_out_grad = contract_first(mixed_rows, grad_branch)
    grad_mixed = (
        contract_last(grad_branch, w_out).astype(jnp.bfloat16).reshape(LEN, HEADS, HEAD_DIM)
    )
    soft_again = jnp.exp(score_of() - log_total)
    soft_again_low = soft_again.astype(jnp.bfloat16)
    grad_value_heads = jnp.einsum(
        "hqk,qhd->khd", soft_again_low, grad_mixed, preferred_element_type=jnp.float32
    )
    grad_value_rows = grad_value_heads.astype(jnp.bfloat16).reshape(LEN, D)
    grad_soft = jnp.einsum(
        "qhd,khd->hqk", grad_mixed, value_heads, preferred_element_type=jnp.float32
    )
    grad_scores = soft_again * (grad_soft - jnp.sum(soft_again * grad_soft, axis=-1, keepdims=True))
    grad_scores = grad_scores.astype(jnp.bfloat16)
    bias_table_grad = jnp.einsum(
        "hij,ijb->bh", grad_scores.astype(jnp.float32), bucket_hot, precision=precise
    )
    grad_query_rows = (
        jnp.einsum("hqk,khd->qhd", grad_scores, key_heads, preferred_element_type=jnp.float32)
        * scaling
    )
    grad_query_rows = grad_query_rows.astype(jnp.bfloat16).reshape(LEN, D)
    grad_key_rows = (
        jnp.einsum("hqk,qhd->khd", grad_scores, query_heads, preferred_element_type=jnp.float32)
        * scaling
    )
    grad_key_rows = grad_key_rows.astype(jnp.bfloat16).reshape(LEN, D)
    query_grad = contract_first(normed_one, grad_query_rows)
    key_grad = contract_first(normed_one, grad_key_rows)
    value_grad = contract_first(normed_one, grad_value_rows)
    grad_normed_one = (
        contract_last(grad_query_rows, w_query)
        + contract_last(grad_key_rows, w_key)
        + contract_last(grad_value_rows, w_value)
    )
    gain_one_grad = jnp.sum(grad_normed_one * inputs * inv_one, axis=0)
    scaled_one = grad_normed_one * gain_one
    tokens_grad = (
        grad_hidden
        + inv_one * scaled_one
        - inputs * inv_one**3 * jnp.mean(scaled_one * inputs, axis=-1, keepdims=True)
    )
    query_grad, key_grad, value_grad, w_out_grad = [
        item.astype(jnp.float32)
        for item in lax.psum(
            [
                item.astype(jnp.bfloat16)
                for item in (query_grad, key_grad, value_grad, w_out_grad)
            ],
            both,
        )
    ]
    bias_table_grad, gain_one_grad, gain_two_grad, router_grad = lax.psum(
        (bias_table_grad, gain_one_grad, gain_two_grad, router_grad), both
    )
    return (
        block_out,
        tokens_grad,
        gain_one_grad,
        query_grad,
        key_grad,
        value_grad,
        w_out_grad,
        bias_table_grad,
        gain_two_grad,
        router_grad,
        gate_grad,
        up_grad,
        down_grad,
    )


def solution(mesh):
    in_specs = (
        P(("expert", "hidden"), None),
        P(),
        P(),
        P(),
        P(),
        P(),
        P(),
        P(),
        P(),
        P("expert", None, "hidden"),
        P("expert", None, "hidden"),
        P("expert", "hidden", None),
        P(("expert", "hidden"), None),
        P(("expert", "hidden"), None),
    )
    out_specs = (
        P(("expert", "hidden"), None),
        P(("expert", "hidden"), None),
        P(),
        P(),
        P(),
        P(),
        P(),
        P(),
        P(),
        P(),
        P("expert", None, "hidden"),
        P("expert", None, "hidden"),
        P("expert", "hidden", None),
    )
    return jax.shard_map(
        functools.partial(per_device, mesh.shape["expert"], mesh.shape["hidden"]),
        mesh=mesh, in_specs=in_specs, out_specs=out_specs, check_vma=False
    )
```

```python
import functools

import jax
import jax.numpy as jnp
from jax import lax
from jax.experimental import pallas as pl
from jax.experimental.pallas import tpu as pltpu
from jax.sharding import PartitionSpec as P

D = 1024
HEADS = 16
HEAD_DIM = 64
BUCKETS = 32
LEN = 512
MICRO = 2
MB_TOK = 256
VMEM = 62 * 1024 * 1024
MESH = pl.DeviceIdType.MESH


eps = 1e-06
precise = lax.Precision.HIGHEST
thresholds = (12, 16, 23, 32, 46, 64, 91)


def contract_last(matrix_a, matrix_b, mode=None):
    return lax.dot_general(
        matrix_a,
        matrix_b,
        (((1,), (1,)), ((), ())),
        precision=mode,
        preferred_element_type=jnp.float32,
    )


def contract_first(matrix_a, matrix_b, mode=None):
    return lax.dot_general(
        matrix_a,
        matrix_b,
        (((0,), (0,)), ((), ())),
        precision=mode,
        preferred_element_type=jnp.float32,
    )


def dot(matrix_a, matrix_b):
    return jnp.dot(matrix_a, matrix_b, preferred_element_type=jnp.float32)


def slot_targets(routes, experts_all, capacity, stride):
    pairs = 2 * MB_TOK
    flat = routes.reshape(-1, pairs)
    hits = (flat[:, :, None] == jnp.arange(experts_all, dtype=jnp.int32)).astype(jnp.bfloat16)
    lower = (
        jnp.arange(pairs, dtype=jnp.int32)[:, None] > jnp.arange(pairs, dtype=jnp.int32)[None, :]
    ).astype(jnp.bfloat16)
    earlier = jnp.einsum("pq,bqe->bpe", lower, hits, preferred_element_type=jnp.float32)
    rank = jnp.sum(earlier * hits.astype(jnp.float32), axis=-1).astype(jnp.int32)
    block = jnp.arange(flat.shape[0], dtype=jnp.int32)[:, None]
    target = flat * stride + block * capacity + rank
    return target.reshape(-1, 2).T


class Plan:
    def __init__(self, n_e, n_h, experts_all, width):
        self.n_e, self.n_h, self.width = n_e, n_h, width
        self.capacity = 10 * MB_TOK // (4 * experts_all)
        self.stride = -(-MICRO * self.capacity // 16) * 16
        self.span = 2 * self.stride
        self.rows = n_e * self.stride
        self.total = n_h * self.rows

    def place(self):
        return lax.axis_index("expert"), lax.axis_index("hidden")

    def source(self, z, chunk):
        sign = 1 - 2 * lax.div(z, self.n_h // 2)
        return lax.rem(z + self.n_h + sign * chunk, self.n_h)


def across(here, mask):
    there, bit = here, 1
    while bit <= mask:
        if mask & bit:
            there = there + bit * (1 - 2 * lax.rem(lax.div(here, bit), 2))
        bit *= 2
    return there


def remote(src, dst, send_sem, recv_sem, device):
    return pltpu.make_async_remote_copy(
        src_ref=src,
        dst_ref=dst,
        send_sem=send_sem,
        recv_sem=recv_sem,
        device_id=device,
        device_id_type=MESH,
    )


def greet(plan):
    e, z = plan.place()
    barrier = pltpu.get_barrier_semaphore()
    for mask in range(1, plan.n_e):
        pl.semaphore_signal(barrier, inc=1, device_id=(across(e, mask), z), device_id_type=MESH)
    for shift in range(1, plan.n_h):
        pl.semaphore_signal(
            barrier, inc=1, device_id=(e, lax.rem(z + shift, plan.n_h)), device_id_type=MESH
        )
    pl.semaphore_wait(barrier, plan.n_e + plan.n_h - 2)


def slot_hits(plan, base, target):
    slots = lax.broadcasted_iota(jnp.int32, (plan.stride, LEN), 0).astype(jnp.float32) + base
    return jnp.where((slots == target[0:1, :]) | (slots == target[1:2, :]), 1.0, 0.0).astype(
        jnp.bfloat16
    )


def slot_base(plan, device, j):
    return (device * plan.span + j * plan.stride).astype(jnp.float32)


class Dispatch:
    def __init__(self, plan, rows, meta, land, out, meta_out, rows_v, meta_v, stage, sems):
        self.plan = plan
        self.rows, self.meta, self.land = rows, meta, land
        self.out, self.meta_out = out, meta_out
        self.rows_v, self.meta_v, self.stage = rows_v, meta_v, stage
        (
            self.z_send,
            self.z_recv,
            self.zm_send,
            self.zm_recv,
            self.a_send,
            self.a_recv,
            self.m_send,
            self.m_recv,
            self.local,
        ) = sems

    @staticmethod
    def sem_shapes(plan):
        dma = pltpu.SemaphoreType.DMA
        n_h, n_e = plan.n_h, plan.n_e
        return [
            dma((n_h, 2)),
            dma((n_h,)),
            dma((n_h, 2)),
            dma((n_h,)),
            dma((2, n_e)),
            dma((n_h, n_e)),
            dma((n_h, n_e)),
            dma((n_h, n_e)),
            dma((3,)),
        ]

    def hop(self, source, way, own):
        e, z = self.plan.place()
        sems = [
            (self.z_send.at[source, (way + 1) // 2], self.z_recv.at[source]),
            (self.zm_send.at[source, (way + 1) // 2], self.zm_recv.at[source]),
        ]
        return (
            remote(self.meta_v.at[source], self.meta_v.at[source], *sems[1], (e, z + way)),
            remote(
                self.rows if own else self.land.at[source],
                self.land.at[source],
                *sems[0],
                (e, z + way),
            ),
        )

    def on_the_way(self, distance, act):
        n_h = self.plan.n_h
        _, z = self.plan.place()

        @pl.when(z + distance < n_h)
        def _():
            act(z + distance, z > 0, -1)

        @pl.when(z >= distance)
        def _():
            act(z - distance, z < n_h - 1, 1)

    def begin(self):
        _, z = self.plan.place()
        copy = pltpu.make_async_copy(self.meta, self.meta_v.at[z], self.local.at[1])
        copy.start()
        copy.wait()

        @pl.when(z > 0)
        def _():
            for copy in self.hop(z, -1, True):
                copy.start()

        @pl.when(z < self.plan.n_h - 1)
        def _():
            for copy in self.hop(z, 1, True):
                copy.start()

    def pass_on(self, distance):
        def act(source, forwarded, way):
            for copy in self.hop(source, way, False):
                copy.wait_recv()

            @pl.when(forwarded)
            def _():
                for copy in self.hop(source, way, False):
                    copy.start()

        self.on_the_way(distance, act)

    def in_plane(self, chunk, mask):
        plan = self.plan
        e, z = plan.place()
        buffer = lax.rem(chunk, 2)
        at = pl.multiple_of((chunk * plan.n_e + mask) * plan.stride, 16)
        return remote(
            self.stage.at[buffer, :, pl.ds(mask * plan.stride, plan.stride), :],
            self.out.at[:, pl.ds(at, plan.stride), :],
            self.a_send.at[buffer, mask],
            self.a_recv.at[chunk, mask],
            (across(e, mask), z),
        )

    def meta_copy(self, chunk, mask):
        e, z = self.plan.place()
        return remote(
            self.meta_v.at[self.plan.source(z, chunk)],
            self.meta_out.at[chunk, mask],
            self.m_send.at[chunk, mask],
            self.m_recv.at[chunk, mask],
            (across(e, mask), z),
        )

    def chunk(self, chunk, target_of):
        plan = self.plan
        e, z = plan.place()
        buffer = lax.rem(chunk, 2)
        source = plan.source(z, chunk)

        @pl.when(chunk == 0)
        def _():
            copy = pltpu.make_async_copy(self.rows, self.rows_v.at[buffer], self.local.at[0])
            copy.start()
            copy.wait()

        @pl.when(chunk > 0)
        def _():
            self.pass_on(chunk)
            copy = pltpu.make_async_copy(
                self.land.at[source], self.rows_v.at[buffer], self.local.at[0]
            )
            copy.start()
            copy.wait()

        for mask in range(1, plan.n_e):
            self.meta_copy(chunk, mask).start()
        own_meta = pltpu.make_async_copy(
            self.meta_v.at[source], self.meta_out.at[chunk, 0], self.local.at[1]
        )
        own_meta.start()

        @pl.when(chunk >= 2)
        def _():
            for mask in range(1, plan.n_e):
                self.in_plane(chunk - 2, mask).wait_send()

        target = target_of(chunk)
        group = min(4, plan.n_e)
        for start in range(0, plan.n_e, group):
            for j in range(2):
                hot = jnp.concatenate(
                    [
                        slot_hits(plan, slot_base(plan, across(e, start + i), j), target)
                        for i in range(group)
                    ],
                    axis=0,
                )
                picked = dot(hot, self.rows_v[buffer]).astype(jnp.bfloat16)
                self.stage[
                    buffer, j, start * plan.stride : (start + group) * plan.stride, :
                ] = picked
            for mask in range(max(start, 1), start + group):
                self.in_plane(chunk, mask).start()
        at = pl.multiple_of(chunk * plan.rows, 16)
        own = pltpu.make_async_copy(
            self.stage.at[buffer, :, pl.ds(0, plan.stride), :],
            self.out.at[:, pl.ds(at, plan.stride), :],
            self.local.at[2],
        )
        own.start()
        own.wait()
        own_meta.wait()

    def arrived(self, chunk):
        for mask in range(1, self.plan.n_e):
            self.meta_copy(chunk, mask).wait_recv()
            self.in_plane(chunk, mask).wait_recv()

    def finish(self):
        plan = self.plan
        for chunk in range(max(0, plan.n_h - 2), plan.n_h):
            for mask in range(1, plan.n_e):
                self.in_plane(chunk, mask).wait_send()
        _, z = plan.place()

        @pl.when(z > 0)
        def _():
            for copy in self.hop(z, -1, True):
                copy.wait_send()

        @pl.when(z < plan.n_h - 1)
        def _():
            for copy in self.hop(z, 1, True):
                copy.wait_send()

        def act(source, forwarded, way):
            @pl.when(forwarded)
            def _():
                for copy in self.hop(source, way, False):
                    copy.wait_send()

        for distance in range(1, plan.n_h):
            self.on_the_way(distance, act)
        for chunk in range(plan.n_h):
            for mask in range(1, plan.n_e):
                self.meta_copy(chunk, mask).wait_send()


class Return:
    def __init__(self, plan, back, land, out, stage, rows_v, total, sems):
        self.plan = plan
        self.back, self.land, self.out = back, land, out
        self.stage, self.rows_v, self.total = stage, rows_v, total
        (self.b_send, self.b_recv, self.s_send, self.s_recv, self.local, self.own) = sems

    @staticmethod
    def sem_shapes(plan):
        dma = pltpu.SemaphoreType.DMA
        n_h, n_e = plan.n_h, plan.n_e
        return [
            dma((n_h, n_e)),
            dma((n_h, n_e)),
            dma((n_h,)),
            dma((n_h,)),
            dma((2,)),
            dma((n_h,)),
        ]

    def source(self, chunk, mask):
        raise NotImplementedError

    def in_plane(self, chunk, mask):
        plan = self.plan
        e, z = plan.place()
        return remote(
            self.source(chunk, mask),
            self.back.at[chunk, :, pl.ds(mask * plan.stride, plan.stride), :],
            self.b_send.at[chunk, mask],
            self.b_recv.at[chunk, mask],
            (across(e, mask), z),
        )

    def own_copy(self, chunk):
        plan = self.plan
        return pltpu.make_async_copy(
            self.source(chunk, 0),
            self.back.at[chunk, :, pl.ds(0, plan.stride), :],
            self.own.at[chunk],
        )

    def send(self, chunk):
        for mask in range(1, self.plan.n_e):
            self.in_plane(chunk, mask).start()
        self.own_copy(chunk).start()

    def along_z(self, chunk):
        e, z = self.plan.place()
        return remote(
            self.rows_v.at[lax.rem(chunk, 2)],
            self.land.at[z],
            self.s_send.at[chunk],
            self.s_recv.at[z],
            (e, self.plan.source(z, chunk)),
        )

    def from_z(self, distance):
        e, z = self.plan.place()
        other = lax.rem(z + distance, self.plan.n_h)
        return other, remote(
            self.rows_v.at[0], self.land.at[other], self.s_send.at[0], self.s_recv.at[other], (e, other)
        )

    def combine(self, chunk, target):
        plan = self.plan
        e, _ = plan.place()
        buffer = lax.rem(chunk, 2)
        for mask in range(1, plan.n_e):
            self.in_plane(chunk, mask).wait_recv()
        self.own_copy(chunk).wait()
        copy = pltpu.make_async_copy(self.back.at[chunk], self.stage.at[buffer], self.local.at[0])
        copy.start()
        hot = [
            jnp.concatenate(
                [
                    slot_hits(plan, slot_base(plan, across(e, mask), j), target)
                    for mask in range(plan.n_e)
                ],
                axis=0,
            )
            for j in range(2)
        ]
        copy.wait()

        @pl.when(chunk >= 3)
        def _():
            self.along_z(chunk - 2).wait_send()

        part = contract_first(hot[0], self.stage[buffer, 0]) + contract_first(
            hot[1], self.stage[buffer, 1]
        )

        @pl.when(chunk == 0)
        def _():
            self.total[...] = part

        @pl.when(chunk > 0)
        def _():
            self.rows_v[buffer] = part.astype(jnp.bfloat16)
            self.along_z(chunk).start()

    def finish(self):
        plan = self.plan
        for chunk in range(max(1, plan.n_h - 2), plan.n_h):
            self.along_z(chunk).wait_send()
        for distance in range(1, plan.n_h):
            other, arrival = self.from_z(distance)
            arrival.wait_recv()
            copy = pltpu.make_async_copy(self.land.at[other], self.rows_v.at[0], self.local.at[0])
            copy.start()
            copy.wait()
            self.total[...] += self.rows_v[0].astype(jnp.float32)
        copy = pltpu.make_async_copy(self.total, self.out, self.local.at[0])
        copy.start()
        copy.wait()


class ReturnHeld(Return):
    def __init__(self, plan, given, *rest):
        super().__init__(plan, *rest)
        self.given = given

    def source(self, chunk, mask):
        plan = self.plan
        at = pl.multiple_of((chunk * plan.n_e + mask) * plan.stride, 16)
        return self.given.at[:, pl.ds(at, plan.stride), :]

    def sent(self):
        for chunk in range(self.plan.n_h):
            for mask in range(1, self.plan.n_e):
                self.in_plane(chunk, mask).wait_send()


class ReturnMade(Return):
    def __init__(self, plan, made, *rest):
        super().__init__(plan, *rest)
        self.made = made
        self.ring = made.shape[0]

    def source(self, chunk, mask):
        plan = self.plan
        return self.made.at[
            lax.rem(chunk, self.ring), :, pl.ds(mask * plan.stride, plan.stride), :
        ]

    def free(self, chunk):
        if self.plan.n_h > self.ring:

            @pl.when(chunk >= self.ring)
            def _():
                self.wait_sent(chunk - self.ring)
                self.own_copy(chunk - self.ring).wait()

    def wait_sent(self, chunk):
        for mask in range(1, self.plan.n_e):
            self.in_plane(chunk, mask).wait_send()

    def sent(self):
        for chunk in range(max(0, self.plan.n_h - self.ring), self.plan.n_h):
            self.wait_sent(chunk)


ANY = pl.BlockSpec(memory_space=pl.ANY)


def send_body(plan, rows, meta, out, meta_out, land, rows_v, meta_v, stage, *sems):
    greet(plan)
    work = Dispatch(plan, rows, meta, land, out, meta_out, rows_v, meta_v, stage, sems)
    work.begin()
    _, z = plan.place()
    pl.loop(0, plan.n_h)(
        lambda chunk: work.chunk(chunk, lambda at: meta_v[plan.source(z, at)])
    )
    for chunk in range(plan.n_h):
        work.arrived(chunk)
    work.finish()


def send_rows(plan, rows, meta):
    n_h, n_e = plan.n_h, plan.n_e
    out = pl.pallas_call(
        functools.partial(send_body, plan),
        in_specs=[ANY, ANY],
        out_specs=[ANY, ANY, ANY],
        out_shape=[
            jax.ShapeDtypeStruct((2, plan.total, D), jnp.bfloat16),
            jax.ShapeDtypeStruct((n_h, n_e, 8, LEN), jnp.float32),
            jax.ShapeDtypeStruct((n_h, LEN, D), jnp.bfloat16),
        ],
        scratch_shapes=[
            pltpu.VMEM((2, LEN, D), jnp.bfloat16),
            pltpu.VMEM((n_h, 8, LEN), jnp.float32),
            pltpu.VMEM((2, 2, plan.rows, D), jnp.bfloat16),
        ]
        + Dispatch.sem_shapes(plan),
        compiler_params=pltpu.CompilerParams(
            collective_id=1, has_side_effects=True, vmem_limit_bytes=VMEM
        ),
        name="send_rows",
    )(rows, meta)
    return out[0], out[1]


def expert_body(plan, halves, n_d, *refs):
    (
        sent,
        gates,
        grads,
        targets,
        w_gate,
        w_up,
        w_down,
        total_out,
        gg_out,
        rows_out,
        y_out,
        dgate_out,
        dup_out,
        act_out,
        meta_out,
        land,
        back,
        land_back,
        rows_v,
        meta_v,
        stage,
        wg_v,
        wu_v,
        wd_v,
        target_v,
        gate_v,
        x_v,
        g_v,
        dx_v,
        y_v,
        dgate_v,
        dup_v,
        act_v,
        gg_v,
        gg_back,
        gg_part,
        gg_land,
        total,
        w_sem,
        t_sem,
        x_sem,
        o_sem,
        gg_send,
        gg_recv,
        ggs_send,
        ggs_recv,
        *sems,
    ) = refs
    n_e, n_h = plan.n_e, plan.n_h
    e, z = plan.place()
    loads = [
        pltpu.make_async_copy(source, held, w_sem.at[i])
        for i, (source, held) in enumerate(((w_gate, wg_v), (w_up, wu_v), (w_down, wd_v)))
    ]
    for load in loads:
        load.start()
    targets_in = pltpu.make_async_copy(targets, target_v, t_sem.at[0])
    targets_in.start()
    greet(plan)
    work = Dispatch(
        plan, sent, gates, land, rows_out, meta_out, rows_v, meta_v, stage, sems[:n_d]
    )
    give = ReturnMade(
        plan, dx_v, back, land_back, total_out, stage, rows_v, total, sems[n_d:]
    )
    work.begin()
    targets_in.wait()
    ahead = min(3, n_h)
    pl.loop(0, ahead)(lambda chunk: work.chunk(chunk, lambda at: target_v[at, 0]))
    for load in loads:
        load.wait()

    def gg_copy(chunk, mask):
        return remote(
            gg_v.at[chunk, mask],
            gg_back.at[chunk, mask],
            gg_send.at[chunk, mask],
            gg_recv.at[chunk, mask],
            (across(e, mask), z),
        )

    def gg_along(chunk):
        return remote(
            gg_part.at[chunk],
            gg_land.at[z],
            ggs_send.at[chunk],
            ggs_recv.at[z],
            (e, plan.source(z, chunk)),
        )

    def gg_from(distance):
        other = lax.rem(z + distance, n_h)
        return other, remote(
            gg_part.at[0], gg_land.at[other], ggs_send.at[0], ggs_recv.at[other], (e, other)
        )

    def outs(chunk, j):
        at = pl.multiple_of(chunk * plan.rows, 16)
        return [
            pltpu.make_async_copy(held.at[j], out.at[j, pl.ds(at, plan.rows), :], o_sem.at[i, j])
            for i, (held, out) in enumerate(
                ((y_v, y_out), (dgate_v, dgate_out), (dup_v, dup_out), (act_v, act_out))
            )
        ]

    own_last = 1 if n_h <= dx_v.shape[0] else 0
    masks = n_e // halves
    piece = masks * plan.stride

    def step(chunk, index):
        j, half = lax.div(index, halves), lax.rem(index, halves)
        at = pl.ds(pl.multiple_of(half * piece, 16), piece)
        rows, grads_in = x_v[j, at, :], g_v[j, at, :]
        gate_pre = contract_last(rows, wg_v[j])
        up_pre = contract_last(rows, wu_v[j])
        raw = contract_last(grads_in, wd_v[j])
        slots = lax.broadcasted_iota(jnp.int32, (plan.stride, LEN), 0).astype(
            jnp.float32
        ) + slot_base(plan, e, j)
        columns = []
        for i in range(masks):
            mask = half * masks + i
            aim, weight = target_v[chunk, mask], gate_v[mask]
            hit = jnp.where(slots == aim[0:1, :], weight[0:1, :], 0.0)
            hit = hit + jnp.where(slots == aim[1:2, :], weight[1:2, :], 0.0)
            columns.append(jnp.sum(hit, axis=1, keepdims=True))
        gate = jnp.concatenate(columns, axis=0)
        square = gate_pre * gate_pre
        tanh = jnp.tanh(0.7978845608028654 * gate_pre * (1.0 + 0.044715 * square))
        side = 0.5 * (1.0 + tanh)
        gelu = gate_pre * side
        slope = side + 0.5 * gate_pre * (1.0 - tanh * tanh) * (
            0.7978845608028654 * (1.0 + 0.134145 * square)
        )
        act = gelu * up_pre
        act_low = act.astype(jnp.bfloat16)
        dots = jnp.sum(act_low.astype(jnp.float32) * raw, axis=1, keepdims=True)
        for i in range(masks):
            mask = half * masks + i
            aim, part = target_v[chunk, mask], dots[i * plan.stride : (i + 1) * plan.stride]
            for k in range(2):
                line = jnp.sum(
                    jnp.where(slots == aim[k : k + 1, :], part, 0.0), axis=0, keepdims=True
                )
                gg_v[chunk, mask, k : k + 1, :] += line
        grad_act = gate * raw
        grad_gate = (grad_act * up_pre * slope).astype(jnp.bfloat16)
        grad_up = (grad_act * gelu).astype(jnp.bfloat16)
        dgate_v[j, at, :] = grad_gate
        dup_v[j, at, :] = grad_up
        act_v[j, at, :] = (act * gate).astype(jnp.bfloat16)
        dx_v[lax.rem(chunk, dx_v.shape[0]), j, at, :] = (
            dot(grad_gate, wg_v[j]) + dot(grad_up, wu_v[j])
        ).astype(jnp.bfloat16)
        y_v[j, at, :] = (dot(act_low, wd_v[j]) * gate).astype(jnp.bfloat16)

    gg_v[...] = jnp.zeros_like(gg_v)

    @pl.loop(0, n_h)
    def _(chunk):
        work.arrived(chunk)
        at = pl.multiple_of(chunk * plan.rows, 16)
        gate_in = pltpu.make_async_copy(meta_out.at[chunk], gate_v, t_sem.at[0])
        gate_in.start()
        ins = [
            pltpu.make_async_copy(source.at[:, pl.ds(at, plan.rows), :], held, x_sem.at[i])
            for i, (source, held) in enumerate(((rows_out, x_v), (grads, g_v)))
        ]
        for copy in ins:
            copy.start()
        give.free(chunk)

        @pl.when(chunk > 0)
        def _():
            for j in range(2):
                for copy in outs(chunk - 1, j):
                    copy.wait()

        gate_in.wait()
        for copy in ins:
            copy.wait()
        pl.loop(0, 2 * halves)(lambda index: step(chunk, index))
        for mask in range(1, n_e):
            gg_copy(chunk, mask).start()

        @pl.when(chunk >= own_last)
        def _():
            give.send(chunk)

        for j in range(2):
            for copy in outs(chunk, j):
                copy.start()

        @pl.when(chunk + ahead < n_h)
        def _():
            work.chunk(chunk + ahead, lambda at: target_v[at, 0])

    if own_last:
        give.send(0)
    work.finish()
    for j in range(2):
        for copy in outs(n_h - 1, j):
            copy.wait()

    @pl.loop(0, n_h)
    def _(turn):
        chunk = lax.rem(turn + own_last, n_h)
        part = gg_v[chunk, 0]
        for mask in range(1, n_e):
            gg_copy(chunk, mask).wait_recv()
            part = part + gg_back[chunk, mask]
        gg_part[chunk] = part

        @pl.when(chunk > 0)
        def _():
            gg_along(chunk).start()

        give.combine(chunk, target_v[chunk, 0])

    give.sent()
    for chunk in range(n_h):
        for mask in range(1, n_e):
            gg_copy(chunk, mask).wait_send()
    sum_gg = gg_part[0]
    for distance in range(1, n_h):
        other, arrival = gg_from(distance)
        arrival.wait_recv()
        sum_gg = sum_gg + gg_land[other]
    gg_out[...] = sum_gg
    for chunk in range(1, n_h):
        gg_along(chunk).wait_send()
    give.finish()


def run_experts(plan, sent, gates, grads, targets, w_gate, w_up, w_down):
    n_h, n_e, width = plan.n_h, plan.n_e, plan.width
    bf16, f32 = jnp.bfloat16, jnp.float32
    shape = jax.ShapeDtypeStruct
    dma = pltpu.SemaphoreType.DMA
    ring = min(4, n_h)
    d_sems, r_sems = Dispatch.sem_shapes(plan), Return.sem_shapes(plan)
    halves = 2 if plan.rows <= 640 else 4
    return pl.pallas_call(
        functools.partial(expert_body, plan, halves, len(d_sems)),
        in_specs=[ANY] * 7,
        out_specs=[ANY, pl.BlockSpec(memory_space=pltpu.VMEM)] + [ANY] * 9,
        out_shape=[
            shape((LEN, D), f32),
            shape((8, LEN), f32),
            shape((2, plan.total, D), bf16),
            shape((2, plan.total, D), bf16),
            shape((2, plan.total, width), bf16),
            shape((2, plan.total, width), bf16),
            shape((2, plan.total, width), bf16),
            shape((n_h, n_e, 8, LEN), f32),
            shape((n_h, LEN, D), bf16),
            shape((n_h, 2, plan.rows, D), bf16),
            shape((n_h, LEN, D), bf16),
        ],
        scratch_shapes=[
            pltpu.VMEM((2, LEN, D), bf16),
            pltpu.VMEM((n_h, 8, LEN), f32),
            pltpu.VMEM((2, 2, plan.rows, D), bf16),
            pltpu.VMEM((2, width, D), bf16),
            pltpu.VMEM((2, width, D), bf16),
            pltpu.VMEM((2, width, D), bf16),
            pltpu.VMEM((n_h, n_e, 8, LEN), f32),
            pltpu.VMEM((n_e, 8, LEN), f32),
            pltpu.VMEM((2, plan.rows, D), bf16),
            pltpu.VMEM((2, plan.rows, D), bf16),
            pltpu.VMEM((ring, 2, plan.rows, D), bf16),
            pltpu.VMEM((2, plan.rows, D), bf16),
            pltpu.VMEM((2, plan.rows, width), bf16),
            pltpu.VMEM((2, plan.rows, width), bf16),
            pltpu.VMEM((2, plan.rows, width), bf16),
            pltpu.VMEM((n_h, n_e, 8, LEN), f32),
            pltpu.VMEM((n_h, n_e, 8, LEN), f32),
            pltpu.VMEM((n_h, 8, LEN), f32),
            pltpu.VMEM((n_h, 8, LEN), f32),
            pltpu.VMEM((LEN, D), f32),
            dma((3,)),
            dma((1,)),
            dma((2,)),
            dma((4, 2)),
            dma((n_h, n_e)),
            dma((n_h, n_e)),
            dma((n_h,)),
            dma((n_h,)),
        ]
        + d_sems
        + r_sems,
        compiler_params=pltpu.CompilerParams(
            collective_id=2, has_side_effects=True, vmem_limit_bytes=VMEM
        ),
        name="run_experts",
    )(sent, gates, grads, targets, jnp.swapaxes(w_gate, 1, 2), jnp.swapaxes(w_up, 1, 2), w_down)


def back_body(plan, given, targets, out, back, land, rows_v, stage, target_v, total, t_sem, *sems):
    targets_in = pltpu.make_async_copy(targets, target_v, t_sem.at[0])
    targets_in.start()
    greet(plan)
    give = ReturnHeld(plan, given, back, land, out, stage, rows_v, total, sems)
    order = [chunk for chunk in range(1, plan.n_h)] + [0]
    for chunk in order:
        give.send(chunk)
    targets_in.wait()

    @pl.loop(0, plan.n_h)
    def _(turn):
        chunk = lax.rem(turn + 1, plan.n_h)
        give.combine(chunk, target_v[chunk, 0])

    give.sent()
    give.finish()


def bring_back(plan, given, targets):
    n_h, n_e = plan.n_h, plan.n_e
    bf16, f32 = jnp.bfloat16, jnp.float32
    shape = jax.ShapeDtypeStruct
    return pl.pallas_call(
        functools.partial(back_body, plan),
        in_specs=[ANY, ANY],
        out_specs=[ANY] * 3,
        out_shape=[
            shape((LEN, D), f32),
            shape((n_h, 2, plan.rows, D), bf16),
            shape((n_h, LEN, D), bf16),
        ],
        scratch_shapes=[
            pltpu.VMEM((2, LEN, D), bf16),
            pltpu.VMEM((2, 2, plan.rows, D), bf16),
            pltpu.VMEM((n_h, n_e, 8, LEN), f32),
            pltpu.VMEM((LEN, D), f32),
            pltpu.SemaphoreType.DMA((1,)),
        ]
        + Return.sem_shapes(plan),
        compiler_params=pltpu.CompilerParams(
            collective_id=3, has_side_effects=True, vmem_limit_bytes=VMEM
        ),
        name="bring_back",
    )(given, targets)[0]


NEAR = 128


def offset_buckets():
    offset = jnp.arange(4 * NEAR, dtype=jnp.int32) - 2 * NEAR
    distance = jnp.abs(offset)
    far_bucket = 8 + sum(((distance >= threshold).astype(jnp.int32) for threshold in thresholds))
    bucket = jnp.where(distance < 8, distance, far_bucket) + 16 * (offset > 0).astype(jnp.int32)
    return (bucket[:, None] == jnp.arange(BUCKETS, dtype=jnp.int32)).astype(jnp.float32)


def bias_tiles(line):
    return pltpu.roll(
        jnp.broadcast_to(line, (NEAR, 4 * NEAR)), 0, 1, stride=1, stride_axis=0
    )


def mix_head(query, key, value, line, soft_ref, head):
    tiles = bias_tiles(line)
    blocks = LEN // NEAR
    outs = []
    for i in range(blocks):
        raw = contract_last(query[i * NEAR : (i + 1) * NEAR], key) * (HEAD_DIM**-0.5)
        parts = []
        for j in range(blocks):
            part = raw[:, j * NEAR : (j + 1) * NEAR]
            if abs(j - i) <= 1:
                parts.append(part + tiles[:, (j - i + 2) * NEAR : (j - i + 3) * NEAR])
            else:
                edge = 1 if j < i else 4 * NEAR - 1
                parts.append(part + line[:, edge : edge + 1])
        scores = jnp.concatenate(parts, axis=1)
        terms = jnp.exp(scores - jnp.max(scores, axis=1, keepdims=True))
        soft = (terms * (1.0 / jnp.sum(terms, axis=1, keepdims=True))).astype(jnp.bfloat16)
        soft_ref[head, i * NEAR : (i + 1) * NEAR, :] = soft
        outs.append(dot(soft, value))
    return jnp.concatenate(outs, axis=0).astype(jnp.bfloat16)


def mix_body(query_ref, key_ref, value_ref, line_ref, soft_ref, mixed_ref):
    for head in range(2):
        at = slice(head * HEAD_DIM, (head + 1) * HEAD_DIM)
        mixed_ref[:, at] = mix_head(
            query_ref[:, at],
            key_ref[:, at],
            value_ref[:, at],
            line_ref[0, head : head + 1, :],
            soft_ref,
            head,
        )


def mix(query, key, value, lines):
    pair = pl.BlockSpec((LEN, 2 * HEAD_DIM), lambda i: (0, i))
    return pl.pallas_call(
        mix_body,
        grid=(HEADS // 2,),
        in_specs=[pair, pair, pair, pl.BlockSpec((1, 2, 4 * NEAR), lambda i: (i, 0, 0))],
        out_specs=[pl.BlockSpec((2, LEN, LEN), lambda i: (i, 0, 0)), pair],
        out_shape=[
            jax.ShapeDtypeStruct((HEADS, LEN, LEN), jnp.bfloat16),
            jax.ShapeDtypeStruct((LEN, D), jnp.bfloat16),
        ],
        compiler_params=pltpu.CompilerParams(vmem_limit_bytes=VMEM),
        name="mix",
    )(query, key, value, lines.reshape(HEADS // 2, 2, 4 * NEAR))


def unmix_head(query, key, value, grad_mixed, soft_ref, grads_v, head):
    blocks = LEN // NEAR
    near = [jnp.zeros((NEAR, NEAR), jnp.float32) for _ in range(3)]
    below = jnp.zeros((NEAR, NEAR), jnp.float32)
    above = jnp.zeros((NEAR, NEAR), jnp.float32)
    grad_query = []
    for i in range(blocks):
        at = slice(i * NEAR, (i + 1) * NEAR)
        soft = soft_ref[head, at, :].astype(jnp.float32)
        grad_soft = contract_last(grad_mixed[at], value)
        product = soft * grad_soft
        grad = product - soft * jnp.sum(product, axis=1, keepdims=True)
        low = grad.astype(jnp.bfloat16)
        grads_v[at, :] = low
        grad_query.append(dot(low, key))
        wide = low.astype(jnp.float32)
        for j in range(blocks):
            part = wide[:, j * NEAR : (j + 1) * NEAR]
            if abs(j - i) <= 1:
                near[j - i + 1] = near[j - i + 1] + part
            elif j < i:
                below = below + part
            else:
                above = above + part
    band = jnp.concatenate([jnp.zeros((NEAR, NEAR), jnp.float32)] + near, axis=1)
    eight = band[0:8]
    for i in range(8, NEAR, 8):
        eight = eight + pltpu.roll(band[i : i + 8], 4 * NEAR - i, 1)
    row = lax.broadcasted_iota(jnp.int32, (8, 4 * NEAR), 0)
    for bit in (1, 2, 4):
        eight = jnp.where(lax.rem(lax.div(row, bit), 2) == 1, pltpu.roll(eight, 4 * NEAR - bit, 1), eight)
    line = jnp.sum(eight, axis=0, keepdims=True)
    column = lax.broadcasted_iota(jnp.int32, (1, 4 * NEAR), 1)
    line = line + jnp.where(column == 1, jnp.sum(below), 0.0)
    line = line + jnp.where(column == 4 * NEAR - 1, jnp.sum(above), 0.0)
    scaling = HEAD_DIM**-0.5
    grad_query = (jnp.concatenate(grad_query, axis=0) * scaling).astype(jnp.bfloat16)
    grad_key = (contract_first(grads_v[...], query) * scaling).astype(jnp.bfloat16)
    grad_value = contract_first(soft_ref[head], grad_mixed).astype(jnp.bfloat16)
    return grad_query, grad_key, grad_value, line


def unmix_body(
    query_ref, key_ref, value_ref, grad_ref, soft_ref, dq_ref, dk_ref, dv_ref, line_ref, grads_v
):
    for head in range(2):
        at = slice(head * HEAD_DIM, (head + 1) * HEAD_DIM)
        dq_ref[:, at], dk_ref[:, at], dv_ref[:, at], line_ref[0, head : head + 1, :] = unmix_head(
            query_ref[:, at],
            key_ref[:, at],
            value_ref[:, at],
            grad_ref[:, at],
            soft_ref,
            grads_v,
            head,
        )


def unmix(query, key, value, grad_mixed, soft):
    pair = pl.BlockSpec((LEN, 2 * HEAD_DIM), lambda i: (0, i))
    rows = jax.ShapeDtypeStruct((LEN, D), jnp.bfloat16)
    out = pl.pallas_call(
        unmix_body,
        grid=(HEADS // 2,),
        in_specs=[pair] * 4 + [pl.BlockSpec((2, LEN, LEN), lambda i: (i, 0, 0))],
        out_specs=[pair] * 3 + [pl.BlockSpec((1, 2, 4 * NEAR), lambda i: (i, 0, 0))],
        out_shape=[rows] * 3 + [jax.ShapeDtypeStruct((HEADS // 2, 2, 4 * NEAR), jnp.float32)],
        scratch_shapes=[pltpu.VMEM((LEN, LEN), jnp.bfloat16)],
        compiler_params=pltpu.CompilerParams(vmem_limit_bytes=VMEM),
        name="unmix",
    )(query, key, value, grad_mixed, soft)
    return out[0], out[1], out[2], out[3].reshape(HEADS, 4 * NEAR)


def per_device(
    n_e,
    n_h,
    tokens,
    gain_one,
    w_query,
    w_key,
    w_value,
    w_out,
    bias_table,
    gain_two,
    w_router,
    w_gate,
    w_up,
    w_down,
    routes,
    cotangent,
):
    experts_all = w_router.shape[1]
    plan = Plan(n_e, n_h, experts_all, w_gate.shape[2])
    both = ("expert", "hidden")

    def small(array):
        return jnp.pad(array.astype(jnp.float32), ((0, 8 - array.shape[0]), (0, 0)))

    targets = small(slot_targets(routes, experts_all, plan.capacity, plan.stride))
    grads_in, targets_all = send_rows(plan, cotangent, targets)
    hot_bucket = offset_buckets()
    inputs = tokens.astype(jnp.float32)
    inv_one = lax.rsqrt(jnp.mean(inputs * inputs, axis=-1, keepdims=True) + eps)
    normed_one = (inputs * inv_one * gain_one).astype(jnp.bfloat16)
    query_rows = dot(normed_one, w_query).astype(jnp.bfloat16)
    key_rows = dot(normed_one, w_key).astype(jnp.bfloat16)
    value_rows = dot(normed_one, w_value).astype(jnp.bfloat16)
    lines = jnp.dot(hot_bucket, bias_table, precision=precise).T
    soft, mixed_rows = mix(query_rows, key_rows, value_rows, lines)
    hidden = inputs + dot(mixed_rows, w_out)
    inv_two = lax.rsqrt(jnp.mean(hidden * hidden, axis=-1, keepdims=True) + eps)
    normed_two = hidden * inv_two * gain_two
    sent = normed_two.astype(jnp.bfloat16)
    logits = jnp.dot(normed_two, w_router, precision=precise)
    route_hot = (routes[:, :, None] == jnp.arange(experts_all, dtype=jnp.int32)).astype(jnp.float32)
    chosen = jnp.sum(route_hot * logits[:, None, :], axis=-1)
    gate_values = jax.nn.softmax(chosen, axis=-1)
    grad_sent, grad_gates, rows_in, y_rows, gate_rows, up_rows, act_rows = run_experts(
        plan, sent, small(gate_values.T), grads_in, targets_all, w_gate, w_up, w_down
    )[:7]
    grad_gates = grad_gates[:2].T
    grad_out = cotangent.astype(jnp.float32)
    grad_chosen = gate_values * (
        grad_gates - jnp.sum(gate_values * grad_gates, axis=-1, keepdims=True)
    )
    grad_logits = jnp.sum(route_hot * grad_chosen[:, :, None], axis=1)
    router_grad = contract_first(grad_logits, normed_two, precise)
    grad_normed_two = contract_last(grad_logits, w_router, precise) + grad_sent
    gain_two_grad = jnp.sum(grad_normed_two * hidden * inv_two, axis=0)
    scaled_two = grad_normed_two * gain_two
    grad_hidden = (
        grad_out
        + inv_two * scaled_two
        - hidden * inv_two**3 * jnp.mean(scaled_two * hidden, axis=-1, keepdims=True)
    )
    grad_branch = grad_hidden.astype(jnp.bfloat16)
    w_out_grad = contract_first(mixed_rows, grad_branch)
    grad_mixed = contract_last(grad_branch, w_out).astype(jnp.bfloat16)
    grad_query, grad_key, grad_value, grad_lines = unmix(
        query_rows, key_rows, value_rows, grad_mixed, soft
    )
    bias_table_grad = jnp.dot(grad_lines, hot_bucket, precision=precise).T
    query_grad = contract_first(normed_one, grad_query)
    key_grad = contract_first(normed_one, grad_key)
    value_grad = contract_first(normed_one, grad_value)
    grad_normed_one = (
        contract_last(grad_query, w_query)
        + contract_last(grad_key, w_key)
        + contract_last(grad_value, w_value)
    )
    gain_one_grad = jnp.sum(grad_normed_one * inputs * inv_one, axis=0)
    scaled_one = grad_normed_one * gain_one
    tokens_grad = (
        grad_hidden
        + inv_one * scaled_one
        - inputs * inv_one**3 * jnp.mean(scaled_one * inputs, axis=-1, keepdims=True)
    )
    last = jnp.pad(bias_table_grad.reshape(1, BUCKETS * HEADS), ((0, 0), (0, D - BUCKETS * HEADS)))
    few = jnp.concatenate([router_grad, gain_one_grad[None], gain_two_grad[None], last], axis=0)
    few = jnp.pad(few, ((0, -few.shape[0] % 16), (0, 0)))
    low = [
        item.astype(jnp.bfloat16) for item in (query_grad, key_grad, value_grad, w_out_grad, few)
    ]
    low, gate_rows, up_rows, act_rows, y_rows = lax.optimization_barrier(
        (low, gate_rows, up_rows, act_rows, y_rows)
    )
    summed = [item.astype(jnp.float32) for item in lax.psum(low, both)]
    few = summed[4]
    branch = bring_back(plan, y_rows, targets_all)
    block_out = (hidden + branch).astype(jnp.bfloat16)
    down_grad = jnp.einsum("xrf,xrd->xfd", act_rows, grads_in, preferred_element_type=jnp.float32)
    gate_grad = jnp.einsum("xrd,xrf->xdf", rows_in, gate_rows, preferred_element_type=jnp.float32)
    up_grad = jnp.einsum("xrd,xrf->xdf", rows_in, up_rows, preferred_element_type=jnp.float32)
    return (
        block_out,
        tokens_grad,
        few[experts_all],
        *summed[:4],
        few[experts_all + 2, : BUCKETS * HEADS].reshape(BUCKETS, HEADS),
        few[experts_all + 1],
        few[:experts_all].T,
        gate_grad,
        up_grad,
        down_grad,
    )


def solution(mesh):
    in_specs = (
        P(("expert", "hidden"), None),
        P(),
        P(),
        P(),
        P(),
        P(),
        P(),
        P(),
        P(),
        P("expert", None, "hidden"),
        P("expert", None, "hidden"),
        P("expert", "hidden", None),
        P(("expert", "hidden"), None),
        P(("expert", "hidden"), None),
    )
    out_specs = (
        P(("expert", "hidden"), None),
        P(("expert", "hidden"), None),
        P(),
        P(),
        P(),
        P(),
        P(),
        P(),
        P(),
        P(),
        P("expert", None, "hidden"),
        P("expert", None, "hidden"),
        P("expert", "hidden", None),
    )
    return jax.shard_map(
        functools.partial(per_device, mesh.shape["expert"], mesh.shape["hidden"]),
        mesh=mesh, in_specs=in_specs, out_specs=out_specs, check_vma=False
    )
```

```python
import functools

import jax
import jax.numpy as jnp
from jax import lax
from jax.experimental import pallas as pl
from jax.experimental.pallas import tpu as pltpu
from jax.sharding import PartitionSpec as P

D = 1024
HEADS = 16
HEAD_DIM = 64
BUCKETS = 32
LEN = 512
MICRO = 2
MB_TOK = 256
VMEM = 62 * 1024 * 1024
MESH = pl.DeviceIdType.MESH


eps = 1e-06
precise = lax.Precision.HIGHEST
thresholds = (12, 16, 23, 32, 46, 64, 91)


def contract_last(matrix_a, matrix_b, mode=None):
    return lax.dot_general(
        matrix_a,
        matrix_b,
        (((1,), (1,)), ((), ())),
        precision=mode,
        preferred_element_type=jnp.float32,
    )


def contract_first(matrix_a, matrix_b, mode=None):
    return lax.dot_general(
        matrix_a,
        matrix_b,
        (((0,), (0,)), ((), ())),
        precision=mode,
        preferred_element_type=jnp.float32,
    )


def dot(matrix_a, matrix_b):
    return jnp.dot(matrix_a, matrix_b, preferred_element_type=jnp.float32)


def slot_targets(routes, experts_all, capacity, stride):
    pairs = 2 * MB_TOK
    flat = routes.reshape(-1, pairs)
    hits = (flat[:, :, None] == jnp.arange(experts_all, dtype=jnp.int32)).astype(jnp.bfloat16)
    lower = (
        jnp.arange(pairs, dtype=jnp.int32)[:, None] > jnp.arange(pairs, dtype=jnp.int32)[None, :]
    ).astype(jnp.bfloat16)
    earlier = jnp.einsum("pq,bqe->bpe", lower, hits, preferred_element_type=jnp.float32)
    rank = jnp.sum(earlier * hits.astype(jnp.float32), axis=-1).astype(jnp.int32)
    block = jnp.arange(flat.shape[0], dtype=jnp.int32)[:, None]
    target = flat * stride + block * capacity + rank
    return target.reshape(-1, 2).T


NEAR = 128


def offset_buckets():
    offset = jnp.arange(4 * NEAR, dtype=jnp.int32) - 2 * NEAR
    distance = jnp.abs(offset)
    far_bucket = 8 + sum(((distance >= threshold).astype(jnp.int32) for threshold in thresholds))
    bucket = jnp.where(distance < 8, distance, far_bucket) + 16 * (offset > 0).astype(jnp.int32)
    return (bucket[:, None] == jnp.arange(BUCKETS, dtype=jnp.int32)).astype(jnp.float32)


def bias_tiles(line):
    return pltpu.roll(
        jnp.broadcast_to(line, (NEAR, 4 * NEAR)), 0, 1, stride=1, stride_axis=0
    )


def mix_head(query, key, value, line, soft_ref, head):
    tiles = bias_tiles(line)
    blocks = LEN // NEAR
    outs = []
    for i in range(blocks):
        raw = contract_last(query[i * NEAR : (i + 1) * NEAR], key) * (HEAD_DIM**-0.5)
        parts = []
        for j in range(blocks):
            part = raw[:, j * NEAR : (j + 1) * NEAR]
            if abs(j - i) <= 1:
                parts.append(part + tiles[:, (j - i + 2) * NEAR : (j - i + 3) * NEAR])
            else:
                edge = 1 if j < i else 4 * NEAR - 1
                parts.append(part + line[:, edge : edge + 1])
        scores = jnp.concatenate(parts, axis=1)
        terms = jnp.exp(scores - jnp.max(scores, axis=1, keepdims=True))
        soft = (terms * (1.0 / jnp.sum(terms, axis=1, keepdims=True))).astype(jnp.bfloat16)
        soft_ref[head, i * NEAR : (i + 1) * NEAR, :] = soft
        outs.append(dot(soft, value))
    return jnp.concatenate(outs, axis=0).astype(jnp.bfloat16)


def unmix_head(query, key, value, grad_mixed, soft_ref, grads_v, head):
    blocks = LEN // NEAR
    near = [jnp.zeros((NEAR, NEAR), jnp.float32) for _ in range(3)]
    below = jnp.zeros((NEAR, NEAR), jnp.float32)
    above = jnp.zeros((NEAR, NEAR), jnp.float32)
    grad_query = []
    for i in range(blocks):
        at = slice(i * NEAR, (i + 1) * NEAR)
        soft = soft_ref[head, at, :].astype(jnp.float32)
        grad_soft = contract_last(grad_mixed[at], value)
        product = soft * grad_soft
        grad = product - soft * jnp.sum(product, axis=1, keepdims=True)
        low = grad.astype(jnp.bfloat16)
        grads_v[at, :] = low
        grad_query.append(dot(low, key))
        wide = low.astype(jnp.float32)
        for j in range(blocks):
            part = wide[:, j * NEAR : (j + 1) * NEAR]
            if abs(j - i) <= 1:
                near[j - i + 1] = near[j - i + 1] + part
            elif j < i:
                below = below + part
            else:
                above = above + part
    band = jnp.concatenate([jnp.zeros((NEAR, NEAR), jnp.float32)] + near, axis=1)
    eight = band[0:8]
    for i in range(8, NEAR, 8):
        eight = eight + pltpu.roll(band[i : i + 8], 4 * NEAR - i, 1)
    row = lax.broadcasted_iota(jnp.int32, (8, 4 * NEAR), 0)
    for bit in (1, 2, 4):
        eight = jnp.where(lax.rem(lax.div(row, bit), 2) == 1, pltpu.roll(eight, 4 * NEAR - bit, 1), eight)
    line = jnp.sum(eight, axis=0, keepdims=True)
    column = lax.broadcasted_iota(jnp.int32, (1, 4 * NEAR), 1)
    line = line + jnp.where(column == 1, jnp.sum(below), 0.0)
    line = line + jnp.where(column == 4 * NEAR - 1, jnp.sum(above), 0.0)
    scaling = HEAD_DIM**-0.5
    grad_query = (jnp.concatenate(grad_query, axis=0) * scaling).astype(jnp.bfloat16)
    grad_key = (contract_first(grads_v[...], query) * scaling).astype(jnp.bfloat16)
    grad_value = contract_first(soft_ref[head], grad_mixed).astype(jnp.bfloat16)
    return grad_query, grad_key, grad_value, line


def unmix_body(
    query_ref, key_ref, value_ref, grad_ref, soft_ref, dq_ref, dk_ref, dv_ref, line_ref, grads_v
):
    for head in range(2):
        at = slice(head * HEAD_DIM, (head + 1) * HEAD_DIM)
        dq_ref[:, at], dk_ref[:, at], dv_ref[:, at], line_ref[0, head : head + 1, :] = unmix_head(
            query_ref[:, at],
            key_ref[:, at],
            value_ref[:, at],
            grad_ref[:, at],
            soft_ref,
            grads_v,
            head,
        )


def unmix(query, key, value, grad_mixed, soft):
    pair = pl.BlockSpec((LEN, 2 * HEAD_DIM), lambda i: (0, i))
    rows = jax.ShapeDtypeStruct((LEN, D), jnp.bfloat16)
    out = pl.pallas_call(
        unmix_body,
        grid=(HEADS // 2,),
        in_specs=[pair] * 4 + [pl.BlockSpec((2, LEN, LEN), lambda i: (i, 0, 0))],
        out_specs=[pair] * 3 + [pl.BlockSpec((1, 2, 4 * NEAR), lambda i: (i, 0, 0))],
        out_shape=[rows] * 3 + [jax.ShapeDtypeStruct((HEADS // 2, 2, 4 * NEAR), jnp.float32)],
        scratch_shapes=[pltpu.VMEM((LEN, LEN), jnp.bfloat16)],
        compiler_params=pltpu.CompilerParams(vmem_limit_bytes=VMEM),
        name="unmix",
    )(query, key, value, grad_mixed, soft)
    return out[0], out[1], out[2], out[3].reshape(HEADS, 4 * NEAR)


class Plan:
    def __init__(self, n_e, n_h, experts_all, width):
        self.n_e, self.n_h, self.width = n_e, n_h, width
        self.capacity = 10 * MB_TOK // (4 * experts_all)
        self.stride = -(-MICRO * self.capacity // 16) * 16
        self.span = 2 * self.stride
        self.rows = n_e * self.stride
        self.total = n_h * self.rows

    def place(self):
        return lax.axis_index("expert"), lax.axis_index("hidden")

    def source(self, z, chunk):
        sign = 1 - 2 * lax.div(z, self.n_h // 2)
        return lax.rem(z + self.n_h + sign * chunk, self.n_h)


def across(here, mask):
    there, bit = here, 1
    while bit <= mask:
        if mask & bit:
            there = there + bit * (1 - 2 * lax.rem(lax.div(here, bit), 2))
        bit *= 2
    return there


def remote(src, dst, send_sem, recv_sem, device):
    return pltpu.make_async_remote_copy(
        src_ref=src,
        dst_ref=dst,
        send_sem=send_sem,
        recv_sem=recv_sem,
        device_id=device,
        device_id_type=MESH,
    )


def greet(plan):
    e, z = plan.place()
    barrier = pltpu.get_barrier_semaphore()
    for mask in range(1, plan.n_e):
        pl.semaphore_signal(barrier, inc=1, device_id=(across(e, mask), z), device_id_type=MESH)
    for shift in range(1, plan.n_h):
        pl.semaphore_signal(
            barrier, inc=1, device_id=(e, lax.rem(z + shift, plan.n_h)), device_id_type=MESH
        )
    pl.semaphore_wait(barrier, plan.n_e + plan.n_h - 2)


def slot_hits(plan, base, target):
    slots = lax.broadcasted_iota(jnp.int32, (plan.stride, LEN), 0).astype(jnp.float32) + base
    return jnp.where((slots == target[0:1, :]) | (slots == target[1:2, :]), 1.0, 0.0).astype(
        jnp.bfloat16
    )


def slot_base(plan, device, j):
    return (device * plan.span + j * plan.stride).astype(jnp.float32)


class Dispatch:
    def __init__(self, plan, rows, meta, land, out, meta_out, rows_v, meta_v, stage, sems):
        self.plan = plan
        self.rows, self.meta, self.land = rows, meta, land
        self.out, self.meta_out = out, meta_out
        self.rows_v, self.meta_v, self.stage = rows_v, meta_v, stage
        (
            self.z_send,
            self.z_recv,
            self.zm_send,
            self.zm_recv,
            self.a_send,
            self.a_recv,
            self.m_send,
            self.m_recv,
            self.local,
        ) = sems

    @staticmethod
    def sem_shapes(plan):
        dma = pltpu.SemaphoreType.DMA
        n_h, n_e = plan.n_h, plan.n_e
        return [
            dma((n_h, 2)),
            dma((n_h,)),
            dma((n_h, 2)),
            dma((n_h,)),
            dma((2, n_e)),
            dma((n_h, n_e)),
            dma((n_h, n_e)),
            dma((n_h, n_e)),
            dma((3,)),
        ]

    def hop(self, source, way, own):
        e, z = self.plan.place()
        sems = [
            (self.z_send.at[source, (way + 1) // 2], self.z_recv.at[source]),
            (self.zm_send.at[source, (way + 1) // 2], self.zm_recv.at[source]),
        ]
        return (
            remote(self.meta_v.at[source], self.meta_v.at[source], *sems[1], (e, z + way)),
            remote(
                self.rows if own else self.land.at[source],
                self.land.at[source],
                *sems[0],
                (e, z + way),
            ),
        )

    def on_the_way(self, distance, act):
        n_h = self.plan.n_h
        _, z = self.plan.place()

        @pl.when(z + distance < n_h)
        def _():
            act(z + distance, z > 0, -1)

        @pl.when(z >= distance)
        def _():
            act(z - distance, z < n_h - 1, 1)

    def begin(self):
        _, z = self.plan.place()
        copy = pltpu.make_async_copy(self.meta, self.meta_v.at[z], self.local.at[1])
        copy.start()
        copy.wait()

        @pl.when(z > 0)
        def _():
            for copy in self.hop(z, -1, True):
                copy.start()

        @pl.when(z < self.plan.n_h - 1)
        def _():
            for copy in self.hop(z, 1, True):
                copy.start()

    def pass_on(self, distance):
        def act(source, forwarded, way):
            for copy in self.hop(source, way, False):
                copy.wait_recv()

            @pl.when(forwarded)
            def _():
                for copy in self.hop(source, way, False):
                    copy.start()

        self.on_the_way(distance, act)

    def in_plane(self, chunk, mask):
        plan = self.plan
        e, z = plan.place()
        buffer = lax.rem(chunk, 2)
        at = pl.multiple_of((chunk * plan.n_e + mask) * plan.stride, 16)
        return remote(
            self.stage.at[buffer, :, pl.ds(mask * plan.stride, plan.stride), :],
            self.out.at[:, pl.ds(at, plan.stride), :],
            self.a_send.at[buffer, mask],
            self.a_recv.at[chunk, mask],
            (across(e, mask), z),
        )

    def meta_copy(self, chunk, mask):
        e, z = self.plan.place()
        return remote(
            self.meta_v.at[self.plan.source(z, chunk)],
            self.meta_out.at[chunk, mask],
            self.m_send.at[chunk, mask],
            self.m_recv.at[chunk, mask],
            (across(e, mask), z),
        )

    def chunk(self, chunk, target_of):
        plan = self.plan
        e, z = plan.place()
        buffer = lax.rem(chunk, 2)
        source = plan.source(z, chunk)

        @pl.when(chunk == 0)
        def _():
            copy = pltpu.make_async_copy(self.rows, self.rows_v.at[buffer], self.local.at[0])
            copy.start()
            copy.wait()

        @pl.when(chunk > 0)
        def _():
            self.pass_on(chunk)
            copy = pltpu.make_async_copy(
                self.land.at[source], self.rows_v.at[buffer], self.local.at[0]
            )
            copy.start()
            copy.wait()

        for mask in range(1, plan.n_e):
            self.meta_copy(chunk, mask).start()
        own_meta = pltpu.make_async_copy(
            self.meta_v.at[source], self.meta_out.at[chunk, 0], self.local.at[1]
        )
        own_meta.start()

        @pl.when(chunk >= 2)
        def _():
            for mask in range(1, plan.n_e):
                self.in_plane(chunk - 2, mask).wait_send()

        target = target_of(chunk)
        group = min(4, plan.n_e)
        for start in range(0, plan.n_e, group):
            for j in range(2):
                hot = jnp.concatenate(
                    [
                        slot_hits(plan, slot_base(plan, across(e, start + i), j), target)
                        for i in range(group)
                    ],
                    axis=0,
                )
                picked = dot(hot, self.rows_v[buffer]).astype(jnp.bfloat16)
                self.stage[
                    buffer, j, start * plan.stride : (start + group) * plan.stride, :
                ] = picked
            for mask in range(max(start, 1), start + group):
                self.in_plane(chunk, mask).start()
        at = pl.multiple_of(chunk * plan.rows, 16)
        own = pltpu.make_async_copy(
            self.stage.at[buffer, :, pl.ds(0, plan.stride), :],
            self.out.at[:, pl.ds(at, plan.stride), :],
            self.local.at[2],
        )
        own.start()
        own.wait()
        own_meta.wait()

    def arrived(self, chunk):
        for mask in range(1, self.plan.n_e):
            self.meta_copy(chunk, mask).wait_recv()
            self.in_plane(chunk, mask).wait_recv()

    def finish(self):
        plan = self.plan
        for chunk in range(max(0, plan.n_h - 2), plan.n_h):
            for mask in range(1, plan.n_e):
                self.in_plane(chunk, mask).wait_send()
        _, z = plan.place()

        @pl.when(z > 0)
        def _():
            for copy in self.hop(z, -1, True):
                copy.wait_send()

        @pl.when(z < plan.n_h - 1)
        def _():
            for copy in self.hop(z, 1, True):
                copy.wait_send()

        def act(source, forwarded, way):
            @pl.when(forwarded)
            def _():
                for copy in self.hop(source, way, False):
                    copy.wait_send()

        for distance in range(1, plan.n_h):
            self.on_the_way(distance, act)
        for chunk in range(plan.n_h):
            for mask in range(1, plan.n_e):
                self.meta_copy(chunk, mask).wait_send()


def same(index, other, count):
    return 1 - lax.div(lax.rem(index - other + count, count) + count - 1, count)


class Return:
    own_first = True

    def __init__(self, plan, back, land, out, stage, rows_v, sum_v, total, sems):
        self.plan = plan
        self.back, self.land, self.out = back, land, out
        self.stage, self.rows_v, self.sum_v, self.total = stage, rows_v, sum_v, total
        (self.b_send, self.b_recv, self.s_send, self.s_recv, self.local, self.own) = sems

    @staticmethod
    def sem_shapes(plan):
        dma = pltpu.SemaphoreType.DMA
        n_h, n_e = plan.n_h, plan.n_e
        return [
            dma((n_h, n_e)),
            dma((n_h, n_e)),
            dma((n_h,)),
            dma((2, n_h)),
            dma((2,)),
            dma((n_h,)),
        ]

    def goal(self, turn):
        n_h = self.plan.n_h
        _, z = self.plan.place()
        found = 0
        for here in range(n_h):
            others = [there for there in range(n_h) if there != here]
            others.sort(key=lambda d: n_h - 1 - d + here if d > here else d + n_h - 1 - here)
            order = [here] + others if self.own_first else others + [here]
            for when, there in enumerate(order):
                found = found + there * same(z, here, n_h) * same(turn, when, n_h)
        return found

    def chunk_of(self, goal):
        n_h = self.plan.n_h
        _, z = self.plan.place()
        sign = 1 - 2 * lax.div(z, n_h // 2)
        return lax.rem(sign * (goal - z) + n_h, n_h)

    def source(self, chunk, mask):
        raise NotImplementedError

    def in_plane(self, chunk, mask):
        plan = self.plan
        e, z = plan.place()
        return remote(
            self.source(chunk, mask),
            self.back.at[chunk, :, pl.ds(mask * plan.stride, plan.stride), :],
            self.b_send.at[chunk, mask],
            self.b_recv.at[chunk, mask],
            (across(e, mask), z),
        )

    def own_copy(self, chunk):
        plan = self.plan
        return pltpu.make_async_copy(
            self.source(chunk, 0),
            self.back.at[chunk, :, pl.ds(0, plan.stride), :],
            self.own.at[chunk],
        )

    def send(self, chunk):
        for mask in range(1, self.plan.n_e):
            self.in_plane(chunk, mask).start()
        self.own_copy(chunk).start()

    def hop(self, turn, goal, way):
        e, z = self.plan.place()
        side = (1 - way) // 2
        return remote(
            self.rows_v.at[lax.rem(turn, 2)],
            self.land.at[side, goal],
            self.s_send.at[turn],
            self.s_recv.at[side, goal],
            (e, z + way),
        )

    def each_way(self, goal, act):
        _, z = self.plan.place()

        @pl.when(goal > z)
        def _():
            act(1, z > 0)

        @pl.when(goal < z)
        def _():
            act(-1, z < self.plan.n_h - 1)

    def take(self, goal, way):
        side = (1 - way) // 2
        e, z = self.plan.place()
        remote(
            self.rows_v.at[0],
            self.land.at[side, goal],
            self.s_send.at[0],
            self.s_recv.at[side, goal],
            (e, z - way),
        ).wait_recv()
        copy = pltpu.make_async_copy(self.land.at[side, goal], self.sum_v, self.local.at[1])
        copy.start()
        copy.wait()
        return self.sum_v[...].astype(jnp.float32)

    def wait_hop(self, turn):
        goal = self.goal(turn)

        def act(way, _):
            self.hop(turn, goal, way).wait_send()

        self.each_way(goal, act)

    def fetched(self, chunk, buffer):
        return pltpu.make_async_copy(self.back.at[chunk], self.stage.at[buffer], self.local.at[0])

    def fetch(self, goal, chunk, buffer):
        for mask in range(1, self.plan.n_e):
            self.in_plane(chunk, mask).wait_recv()
        self.own_copy(chunk).wait()
        self.fetched(chunk, buffer).start()

    def combine(self, turn, target_of):
        plan = self.plan
        e, z = plan.place()
        goal = self.goal(turn)
        chunk = self.chunk_of(goal)
        target = target_of(chunk)
        buffer = lax.rem(turn, 2)
        self.fetch(goal, chunk, buffer)
        hot = [
            jnp.concatenate(
                [
                    slot_hits(plan, slot_base(plan, across(e, mask), j), target)
                    for mask in range(plan.n_e)
                ],
                axis=0,
            )
            for j in range(2)
        ]
        self.fetched(chunk, buffer).wait()

        @pl.when(turn >= 2)
        def _():
            self.wait_hop(turn - 2)

        part = contract_first(hot[0], self.stage[buffer, 0]) + contract_first(
            hot[1], self.stage[buffer, 1]
        )

        @pl.when(goal == z)
        def _():
            self.total[...] = part

        @pl.when(goal != z)
        def _():
            self.rows_v[buffer] = part.astype(jnp.bfloat16)

        def act(way, more):
            @pl.when(more)
            def _():
                so_far = self.take(goal, way)
                self.rows_v[buffer] = (self.rows_v[buffer].astype(jnp.float32) + so_far).astype(
                    jnp.bfloat16
                )

            self.hop(turn, goal, way).start()

        self.each_way(goal, act)

    def finish(self):
        plan = self.plan
        _, z = plan.place()
        for turn in range(plan.n_h - 2, plan.n_h):
            self.wait_hop(turn)

        @pl.when(z > 0)
        def _():
            self.total[...] += self.take(z, 1)

        @pl.when(z < plan.n_h - 1)
        def _():
            self.total[...] += self.take(z, -1)

        copy = pltpu.make_async_copy(self.total, self.out, self.local.at[0])
        copy.start()
        copy.wait()


class ReturnHeld(Return):
    own_first = False

    def __init__(self, plan, given, early, *rest):
        super().__init__(plan, *rest)
        self.given, self.early = given, early

    def fetch(self, goal, chunk, buffer):
        _, z = self.plan.place()

        @pl.when(goal != z)
        def _():
            Return.fetch(self, goal, chunk, buffer)

        @pl.when(goal == z)
        def _():
            pltpu.make_async_copy(self.early, self.stage.at[buffer], self.local.at[0]).start()

    def source(self, chunk, mask):
        plan = self.plan
        at = pl.multiple_of((chunk * plan.n_e + mask) * plan.stride, 16)
        return self.given.at[:, pl.ds(at, plan.stride), :]

    def sent(self):
        for chunk in range(1, self.plan.n_h):
            for mask in range(1, self.plan.n_e):
                self.in_plane(chunk, mask).wait_send()


class ReturnMade(Return):
    def __init__(self, plan, made, *rest):
        super().__init__(plan, *rest)
        self.made = made
        self.ring = made.shape[0]

    def source(self, chunk, mask):
        plan = self.plan
        return self.made.at[
            lax.rem(chunk, self.ring), :, pl.ds(mask * plan.stride, plan.stride), :
        ]

    def free(self, chunk):
        if self.plan.n_h > self.ring:

            @pl.when(chunk >= self.ring)
            def _():
                self.wait_sent(chunk - self.ring)
                self.own_copy(chunk - self.ring).wait()

    def wait_sent(self, chunk):
        for mask in range(1, self.plan.n_e):
            self.in_plane(chunk, mask).wait_send()

    def sent(self):
        for chunk in range(max(0, self.plan.n_h - self.ring), self.plan.n_h):
            self.wait_sent(chunk)


ANY = pl.BlockSpec(memory_space=pl.ANY)


def send_body(
    plan,
    n_d,
    rows,
    meta,
    query,
    key,
    value,
    lines,
    out,
    meta_out,
    land,
    soft_out,
    mixed_out,
    rows_v,
    meta_v,
    stage,
    query_v,
    key_v,
    value_v,
    soft_v,
    mixed_v,
    in_sem,
    soft_sem,
    mixed_sem,
    *sems,
):
    loads = [
        pltpu.make_async_copy(given, held, in_sem.at[i])
        for i, (given, held) in enumerate(((query, query_v), (key, key_v), (value, value_v)))
    ]
    for load in loads:
        load.start()
    greet(plan)
    work = Dispatch(plan, rows, meta, land, out, meta_out, rows_v, meta_v, stage, sems)
    work.begin()
    _, z = plan.place()
    for load in loads:
        load.wait()

    def soft_copy(pair):
        buffer = lax.rem(pair, 2)
        return pltpu.make_async_copy(
            soft_v.at[buffer], soft_out.at[pl.ds(2 * pair, 2)], soft_sem.at[buffer]
        )

    def mix_pair(pair):
        lanes = pl.ds(pl.multiple_of(pair * 2 * HEAD_DIM, 2 * HEAD_DIM), 2 * HEAD_DIM)
        both = [held[:, lanes] for held in (query_v, key_v, value_v)]

        @pl.when(pair >= 2)
        def _():
            soft_copy(pair - 2).wait()

        heads = []
        for head in range(2):
            at = slice(head * HEAD_DIM, (head + 1) * HEAD_DIM)
            heads.append(
                mix_head(
                    *[item[:, at] for item in both],
                    lines[pair, head : head + 1, :],
                    soft_v.at[lax.rem(pair, 2)],
                    head,
                )
            )
        mixed_v[:, lanes] = jnp.concatenate(heads, axis=1)
        soft_copy(pair).start()

    pairs = HEADS // 2
    each = -(-pairs // plan.n_h)

    @pl.loop(0, plan.n_h)
    def _(chunk):
        work.chunk(chunk, lambda at: meta_v[plan.source(z, at)])
        pl.loop(0, each)(lambda i: mix_pair(chunk * each + i))

    mixed_copy = pltpu.make_async_copy(mixed_v, mixed_out, mixed_sem.at[0])
    mixed_copy.start()
    soft_copy(pairs - 2).wait()
    soft_copy(pairs - 1).wait()
    mixed_copy.wait()
    for chunk in range(plan.n_h):
        work.arrived(chunk)
    work.finish()


def send_rows(plan, rows, meta, query, key, value, lines):
    n_h, n_e = plan.n_h, plan.n_e
    bf16, f32 = jnp.bfloat16, jnp.float32
    shape = jax.ShapeDtypeStruct
    sems = Dispatch.sem_shapes(plan)
    out = pl.pallas_call(
        functools.partial(send_body, plan, len(sems)),
        in_specs=[ANY] * 5 + [pl.BlockSpec(memory_space=pltpu.VMEM)],
        out_specs=[ANY] * 5,
        out_shape=[
            shape((2, plan.total, D), bf16),
            shape((n_h, n_e, 8, LEN), f32),
            shape((n_h, LEN, D), bf16),
            shape((HEADS, LEN, LEN), bf16),
            shape((LEN, D), bf16),
        ],
        scratch_shapes=[
            pltpu.VMEM((2, LEN, D), bf16),
            pltpu.VMEM((n_h, 8, LEN), f32),
            pltpu.VMEM((2, 2, plan.rows, D), bf16),
            pltpu.VMEM((LEN, D), bf16),
            pltpu.VMEM((LEN, D), bf16),
            pltpu.VMEM((LEN, D), bf16),
            pltpu.VMEM((2, 2, LEN, LEN), bf16),
            pltpu.VMEM((LEN, D), bf16),
            pltpu.SemaphoreType.DMA((3,)),
            pltpu.SemaphoreType.DMA((2,)),
            pltpu.SemaphoreType.DMA((1,)),
        ]
        + sems,
        compiler_params=pltpu.CompilerParams(
            collective_id=1, has_side_effects=True, vmem_limit_bytes=VMEM
        ),
        name="send_rows",
    )(rows, meta, query, key, value, lines.reshape(HEADS // 2, 2, 4 * NEAR))
    return out[0], out[1], out[3], out[4]


def expert_body(plan, halves, n_d, *refs):
    (
        sent,
        gates,
        grads,
        targets,
        w_gate,
        w_up,
        w_down,
        total_out,
        gg_out,
        rows_out,
        y_out,
        dgate_out,
        dup_out,
        act_out,
        meta_out,
        land,
        back,
        land_back,
        early,
        rows_v,
        meta_v,
        stage,
        wg_v,
        wu_v,
        wd_v,
        target_v,
        gate_v,
        x_v,
        g_v,
        dx_v,
        y_v,
        dgate_v,
        dup_v,
        act_v,
        gg_v,
        gg_back,
        gg_part,
        gg_land,
        sum_v,
        total,
        w_sem,
        t_sem,
        x_sem,
        o_sem,
        gg_send,
        gg_recv,
        ggs_send,
        ggs_recv,
        e_send,
        e_recv,
        *sems,
    ) = refs
    n_e, n_h = plan.n_e, plan.n_h
    e, z = plan.place()
    loads = [
        pltpu.make_async_copy(source, held, w_sem.at[i])
        for i, (source, held) in enumerate(((w_gate, wg_v), (w_up, wu_v), (w_down, wd_v)))
    ]
    for load in loads:
        load.start()
    targets_in = pltpu.make_async_copy(targets, target_v, t_sem.at[0])
    targets_in.start()
    greet(plan)
    work = Dispatch(
        plan, sent, gates, land, rows_out, meta_out, rows_v, meta_v, stage, sems[:n_d]
    )
    give = ReturnMade(
        plan, dx_v, back, land_back, total_out, stage, rows_v, sum_v, total, sems[n_d:]
    )
    work.begin()
    targets_in.wait()
    ahead = min(3, n_h)
    pl.loop(0, ahead)(lambda chunk: work.chunk(chunk, lambda at: target_v[at, 0]))
    for load in loads:
        load.wait()

    def gg_copy(chunk, mask):
        return remote(
            gg_v.at[chunk, mask],
            gg_back.at[chunk, mask],
            gg_send.at[chunk, mask],
            gg_recv.at[chunk, mask],
            (across(e, mask), z),
        )

    def gg_along(chunk):
        return remote(
            gg_part.at[chunk],
            gg_land.at[z],
            ggs_send.at[chunk],
            ggs_recv.at[z],
            (e, plan.source(z, chunk)),
        )

    def gg_from(distance):
        other = lax.rem(z + distance, n_h)
        return other, remote(
            gg_part.at[0], gg_land.at[other], ggs_send.at[0], ggs_recv.at[other], (e, other)
        )

    def outs(chunk, j):
        at = pl.multiple_of(chunk * plan.rows, 16)
        return [
            pltpu.make_async_copy(held.at[j], out.at[j, pl.ds(at, plan.rows), :], o_sem.at[i, j])
            for i, (held, out) in enumerate(
                ((y_v, y_out), (dgate_v, dgate_out), (dup_v, dup_out), (act_v, act_out))
            )
        ]

    all_held = n_h <= dx_v.shape[0]
    masks = n_e // halves
    piece = masks * plan.stride

    def step(chunk, index):
        j, half = lax.div(index, halves), lax.rem(index, halves)
        at = pl.ds(pl.multiple_of(half * piece, 16), piece)
        rows, grads_in = x_v[j, at, :], g_v[j, at, :]
        gate_pre = contract_last(rows, wg_v[j])
        up_pre = contract_last(rows, wu_v[j])
        raw = contract_last(grads_in, wd_v[j])
        slots = lax.broadcasted_iota(jnp.int32, (plan.stride, LEN), 0).astype(
            jnp.float32
        ) + slot_base(plan, e, j)
        columns = []
        for i in range(masks):
            mask = half * masks + i
            aim, weight = target_v[chunk, mask], gate_v[mask]
            hit = jnp.where(slots == aim[0:1, :], weight[0:1, :], 0.0)
            hit = hit + jnp.where(slots == aim[1:2, :], weight[1:2, :], 0.0)
            columns.append(jnp.sum(hit, axis=1, keepdims=True))
        gate = jnp.concatenate(columns, axis=0)
        square = gate_pre * gate_pre
        tanh = jnp.tanh(0.7978845608028654 * gate_pre * (1.0 + 0.044715 * square))
        side = 0.5 * (1.0 + tanh)
        gelu = gate_pre * side
        slope = side + 0.5 * gate_pre * (1.0 - tanh * tanh) * (
            0.7978845608028654 * (1.0 + 0.134145 * square)
        )
        act = gelu * up_pre
        act_low = act.astype(jnp.bfloat16)
        dots = jnp.sum(act_low.astype(jnp.float32) * raw, axis=1, keepdims=True)
        for i in range(masks):
            mask = half * masks + i
            aim, part = target_v[chunk, mask], dots[i * plan.stride : (i + 1) * plan.stride]
            for k in range(2):
                line = jnp.sum(
                    jnp.where(slots == aim[k : k + 1, :], part, 0.0), axis=0, keepdims=True
                )
                gg_v[chunk, mask, k : k + 1, :] += line
        grad_act = gate * raw
        grad_gate = (grad_act * up_pre * slope).astype(jnp.bfloat16)
        grad_up = (grad_act * gelu).astype(jnp.bfloat16)
        dgate_v[j, at, :] = grad_gate
        dup_v[j, at, :] = grad_up
        act_v[j, at, :] = (act * gate).astype(jnp.bfloat16)
        dx_v[lax.rem(chunk, dx_v.shape[0]), j, at, :] = (
            dot(grad_gate, wg_v[j]) + dot(grad_up, wu_v[j])
        ).astype(jnp.bfloat16)
        y_v[j, at, :] = (dot(act_low, wd_v[j]) * gate).astype(jnp.bfloat16)

    gg_v[...] = jnp.zeros_like(gg_v)

    @pl.loop(0, n_h)
    def _(chunk):
        work.arrived(chunk)
        at = pl.multiple_of(chunk * plan.rows, 16)
        gate_in = pltpu.make_async_copy(meta_out.at[chunk], gate_v, t_sem.at[0])
        gate_in.start()
        ins = [
            pltpu.make_async_copy(source.at[:, pl.ds(at, plan.rows), :], held, x_sem.at[i])
            for i, (source, held) in enumerate(((rows_out, x_v), (grads, g_v)))
        ]
        for copy in ins:
            copy.start()
        give.free(chunk)

        @pl.when(chunk > 0)
        def _():
            for j in range(2):
                for copy in outs(chunk - 1, j):
                    copy.wait()

        gate_in.wait()
        for copy in ins:
            copy.wait()
        pl.loop(0, 2 * halves)(lambda index: step(chunk, index))
        for j in range(2):
            for copy in outs(chunk, j):
                copy.start()

        @pl.when(chunk + ahead < n_h)
        def _():
            work.chunk(chunk + ahead, lambda at: target_v[at, 0])

        for mask in range(1, n_e):
            gg_copy(chunk, mask).start()

        @pl.when((chunk < 1) | (not all_held))
        def _():
            give.send(chunk)

    def early_copy(mask):
        at = pl.ds(mask * plan.stride, plan.stride)
        if mask == 0:
            return pltpu.make_async_copy(y_out.at[:, at, :], early.at[:, at, :], e_send.at[0])
        return remote(
            y_out.at[:, at, :],
            early.at[:, at, :],
            e_send.at[mask],
            e_recv.at[mask],
            (across(e, mask), z),
        )

    if all_held:
        pl.loop(1, n_h)(lambda turn: give.send(give.chunk_of(give.goal(turn))))
    for mask in range(n_e):
        early_copy(mask).start()
    work.finish()
    for j in range(2):
        for copy in outs(n_h - 1, j):
            copy.wait()

    @pl.loop(0, n_h)
    def _(turn):
        chunk = give.chunk_of(give.goal(turn))
        part = gg_v[chunk, 0]
        for mask in range(1, n_e):
            gg_copy(chunk, mask).wait_recv()
            part = part + gg_back[chunk, mask]
        gg_part[chunk] = part

        @pl.when(chunk > 0)
        def _():
            gg_along(chunk).start()

        give.combine(turn, lambda at: target_v[at, 0])

    give.sent()
    early_copy(0).wait()
    for mask in range(1, n_e):
        early_copy(mask).wait()
    for chunk in range(n_h):
        for mask in range(1, n_e):
            gg_copy(chunk, mask).wait_send()
    sum_gg = gg_part[0]
    for distance in range(1, n_h):
        other, arrival = gg_from(distance)
        arrival.wait_recv()
        sum_gg = sum_gg + gg_land[other]
    gg_out[...] = sum_gg
    for chunk in range(1, n_h):
        gg_along(chunk).wait_send()
    give.finish()


def run_experts(plan, sent, gates, grads, targets, w_gate, w_up, w_down):
    n_h, n_e, width = plan.n_h, plan.n_e, plan.width
    bf16, f32 = jnp.bfloat16, jnp.float32
    shape = jax.ShapeDtypeStruct
    dma = pltpu.SemaphoreType.DMA
    ring = min(4, n_h)
    d_sems, r_sems = Dispatch.sem_shapes(plan), Return.sem_shapes(plan)
    halves = 2 if plan.rows <= 640 else 4
    return pl.pallas_call(
        functools.partial(expert_body, plan, halves, len(d_sems)),
        in_specs=[ANY] * 7,
        out_specs=[ANY, pl.BlockSpec(memory_space=pltpu.VMEM)] + [ANY] * 10,
        out_shape=[
            shape((LEN, D), f32),
            shape((8, LEN), f32),
            shape((2, plan.total, D), bf16),
            shape((2, plan.total, D), bf16),
            shape((2, plan.total, width), bf16),
            shape((2, plan.total, width), bf16),
            shape((2, plan.total, width), bf16),
            shape((n_h, n_e, 8, LEN), f32),
            shape((n_h, LEN, D), bf16),
            shape((n_h, 2, plan.rows, D), bf16),
            shape((2, n_h, LEN, D), bf16),
            shape((2, plan.rows, D), bf16),
        ],
        scratch_shapes=[
            pltpu.VMEM((2, LEN, D), bf16),
            pltpu.VMEM((n_h, 8, LEN), f32),
            pltpu.VMEM((2, 2, plan.rows, D), bf16),
            pltpu.VMEM((2, width, D), bf16),
            pltpu.VMEM((2, width, D), bf16),
            pltpu.VMEM((2, width, D), bf16),
            pltpu.VMEM((n_h, n_e, 8, LEN), f32),
            pltpu.VMEM((n_e, 8, LEN), f32),
            pltpu.VMEM((2, plan.rows, D), bf16),
            pltpu.VMEM((2, plan.rows, D), bf16),
            pltpu.VMEM((ring, 2, plan.rows, D), bf16),
            pltpu.VMEM((2, plan.rows, D), bf16),
            pltpu.VMEM((2, plan.rows, width), bf16),
            pltpu.VMEM((2, plan.rows, width), bf16),
            pltpu.VMEM((2, plan.rows, width), bf16),
            pltpu.VMEM((n_h, n_e, 8, LEN), f32),
            pltpu.VMEM((n_h, n_e, 8, LEN), f32),
            pltpu.VMEM((n_h, 8, LEN), f32),
            pltpu.VMEM((n_h, 8, LEN), f32),
            pltpu.VMEM((LEN, D), bf16),
            pltpu.VMEM((LEN, D), f32),
            dma((3,)),
            dma((1,)),
            dma((2,)),
            dma((4, 2)),
            dma((n_h, n_e)),
            dma((n_h, n_e)),
            dma((n_h,)),
            dma((n_h,)),
            dma((n_e,)),
            dma((n_e,)),
        ]
        + d_sems
        + r_sems,
        compiler_params=pltpu.CompilerParams(
            collective_id=2, has_side_effects=True, vmem_limit_bytes=VMEM
        ),
        name="run_experts",
    )(sent, gates, grads, targets, jnp.swapaxes(w_gate, 1, 2), jnp.swapaxes(w_up, 1, 2), w_down)


def back_body(
    plan, given, early, targets, out, back, land, rows_v, stage, target_v, sum_v, total, t_sem, *sems
):
    targets_in = pltpu.make_async_copy(targets, target_v, t_sem.at[0])
    targets_in.start()
    greet(plan)
    give = ReturnHeld(plan, given, early, back, land, out, stage, rows_v, sum_v, total, sems)
    pl.loop(0, plan.n_h - 1)(lambda turn: give.send(give.chunk_of(give.goal(turn))))
    targets_in.wait()
    pl.loop(0, plan.n_h)(lambda turn: give.combine(turn, lambda at: target_v[at, 0]))
    give.sent()
    give.finish()


def bring_back(plan, given, early, targets):
    n_h, n_e = plan.n_h, plan.n_e
    bf16, f32 = jnp.bfloat16, jnp.float32
    shape = jax.ShapeDtypeStruct
    return pl.pallas_call(
        functools.partial(back_body, plan),
        in_specs=[ANY] * 3,
        out_specs=[ANY] * 3,
        out_shape=[
            shape((LEN, D), f32),
            shape((n_h, 2, plan.rows, D), bf16),
            shape((2, n_h, LEN, D), bf16),
        ],
        scratch_shapes=[
            pltpu.VMEM((2, LEN, D), bf16),
            pltpu.VMEM((2, 2, plan.rows, D), bf16),
            pltpu.VMEM((n_h, n_e, 8, LEN), f32),
            pltpu.VMEM((LEN, D), bf16),
            pltpu.VMEM((LEN, D), f32),
            pltpu.SemaphoreType.DMA((1,)),
        ]
        + Return.sem_shapes(plan),
        compiler_params=pltpu.CompilerParams(
            collective_id=3, has_side_effects=True, vmem_limit_bytes=VMEM
        ),
        name="bring_back",
    )(given, early, targets)[0]


def per_device(
    n_e,
    n_h,
    tokens,
    gain_one,
    w_query,
    w_key,
    w_value,
    w_out,
    bias_table,
    gain_two,
    w_router,
    w_gate,
    w_up,
    w_down,
    routes,
    cotangent,
):
    experts_all = w_router.shape[1]
    plan = Plan(n_e, n_h, experts_all, w_gate.shape[2])
    both = ("expert", "hidden")

    def small(array):
        return jnp.pad(array.astype(jnp.float32), ((0, 8 - array.shape[0]), (0, 0)))

    targets = small(slot_targets(routes, experts_all, plan.capacity, plan.stride))
    hot_bucket = offset_buckets()
    inputs = tokens.astype(jnp.float32)
    inv_one = lax.rsqrt(jnp.mean(inputs * inputs, axis=-1, keepdims=True) + eps)
    normed_one = (inputs * inv_one * gain_one).astype(jnp.bfloat16)
    query_rows = dot(normed_one, w_query).astype(jnp.bfloat16)
    key_rows = dot(normed_one, w_key).astype(jnp.bfloat16)
    value_rows = dot(normed_one, w_value).astype(jnp.bfloat16)
    lines = jnp.dot(hot_bucket, bias_table, precision=precise).T
    grads_in, targets_all, soft, mixed_rows = send_rows(
        plan, cotangent, targets, query_rows, key_rows, value_rows, lines
    )
    hidden = inputs + dot(mixed_rows, w_out)
    inv_two = lax.rsqrt(jnp.mean(hidden * hidden, axis=-1, keepdims=True) + eps)
    normed_two = hidden * inv_two * gain_two
    sent = normed_two.astype(jnp.bfloat16)
    logits = jnp.dot(normed_two, w_router, precision=precise)
    route_hot = (routes[:, :, None] == jnp.arange(experts_all, dtype=jnp.int32)).astype(jnp.float32)
    chosen = jnp.sum(route_hot * logits[:, None, :], axis=-1)
    gate_values = jax.nn.softmax(chosen, axis=-1)
    made = run_experts(
        plan, sent, small(gate_values.T), grads_in, targets_all, w_gate, w_up, w_down
    )
    grad_sent, grad_gates, rows_in, y_rows, gate_rows, up_rows, act_rows = made[:7]
    y_early = made[-1]
    grad_gates = grad_gates[:2].T
    grad_out = cotangent.astype(jnp.float32)
    grad_chosen = gate_values * (
        grad_gates - jnp.sum(gate_values * grad_gates, axis=-1, keepdims=True)
    )
    grad_logits = jnp.sum(route_hot * grad_chosen[:, :, None], axis=1)
    router_grad = contract_first(grad_logits, normed_two, precise)
    grad_normed_two = contract_last(grad_logits, w_router, precise) + grad_sent
    gain_two_grad = jnp.sum(grad_normed_two * hidden * inv_two, axis=0)
    scaled_two = grad_normed_two * gain_two
    grad_hidden = (
        grad_out
        + inv_two * scaled_two
        - hidden * inv_two**3 * jnp.mean(scaled_two * hidden, axis=-1, keepdims=True)
    )
    grad_branch = grad_hidden.astype(jnp.bfloat16)
    w_out_grad = contract_first(mixed_rows, grad_branch)
    grad_mixed = contract_last(grad_branch, w_out).astype(jnp.bfloat16)
    grad_query, grad_key, grad_value, grad_lines = unmix(
        query_rows, key_rows, value_rows, grad_mixed, soft
    )
    bias_table_grad = jnp.dot(grad_lines, hot_bucket, precision=precise).T
    query_grad = contract_first(normed_one, grad_query)
    key_grad = contract_first(normed_one, grad_key)
    value_grad = contract_first(normed_one, grad_value)
    grad_normed_one = (
        contract_last(grad_query, w_query)
        + contract_last(grad_key, w_key)
        + contract_last(grad_value, w_value)
    )
    gain_one_grad = jnp.sum(grad_normed_one * inputs * inv_one, axis=0)
    scaled_one = grad_normed_one * gain_one
    tokens_grad = (
        grad_hidden
        + inv_one * scaled_one
        - inputs * inv_one**3 * jnp.mean(scaled_one * inputs, axis=-1, keepdims=True)
    )
    last = jnp.pad(bias_table_grad.reshape(1, BUCKETS * HEADS), ((0, 0), (0, D - BUCKETS * HEADS)))
    few = jnp.concatenate([router_grad, gain_one_grad[None], gain_two_grad[None], last], axis=0)
    few = jnp.pad(few, ((0, -few.shape[0] % 16), (0, 0)))
    low = [
        item.astype(jnp.bfloat16) for item in (query_grad, key_grad, value_grad, w_out_grad, few)
    ]
    low, gate_rows, up_rows, act_rows, y_rows = lax.optimization_barrier(
        (low, gate_rows, up_rows, act_rows, y_rows)
    )
    summed = [item.astype(jnp.float32) for item in lax.psum(low, both)]
    few = summed[4]
    branch = bring_back(plan, y_rows, y_early, targets_all)
    block_out = (hidden + branch).astype(jnp.bfloat16)
    down_grad = jnp.einsum("xrf,xrd->xfd", act_rows, grads_in, preferred_element_type=jnp.float32)
    gate_grad = jnp.einsum("xrd,xrf->xdf", rows_in, gate_rows, preferred_element_type=jnp.float32)
    up_grad = jnp.einsum("xrd,xrf->xdf", rows_in, up_rows, preferred_element_type=jnp.float32)
    return (
        block_out,
        tokens_grad,
        few[experts_all],
        *summed[:4],
        few[experts_all + 2, : BUCKETS * HEADS].reshape(BUCKETS, HEADS),
        few[experts_all + 1],
        few[:experts_all].T,
        gate_grad,
        up_grad,
        down_grad,
    )


def solution(mesh):
    in_specs = (
        P(("expert", "hidden"), None),
        P(),
        P(),
        P(),
        P(),
        P(),
        P(),
        P(),
        P(),
        P("expert", None, "hidden"),
        P("expert", None, "hidden"),
        P("expert", "hidden", None),
        P(("expert", "hidden"), None),
        P(("expert", "hidden"), None),
    )
    out_specs = (
        P(("expert", "hidden"), None),
        P(("expert", "hidden"), None),
        P(),
        P(),
        P(),
        P(),
        P(),
        P(),
        P(),
        P(),
        P("expert", None, "hidden"),
        P("expert", None, "hidden"),
        P("expert", "hidden", None),
    )
    return jax.shard_map(
        functools.partial(per_device, mesh.shape["expert"], mesh.shape["hidden"]),
        mesh=mesh, in_specs=in_specs, out_specs=out_specs, check_vma=False
    )
```

```python
import functools

import jax
import jax.numpy as jnp
from jax import lax
from jax.experimental import pallas as pl
from jax.experimental.pallas import tpu as pltpu
from jax.sharding import PartitionSpec as P

D = 1024
HEADS = 16
HEAD_DIM = 64
BUCKETS = 32
LEN = 512
MICRO = 2
MB_TOK = 256
VMEM = 62 * 1024 * 1024
MESH = pl.DeviceIdType.MESH


eps = 1e-06
precise = lax.Precision.HIGHEST
thresholds = (12, 16, 23, 32, 46, 64, 91)


def contract_last(matrix_a, matrix_b, mode=None):
    return lax.dot_general(
        matrix_a,
        matrix_b,
        (((1,), (1,)), ((), ())),
        precision=mode,
        preferred_element_type=jnp.float32,
    )


def contract_first(matrix_a, matrix_b, mode=None):
    return lax.dot_general(
        matrix_a,
        matrix_b,
        (((0,), (0,)), ((), ())),
        precision=mode,
        preferred_element_type=jnp.float32,
    )


def dot(matrix_a, matrix_b):
    return jnp.dot(matrix_a, matrix_b, preferred_element_type=jnp.float32)


def dot_high(matrix_a, matrix_b):
    return jnp.dot(matrix_a, matrix_b, precision=precise, preferred_element_type=jnp.float32)


def slot_targets(routes, experts_all, capacity, stride):
    pairs = 2 * MB_TOK
    flat = routes.reshape(-1, pairs)
    hits = (flat[:, :, None] == jnp.arange(experts_all, dtype=jnp.int32)).astype(jnp.bfloat16)
    lower = (
        jnp.arange(pairs, dtype=jnp.int32)[:, None] > jnp.arange(pairs, dtype=jnp.int32)[None, :]
    ).astype(jnp.bfloat16)
    earlier = jnp.einsum("pq,bqe->bpe", lower, hits, preferred_element_type=jnp.float32)
    rank = jnp.sum(earlier * hits.astype(jnp.float32), axis=-1).astype(jnp.int32)
    block = jnp.arange(flat.shape[0], dtype=jnp.int32)[:, None]
    target = flat * stride + block * capacity + rank
    return target.reshape(-1, 2).T


NEAR = 128


def offset_buckets():
    offset = jnp.arange(4 * NEAR, dtype=jnp.int32) - 2 * NEAR
    distance = jnp.abs(offset)
    far_bucket = 8 + sum(((distance >= threshold).astype(jnp.int32) for threshold in thresholds))
    bucket = jnp.where(distance < 8, distance, far_bucket) + 16 * (offset > 0).astype(jnp.int32)
    return (bucket[:, None] == jnp.arange(BUCKETS, dtype=jnp.int32)).astype(jnp.float32)


def bias_tiles(line):
    return pltpu.roll(
        jnp.broadcast_to(line, (NEAR, 4 * NEAR)), 0, 1, stride=1, stride_axis=0
    )


def mix_head(query, key, value, line, soft_ref, head):
    tiles = bias_tiles(line)
    blocks = LEN // NEAR
    outs = []
    for i in range(blocks):
        raw = contract_last(query[i * NEAR : (i + 1) * NEAR], key) * (HEAD_DIM**-0.5)
        parts = []
        for j in range(blocks):
            part = raw[:, j * NEAR : (j + 1) * NEAR]
            if abs(j - i) <= 1:
                parts.append(part + tiles[:, (j - i + 2) * NEAR : (j - i + 3) * NEAR])
            else:
                edge = 1 if j < i else 4 * NEAR - 1
                parts.append(part + line[:, edge : edge + 1])
        scores = jnp.concatenate(parts, axis=1)
        terms = jnp.exp(scores - jnp.max(scores, axis=1, keepdims=True))
        soft = (terms * (1.0 / jnp.sum(terms, axis=1, keepdims=True))).astype(jnp.bfloat16)
        soft_ref[head, i * NEAR : (i + 1) * NEAR, :] = soft
        outs.append(dot(soft, value))
    return jnp.concatenate(outs, axis=0).astype(jnp.bfloat16)


def unmix_head(query, key, value, grad_mixed, soft_ref, grads_v, head):
    blocks = LEN // NEAR
    near = [jnp.zeros((NEAR, NEAR), jnp.float32) for _ in range(3)]
    below = jnp.zeros((NEAR, NEAR), jnp.float32)
    above = jnp.zeros((NEAR, NEAR), jnp.float32)
    grad_query = []
    for i in range(blocks):
        at = slice(i * NEAR, (i + 1) * NEAR)
        soft = soft_ref[head, at, :].astype(jnp.float32)
        grad_soft = contract_last(grad_mixed[at], value)
        product = soft * grad_soft
        grad = product - soft * jnp.sum(product, axis=1, keepdims=True)
        low = grad.astype(jnp.bfloat16)
        grads_v[at, :] = low
        grad_query.append(dot(low, key))
        wide = low.astype(jnp.float32)
        for j in range(blocks):
            part = wide[:, j * NEAR : (j + 1) * NEAR]
            if abs(j - i) <= 1:
                near[j - i + 1] = near[j - i + 1] + part
            elif j < i:
                below = below + part
            else:
                above = above + part
    band = jnp.concatenate([jnp.zeros((NEAR, NEAR), jnp.float32)] + near, axis=1)
    eight = band[0:8]
    for i in range(8, NEAR, 8):
        eight = eight + pltpu.roll(band[i : i + 8], 4 * NEAR - i, 1)
    row = lax.broadcasted_iota(jnp.int32, (8, 4 * NEAR), 0)
    for bit in (1, 2, 4):
        eight = jnp.where(lax.rem(lax.div(row, bit), 2) == 1, pltpu.roll(eight, 4 * NEAR - bit, 1), eight)
    line = jnp.sum(eight, axis=0, keepdims=True)
    column = lax.broadcasted_iota(jnp.int32, (1, 4 * NEAR), 1)
    line = line + jnp.where(column == 1, jnp.sum(below), 0.0)
    line = line + jnp.where(column == 4 * NEAR - 1, jnp.sum(above), 0.0)
    scaling = HEAD_DIM**-0.5
    grad_query = (jnp.concatenate(grad_query, axis=0) * scaling).astype(jnp.bfloat16)
    grad_key = (contract_first(grads_v[...], query) * scaling).astype(jnp.bfloat16)
    grad_value = contract_first(soft_ref[head], grad_mixed).astype(jnp.bfloat16)
    return grad_query, grad_key, grad_value, line


class Plan:
    def __init__(self, n_e, n_h, experts_all, width):
        self.n_e, self.n_h, self.width = n_e, n_h, width
        self.capacity = 10 * MB_TOK // (4 * experts_all)
        self.stride = -(-MICRO * self.capacity // 16) * 16
        self.span = 2 * self.stride
        self.rows = n_e * self.stride
        self.total = n_h * self.rows
        self.relayed = n_e - 1 if (n_e, n_h) == (8, 4) else n_e
        self.summed = (n_e, n_h) == (8, 4)

    def place(self):
        return lax.axis_index("expert"), lax.axis_index("hidden")

    def chunk(self, z, source):
        sign = 1 - 2 * lax.div(z, self.n_h // 2)
        return lax.rem(sign * (source - z) + self.n_h, self.n_h)

    def source(self, z, chunk):
        sign = 1 - 2 * lax.div(z, self.n_h // 2)
        return lax.rem(z + self.n_h + sign * chunk, self.n_h)


def across(here, mask):
    there, bit = here, 1
    while bit <= mask:
        if mask & bit:
            there = there + bit * (1 - 2 * lax.rem(lax.div(here, bit), 2))
        bit *= 2
    return there


def remote(src, dst, send_sem, recv_sem, device):
    return pltpu.make_async_remote_copy(
        src_ref=src,
        dst_ref=dst,
        send_sem=send_sem,
        recv_sem=recv_sem,
        device_id=device,
        device_id_type=MESH,
    )


def greet(plan):
    e, z = plan.place()
    barrier = pltpu.get_barrier_semaphore()
    for mask in range(1, plan.n_e):
        pl.semaphore_signal(barrier, inc=1, device_id=(across(e, mask), z), device_id_type=MESH)
    for shift in range(1, plan.n_h):
        pl.semaphore_signal(
            barrier, inc=1, device_id=(e, lax.rem(z + shift, plan.n_h)), device_id_type=MESH
        )
    pl.semaphore_wait(barrier, plan.n_e + plan.n_h - 2)


def slot_hits(plan, base, target):
    slots = lax.broadcasted_iota(jnp.int32, (plan.stride, LEN), 0).astype(jnp.float32) + base
    return jnp.where((slots == target[0:1, :]) | (slots == target[1:2, :]), 1.0, 0.0).astype(
        jnp.bfloat16
    )


def slot_base(plan, device, j):
    return (device * plan.span + j * plan.stride).astype(jnp.float32)


class Dispatch:
    def __init__(self, plan, rows, meta, land, out, meta_out, rows_v, meta_v, stage, sems):
        self.plan = plan
        self.rows, self.meta, self.land = rows, meta, land
        self.out, self.meta_out = out, meta_out
        self.rows_v, self.meta_v, self.stage = rows_v, meta_v, stage
        (
            self.z_send,
            self.z_recv,
            self.zm_send,
            self.zm_recv,
            self.a_send,
            self.a_recv,
            self.m_send,
            self.m_recv,
            self.r_send,
            self.r_recv,
            self.local,
        ) = sems

    @staticmethod
    def sem_shapes(plan):
        dma = pltpu.SemaphoreType.DMA
        n_h, n_e = plan.n_h, plan.n_e
        return [
            dma((n_h, 2)),
            dma((n_h,)),
            dma((n_h, 2)),
            dma((n_h,)),
            dma((2, n_e)),
            dma((n_h, n_e)),
            dma((n_h, n_e)),
            dma((n_h, n_e)),
            dma((n_h, 2)),
            dma((n_h,)),
            dma((3,)),
        ]

    def hop(self, source, way, own):
        e, z = self.plan.place()
        sems = [
            (self.z_send.at[source, (way + 1) // 2], self.z_recv.at[source]),
            (self.zm_send.at[source, (way + 1) // 2], self.zm_recv.at[source]),
        ]
        return (
            remote(self.meta_v.at[source], self.meta_v.at[source], *sems[1], (e, z + way)),
            remote(
                self.rows if own else self.land.at[source],
                self.land.at[source],
                *sems[0],
                (e, z + way),
            ),
        )

    def on_the_way(self, distance, act):
        n_h = self.plan.n_h
        _, z = self.plan.place()

        @pl.when(z + distance < n_h)
        def _():
            act(z + distance, z > 0, -1)

        @pl.when(z >= distance)
        def _():
            act(z - distance, z < n_h - 1, 1)

    def begin(self):
        _, z = self.plan.place()
        copy = pltpu.make_async_copy(self.meta, self.meta_v.at[z], self.local.at[1])
        copy.start()
        copy.wait()

        @pl.when(z > 0)
        def _():
            for copy in self.hop(z, -1, True):
                copy.start()

        @pl.when(z < self.plan.n_h - 1)
        def _():
            for copy in self.hop(z, 1, True):
                copy.start()

    def pass_on(self, distance):
        def act(source, forwarded, way):
            for copy in self.hop(source, way, False):
                copy.wait_recv()

            @pl.when(forwarded)
            def _():
                for copy in self.hop(source, way, False):
                    copy.start()

        self.on_the_way(distance, act)

    def in_plane(self, chunk, mask):
        plan = self.plan
        e, z = plan.place()
        buffer = lax.rem(chunk, 2)
        at = pl.multiple_of((chunk * plan.n_e + mask) * plan.stride, 16)
        return remote(
            self.stage.at[buffer, :, pl.ds(mask * plan.stride, plan.stride), :],
            self.out.at[:, pl.ds(at, plan.stride), :],
            self.a_send.at[buffer, mask],
            self.a_recv.at[chunk, mask],
            (across(e, mask), z),
        )

    def meta_copy(self, chunk, mask):
        e, z = self.plan.place()
        return remote(
            self.meta_v.at[self.plan.source(z, chunk)],
            self.meta_out.at[chunk, mask],
            self.m_send.at[chunk, mask],
            self.m_recv.at[chunk, mask],
            (across(e, mask), z),
        )

    def relay_copy(self, source, way):
        plan = self.plan
        e, z = plan.place()

        def at(place):
            chunk = plan.chunk(place, source)
            return pl.ds(
                pl.multiple_of((chunk * plan.n_e + plan.relayed) * plan.stride, 16), plan.stride
            )

        return remote(
            self.out.at[:, at(z), :],
            self.out.at[:, at(z + way), :],
            self.r_send.at[source, (way + 1) // 2],
            self.r_recv.at[source],
            (e, z + way),
        )

    def relay(self, distance):
        plan = self.plan
        if plan.relayed == plan.n_e:
            return
        _, z = plan.place()

        @pl.when(distance == 0)
        def _():
            self.in_plane(0, plan.relayed).wait_recv()

            @pl.when(z > 0)
            def _():
                self.relay_copy(z, -1).start()

            @pl.when(z < plan.n_h - 1)
            def _():
                self.relay_copy(z, 1).start()

        def act(source, forwarded, way):
            chunk = plan.chunk(z, source)
            at = pl.ds(
                pl.multiple_of((chunk * plan.n_e + plan.relayed) * plan.stride, 16), plan.stride
            )
            e, _ = plan.place()
            remote(
                self.out.at[:, at, :],
                self.out.at[:, at, :],
                self.r_send.at[source, 0],
                self.r_recv.at[source],
                (e, z - way),
            ).wait_recv()

            @pl.when(forwarded)
            def _():
                self.relay_copy(source, way).start()

        @pl.when(distance > 0)
        def _():
            self.on_the_way(distance, act)

    def chunk(self, chunk, target_of):
        plan = self.plan
        e, z = plan.place()
        buffer = lax.rem(chunk, 2)
        source = plan.source(z, chunk)

        @pl.when(chunk == 0)
        def _():
            copy = pltpu.make_async_copy(self.rows, self.rows_v.at[buffer], self.local.at[0])
            copy.start()
            copy.wait()

        @pl.when(chunk > 0)
        def _():
            self.pass_on(chunk)
            copy = pltpu.make_async_copy(
                self.land.at[source], self.rows_v.at[buffer], self.local.at[0]
            )
            copy.start()
            copy.wait()

        for mask in range(1, plan.n_e):
            self.meta_copy(chunk, mask).start()
        own_meta = pltpu.make_async_copy(
            self.meta_v.at[source], self.meta_out.at[chunk, 0], self.local.at[1]
        )
        own_meta.start()

        @pl.when(chunk >= 2)
        def _():
            self.wait_sent(chunk - 2)

        target = target_of(chunk)
        group = min(4, plan.n_e)
        for start in range(plan.n_e - group, -1, -group):
            for j in range(2):
                hot = jnp.concatenate(
                    [
                        slot_hits(plan, slot_base(plan, across(e, start + i), j), target)
                        for i in range(group)
                    ],
                    axis=0,
                )
                picked = dot(hot, self.rows_v[buffer]).astype(jnp.bfloat16)
                self.stage[
                    buffer, j, start * plan.stride : (start + group) * plan.stride, :
                ] = picked
            if start <= plan.relayed < start + group:

                @pl.when(chunk == 0)
                def _():
                    self.in_plane(chunk, plan.relayed).start()

            for mask in range(max(start, 1), min(start + group, plan.relayed)):
                self.in_plane(chunk, mask).start()
        at = pl.multiple_of(chunk * plan.rows, 16)
        own = pltpu.make_async_copy(
            self.stage.at[buffer, :, pl.ds(0, plan.stride), :],
            self.out.at[:, pl.ds(at, plan.stride), :],
            self.local.at[2],
        )
        own.start()
        own.wait()
        own_meta.wait()

    def wait_sent(self, chunk):
        for mask in range(1, self.plan.relayed):
            self.in_plane(chunk, mask).wait_send()
        if self.plan.relayed < self.plan.n_e:

            @pl.when(chunk == 0)
            def _():
                self.in_plane(chunk, self.plan.relayed).wait_send()

    def told(self, chunk):
        for mask in range(1, self.plan.n_e):
            self.meta_copy(chunk, mask).wait_recv()

    def arrived(self, chunk):
        for mask in range(1, self.plan.relayed):
            self.in_plane(chunk, mask).wait_recv()

    def finish(self):
        plan = self.plan
        for chunk in range(max(0, plan.n_h - 2), plan.n_h):
            self.wait_sent(chunk)
        _, z = plan.place()

        @pl.when(z > 0)
        def _():
            for copy in self.hop(z, -1, True):
                copy.wait_send()

        @pl.when(z < plan.n_h - 1)
        def _():
            for copy in self.hop(z, 1, True):
                copy.wait_send()

        def act(source, forwarded, way):
            @pl.when(forwarded)
            def _():
                for copy in self.hop(source, way, False):
                    copy.wait_send()

        for distance in range(1, plan.n_h):
            self.on_the_way(distance, act)
        for chunk in range(plan.n_h):
            for mask in range(1, plan.n_e):
                self.meta_copy(chunk, mask).wait_send()
        if plan.relayed < plan.n_e:

            @pl.when(z > 0)
            def _():
                self.relay_copy(z, -1).wait_send()

            @pl.when(z < plan.n_h - 1)
            def _():
                self.relay_copy(z, 1).wait_send()

            def passed(source, forwarded, way):
                @pl.when(forwarded)
                def _():
                    self.relay_copy(source, way).wait_send()

            for distance in range(1, plan.n_h):
                self.on_the_way(distance, passed)


def same(index, other, count):
    return 1 - lax.div(lax.rem(index - other + count, count) + count - 1, count)


class Return:
    own_first = True

    def __init__(self, plan, back, land, out, stage, rows_v, sum_v, total, sems):
        self.plan = plan
        self.back, self.land, self.out = back, land, out
        self.stage, self.rows_v, self.sum_v, self.total = stage, rows_v, sum_v, total
        (self.b_send, self.b_recv, self.s_send, self.s_recv, self.local, self.own) = sems

    @staticmethod
    def sem_shapes(plan):
        dma = pltpu.SemaphoreType.DMA
        n_h, n_e = plan.n_h, plan.n_e
        return [
            dma((n_h, n_e)),
            dma((n_h, n_e)),
            dma((n_h,)),
            dma((2, n_h)),
            dma((2,)),
            dma((n_h,)),
        ]

    def goal(self, turn):
        n_h = self.plan.n_h
        _, z = self.plan.place()
        found = 0
        for here in range(n_h):
            others = [there for there in range(n_h) if there != here]
            others.sort(key=lambda d: n_h - 1 - d + here if d > here else d + n_h - 1 - here)
            order = [here] + others if self.own_first else others + [here]
            for when, there in enumerate(order):
                found = found + there * same(z, here, n_h) * same(turn, when, n_h)
        return found

    def chunk_of(self, goal):
        _, z = self.plan.place()
        return self.plan.chunk(z, goal)

    def source(self, chunk, mask):
        raise NotImplementedError

    def in_plane(self, chunk, mask):
        plan = self.plan
        e, z = plan.place()
        return remote(
            self.source(chunk, mask),
            self.back.at[chunk, :, pl.ds(mask * plan.stride, plan.stride), :],
            self.b_send.at[chunk, mask],
            self.b_recv.at[chunk, mask],
            (across(e, mask), z),
        )

    def own_copy(self, chunk):
        plan = self.plan
        return pltpu.make_async_copy(
            self.source(chunk, 0),
            self.back.at[chunk, :, pl.ds(0, plan.stride), :],
            self.own.at[chunk],
        )

    def send(self, chunk):
        for mask in range(1, self.plan.n_e):
            self.in_plane(chunk, mask).start()
        self.own_copy(chunk).start()

    def hop(self, turn, goal, way):
        e, z = self.plan.place()
        side = (1 - way) // 2
        return remote(
            self.rows_v.at[lax.rem(turn, 2)],
            self.land.at[side, goal],
            self.s_send.at[turn],
            self.s_recv.at[side, goal],
            (e, z + way),
        )

    def each_way(self, goal, act):
        _, z = self.plan.place()

        @pl.when(goal > z)
        def _():
            act(1, z > 0)

        @pl.when(goal < z)
        def _():
            act(-1, z < self.plan.n_h - 1)

    def take(self, goal, way):
        side = (1 - way) // 2
        e, z = self.plan.place()
        remote(
            self.rows_v.at[0],
            self.land.at[side, goal],
            self.s_send.at[0],
            self.s_recv.at[side, goal],
            (e, z - way),
        ).wait_recv()
        copy = pltpu.make_async_copy(self.land.at[side, goal], self.sum_v, self.local.at[1])
        copy.start()
        copy.wait()
        return self.sum_v[...].astype(jnp.float32)

    def wait_hop(self, turn):
        goal = self.goal(turn)

        def act(way, _):
            self.hop(turn, goal, way).wait_send()

        self.each_way(goal, act)

    def fetched(self, chunk, buffer):
        return pltpu.make_async_copy(self.back.at[chunk], self.stage.at[buffer], self.local.at[0])

    def fetch(self, goal, chunk, buffer):
        for mask in range(1, self.plan.n_e):
            self.in_plane(chunk, mask).wait_recv()
        self.own_copy(chunk).wait()
        self.fetched(chunk, buffer).start()

    def combine(self, turn, target_of):
        plan = self.plan
        e, z = plan.place()
        goal = self.goal(turn)
        chunk = self.chunk_of(goal)
        target = target_of(chunk)
        buffer = lax.rem(turn, 2)
        self.fetch(goal, chunk, buffer)
        hot = [
            jnp.concatenate(
                [
                    slot_hits(plan, slot_base(plan, across(e, mask), j), target)
                    for mask in range(plan.n_e)
                ],
                axis=0,
            )
            for j in range(2)
        ]
        self.fetched(chunk, buffer).wait()

        @pl.when(turn >= 2)
        def _():
            self.wait_hop(turn - 2)

        part = contract_first(hot[0], self.stage[buffer, 0]) + contract_first(
            hot[1], self.stage[buffer, 1]
        )

        @pl.when(goal == z)
        def _():
            self.total[...] = part

        @pl.when(goal != z)
        def _():
            self.rows_v[buffer] = part.astype(jnp.bfloat16)

        def act(way, more):
            @pl.when(more)
            def _():
                so_far = self.take(goal, way)
                self.rows_v[buffer] = (self.rows_v[buffer].astype(jnp.float32) + so_far).astype(
                    jnp.bfloat16
                )

            self.hop(turn, goal, way).start()

        self.each_way(goal, act)

    def finish(self):
        plan = self.plan
        _, z = plan.place()
        for turn in range(plan.n_h - 2, plan.n_h):
            self.wait_hop(turn)

        @pl.when(z > 0)
        def _():
            self.total[...] += self.take(z, 1)

        @pl.when(z < plan.n_h - 1)
        def _():
            self.total[...] += self.take(z, -1)

        copy = pltpu.make_async_copy(self.total, self.out, self.local.at[0])
        copy.start()
        copy.wait()


class ReturnHeld(Return):
    own_first = False

    def __init__(self, plan, given, early, *rest):
        super().__init__(plan, *rest)
        self.given, self.early = given, early

    def fetch(self, goal, chunk, buffer):
        _, z = self.plan.place()

        @pl.when(goal != z)
        def _():
            Return.fetch(self, goal, chunk, buffer)

        @pl.when(goal == z)
        def _():
            pltpu.make_async_copy(self.early, self.stage.at[buffer], self.local.at[0]).start()

    def source(self, chunk, mask):
        plan = self.plan
        at = pl.multiple_of((chunk * plan.n_e + mask) * plan.stride, 16)
        return self.given.at[:, pl.ds(at, plan.stride), :]

    def sent(self):
        for chunk in range(1, self.plan.n_h):
            for mask in range(1, self.plan.n_e):
                self.in_plane(chunk, mask).wait_send()


class ReturnMade(Return):
    def __init__(self, plan, made, *rest):
        super().__init__(plan, *rest)
        self.made = made
        self.ring = made.shape[0]

    def source(self, chunk, mask):
        plan = self.plan
        return self.made.at[
            lax.rem(chunk, self.ring), :, pl.ds(mask * plan.stride, plan.stride), :
        ]

    def free(self, chunk):
        if self.plan.n_h > self.ring:

            @pl.when(chunk >= self.ring)
            def _():
                self.wait_sent(chunk - self.ring)
                self.own_copy(chunk - self.ring).wait()

    def wait_sent(self, chunk):
        for mask in range(1, self.plan.n_e):
            self.in_plane(chunk, mask).wait_send()

    def sent(self):
        for chunk in range(max(0, self.plan.n_h - self.ring), self.plan.n_h):
            self.wait_sent(chunk)


ANY = pl.BlockSpec(memory_space=pl.ANY)


def inverse_root(rows):
    return lax.rsqrt(jnp.mean(rows * rows, axis=1, keepdims=True) + eps)


def attend_body(plan, *refs):
    (
        grads,
        targets,
        tokens,
        w_query,
        w_key,
        w_value,
        w_out,
        lines,
        gains,
        w_router,
        routes,
        grads_out,
        targets_out,
        land,
        soft_out,
        mixed_out,
        normed_out,
        query_out,
        key_out,
        value_out,
        hidden_out,
        sent_out,
        gates_out,
        roots_out,
        rows_v,
        meta_v,
        stage,
        tokens_v,
        weights_v,
        normed_v,
        heads_v,
        soft_v,
        mixed_v,
        hidden_v,
        in_sem,
        soft_sem,
        out_sem,
        *sems,
    ) = refs
    loads = [
        pltpu.make_async_copy(given, held, in_sem.at[i])
        for i, (given, held) in enumerate(
            [(tokens, tokens_v)]
            + [
                (weight, weights_v.at[k])
                for k, weight in enumerate((w_query, w_key, w_value, w_out))
            ]
        )
    ]
    for load in loads:
        load.start()
    greet(plan)
    work = Dispatch(plan, grads, targets, land, grads_out, targets_out, rows_v, meta_v, stage, sems)
    work.begin()
    _, z = plan.place()
    stores = [
        pltpu.make_async_copy(held, out, out_sem.at[i])
        for i, (held, out) in enumerate(
            (
                (normed_v, normed_out),
                (heads_v.at[0], query_out),
                (heads_v.at[1], key_out),
                (heads_v.at[2], value_out),
                (mixed_v, mixed_out),
                (hidden_v, hidden_out),
                (normed_v, sent_out),
            )
        )
    ]

    def project():
        for load in loads:
            load.wait()
        rows = tokens_v[...].astype(jnp.float32)
        root = inverse_root(rows)
        roots_out[:, 0:128] = jnp.broadcast_to(root, (LEN, 128))
        normed_v[...] = (rows * root * gains[0:1, :]).astype(jnp.bfloat16)
        for k in range(3):
            heads_v[k] = dot(normed_v[...], weights_v[k]).astype(jnp.bfloat16)
        for store in stores[:4]:
            store.start()

    def soft_copy(pair):
        buffer = lax.rem(pair, 2)
        return pltpu.make_async_copy(
            soft_v.at[buffer], soft_out.at[pl.ds(2 * pair, 2)], soft_sem.at[buffer]
        )

    def mix_pair(pair):
        lanes = pl.ds(pl.multiple_of(pair * 2 * HEAD_DIM, 2 * HEAD_DIM), 2 * HEAD_DIM)
        both = [heads_v[k, :, lanes] for k in range(3)]

        @pl.when(pair >= 2)
        def _():
            soft_copy(pair - 2).wait()

        heads = []
        for head in range(2):
            at = slice(head * HEAD_DIM, (head + 1) * HEAD_DIM)
            heads.append(
                mix_head(
                    *[item[:, at] for item in both],
                    lines[pair, head : head + 1, :],
                    soft_v.at[lax.rem(pair, 2)],
                    head,
                )
            )
        mixed_v[:, lanes] = jnp.concatenate(heads, axis=1)
        soft_copy(pair).start()

    def route():
        stores[4].start()
        hidden = tokens_v[...].astype(jnp.float32) + dot(mixed_v[...], weights_v[3])
        hidden_v[...] = hidden
        stores[5].start()
        root = inverse_root(hidden)
        roots_out[:, 128:256] = jnp.broadcast_to(root, (LEN, 128))
        normed = hidden * root * gains[1:2, :]
        stores[0].wait()
        normed_v[...] = normed.astype(jnp.bfloat16)
        stores[6].start()
        logits = contract_last(w_router[...], normed, precise)
        experts = lax.broadcasted_iota(jnp.int32, logits.shape, 0).astype(jnp.float32)
        chosen = [
            jnp.sum(jnp.where(experts == routes[k : k + 1, :], logits, 0.0), axis=0, keepdims=True)
            for k in range(2)
        ]
        peak = jnp.maximum(chosen[0], chosen[1])
        terms = [jnp.exp(item - peak) for item in chosen]
        for k in range(2):
            gates_out[k : k + 1, :] = terms[k] / (terms[0] + terms[1])
        gates_out[2:8, :] = jnp.zeros((6, LEN), jnp.float32)

    pairs = HEADS // 2
    each = -(-pairs // (plan.n_h - 1))

    @pl.loop(0, plan.n_h)
    def _(chunk):
        work.chunk(chunk, lambda at: meta_v[plan.source(z, at)])
        pl.when(chunk == 0)(project)
        work.relay(chunk)

        @pl.loop(0, each)
        def _(i):
            pair = chunk * each + i
            pl.when(pair < pairs)(lambda: mix_pair(pair))

    soft_copy(pairs - 2).wait()
    soft_copy(pairs - 1).wait()
    route()
    for store in stores[1:]:
        store.wait()
    for chunk in range(plan.n_h):
        work.told(chunk)
        work.arrived(chunk)
    work.finish()


def attend(
    plan,
    grads,
    targets,
    tokens,
    w_query,
    w_key,
    w_value,
    w_out,
    lines,
    gains,
    w_router,
    routes,
):
    n_h, n_e = plan.n_h, plan.n_e
    bf16, f32 = jnp.bfloat16, jnp.float32
    shape = jax.ShapeDtypeStruct
    vmem = pl.BlockSpec(memory_space=pltpu.VMEM)
    rows = shape((LEN, D), bf16)
    return pl.pallas_call(
        functools.partial(attend_body, plan),
        in_specs=[ANY] * 7 + [vmem] * 4,
        out_specs=[ANY] * 11 + [vmem] * 2,
        out_shape=[
            shape((2, plan.total, D), bf16),
            shape((n_h, n_e, 8, LEN), f32),
            shape((n_h, LEN, D), bf16),
            shape((HEADS, LEN, LEN), bf16),
            rows,
            rows,
            rows,
            rows,
            rows,
            shape((LEN, D), f32),
            rows,
            shape((8, LEN), f32),
            shape((LEN, 256), f32),
        ],
        scratch_shapes=[
            pltpu.VMEM((2, LEN, D), bf16),
            pltpu.VMEM((n_h, 8, LEN), f32),
            pltpu.VMEM((2, 2, plan.rows, D), bf16),
            pltpu.VMEM((LEN, D), bf16),
            pltpu.VMEM((4, D, D), bf16),
            pltpu.VMEM((LEN, D), bf16),
            pltpu.VMEM((3, LEN, D), bf16),
            pltpu.VMEM((2, 2, LEN, LEN), bf16),
            pltpu.VMEM((LEN, D), bf16),
            pltpu.VMEM((LEN, D), f32),
            pltpu.SemaphoreType.DMA((5,)),
            pltpu.SemaphoreType.DMA((2,)),
            pltpu.SemaphoreType.DMA((7,)),
        ]
        + Dispatch.sem_shapes(plan),
        compiler_params=pltpu.CompilerParams(
            collective_id=1, has_side_effects=True, vmem_limit_bytes=VMEM
        ),
        name="attend",
    )(
        grads,
        targets,
        tokens,
        w_query,
        w_key,
        w_value,
        w_out,
        lines.reshape(HEADS // 2, 2, 4 * NEAR),
        gains,
        w_router,
        routes,
    )


def expert_body(plan, halves, n_d, *refs):
    (
        sent,
        gates,
        grads,
        targets,
        w_gate,
        w_up,
        w_down,
        total_out,
        gg_out,
        rows_out,
        y_out,
        dgate_out,
        dup_out,
        act_out,
        meta_out,
        land,
        back,
        land_back,
        early,
        rows_v,
        meta_v,
        stage,
        wg_v,
        wu_v,
        wd_v,
        target_v,
        gate_v,
        x_v,
        g_v,
        dx_v,
        y_v,
        dgate_v,
        dup_v,
        act_v,
        gg_v,
        gg_back,
        gg_part,
        gg_land,
        column_v,
        dots_v,
        sum_v,
        total,
        w_sem,
        t_sem,
        x_sem,
        o_sem,
        gg_send,
        gg_recv,
        ggs_send,
        ggs_recv,
        e_send,
        e_recv,
        *sems,
    ) = refs
    n_e, n_h = plan.n_e, plan.n_h
    e, z = plan.place()
    loads = [
        pltpu.make_async_copy(source, held, w_sem.at[i])
        for i, (source, held) in enumerate(((w_gate, wg_v), (w_up, wu_v), (w_down, wd_v)))
    ]
    for load in loads:
        load.start()
    targets_in = pltpu.make_async_copy(targets, target_v, t_sem.at[0])
    targets_in.start()
    greet(plan)
    work = Dispatch(
        plan, sent, gates, land, rows_out, meta_out, rows_v, meta_v, stage, sems[:n_d]
    )
    give = ReturnMade(
        plan, dx_v, back, land_back, total_out, stage, rows_v, sum_v, total, sems[n_d:]
    )
    work.begin()
    targets_in.wait()
    ahead = min(3, n_h)

    @pl.loop(0, ahead)
    def _(chunk):
        work.chunk(chunk, lambda at: target_v[at, 0])
        work.relay(chunk)

    for load in loads:
        load.wait()

    def gg_copy(chunk, mask):
        return remote(
            gg_v.at[chunk, mask],
            gg_back.at[chunk, mask],
            gg_send.at[chunk, mask],
            gg_recv.at[chunk, mask],
            (across(e, mask), z),
        )

    def gg_along(chunk):
        return remote(
            gg_part.at[chunk],
            gg_land.at[z],
            ggs_send.at[chunk],
            ggs_recv.at[z],
            (e, plan.source(z, chunk)),
        )

    def gg_from(distance):
        other = lax.rem(z + distance, n_h)
        return other, remote(
            gg_part.at[0], gg_land.at[other], ggs_send.at[0], ggs_recv.at[other], (e, other)
        )

    def outs(chunk, j):
        at = pl.multiple_of(chunk * plan.rows, 16)
        return [
            pltpu.make_async_copy(held.at[j], out.at[j, pl.ds(at, plan.rows), :], o_sem.at[i, j])
            for i, (held, out) in enumerate(
                ((y_v, y_out), (dgate_v, dgate_out), (dup_v, dup_out), (act_v, act_out))
            )
        ]

    all_held = n_h <= dx_v.shape[0]
    masks = n_e // halves
    piece = masks * plan.stride

    def own_slots(j):
        slots = lax.broadcasted_iota(jnp.int32, (plan.stride, LEN), 0).astype(jnp.float32)
        return slots + slot_base(plan, e, j)

    def weigh(chunk, mask):
        aim, weight = target_v[chunk, mask], gate_v[mask]
        at = pl.ds(pl.multiple_of(mask * plan.stride, 16), plan.stride)
        for j in range(2):
            hit = jnp.where(own_slots(j) == aim[0:1, :], weight[0:1, :], 0.0)
            hit = hit + jnp.where(own_slots(j) == aim[1:2, :], weight[1:2, :], 0.0)
            column_v[j, at, :] = jnp.broadcast_to(
                jnp.sum(hit, axis=1, keepdims=True), (plan.stride, 128)
            )

    def spread(chunk, mask):
        aim = target_v[chunk, mask]
        at = pl.ds(pl.multiple_of(mask * plan.stride, 16), plan.stride)
        for k in range(2):
            line = jnp.zeros((1, LEN), jnp.float32)
            for j in range(2):
                hit = own_slots(j) == aim[k : k + 1, :]
                line = line + jnp.sum(
                    jnp.where(hit, dots_v[j, at, 0:1], 0.0), axis=0, keepdims=True
                )
            gg_v[chunk, mask, k : k + 1, :] = line

    def step(chunk, index):
        j, half = lax.div(index, halves), lax.rem(index, halves)
        at = pl.ds(pl.multiple_of(half * piece, 16), piece)
        gate_pre = contract_last(x_v[j, at, :], wg_v[j])
        up_pre = contract_last(x_v[j, at, :], wu_v[j])
        raw = contract_last(g_v[j, at, :], wd_v[j])
        gate = column_v[j, at, 0:1]
        square = gate_pre * gate_pre
        tanh = jnp.tanh(gate_pre * (0.7978845608028654 + 0.035677408136300125 * square))
        side = 0.5 + 0.5 * tanh
        gelu = gate_pre * side
        slope = side + gelu * (1.0 - side) * (1.5957691216057308 + 0.21406444881780075 * square)
        act = gelu * up_pre
        act_low = act.astype(jnp.bfloat16)
        dots_v[j, at, :] = jnp.broadcast_to(
            jnp.sum(act_low.astype(jnp.float32) * raw, axis=1, keepdims=True), (piece, 128)
        )
        grad_act = gate * raw
        grad_gate = (grad_act * up_pre * slope).astype(jnp.bfloat16)
        grad_up = (grad_act * gelu).astype(jnp.bfloat16)
        dgate_v[j, at, :] = grad_gate
        dup_v[j, at, :] = grad_up
        act_v[j, at, :] = (act * gate).astype(jnp.bfloat16)
        dx_v[lax.rem(chunk, dx_v.shape[0]), j, at, :] = (
            dot(grad_gate, wg_v[j]) + dot(grad_up, wu_v[j])
        ).astype(jnp.bfloat16)
        y_v[j, at, :] = (dot(act_low, wd_v[j]) * gate).astype(jnp.bfloat16)

    gg_v[...] = jnp.zeros_like(gg_v)

    @pl.loop(0, n_h)
    def _(chunk):
        at = pl.multiple_of(chunk * plan.rows, 16)
        ins = [
            pltpu.make_async_copy(source.at[:, pl.ds(at, plan.rows), :], held, x_sem.at[i])
            for i, (source, held) in enumerate(((rows_out, x_v), (grads, g_v)))
        ]
        ins[1].start()
        work.told(chunk)
        gate_in = pltpu.make_async_copy(meta_out.at[chunk], gate_v, t_sem.at[0])
        gate_in.start()
        gate_in.wait()
        pl.loop(0, n_e)(lambda mask: weigh(chunk, mask))
        give.free(chunk)

        @pl.when(chunk > 0)
        def _():
            for j in range(2):
                for copy in outs(chunk - 1, j):
                    copy.wait()

        work.arrived(chunk)
        ins[0].start()
        for copy in ins:
            copy.wait()
        pl.loop(0, 2 * halves)(lambda index: step(chunk, index))
        for j in range(2):
            for copy in outs(chunk, j):
                copy.start()

        @pl.when(chunk + ahead < n_h)
        def _():
            work.chunk(chunk + ahead, lambda at: target_v[at, 0])
            work.relay(chunk + ahead)

        @pl.when((chunk < 1) | (not all_held))
        def _():
            give.send(chunk)

        pl.loop(0, n_e)(lambda mask: spread(chunk, mask))
        for mask in range(1, n_e):
            gg_copy(chunk, mask).start()

    def early_copy(mask):
        at = pl.ds(mask * plan.stride, plan.stride)
        if mask == 0:
            return pltpu.make_async_copy(y_out.at[:, at, :], early.at[:, at, :], e_send.at[0])
        return remote(
            y_out.at[:, at, :],
            early.at[:, at, :],
            e_send.at[mask],
            e_recv.at[mask],
            (across(e, mask), z),
        )

    if all_held:
        pl.loop(1, n_h)(lambda turn: give.send(give.chunk_of(give.goal(turn))))
    for mask in range(n_e):
        early_copy(mask).start()
    work.finish()
    for j in range(2):
        for copy in outs(n_h - 1, j):
            copy.wait()

    @pl.loop(0, n_h)
    def _(turn):
        chunk = give.chunk_of(give.goal(turn))
        part = gg_v[chunk, 0]
        for mask in range(1, n_e):
            gg_copy(chunk, mask).wait_recv()
            part = part + gg_back[chunk, mask]
        gg_part[chunk] = part

        @pl.when(chunk > 0)
        def _():
            gg_along(chunk).start()

        give.combine(turn, lambda at: target_v[at, 0])

    give.sent()
    early_copy(0).wait()
    for mask in range(1, n_e):
        early_copy(mask).wait()
    for chunk in range(n_h):
        for mask in range(1, n_e):
            gg_copy(chunk, mask).wait_send()
    sum_gg = gg_part[0]
    for distance in range(1, n_h):
        other, arrival = gg_from(distance)
        arrival.wait_recv()
        sum_gg = sum_gg + gg_land[other]
    gg_out[...] = sum_gg
    for chunk in range(1, n_h):
        gg_along(chunk).wait_send()
    give.finish()


def run_experts(plan, sent, gates, grads, targets, w_gate, w_up, w_down):
    n_h, n_e, width = plan.n_h, plan.n_e, plan.width
    bf16, f32 = jnp.bfloat16, jnp.float32
    shape = jax.ShapeDtypeStruct
    dma = pltpu.SemaphoreType.DMA
    ring = min(4, n_h)
    d_sems, r_sems = Dispatch.sem_shapes(plan), Return.sem_shapes(plan)
    halves = 2 if plan.rows <= 640 else 4
    return pl.pallas_call(
        functools.partial(expert_body, plan, halves, len(d_sems)),
        in_specs=[ANY] * 7,
        out_specs=[ANY, pl.BlockSpec(memory_space=pltpu.VMEM)] + [ANY] * 10,
        out_shape=[
            shape((LEN, D), f32),
            shape((8, LEN), f32),
            shape((2, plan.total, D), bf16),
            shape((2, plan.total, D), bf16),
            shape((2, plan.total, width), bf16),
            shape((2, plan.total, width), bf16),
            shape((2, plan.total, width), bf16),
            shape((n_h, n_e, 8, LEN), f32),
            shape((n_h, LEN, D), bf16),
            shape((n_h, 2, plan.rows, D), bf16),
            shape((2, n_h, LEN, D), bf16),
            shape((2, plan.rows, D), bf16),
        ],
        scratch_shapes=[
            pltpu.VMEM((2, LEN, D), bf16),
            pltpu.VMEM((n_h, 8, LEN), f32),
            pltpu.VMEM((2, 2, plan.rows, D), bf16),
            pltpu.VMEM((2, width, D), bf16),
            pltpu.VMEM((2, width, D), bf16),
            pltpu.VMEM((2, width, D), bf16),
            pltpu.VMEM((n_h, n_e, 8, LEN), f32),
            pltpu.VMEM((n_e, 8, LEN), f32),
            pltpu.VMEM((2, plan.rows, D), bf16),
            pltpu.VMEM((2, plan.rows, D), bf16),
            pltpu.VMEM((ring, 2, plan.rows, D), bf16),
            pltpu.VMEM((2, plan.rows, D), bf16),
            pltpu.VMEM((2, plan.rows, width), bf16),
            pltpu.VMEM((2, plan.rows, width), bf16),
            pltpu.VMEM((2, plan.rows, width), bf16),
            pltpu.VMEM((n_h, n_e, 8, LEN), f32),
            pltpu.VMEM((n_h, n_e, 8, LEN), f32),
            pltpu.VMEM((n_h, 8, LEN), f32),
            pltpu.VMEM((n_h, 8, LEN), f32),
            pltpu.VMEM((2, plan.rows, 128), f32),
            pltpu.VMEM((2, plan.rows, 128), f32),
            pltpu.VMEM((LEN, D), bf16),
            pltpu.VMEM((LEN, D), f32),
            dma((3,)),
            dma((1,)),
            dma((2,)),
            dma((4, 2)),
            dma((n_h, n_e)),
            dma((n_h, n_e)),
            dma((n_h,)),
            dma((n_h,)),
            dma((n_e,)),
            dma((n_e,)),
        ]
        + d_sems
        + r_sems,
        compiler_params=pltpu.CompilerParams(
            collective_id=2, has_side_effects=True, vmem_limit_bytes=VMEM
        ),
        name="run_experts",
    )(sent, gates, grads, targets, jnp.swapaxes(w_gate, 1, 2), jnp.swapaxes(w_up, 1, 2), w_down)


class Sum:
    pieces, stages, few = 4, 5, 32

    def __init__(self, plan, held, whole, few_v, few_in, *rest):
        self.plan = plan
        self.held, self.whole, self.few_v, self.few_in = held, whole, few_v, few_in
        self.landed, (self.send, self.recv, self.f_send, self.f_recv) = rest[:5], rest[5:]

    @classmethod
    def scratch_shapes(cls):
        dma = pltpu.SemaphoreType.DMA
        bf16, f32 = jnp.bfloat16, jnp.float32
        rows = (D // 2, D // 4, D // 8, D // 16, D // 32)
        return (
            [
                pltpu.VMEM((cls.pieces, D, D), bf16),
                pltpu.VMEM((cls.pieces, D, D), bf16),
                pltpu.VMEM((cls.stages + 1, cls.few, D), f32),
                pltpu.VMEM((cls.stages, cls.few, D), f32),
            ]
            + [pltpu.VMEM((cls.pieces, count, D), bf16) for count in rows]
            + [
                dma((2 * cls.stages, cls.pieces, 2)),
                dma((2 * cls.stages, cls.pieces, 2)),
                dma((cls.stages,)),
                dma((cls.stages,)),
            ]
        )

    def partner(self, bit):
        e, z = self.plan.place()
        if bit < 3:
            return (across(e, 1 << bit), z)
        return (e, across(z, 1 << (bit - 3)))

    def parts(self, stage):
        e, z = self.plan.place()
        place = [lax.rem(lax.div(e, 1 << k), 2) for k in range(3)]
        place += [lax.rem(lax.div(z, 1 << k), 2) for k in range(2)]
        base, count = place[0] * (D // 2), D // 2
        if stage == 1:
            return [(self.partner(0), base, D // 2 - base, count)]
        out = []
        for part, order in enumerate(((1, 2, 3, 4), (2, 1, 3, 4))):
            at, count = base + part * (D // 4), D // 4
            for bit in order[: stage - 1]:
                count //= 2
                keep, give = at + place[bit] * count, at + (1 - place[bit]) * count
                at = keep
            out.append((self.partner(bit), keep, give, count))
        return out

    def copies(self, stage, piece):
        halving = stage <= self.stages
        out = []
        parts = self.parts(stage if halving else 2 * self.stages + 1 - stage)
        for part, (device, keep, give, count) in enumerate(parts):
            here = pl.ds(pl.multiple_of(give if halving else keep, 16), count)
            there = (
                self.landed[stage - 1].at[piece, part * count : (part + 1) * count, :]
                if halving
                else self.whole.at[piece, here, :]
            )
            out.append(
                remote(
                    (self.held if halving else self.whole).at[piece, here, :],
                    there,
                    self.send.at[stage - 1, piece, part],
                    self.recv.at[stage - 1, piece, part],
                    device,
                )
            )
        return out

    def few_copy(self, stage):
        return remote(
            self.few_v.at[stage - 1],
            self.few_in.at[stage - 1],
            self.f_send.at[stage - 1],
            self.f_recv.at[stage - 1],
            self.partner(stage - 1),
        )

    def add(self, stage, piece):
        for part, (_, keep, _, count) in enumerate(self.parts(stage)):
            tile = min(count, 64)

            @pl.loop(0, count // tile)
            def _(i):
                at = pl.ds(pl.multiple_of(keep + i * tile, 16), tile)
                come = pl.ds(pl.multiple_of(part * count + i * tile, 16), tile)
                total = self.held[piece, at, :].astype(jnp.float32) + self.landed[stage - 1][
                    piece, come, :
                ].astype(jnp.float32)
                into = self.whole if stage == self.stages else self.held
                into[piece, at, :] = total.astype(jnp.bfloat16)

    slots = pieces + 2 * stages

    def slot(self, slot, ready, done):
        for piece in range(self.pieces):
            stage = slot - piece + 1
            if stage == 1:
                ready(piece)
            if 2 <= stage <= 2 * self.stages + 1:
                for copy in self.copies(stage - 1, piece):
                    copy.wait_recv()
                if stage - 1 <= self.stages:
                    self.add(stage - 1, piece)
            if 1 <= stage <= 2 * self.stages:
                for copy in self.copies(stage, piece):
                    copy.start()
            if stage == 2 * self.stages + 1:
                done(piece)
        stage = slot + 1
        if 2 <= stage <= self.stages + 1:
            self.few_copy(stage - 1).wait_recv()
            self.few_v[stage - 1] = self.few_v[stage - 2] + self.few_in[stage - 2]
        if stage <= self.stages:
            self.few_copy(stage).start()

    def finish(self):
        for stage in range(1, 2 * self.stages + 1):
            for piece in range(self.pieces):
                for copy in self.copies(stage, piece):
                    copy.wait_send()
        for stage in range(1, self.stages + 1):
            self.few_copy(stage).wait_send()


def sum_body(plan, *refs):
    n_h = plan.n_h
    dgate, dup, act, rows, grads = refs[:5]
    refs = refs[5:]
    if plan.summed:
        low, few = refs[:2]
        refs = refs[2:]
    outs, refs = refs[:3], refs[3:]
    if plan.summed:
        sums_out, few_out = refs[:2]
        refs = refs[2:]
    left_v, right_v, made_v, p_sem, g_sem = refs[:5]
    steps = 3 * n_h

    def factors(q, act_on):
        buffer = lax.rem(q, 2)
        at = pl.ds(pl.multiple_of(lax.rem(q, n_h) * plan.rows, 16), plan.rows)

        def copies(lefts, rights):
            for i in range(2):
                for k, ((source, j), held) in enumerate(((lefts[i], left_v), (rights[i], right_v))):
                    act_on(
                        pltpu.make_async_copy(
                            source.at[j, at, :], held.at[buffer, i], p_sem.at[buffer, 2 * i + k]
                        )
                    )

        @pl.when(q < 2 * n_h)
        def _():
            j = lax.div(q, n_h)
            copies(((dgate, j), (dup, j)), ((rows, j), (rows, j)))

        @pl.when(q >= 2 * n_h)
        def _():
            copies(((act, 0), (act, 1)), ((grads, 0), (grads, 1)))

    def results(group, act_on):
        @pl.when(group < 2)
        def _():
            for i in range(2):
                act_on(pltpu.make_async_copy(made_v.at[i], outs[i].at[group], g_sem.at[i]))

        @pl.when(group == 2)
        def _():
            for i in range(2):
                act_on(pltpu.make_async_copy(made_v.at[i], outs[2].at[i], g_sem.at[i]))

    def product(q):
        buffer, turn, group = lax.rem(q, 2), lax.rem(q, n_h), lax.div(q, n_h)
        factors(q, lambda copy: copy.wait())

        @pl.when(q + 1 < steps)
        def _():
            factors(q + 1, lambda copy: copy.start())

        @pl.when((turn == 0) & (q > 0))
        def _():
            results(group - 1, lambda copy: copy.wait())

        @pl.when(turn == 0)
        def _():
            made_v[...] = jnp.zeros_like(made_v)

        for i in range(2):
            made_v[i] += contract_first(left_v[buffer, i], right_v[buffer, i])

        @pl.when(turn == n_h - 1)
        def _():
            results(group, lambda copy: copy.start())

    factors(0, lambda copy: copy.start())
    if plan.summed:
        load_sem, store_sem = refs[5:7]
        total = Sum(plan, *refs[7:])
        loads = [
            pltpu.make_async_copy(low.at[i], total.held.at[i], load_sem.at[i]) for i in range(4)
        ]
        stores = [
            pltpu.make_async_copy(total.whole.at[i], sums_out.at[i], store_sem.at[i])
            for i in range(4)
        ]
        for load in loads:
            load.start()
        total.few_v[0] = few[...]
        greet(plan)
        done = 0
        for slot in range(total.slots):
            total.slot(slot, lambda i: loads[i].wait(), lambda i: stores[i].start())
            if slot % 2 == 0 and done < steps:
                pl.loop(done, min(done + 2, steps))(product)
                done = min(done + 2, steps)
        few_out[...] = total.few_v[total.stages]
        total.finish()
        for store in stores:
            store.wait()
    else:
        pl.loop(0, steps)(product)
    results(2, lambda copy: copy.wait())


def sum_all(plan, dgate, dup, act, rows, grads, low, few):
    bf16, f32 = jnp.bfloat16, jnp.float32
    shape = jax.ShapeDtypeStruct
    vmem = pl.BlockSpec(memory_space=pltpu.VMEM)
    dma = pltpu.SemaphoreType.DMA
    args = [dgate, dup, act, rows, grads]
    in_specs, out_specs = [ANY] * 5, [ANY] * 3
    out_shape = [shape((2, plan.width, D), f32)] * 3
    scratch_shapes = [
        pltpu.VMEM((2, 2, plan.rows, plan.width), bf16),
        pltpu.VMEM((2, 2, plan.rows, D), bf16),
        pltpu.VMEM((2, plan.width, D), f32),
        dma((2, 4)),
        dma((2,)),
    ]
    params = {"vmem_limit_bytes": VMEM}
    if plan.summed:
        args += [low, few]
        in_specs += [ANY, vmem]
        out_specs += [ANY, vmem]
        out_shape += [shape((4, D, D), bf16), shape((Sum.few, D), f32)]
        scratch_shapes += [dma((4,)), dma((4,))] + Sum.scratch_shapes()
        params.update(collective_id=4, has_side_effects=True)
    out = pl.pallas_call(
        functools.partial(sum_body, plan),
        in_specs=in_specs,
        out_specs=out_specs,
        out_shape=out_shape,
        scratch_shapes=scratch_shapes,
        compiler_params=pltpu.CompilerParams(**params),
        name="sum_all",
    )(*args)
    if plan.summed:
        return out[:3], out[3], out[4]
    return out[:3], *lax.psum((low, few), ("expert", "hidden"))


def unattend_body(plan, n_r, *refs):
    (
        given,
        early,
        targets,
        grad_sent,
        hidden,
        grad_out,
        tokens,
        mixed,
        normed,
        query,
        key,
        value,
        soft,
        w_query,
        w_key,
        w_value,
        w_out,
        grad_gates,
        gates,
        routes,
        w_router,
        gains,
        roots,
        branch_out,
        back,
        land,
        low_out,
        tokens_out,
        few_out,
        lines_out,
        rows_v,
        stage,
        target_v,
        sum_v,
        total,
        grad_sent_v,
        hidden_v,
        grad_out_v,
        tokens_v,
        mixed_v,
        normed_v,
        heads_v,
        soft_v,
        weights_v,
        grad_hidden_v,
        branch_v,
        grad_heads_v,
        grads_v,
        low_v,
        wide_v,
        t_sem,
        in_sem,
        soft_sem,
        low_sem,
        out_sem,
        *sems,
    ) = refs
    f32, bf16 = jnp.float32, jnp.bfloat16
    ins = [
        (grad_sent, grad_sent_v),
        (hidden, hidden_v),
        (grad_out, grad_out_v),
        (mixed, mixed_v),
        (w_out, weights_v.at[3]),
        (query, heads_v.at[0]),
        (key, heads_v.at[1]),
        (value, heads_v.at[2]),
        (normed, normed_v),
        (w_query, weights_v.at[0]),
        (w_key, weights_v.at[1]),
        (w_value, weights_v.at[2]),
        (tokens, tokens_v),
    ]
    loads = [
        pltpu.make_async_copy(source, held, in_sem.at[i]) for i, (source, held) in enumerate(ins)
    ]
    targets_in = pltpu.make_async_copy(targets, target_v, t_sem.at[0])

    def soft_copy(pair):
        buffer = lax.rem(pair, 2)
        return pltpu.make_async_copy(
            soft.at[pl.ds(2 * pair, 2)], soft_v.at[buffer], soft_sem.at[buffer]
        )

    targets_in.start()
    for load in loads:
        load.start()
    soft_copy(0).start()
    greet(plan)
    give = ReturnHeld(plan, given, early, back, land, branch_out, stage, rows_v, sum_v, total, sems)
    turns = plan.n_h
    pl.loop(0, turns - 1)(lambda turn: give.send(give.chunk_of(give.goal(turn))))
    targets_in.wait()

    def combine(turn):
        give.combine(turn, lambda at: target_v[at, 0])

    tile = 64

    def low_copy(i):
        return pltpu.make_async_copy(low_v.at[i % 2], low_out.at[i], low_sem.at[i % 2])

    for load in loads[:3]:
        load.wait()
    few_out[...] = jnp.zeros_like(few_out)
    mean = gates[0:1, :] * grad_gates[0:1, :] + gates[1:2, :] * grad_gates[1:2, :]
    experts = w_router.shape[0]
    numbers = lax.broadcasted_iota(jnp.int32, (experts, LEN), 0).astype(f32)
    grad_logits = jnp.zeros((experts, LEN), f32)
    for k in range(2):
        chosen = gates[k : k + 1, :] * (grad_gates[k : k + 1, :] - mean)
        grad_logits = grad_logits + jnp.where(numbers == routes[k : k + 1, :], chosen, 0.0)
    wide_v[...] = contract_first(grad_logits, w_router[...], precise)

    @pl.loop(0, LEN // tile)
    def _(i):
        at = pl.ds(pl.multiple_of(i * tile, 16), tile)
        rows, root = hidden_v[at, :], roots[at, 128:129]
        grad = wide_v[at, :] + grad_sent_v[at, :]
        near = rows * root
        few_out[experts + 1 : experts + 2, :] += jnp.sum(grad * near, axis=0, keepdims=True)
        scaled = grad * gains[1:2, :]
        pull = jnp.mean(scaled * rows, axis=1, keepdims=True) * (root * root * root)
        grad = grad_out_v[at, :].astype(f32) + root * scaled - rows * pull
        grad_hidden_v[at, :] = grad
        branch_v[at, :] = grad.astype(bf16)
        grad_sent_v[at, :] = near * gains[1:2, :]

    few_out[0:experts, :] = dot_high(grad_logits, grad_sent_v[...])
    for load in loads[3:5]:
        load.wait()
    low_v[1] = contract_first(mixed_v[...], branch_v[...]).astype(bf16)
    low_copy(3).start()
    mixed_v[...] = contract_last(branch_v[...], weights_v[3]).astype(bf16)
    for load in loads[5:8]:
        load.wait()

    def unmix_pair(pair):
        lanes = pl.ds(pl.multiple_of(pair * 2 * HEAD_DIM, 2 * HEAD_DIM), 2 * HEAD_DIM)
        soft_copy(pair).wait()

        @pl.when(pair + 1 < HEADS // 2)
        def _():
            soft_copy(pair + 1).start()

        both = [heads_v[k, :, lanes] for k in range(3)] + [mixed_v[:, lanes]]
        found = []
        for head in range(2):
            at = slice(head * HEAD_DIM, (head + 1) * HEAD_DIM)
            found.append(
                unmix_head(
                    *[item[:, at] for item in both], soft_v.at[lax.rem(pair, 2)], grads_v, head
                )
            )
        for k in range(3):
            grad_heads_v[k, :, lanes] = jnp.concatenate([found[0][k], found[1][k]], axis=1)
        lines_out[pair] = jnp.concatenate([found[0][3], found[1][3]], axis=0)

    pairs = HEADS // 2
    pl.loop(0, pairs // 2)(unmix_pair)
    combine(0)
    pl.loop(pairs // 2, pairs)(unmix_pair)
    combine(1)
    for load in loads[8:]:
        load.wait()
    for k in range(3):
        if k == 1:
            low_copy(3).wait()
        if k == 2:
            low_copy(0).wait()
        low_v[k % 2] = contract_first(normed_v[...], grad_heads_v[k]).astype(bf16)
        low_copy(k).start()
    wide_v[...] = (
        contract_last(grad_heads_v[0], weights_v[0])
        + contract_last(grad_heads_v[1], weights_v[1])
        + contract_last(grad_heads_v[2], weights_v[2])
    )

    @pl.loop(0, LEN // tile)
    def _(i):
        at = pl.ds(pl.multiple_of(i * tile, 16), tile)
        rows, root = tokens_v[at, :].astype(f32), roots[at, 0:1]
        grad = wide_v[at, :]
        few_out[experts : experts + 1, :] += jnp.sum(grad * rows * root, axis=0, keepdims=True)
        scaled = grad * gains[0:1, :]
        pull = jnp.mean(scaled * rows, axis=1, keepdims=True) * (root * root * root)
        grad_hidden_v[at, :] = grad_hidden_v[at, :] + root * scaled - rows * pull

    tokens_copy = pltpu.make_async_copy(grad_hidden_v, tokens_out, out_sem.at[0])
    tokens_copy.start()
    for turn in range(2, turns):
        combine(turn)
    give.sent()
    give.finish()
    for i in (1, 2):
        low_copy(i).wait()
    tokens_copy.wait()


def unattend(
    plan,
    given,
    early,
    targets,
    grad_sent,
    hidden,
    grad_out,
    tokens,
    mixed,
    normed,
    query,
    key,
    value,
    soft,
    w_query,
    w_key,
    w_value,
    w_out,
    grad_gates,
    gates,
    routes,
    w_router,
    gains,
    roots,
):
    n_h, n_e = plan.n_h, plan.n_e
    bf16, f32 = jnp.bfloat16, jnp.float32
    shape = jax.ShapeDtypeStruct
    vmem = pl.BlockSpec(memory_space=pltpu.VMEM)
    dma = pltpu.SemaphoreType.DMA
    sems = Return.sem_shapes(plan)
    few = -(-(w_router.shape[0] + 3) // Sum.few) * Sum.few
    rows, wide = pltpu.VMEM((LEN, D), bf16), pltpu.VMEM((LEN, D), f32)
    out = pl.pallas_call(
        functools.partial(unattend_body, plan, len(sems)),
        in_specs=[ANY] * 17 + [vmem] * 6,
        out_specs=[ANY] * 5 + [vmem] * 2,
        out_shape=[
            shape((LEN, D), f32),
            shape((n_h, 2, plan.rows, D), bf16),
            shape((2, n_h, LEN, D), bf16),
            shape((4, D, D), bf16),
            shape((LEN, D), f32),
            shape((few, D), f32),
            shape((HEADS // 2, 2, 4 * NEAR), f32),
        ],
        scratch_shapes=[
            pltpu.VMEM((2, LEN, D), bf16),
            pltpu.VMEM((2, 2, plan.rows, D), bf16),
            pltpu.VMEM((n_h, n_e, 8, LEN), f32),
            rows,
            wide,
            wide,
            wide,
            rows,
            rows,
            rows,
            rows,
            pltpu.VMEM((3, LEN, D), bf16),
            pltpu.VMEM((2, 2, LEN, LEN), bf16),
            pltpu.VMEM((4, D, D), bf16),
            wide,
            rows,
            pltpu.VMEM((3, LEN, D), bf16),
            pltpu.VMEM((LEN, LEN), bf16),
            pltpu.VMEM((2, D, D), bf16),
            wide,
            dma((1,)),
            dma((13,)),
            dma((2,)),
            dma((2,)),
            dma((1,)),
        ]
        + sems,
        compiler_params=pltpu.CompilerParams(
            collective_id=3, has_side_effects=True, vmem_limit_bytes=VMEM
        ),
        name="unattend",
    )(
        given,
        early,
        targets,
        grad_sent,
        hidden,
        grad_out,
        tokens,
        mixed,
        normed,
        query,
        key,
        value,
        soft,
        w_query,
        w_key,
        w_value,
        w_out,
        grad_gates,
        gates,
        routes,
        w_router,
        gains,
        roots,
    )
    return out[0], out[3], out[4], out[5], out[6].reshape(HEADS, 4 * NEAR)


def per_device(
    n_e,
    n_h,
    tokens,
    gain_one,
    w_query,
    w_key,
    w_value,
    w_out,
    bias_table,
    gain_two,
    w_router,
    w_gate,
    w_up,
    w_down,
    routes,
    cotangent,
):
    experts_all = w_router.shape[1]
    plan = Plan(n_e, n_h, experts_all, w_gate.shape[2])
    both = ("expert", "hidden")

    def small(array):
        return jnp.pad(array.astype(jnp.float32), ((0, 8 - array.shape[0]), (0, 0)))

    targets = small(slot_targets(routes, experts_all, plan.capacity, plan.stride))
    gains, route_rows = small(jnp.stack([gain_one, gain_two])), small(routes.T)
    hot_bucket = offset_buckets()
    lines = jnp.dot(hot_bucket, bias_table, precision=precise).T
    (
        grads_in,
        targets_all,
        _,
        soft,
        mixed_rows,
        normed_one,
        query_rows,
        key_rows,
        value_rows,
        hidden,
        sent,
        gates,
        roots,
    ) = attend(
        plan,
        cotangent,
        targets,
        tokens,
        w_query,
        w_key,
        w_value,
        w_out,
        lines,
        gains,
        w_router.T,
        route_rows,
    )
    made = run_experts(
        plan, sent, gates, grads_in, targets_all, w_gate, w_up, w_down
    )
    grad_sent, grad_gates, rows_in, y_rows, gate_rows, up_rows, act_rows = made[:7]
    branch, low, tokens_grad, few, grad_lines = unattend(
        plan,
        y_rows,
        made[-1],
        targets_all,
        grad_sent,
        hidden,
        cotangent,
        tokens,
        mixed_rows,
        normed_one,
        query_rows,
        key_rows,
        value_rows,
        soft,
        w_query,
        w_key,
        w_value,
        w_out,
        grad_gates,
        gates,
        route_rows,
        w_router.T,
        gains,
        roots,
    )
    block_out = (hidden + branch).astype(jnp.bfloat16)
    bias_table_grad = jnp.dot(grad_lines, hot_bucket, precision=precise).T
    last = jnp.pad(bias_table_grad.reshape(1, BUCKETS * HEADS), ((0, 0), (0, D - BUCKETS * HEADS)))
    few = lax.dynamic_update_slice(few, last, (experts_all + 2, 0))
    weight_grads, summed, few = sum_all(
        plan, gate_rows, up_rows, act_rows, rows_in, grads_in, low, few
    )
    summed = [summed[i].astype(jnp.float32) for i in range(4)]
    return (
        block_out,
        tokens_grad,
        few[experts_all],
        *summed,
        few[experts_all + 2, : BUCKETS * HEADS].reshape(BUCKETS, HEADS),
        few[experts_all + 1],
        few[:experts_all].T,
        jnp.swapaxes(weight_grads[0], 1, 2),
        jnp.swapaxes(weight_grads[1], 1, 2),
        weight_grads[2],
    )


def solution(mesh):
    in_specs = (
        P(("expert", "hidden"), None),
        P(),
        P(),
        P(),
        P(),
        P(),
        P(),
        P(),
        P(),
        P("expert", None, "hidden"),
        P("expert", None, "hidden"),
        P("expert", "hidden", None),
        P(("expert", "hidden"), None),
        P(("expert", "hidden"), None),
    )
    out_specs = (
        P(("expert", "hidden"), None),
        P(("expert", "hidden"), None),
        P(),
        P(),
        P(),
        P(),
        P(),
        P(),
        P(),
        P(),
        P("expert", None, "hidden"),
        P("expert", None, "hidden"),
        P("expert", "hidden", None),
    )
    return jax.shard_map(
        functools.partial(per_device, mesh.shape["expert"], mesh.shape["hidden"]),
        mesh=mesh, in_specs=in_specs, out_specs=out_specs, check_vma=False
    )
```

```python
import functools

import jax
import jax.numpy as jnp
from jax import lax
from jax.experimental import pallas as pl
from jax.experimental.pallas import tpu as pltpu
from jax.sharding import PartitionSpec as P

D = 1024
HEADS = 16
HEAD_DIM = 64
BUCKETS = 32
LEN = 512
MICRO = 2
MB_TOK = 256
VMEM = 62 * 1024 * 1024
MESH = pl.DeviceIdType.MESH


eps = 1e-06
precise = lax.Precision.HIGHEST
thresholds = (12, 16, 23, 32, 46, 64, 91)


def contract_last(matrix_a, matrix_b, mode=None):
    return lax.dot_general(
        matrix_a,
        matrix_b,
        (((1,), (1,)), ((), ())),
        precision=mode,
        preferred_element_type=jnp.float32,
    )


def contract_first(matrix_a, matrix_b, mode=None):
    return lax.dot_general(
        matrix_a,
        matrix_b,
        (((0,), (0,)), ((), ())),
        precision=mode,
        preferred_element_type=jnp.float32,
    )


def dot(matrix_a, matrix_b):
    return jnp.dot(matrix_a, matrix_b, preferred_element_type=jnp.float32)


def dot_high(matrix_a, matrix_b):
    return jnp.dot(matrix_a, matrix_b, precision=precise, preferred_element_type=jnp.float32)


def slot_targets(routes, experts_all, capacity, stride):
    pairs = 2 * MB_TOK
    flat = routes.reshape(-1, pairs)
    hits = (flat[:, :, None] == jnp.arange(experts_all, dtype=jnp.int32)).astype(jnp.bfloat16)
    lower = (
        jnp.arange(pairs, dtype=jnp.int32)[:, None] > jnp.arange(pairs, dtype=jnp.int32)[None, :]
    ).astype(jnp.bfloat16)
    earlier = jnp.einsum("pq,bqe->bpe", lower, hits, preferred_element_type=jnp.float32)
    rank = jnp.sum(earlier * hits.astype(jnp.float32), axis=-1).astype(jnp.int32)
    block = jnp.arange(flat.shape[0], dtype=jnp.int32)[:, None]
    target = flat * stride + block * capacity + rank
    return target.reshape(-1, 2).T


NEAR = 128


def offset_buckets():
    offset = jnp.arange(4 * NEAR, dtype=jnp.int32) - 2 * NEAR
    distance = jnp.abs(offset)
    far_bucket = 8 + sum(((distance >= threshold).astype(jnp.int32) for threshold in thresholds))
    bucket = jnp.where(distance < 8, distance, far_bucket) + 16 * (offset > 0).astype(jnp.int32)
    return (bucket[:, None] == jnp.arange(BUCKETS, dtype=jnp.int32)).astype(jnp.float32)


def bias_tiles(line):
    return pltpu.roll(
        jnp.broadcast_to(line, (NEAR, 4 * NEAR)), 0, 1, stride=1, stride_axis=0
    )


def mix_head(query, key, value, line, soft_ref, head):
    tiles = bias_tiles(line)
    blocks = LEN // NEAR
    outs = []
    for i in range(blocks):
        raw = contract_last(query[i * NEAR : (i + 1) * NEAR], key) * (HEAD_DIM**-0.5)
        parts = []
        for j in range(blocks):
            part = raw[:, j * NEAR : (j + 1) * NEAR]
            if abs(j - i) <= 1:
                parts.append(part + tiles[:, (j - i + 2) * NEAR : (j - i + 3) * NEAR])
            else:
                edge = 1 if j < i else 4 * NEAR - 1
                parts.append(part + line[:, edge : edge + 1])
        scores = jnp.concatenate(parts, axis=1)
        terms = jnp.exp(scores - jnp.max(scores, axis=1, keepdims=True))
        soft = (terms * (1.0 / jnp.sum(terms, axis=1, keepdims=True))).astype(jnp.bfloat16)
        soft_ref[head, i * NEAR : (i + 1) * NEAR, :] = soft
        outs.append(dot(soft, value))
    return jnp.concatenate(outs, axis=0).astype(jnp.bfloat16)


def unmix_head(query, key, value, grad_mixed, soft_ref, grads_v, head):
    blocks = LEN // NEAR
    near = [jnp.zeros((NEAR, NEAR), jnp.float32) for _ in range(3)]
    below = jnp.zeros((NEAR, NEAR), jnp.float32)
    above = jnp.zeros((NEAR, NEAR), jnp.float32)
    grad_query = []
    for i in range(blocks):
        at = slice(i * NEAR, (i + 1) * NEAR)
        soft = soft_ref[head, at, :].astype(jnp.float32)
        grad_soft = contract_last(grad_mixed[at], value)
        product = soft * grad_soft
        grad = product - soft * jnp.sum(product, axis=1, keepdims=True)
        low = grad.astype(jnp.bfloat16)
        grads_v[at, :] = low
        grad_query.append(dot(low, key))
        wide = low.astype(jnp.float32)
        for j in range(blocks):
            part = wide[:, j * NEAR : (j + 1) * NEAR]
            if abs(j - i) <= 1:
                near[j - i + 1] = near[j - i + 1] + part
            elif j < i:
                below = below + part
            else:
                above = above + part
    band = jnp.concatenate([jnp.zeros((NEAR, NEAR), jnp.float32)] + near, axis=1)
    eight = band[0:8]
    for i in range(8, NEAR, 8):
        eight = eight + pltpu.roll(band[i : i + 8], 4 * NEAR - i, 1)
    row = lax.broadcasted_iota(jnp.int32, (8, 4 * NEAR), 0)
    for bit in (1, 2, 4):
        eight = jnp.where(lax.rem(lax.div(row, bit), 2) == 1, pltpu.roll(eight, 4 * NEAR - bit, 1), eight)
    line = jnp.sum(eight, axis=0, keepdims=True)
    column = lax.broadcasted_iota(jnp.int32, (1, 4 * NEAR), 1)
    line = line + jnp.where(column == 1, jnp.sum(below), 0.0)
    line = line + jnp.where(column == 4 * NEAR - 1, jnp.sum(above), 0.0)
    scaling = HEAD_DIM**-0.5
    grad_query = (jnp.concatenate(grad_query, axis=0) * scaling).astype(jnp.bfloat16)
    grad_key = (contract_first(grads_v[...], query) * scaling).astype(jnp.bfloat16)
    grad_value = contract_first(soft_ref[head], grad_mixed).astype(jnp.bfloat16)
    return grad_query, grad_key, grad_value, line


class Plan:
    def __init__(self, n_e, n_h, experts_all, width):
        self.n_e, self.n_h, self.width = n_e, n_h, width
        self.capacity = 10 * MB_TOK // (4 * experts_all)
        self.stride = -(-MICRO * self.capacity // 16) * 16
        self.span = 2 * self.stride
        self.rows = n_e * self.stride
        self.total = n_h * self.rows
        self.relayed = n_e - 1 if (n_e, n_h) == (8, 4) else n_e
        self.summed = (n_e, n_h) == (8, 4)
        self.direct = n_h == 4

    def place(self):
        return lax.axis_index("expert"), lax.axis_index("hidden")

    def chunk(self, z, source):
        sign = 1 - 2 * lax.div(z, self.n_h // 2)
        return lax.rem(sign * (source - z) + self.n_h, self.n_h)

    def source(self, z, chunk):
        sign = 1 - 2 * lax.div(z, self.n_h // 2)
        return lax.rem(z + self.n_h + sign * chunk, self.n_h)


def across(here, mask):
    there, bit = here, 1
    while bit <= mask:
        if mask & bit:
            there = there + bit * (1 - 2 * lax.rem(lax.div(here, bit), 2))
        bit *= 2
    return there


def remote(src, dst, send_sem, recv_sem, device):
    return pltpu.make_async_remote_copy(
        src_ref=src,
        dst_ref=dst,
        send_sem=send_sem,
        recv_sem=recv_sem,
        device_id=device,
        device_id_type=MESH,
    )


def greet(plan):
    e, z = plan.place()
    barrier = pltpu.get_barrier_semaphore()
    for mask in range(1, plan.n_e):
        pl.semaphore_signal(barrier, inc=1, device_id=(across(e, mask), z), device_id_type=MESH)
    for shift in range(1, plan.n_h):
        pl.semaphore_signal(
            barrier, inc=1, device_id=(e, lax.rem(z + shift, plan.n_h)), device_id_type=MESH
        )
    pl.semaphore_wait(barrier, plan.n_e + plan.n_h - 2)


def slot_hits(plan, base, target):
    slots = lax.broadcasted_iota(jnp.int32, (plan.stride, LEN), 0).astype(jnp.float32) + base
    return jnp.where((slots == target[0:1, :]) | (slots == target[1:2, :]), 1.0, 0.0).astype(
        jnp.bfloat16
    )


def slot_base(plan, device, j):
    return (device * plan.span + j * plan.stride).astype(jnp.float32)


class Dispatch:
    def __init__(self, plan, rows, meta, land, out, meta_out, rows_v, meta_v, stage, sems):
        self.plan = plan
        self.rows, self.meta, self.land = rows, meta, land
        self.out, self.meta_out = out, meta_out
        self.rows_v, self.meta_v, self.stage = rows_v, meta_v, stage
        (
            self.z_send,
            self.z_recv,
            self.zm_send,
            self.zm_recv,
            self.a_send,
            self.a_recv,
            self.m_send,
            self.m_recv,
            self.r_send,
            self.r_recv,
            self.local,
        ) = sems

    @staticmethod
    def sem_shapes(plan):
        dma = pltpu.SemaphoreType.DMA
        n_h, n_e = plan.n_h, plan.n_e
        return [
            dma((n_h, 2)),
            dma((n_h,)),
            dma((n_h, 2)),
            dma((n_h,)),
            dma((2, n_e)),
            dma((n_h, n_e)),
            dma((n_h, n_e)),
            dma((n_h, n_e)),
            dma((n_h, 2)),
            dma((n_h,)),
            dma((3,)),
        ]

    def hop(self, source, way, own):
        e, z = self.plan.place()
        sems = [
            (self.z_send.at[source, (way + 1) // 2], self.z_recv.at[source]),
            (self.zm_send.at[source, (way + 1) // 2], self.zm_recv.at[source]),
        ]
        return (
            remote(self.meta_v.at[source], self.meta_v.at[source], *sems[1], (e, z + way)),
            remote(
                self.rows if own else self.land.at[source],
                self.land.at[source],
                *sems[0],
                (e, z + way),
            ),
        )

    def on_the_way(self, distance, act):
        n_h = self.plan.n_h
        _, z = self.plan.place()

        @pl.when(z + distance < n_h)
        def _():
            act(z + distance, z > 0, -1)

        @pl.when(z >= distance)
        def _():
            act(z - distance, z < n_h - 1, 1)

    def begin(self):
        _, z = self.plan.place()
        copy = pltpu.make_async_copy(self.meta, self.meta_v.at[z], self.local.at[1])
        copy.start()
        copy.wait()

        @pl.when(z > 0)
        def _():
            for copy in self.hop(z, -1, True):
                copy.start()

        @pl.when(z < self.plan.n_h - 1)
        def _():
            for copy in self.hop(z, 1, True):
                copy.start()

    def pass_on(self, distance):
        def act(source, forwarded, way):
            for copy in self.hop(source, way, False):
                copy.wait_recv()

            @pl.when(forwarded)
            def _():
                for copy in self.hop(source, way, False):
                    copy.start()

        self.on_the_way(distance, act)

    def in_plane(self, chunk, mask):
        plan = self.plan
        e, z = plan.place()
        buffer = lax.rem(chunk, 2)
        at = pl.multiple_of((chunk * plan.n_e + mask) * plan.stride, 16)
        return remote(
            self.stage.at[buffer, :, pl.ds(mask * plan.stride, plan.stride), :],
            self.out.at[:, pl.ds(at, plan.stride), :],
            self.a_send.at[buffer, mask],
            self.a_recv.at[chunk, mask],
            (across(e, mask), z),
        )

    def meta_copy(self, chunk, mask):
        e, z = self.plan.place()
        return remote(
            self.meta_v.at[self.plan.source(z, chunk)],
            self.meta_out.at[chunk, mask],
            self.m_send.at[chunk, mask],
            self.m_recv.at[chunk, mask],
            (across(e, mask), z),
        )

    def relay_copy(self, source, way):
        plan = self.plan
        e, z = plan.place()

        def at(place):
            chunk = plan.chunk(place, source)
            return pl.ds(
                pl.multiple_of((chunk * plan.n_e + plan.relayed) * plan.stride, 16), plan.stride
            )

        return remote(
            self.out.at[:, at(z), :],
            self.out.at[:, at(z + way), :],
            self.r_send.at[source, (way + 1) // 2],
            self.r_recv.at[source],
            (e, z + way),
        )

    def relay(self, distance):
        plan = self.plan
        if plan.relayed == plan.n_e:
            return
        _, z = plan.place()

        @pl.when(distance == 0)
        def _():
            self.in_plane(0, plan.relayed).wait_recv()

            @pl.when(z > 0)
            def _():
                self.relay_copy(z, -1).start()

            @pl.when(z < plan.n_h - 1)
            def _():
                self.relay_copy(z, 1).start()

        def act(source, forwarded, way):
            chunk = plan.chunk(z, source)
            at = pl.ds(
                pl.multiple_of((chunk * plan.n_e + plan.relayed) * plan.stride, 16), plan.stride
            )
            e, _ = plan.place()
            remote(
                self.out.at[:, at, :],
                self.out.at[:, at, :],
                self.r_send.at[source, 0],
                self.r_recv.at[source],
                (e, z - way),
            ).wait_recv()

            @pl.when(forwarded)
            def _():
                self.relay_copy(source, way).start()

        @pl.when(distance > 0)
        def _():
            self.on_the_way(distance, act)

    def chunk(self, chunk, target_of):
        plan = self.plan
        e, z = plan.place()
        buffer = lax.rem(chunk, 2)
        source = plan.source(z, chunk)

        @pl.when(chunk == 0)
        def _():
            copy = pltpu.make_async_copy(self.rows, self.rows_v.at[buffer], self.local.at[0])
            copy.start()
            copy.wait()

        @pl.when(chunk > 0)
        def _():
            self.pass_on(chunk)
            copy = pltpu.make_async_copy(
                self.land.at[source], self.rows_v.at[buffer], self.local.at[0]
            )
            copy.start()
            copy.wait()

        for mask in range(1, plan.n_e):
            self.meta_copy(chunk, mask).start()
        own_meta = pltpu.make_async_copy(
            self.meta_v.at[source], self.meta_out.at[chunk, 0], self.local.at[1]
        )
        own_meta.start()

        @pl.when(chunk >= 2)
        def _():
            self.wait_sent(chunk - 2)

        target = target_of(chunk)
        group = min(4, plan.n_e)
        for start in range(plan.n_e - group, -1, -group):
            for j in range(2):
                hot = jnp.concatenate(
                    [
                        slot_hits(plan, slot_base(plan, across(e, start + i), j), target)
                        for i in range(group)
                    ],
                    axis=0,
                )
                picked = dot(hot, self.rows_v[buffer]).astype(jnp.bfloat16)
                self.stage[
                    buffer, j, start * plan.stride : (start + group) * plan.stride, :
                ] = picked
            if start <= plan.relayed < start + group:

                @pl.when(chunk == 0)
                def _():
                    self.in_plane(chunk, plan.relayed).start()

            for mask in range(max(start, 1), min(start + group, plan.relayed)):
                self.in_plane(chunk, mask).start()
        at = pl.multiple_of(chunk * plan.rows, 16)
        own = pltpu.make_async_copy(
            self.stage.at[buffer, :, pl.ds(0, plan.stride), :],
            self.out.at[:, pl.ds(at, plan.stride), :],
            self.local.at[2],
        )
        own.start()
        own.wait()
        own_meta.wait()

    def wait_sent(self, chunk):
        for mask in range(1, self.plan.relayed):
            self.in_plane(chunk, mask).wait_send()
        if self.plan.relayed < self.plan.n_e:

            @pl.when(chunk == 0)
            def _():
                self.in_plane(chunk, self.plan.relayed).wait_send()

    def told(self, chunk):
        for mask in range(1, self.plan.n_e):
            self.meta_copy(chunk, mask).wait_recv()

    def arrived(self, chunk):
        for mask in range(1, self.plan.relayed):
            self.in_plane(chunk, mask).wait_recv()

    def finish(self):
        plan = self.plan
        for chunk in range(max(0, plan.n_h - 2), plan.n_h):
            self.wait_sent(chunk)
        _, z = plan.place()

        @pl.when(z > 0)
        def _():
            for copy in self.hop(z, -1, True):
                copy.wait_send()

        @pl.when(z < plan.n_h - 1)
        def _():
            for copy in self.hop(z, 1, True):
                copy.wait_send()

        def act(source, forwarded, way):
            @pl.when(forwarded)
            def _():
                for copy in self.hop(source, way, False):
                    copy.wait_send()

        for distance in range(1, plan.n_h):
            self.on_the_way(distance, act)
        for chunk in range(plan.n_h):
            for mask in range(1, plan.n_e):
                self.meta_copy(chunk, mask).wait_send()
        if plan.relayed < plan.n_e:

            @pl.when(z > 0)
            def _():
                self.relay_copy(z, -1).wait_send()

            @pl.when(z < plan.n_h - 1)
            def _():
                self.relay_copy(z, 1).wait_send()

            def passed(source, forwarded, way):
                @pl.when(forwarded)
                def _():
                    self.relay_copy(source, way).wait_send()

            for distance in range(1, plan.n_h):
                self.on_the_way(distance, passed)


def same(index, other, count):
    return 1 - lax.div(lax.rem(index - other + count, count) + count - 1, count)


class Return:
    own_first = True

    def __init__(self, plan, back, land, out, stage, rows_v, sum_v, total, sems):
        self.plan = plan
        self.back, self.land, self.out = back, land, out
        self.stage, self.rows_v, self.sum_v, self.total = stage, rows_v, sum_v, total
        (self.b_send, self.b_recv, self.s_send, self.s_recv, self.local, self.own) = sems

    @staticmethod
    def sem_shapes(plan):
        dma = pltpu.SemaphoreType.DMA
        n_h, n_e = plan.n_h, plan.n_e
        return [
            dma((n_h, n_e)),
            dma((n_h, n_e)),
            dma((n_h, 2)),
            dma((3, n_h, 2)),
            dma((2,)),
            dma((n_h,)),
        ]

    def goal(self, turn):
        n_h = self.plan.n_h
        _, z = self.plan.place()
        found = 0
        for here in range(n_h):
            if self.plan.direct:
                order = ((2, 3, 1, 0), (3, 0, 2, 1), (0, 3, 1, 2), (1, 0, 2, 3))[here]
                for when, there in enumerate(order):
                    found = found + there * same(z, here, n_h) * same(turn, when, n_h)
                continue
            others = [there for there in range(n_h) if there != here]
            others.sort(key=lambda d: n_h - 1 - d + here if d > here else d + n_h - 1 - here)
            order = [here] + others if self.own_first else others + [here]
            for when, there in enumerate(order):
                found = found + there * same(z, here, n_h) * same(turn, when, n_h)
        return found

    def chunk_of(self, goal):
        _, z = self.plan.place()
        return self.plan.chunk(z, goal)

    def source(self, chunk, mask):
        raise NotImplementedError

    def in_plane(self, chunk, mask):
        plan = self.plan
        e, z = plan.place()
        return remote(
            self.source(chunk, mask),
            self.back.at[chunk, :, pl.ds(mask * plan.stride, plan.stride), :],
            self.b_send.at[chunk, mask],
            self.b_recv.at[chunk, mask],
            (across(e, mask), z),
        )

    def own_copy(self, chunk):
        plan = self.plan
        return pltpu.make_async_copy(
            self.source(chunk, 0),
            self.back.at[chunk, :, pl.ds(0, plan.stride), :],
            self.own.at[chunk],
        )

    def send(self, chunk, first=0, end=None):
        for mask in range(first, self.plan.n_e if end is None else end):
            if mask == 0:
                self.own_copy(chunk).start()
            else:
                self.in_plane(chunk, mask).start()

    def hop(self, turn, goal, way, half, far=False):
        e, z = self.plan.place()
        side = 2 if far else (1 - way) // 2
        return remote(
            self.rows_v.at[lax.rem(turn, 2), half, :],
            self.land.at[side, goal, half, :],
            self.s_send.at[turn, half.start // half.size],
            self.s_recv.at[side, goal, half.start // half.size],
            (e, goal if far else z + way),
        )

    def each_hop(self, turn, goal, way, half, act):
        last = self.plan.n_h - 1
        _, z = self.plan.place()
        if not self.plan.direct:
            act(self.hop(turn, goal, way, half))
            return
        far = (z == 0) & (goal == last) if way > 0 else (z == last) & (goal == 0)

        @pl.when(far)
        def _():
            act(self.hop(turn, goal, way, half, True))

        @pl.when(jnp.logical_not(far))
        def _():
            act(self.hop(turn, goal, way, half))

    def each_way(self, goal, act):
        _, z = self.plan.place()
        last = self.plan.n_h - 1
        below, above = z > 0, z < last
        if self.plan.direct:
            below = below & ((z > 1) | (goal < last))
            above = above & ((z < last - 1) | (goal > 0))

        @pl.when(goal > z)
        def _():
            act(1, below)

        @pl.when(goal < z)
        def _():
            act(-1, above)

    halves = (pl.ds(0, LEN // 2), pl.ds(LEN // 2, LEN // 2))

    def take(self, goal, way, half, far=False):
        side = 2 if far else (1 - way) // 2
        e, z = self.plan.place()
        remote(
            self.rows_v.at[0, half, :],
            self.land.at[side, goal, half, :],
            self.s_send.at[0, half.start // half.size],
            self.s_recv.at[side, goal, half.start // half.size],
            (e, self.plan.n_h - 1 - z if far else z - way),
        ).wait_recv()
        copy = pltpu.make_async_copy(
            self.land.at[side, goal, half, :], self.sum_v.at[half, :], self.local.at[1]
        )
        copy.start()
        copy.wait()
        return self.sum_v[half, :].astype(jnp.float32)

    def wait_hop(self, turn):
        goal = self.goal(turn)

        def act(way, _):
            for half in self.halves:
                self.each_hop(turn, goal, way, half, lambda copy: copy.wait_send())

        self.each_way(goal, act)

    def fetched(self, chunk, buffer):
        return pltpu.make_async_copy(self.back.at[chunk], self.stage.at[buffer], self.local.at[0])

    def fetch(self, goal, chunk, buffer):
        for mask in range(1, self.plan.n_e):
            self.in_plane(chunk, mask).wait_recv()
        self.own_copy(chunk).wait()
        self.fetched(chunk, buffer).start()

    def combine(self, turn, target_of):
        plan = self.plan
        e, z = plan.place()
        goal = self.goal(turn)
        chunk = self.chunk_of(goal)
        target = target_of(chunk)
        buffer = lax.rem(turn, 2)
        self.fetch(goal, chunk, buffer)
        hot = [
            jnp.concatenate(
                [
                    slot_hits(plan, slot_base(plan, across(e, mask), j), target)
                    for mask in range(plan.n_e)
                ],
                axis=0,
            )
            for j in range(2)
        ]
        self.fetched(chunk, buffer).wait()

        @pl.when(turn >= 2)
        def _():
            self.wait_hop(turn - 2)

        part = contract_first(hot[0], self.stage[buffer, 0]) + contract_first(
            hot[1], self.stage[buffer, 1]
        )

        @pl.when(goal == z)
        def _():
            self.total[...] = part

        @pl.when(goal != z)
        def _():
            self.rows_v[buffer] = part.astype(jnp.bfloat16)

        def act(way, more):
            for half in self.halves:

                @pl.when(more)
                def _():
                    so_far = self.take(goal, way, half)
                    self.rows_v[buffer, half, :] = (
                        self.rows_v[buffer, half, :].astype(jnp.float32) + so_far
                    ).astype(jnp.bfloat16)

                self.each_hop(turn, goal, way, half, lambda copy: copy.start())

        self.each_way(goal, act)

    def finish(self):
        plan = self.plan
        _, z = plan.place()
        for turn in range(plan.n_h - 2, plan.n_h):
            self.wait_hop(turn)

        @pl.when(z > 0)
        def _():
            for half in self.halves:
                self.total[half, :] += self.take(z, 1, half)

        @pl.when(z < plan.n_h - 1)
        def _():
            for half in self.halves:
                self.total[half, :] += self.take(z, -1, half)

        if plan.direct:

            @pl.when((z == 0) | (z == plan.n_h - 1))
            def _():
                for half in self.halves:
                    self.total[half, :] += self.take(z, 1, half, True)

        copy = pltpu.make_async_copy(self.total, self.out, self.local.at[0])
        copy.start()
        copy.wait()


class ReturnHeld(Return):
    own_first = False

    def __init__(self, plan, given, *rest):
        super().__init__(plan, *rest)
        self.given = given

    def source(self, chunk, mask):
        plan = self.plan
        at = pl.multiple_of((chunk * plan.n_e + mask) * plan.stride, 16)
        return self.given.at[:, pl.ds(at, plan.stride), :]

    def sent(self):
        for chunk in range(self.plan.n_h):
            for mask in range(1, self.plan.n_e):
                self.in_plane(chunk, mask).wait_send()


class ReturnMade(Return):
    def __init__(self, plan, made, *rest):
        super().__init__(plan, *rest)
        self.made = made
        self.ring = made.shape[0]

    def source(self, chunk, mask):
        plan = self.plan
        return self.made.at[
            lax.rem(chunk, self.ring), :, pl.ds(mask * plan.stride, plan.stride), :
        ]

    def free(self, chunk):
        if self.plan.n_h > self.ring:

            @pl.when(chunk >= self.ring)
            def _():
                self.wait_sent(chunk - self.ring)
                self.own_copy(chunk - self.ring).wait()

    def wait_sent(self, chunk):
        for mask in range(1, self.plan.n_e):
            self.in_plane(chunk, mask).wait_send()

    def sent(self):
        for chunk in range(max(0, self.plan.n_h - self.ring), self.plan.n_h):
            self.wait_sent(chunk)


ANY = pl.BlockSpec(memory_space=pl.ANY)


def inverse_root(rows):
    return lax.rsqrt(jnp.mean(rows * rows, axis=1, keepdims=True) + eps)


def attend_body(plan, *refs):
    (
        grads,
        targets,
        tokens,
        w_query,
        w_key,
        w_value,
        w_out,
        lines,
        gains,
        w_router,
        routes,
        grads_out,
        targets_out,
        land,
        soft_out,
        mixed_out,
        normed_out,
        query_out,
        key_out,
        value_out,
        hidden_out,
        sent_out,
        gates_out,
        roots_out,
        rows_v,
        meta_v,
        stage,
        tokens_v,
        weights_v,
        normed_v,
        heads_v,
        soft_v,
        mixed_v,
        hidden_v,
        in_sem,
        soft_sem,
        out_sem,
        *sems,
    ) = refs
    loads = [
        pltpu.make_async_copy(given, held, in_sem.at[i])
        for i, (given, held) in enumerate(
            [(tokens, tokens_v)]
            + [
                (weight, weights_v.at[k])
                for k, weight in enumerate((w_query, w_key, w_value, w_out))
            ]
        )
    ]
    for load in loads:
        load.start()
    greet(plan)
    work = Dispatch(plan, grads, targets, land, grads_out, targets_out, rows_v, meta_v, stage, sems)
    work.begin()
    _, z = plan.place()
    stores = [
        pltpu.make_async_copy(held, out, out_sem.at[i])
        for i, (held, out) in enumerate(
            (
                (normed_v, normed_out),
                (heads_v.at[0], query_out),
                (heads_v.at[1], key_out),
                (heads_v.at[2], value_out),
                (mixed_v, mixed_out),
                (hidden_v, hidden_out),
                (normed_v, sent_out),
            )
        )
    ]

    def project():
        for load in loads:
            load.wait()
        rows = tokens_v[...].astype(jnp.float32)
        root = inverse_root(rows)
        roots_out[:, 0:128] = jnp.broadcast_to(root, (LEN, 128))
        normed_v[...] = (rows * root * gains[0:1, :]).astype(jnp.bfloat16)
        for k in range(3):
            heads_v[k] = dot(normed_v[...], weights_v[k]).astype(jnp.bfloat16)
        for store in stores[:4]:
            store.start()

    def soft_copy(pair):
        buffer = lax.rem(pair, 2)
        return pltpu.make_async_copy(
            soft_v.at[buffer], soft_out.at[pl.ds(2 * pair, 2)], soft_sem.at[buffer]
        )

    def mix_pair(pair):
        lanes = pl.ds(pl.multiple_of(pair * 2 * HEAD_DIM, 2 * HEAD_DIM), 2 * HEAD_DIM)
        both = [heads_v[k, :, lanes] for k in range(3)]

        @pl.when(pair >= 2)
        def _():
            soft_copy(pair - 2).wait()

        heads = []
        for head in range(2):
            at = slice(head * HEAD_DIM, (head + 1) * HEAD_DIM)
            heads.append(
                mix_head(
                    *[item[:, at] for item in both],
                    lines[pair, head : head + 1, :],
                    soft_v.at[lax.rem(pair, 2)],
                    head,
                )
            )
        mixed_v[:, lanes] = jnp.concatenate(heads, axis=1)
        soft_copy(pair).start()

    def route():
        stores[4].start()
        hidden = tokens_v[...].astype(jnp.float32) + dot(mixed_v[...], weights_v[3])
        hidden_v[...] = hidden
        stores[5].start()
        root = inverse_root(hidden)
        roots_out[:, 128:256] = jnp.broadcast_to(root, (LEN, 128))
        normed = hidden * root * gains[1:2, :]
        stores[0].wait()
        normed_v[...] = normed.astype(jnp.bfloat16)
        stores[6].start()
        logits = contract_last(w_router[...], normed, precise)
        experts = lax.broadcasted_iota(jnp.int32, logits.shape, 0).astype(jnp.float32)
        chosen = [
            jnp.sum(jnp.where(experts == routes[k : k + 1, :], logits, 0.0), axis=0, keepdims=True)
            for k in range(2)
        ]
        peak = jnp.maximum(chosen[0], chosen[1])
        terms = [jnp.exp(item - peak) for item in chosen]
        for k in range(2):
            gates_out[k : k + 1, :] = terms[k] / (terms[0] + terms[1])
        gates_out[2:8, :] = jnp.zeros((6, LEN), jnp.float32)

    pairs = HEADS // 2

    def mixed_by(chunk):
        n_h, found = plan.n_h, 0
        for when in range(1, n_h + 1):
            share = (0, 0, 6, 8, 8)[when] if n_h == 4 else pairs * when // n_h
            found = found + same(chunk, when, n_h + 1) * share
        return found

    @pl.loop(0, plan.n_h)
    def _(chunk):
        work.chunk(chunk, lambda at: meta_v[plan.source(z, at)])
        pl.when(chunk == 0)(project)
        pl.when(chunk > 0)(lambda: work.relay(chunk - 1))
        pl.loop(mixed_by(chunk), mixed_by(chunk + 1))(mix_pair)

    work.relay(plan.n_h - 1)
    soft_copy(pairs - 2).wait()
    soft_copy(pairs - 1).wait()
    route()
    for store in stores[1:]:
        store.wait()
    for chunk in range(plan.n_h):
        work.told(chunk)
        work.arrived(chunk)
    work.finish()


def attend(
    plan,
    grads,
    targets,
    tokens,
    w_query,
    w_key,
    w_value,
    w_out,
    lines,
    gains,
    w_router,
    routes,
):
    n_h, n_e = plan.n_h, plan.n_e
    bf16, f32 = jnp.bfloat16, jnp.float32
    shape = jax.ShapeDtypeStruct
    vmem = pl.BlockSpec(memory_space=pltpu.VMEM)
    rows = shape((LEN, D), bf16)
    return pl.pallas_call(
        functools.partial(attend_body, plan),
        in_specs=[ANY] * 7 + [vmem] * 4,
        out_specs=[ANY] * 11 + [vmem] * 2,
        out_shape=[
            shape((2, plan.total, D), bf16),
            shape((n_h, n_e, 8, LEN), f32),
            shape((n_h, LEN, D), bf16),
            shape((HEADS, LEN, LEN), bf16),
            rows,
            rows,
            rows,
            rows,
            rows,
            shape((LEN, D), f32),
            rows,
            shape((8, LEN), f32),
            shape((LEN, 256), f32),
        ],
        scratch_shapes=[
            pltpu.VMEM((2, LEN, D), bf16),
            pltpu.VMEM((n_h, 8, LEN), f32),
            pltpu.VMEM((2, 2, plan.rows, D), bf16),
            pltpu.VMEM((LEN, D), bf16),
            pltpu.VMEM((4, D, D), bf16),
            pltpu.VMEM((LEN, D), bf16),
            pltpu.VMEM((3, LEN, D), bf16),
            pltpu.VMEM((2, 2, LEN, LEN), bf16),
            pltpu.VMEM((LEN, D), bf16),
            pltpu.VMEM((LEN, D), f32),
            pltpu.SemaphoreType.DMA((5,)),
            pltpu.SemaphoreType.DMA((2,)),
            pltpu.SemaphoreType.DMA((7,)),
        ]
        + Dispatch.sem_shapes(plan),
        compiler_params=pltpu.CompilerParams(
            collective_id=1, has_side_effects=True, vmem_limit_bytes=VMEM
        ),
        name="attend",
    )(
        grads,
        targets,
        tokens,
        w_query,
        w_key,
        w_value,
        w_out,
        lines.reshape(HEADS // 2, 2, 4 * NEAR),
        gains,
        w_router,
        routes,
    )


def expert_body(plan, halves, n_d, *refs):
    (
        sent,
        gates,
        grads,
        targets,
        w_gate,
        w_up,
        w_down,
        total_out,
        gg_out,
        rows_out,
        y_out,
        dgate_out,
        dup_out,
        act_out,
        meta_out,
        land,
        back,
        land_back,
        rows_v,
        meta_v,
        stage,
        wg_v,
        wu_v,
        wd_v,
        target_v,
        gate_v,
        x_v,
        g_v,
        dx_v,
        y_v,
        dgate_v,
        dup_v,
        act_v,
        gg_v,
        gg_back,
        gg_part,
        gg_land,
        column_v,
        dots_v,
        sum_v,
        total,
        w_sem,
        t_sem,
        x_sem,
        o_sem,
        gg_send,
        gg_recv,
        ggs_send,
        ggs_recv,
        y_sem,
        *sems,
    ) = refs
    n_e, n_h = plan.n_e, plan.n_h
    e, z = plan.place()
    loads = [
        pltpu.make_async_copy(source, held, w_sem.at[i])
        for i, (source, held) in enumerate(((w_gate, wg_v), (w_up, wu_v), (w_down, wd_v)))
    ]
    for load in loads:
        load.start()
    targets_in = pltpu.make_async_copy(targets, target_v, t_sem.at[0])
    targets_in.start()
    greet(plan)
    work = Dispatch(
        plan, sent, gates, land, rows_out, meta_out, rows_v, meta_v, stage, sems[:n_d]
    )
    give = ReturnMade(
        plan, dx_v, back, land_back, total_out, stage, rows_v, sum_v, total, sems[n_d:]
    )
    work.begin()
    targets_in.wait()
    ahead = min(3, n_h)

    @pl.loop(0, ahead)
    def _(chunk):
        work.chunk(chunk, lambda at: target_v[at, 0])
        pl.when(chunk > 0)(lambda: work.relay(chunk - 1))

    for load in loads:
        load.wait()

    def gg_copy(chunk, mask):
        return remote(
            gg_v.at[chunk, mask],
            gg_back.at[chunk, mask],
            gg_send.at[chunk, mask],
            gg_recv.at[chunk, mask],
            (across(e, mask), z),
        )

    def gg_along(chunk):
        return remote(
            gg_part.at[chunk],
            gg_land.at[z],
            ggs_send.at[chunk],
            ggs_recv.at[z],
            (e, plan.source(z, chunk)),
        )

    def gg_from(distance):
        other = lax.rem(z + distance, n_h)
        return other, remote(
            gg_part.at[0], gg_land.at[other], ggs_send.at[0], ggs_recv.at[other], (e, other)
        )

    def outs(chunk, j):
        at = pl.multiple_of(chunk * plan.rows, 16)
        return [
            pltpu.make_async_copy(held.at[j], out.at[j, pl.ds(at, plan.rows), :], o_sem.at[i, j])
            for i, (held, out) in enumerate(
                ((dgate_v, dgate_out), (dup_v, dup_out), (act_v, act_out))
            )
        ]

    all_held = n_h <= dx_v.shape[0]
    masks = n_e // halves
    piece = masks * plan.stride

    def own_slots(j):
        slots = lax.broadcasted_iota(jnp.int32, (plan.stride, LEN), 0).astype(jnp.float32)
        return slots + slot_base(plan, e, j)

    def weigh(chunk, mask):
        aim, weight = target_v[chunk, mask], gate_v[mask]
        at = pl.ds(pl.multiple_of(mask * plan.stride, 16), plan.stride)
        for j in range(2):
            hit = jnp.where(own_slots(j) == aim[0:1, :], weight[0:1, :], 0.0)
            hit = hit + jnp.where(own_slots(j) == aim[1:2, :], weight[1:2, :], 0.0)
            column_v[j, at, :] = jnp.broadcast_to(
                jnp.sum(hit, axis=1, keepdims=True), (plan.stride, 128)
            )

    def spread(chunk, mask):
        aim = target_v[chunk, mask]
        at = pl.ds(pl.multiple_of(mask * plan.stride, 16), plan.stride)
        for k in range(2):
            line = jnp.zeros((1, LEN), jnp.float32)
            for j in range(2):
                hit = own_slots(j) == aim[k : k + 1, :]
                line = line + jnp.sum(
                    jnp.where(hit, dots_v[chunk, j, at, 0:1], 0.0), axis=0, keepdims=True
                )
            gg_v[chunk, mask, k : k + 1, :] = line

    def y_copy(chunk):
        at = pl.ds(pl.multiple_of(chunk * plan.rows, 16), plan.rows)
        return pltpu.make_async_copy(y_v, y_out.at[:, at, :], y_sem.at[1])

    def make_y(chunk):
        at = pl.ds(pl.multiple_of(chunk * plan.rows, 16), plan.rows)
        kept = pltpu.make_async_copy(act_out.at[:, at, :], act_v, y_sem.at[0])
        kept.start()

        @pl.when(chunk > 0)
        def _():
            y_copy(chunk - 1).wait()

        kept.wait()

        @pl.loop(0, 2)
        def _(j):
            y_v[j] = dot(act_v[j], wd_v[j]).astype(jnp.bfloat16)

        y_copy(chunk).start()

    def step(chunk, index):
        j, half = lax.div(index, halves), lax.rem(index, halves)
        at = pl.ds(pl.multiple_of(half * piece, 16), piece)
        gate_pre = contract_last(x_v[j, at, :], wg_v[j])
        up_pre = contract_last(x_v[j, at, :], wu_v[j])
        raw = contract_last(g_v[j, at, :], wd_v[j])
        gate = column_v[j, at, 0:1]
        square = gate_pre * gate_pre
        tanh = jnp.tanh(gate_pre * (0.7978845608028654 + 0.035677408136300125 * square))
        side = 0.5 + 0.5 * tanh
        gelu = gate_pre * side
        slope = side + gelu * (1.0 - side) * (1.5957691216057308 + 0.21406444881780075 * square)
        act = gelu * up_pre
        dots_v[chunk, j, at, :] = jnp.broadcast_to(
            jnp.sum(act * raw, axis=1, keepdims=True), (piece, 128)
        )
        grad_act = gate * raw
        grad_gate = (grad_act * up_pre * slope).astype(jnp.bfloat16)
        grad_up = (grad_act * gelu).astype(jnp.bfloat16)
        dgate_v[j, at, :] = grad_gate
        dup_v[j, at, :] = grad_up
        act_v[j, at, :] = (act * gate).astype(jnp.bfloat16)
        dx_v[lax.rem(chunk, dx_v.shape[0]), j, at, :] = (
            dot(grad_gate, wg_v[j]) + dot(grad_up, wu_v[j])
        ).astype(jnp.bfloat16)

    split = n_e - n_e // 4

    def now(chunk):
        if plan.direct:
            return chunk > 1
        return (chunk < 1) | (not all_held)

    gg_v[...] = jnp.zeros_like(gg_v)

    @pl.loop(0, n_h)
    def _(chunk):
        at = pl.multiple_of(chunk * plan.rows, 16)
        ins = [
            pltpu.make_async_copy(source.at[:, pl.ds(at, plan.rows), :], held, x_sem.at[i])
            for i, (source, held) in enumerate(((rows_out, x_v), (grads, g_v)))
        ]
        ins[1].start()
        work.told(chunk)
        gate_in = pltpu.make_async_copy(meta_out.at[chunk], gate_v, t_sem.at[0])
        gate_in.start()
        gate_in.wait()
        pl.loop(0, n_e)(lambda mask: weigh(chunk, mask))
        give.free(chunk)

        @pl.when(chunk > 0)
        def _():
            for j in range(2):
                for copy in outs(chunk - 1, j):
                    copy.wait()

        work.arrived(chunk)
        ins[0].start()
        for copy in ins:
            copy.wait()
        pl.loop(0, 2 * halves)(lambda index: step(chunk, index))
        for j in range(2):
            for copy in outs(chunk, j):
                copy.start()

        @pl.when(chunk + ahead < n_h)
        def _():
            work.chunk(chunk + ahead, lambda at: target_v[at, 0])

        pl.when(chunk + ahead <= n_h)(lambda: work.relay(chunk + ahead - 1))
        pl.loop(0, n_e)(lambda mask: spread(chunk, mask))
        for mask in range(1, n_e):
            gg_copy(chunk, mask).start()

        @pl.when(now(chunk))
        def _():
            give.send(chunk)

        if plan.direct:
            pl.when(chunk == 0)(lambda: give.send(0, 0, split))


    if plan.direct:
        give.send(1)
        give.send(0, split, n_e)
    elif all_held:
        pl.loop(1, n_h)(lambda turn: give.send(give.chunk_of(give.goal(turn))))
    for j in range(2):
        for copy in outs(n_h - 1, j):
            copy.wait()
    make_y(0)
    work.finish()

    @pl.loop(0, n_h)
    def _(turn):
        chunk = give.chunk_of(give.goal(turn))
        part = gg_v[chunk, 0]
        for mask in range(1, n_e):
            gg_copy(chunk, mask).wait_recv()
            part = part + gg_back[chunk, mask]
        gg_part[chunk] = part

        @pl.when(chunk > 0)
        def _():
            gg_along(chunk).start()

        give.combine(turn, lambda at: target_v[at, 0])
        pl.when(turn + 1 < n_h)(lambda: make_y(turn + 1))

    y_copy(n_h - 1).wait()
    give.sent()
    for chunk in range(n_h):
        for mask in range(1, n_e):
            gg_copy(chunk, mask).wait_send()
    sum_gg = gg_part[0]
    for distance in range(1, n_h):
        other, arrival = gg_from(distance)
        arrival.wait_recv()
        sum_gg = sum_gg + gg_land[other]
    gg_out[...] = sum_gg
    for chunk in range(1, n_h):
        gg_along(chunk).wait_send()
    give.finish()


def run_experts(plan, sent, gates, grads, targets, w_gate, w_up, w_down):
    n_h, n_e, width = plan.n_h, plan.n_e, plan.width
    bf16, f32 = jnp.bfloat16, jnp.float32
    shape = jax.ShapeDtypeStruct
    dma = pltpu.SemaphoreType.DMA
    ring = min(4, n_h)
    d_sems, r_sems = Dispatch.sem_shapes(plan), Return.sem_shapes(plan)
    halves = 2 if plan.rows <= 640 else 4
    return pl.pallas_call(
        functools.partial(expert_body, plan, halves, len(d_sems)),
        in_specs=[ANY] * 7,
        out_specs=[ANY, pl.BlockSpec(memory_space=pltpu.VMEM)] + [ANY] * 9,
        out_shape=[
            shape((LEN, D), f32),
            shape((8, LEN), f32),
            shape((2, plan.total, D), bf16),
            shape((2, plan.total, D), bf16),
            shape((2, plan.total, width), bf16),
            shape((2, plan.total, width), bf16),
            shape((2, plan.total, width), bf16),
            shape((n_h, n_e, 8, LEN), f32),
            shape((n_h, LEN, D), bf16),
            shape((n_h, 2, plan.rows, D), bf16),
            shape((3, n_h, LEN, D), bf16),
        ],
        scratch_shapes=[
            pltpu.VMEM((2, LEN, D), bf16),
            pltpu.VMEM((n_h, 8, LEN), f32),
            pltpu.VMEM((2, 2, plan.rows, D), bf16),
            pltpu.VMEM((2, width, D), bf16),
            pltpu.VMEM((2, width, D), bf16),
            pltpu.VMEM((2, width, D), bf16),
            pltpu.VMEM((n_h, n_e, 8, LEN), f32),
            pltpu.VMEM((n_e, 8, LEN), f32),
            pltpu.VMEM((2, plan.rows, D), bf16),
            pltpu.VMEM((2, plan.rows, D), bf16),
            pltpu.VMEM((ring, 2, plan.rows, D), bf16),
            pltpu.VMEM((2, plan.rows, D), bf16),
            pltpu.VMEM((2, plan.rows, width), bf16),
            pltpu.VMEM((2, plan.rows, width), bf16),
            pltpu.VMEM((2, plan.rows, width), bf16),
            pltpu.VMEM((n_h, n_e, 8, LEN), f32),
            pltpu.VMEM((n_h, n_e, 8, LEN), f32),
            pltpu.VMEM((n_h, 8, LEN), f32),
            pltpu.VMEM((n_h, 8, LEN), f32),
            pltpu.VMEM((2, plan.rows, 128), f32),
            pltpu.VMEM((n_h, 2, plan.rows, 128), f32),
            pltpu.VMEM((LEN, D), bf16),
            pltpu.VMEM((LEN, D), f32),
            dma((3,)),
            dma((1,)),
            dma((2,)),
            dma((3, 2)),
            dma((n_h, n_e)),
            dma((n_h, n_e)),
            dma((n_h,)),
            dma((n_h,)),
            dma((2,)),
        ]
        + d_sems
        + r_sems,
        compiler_params=pltpu.CompilerParams(
            collective_id=2, has_side_effects=True, vmem_limit_bytes=VMEM
        ),
        name="run_experts",
    )(sent, gates, grads, targets, jnp.swapaxes(w_gate, 1, 2), jnp.swapaxes(w_up, 1, 2), w_down)


class Sum:
    pieces, stages, few = 4, 5, 32

    def __init__(self, plan, held, whole, few_v, few_in, *rest):
        self.plan = plan
        self.held, self.whole, self.few_v, self.few_in = held, whole, few_v, few_in
        self.landed, (self.send, self.recv, self.f_send, self.f_recv) = rest[:5], rest[5:]

    @classmethod
    def scratch_shapes(cls):
        dma = pltpu.SemaphoreType.DMA
        bf16, f32 = jnp.bfloat16, jnp.float32
        rows = (D // 2, D // 4, D // 8, D // 16, D // 32)
        return (
            [
                pltpu.VMEM((cls.pieces, D, D), bf16),
                pltpu.VMEM((cls.pieces, D, D), bf16),
                pltpu.VMEM((cls.stages + 1, cls.few, D), f32),
                pltpu.VMEM((cls.stages, cls.few, D), f32),
            ]
            + [pltpu.VMEM((cls.pieces, count, D), bf16) for count in rows]
            + [
                dma((2 * cls.stages, cls.pieces, 2)),
                dma((2 * cls.stages, cls.pieces, 2)),
                dma((cls.stages,)),
                dma((cls.stages,)),
            ]
        )

    def partner(self, bit):
        e, z = self.plan.place()
        if bit < 3:
            return (across(e, 1 << bit), z)
        return (e, across(z, 1 << (bit - 3)))

    def parts(self, stage):
        e, z = self.plan.place()
        place = [lax.rem(lax.div(e, 1 << k), 2) for k in range(3)]
        place += [lax.rem(lax.div(z, 1 << k), 2) for k in range(2)]
        base, count = place[0] * (D // 2), D // 2
        if stage == 1:
            return [(self.partner(0), base, D // 2 - base, count)]
        out = []
        for part, order in enumerate(((1, 2, 3, 4), (2, 1, 3, 4))):
            at, count = base + part * (D // 4), D // 4
            for bit in order[: stage - 1]:
                count //= 2
                keep, give = at + place[bit] * count, at + (1 - place[bit]) * count
                at = keep
            out.append((self.partner(bit), keep, give, count))
        return out

    def copies(self, stage, piece):
        halving = stage <= self.stages
        out = []
        parts = self.parts(stage if halving else 2 * self.stages + 1 - stage)
        for part, (device, keep, give, count) in enumerate(parts):
            here = pl.ds(pl.multiple_of(give if halving else keep, 16), count)
            there = (
                self.landed[stage - 1].at[piece, part * count : (part + 1) * count, :]
                if halving
                else self.whole.at[piece, here, :]
            )
            out.append(
                remote(
                    (self.held if halving else self.whole).at[piece, here, :],
                    there,
                    self.send.at[stage - 1, piece, part],
                    self.recv.at[stage - 1, piece, part],
                    device,
                )
            )
        return out

    def few_copy(self, stage):
        return remote(
            self.few_v.at[stage - 1],
            self.few_in.at[stage - 1],
            self.f_send.at[stage - 1],
            self.f_recv.at[stage - 1],
            self.partner(stage - 1),
        )

    def add(self, stage, piece):
        for part, (_, keep, _, count) in enumerate(self.parts(stage)):
            tile = min(count, 64)

            @pl.loop(0, count // tile)
            def _(i):
                at = pl.ds(pl.multiple_of(keep + i * tile, 16), tile)
                come = pl.ds(pl.multiple_of(part * count + i * tile, 16), tile)
                total = self.held[piece, at, :].astype(jnp.float32) + self.landed[stage - 1][
                    piece, come, :
                ].astype(jnp.float32)
                into = self.whole if stage == self.stages else self.held
                into[piece, at, :] = total.astype(jnp.bfloat16)

    slots = pieces + 2 * stages

    def slot(self, slot, ready, done):
        for piece in range(self.pieces):
            stage = slot - piece + 1
            if stage == 1:
                ready(piece)
            if 2 <= stage <= 2 * self.stages + 1:
                for copy in self.copies(stage - 1, piece):
                    copy.wait_recv()
                if stage - 1 <= self.stages:
                    self.add(stage - 1, piece)
            if 1 <= stage <= 2 * self.stages:
                for copy in self.copies(stage, piece):
                    copy.start()
            if stage == 2 * self.stages + 1:
                done(piece)
        stage = slot + 1
        if 2 <= stage <= self.stages + 1:
            self.few_copy(stage - 1).wait_recv()
            self.few_v[stage - 1] = self.few_v[stage - 2] + self.few_in[stage - 2]
        if stage <= self.stages:
            self.few_copy(stage).start()

    def finish(self):
        for stage in range(1, 2 * self.stages + 1):
            for piece in range(self.pieces):
                for copy in self.copies(stage, piece):
                    copy.wait_send()
        for stage in range(1, self.stages + 1):
            self.few_copy(stage).wait_send()


def sum_body(plan, *refs):
    n_h = plan.n_h
    dgate, dup, act, rows, grads = refs[:5]
    refs = refs[5:]
    if plan.summed:
        low, few = refs[:2]
        refs = refs[2:]
    outs, refs = refs[:3], refs[3:]
    if plan.summed:
        sums_out, few_out = refs[:2]
        refs = refs[2:]
    left_v, right_v, made_v, p_sem, g_sem = refs[:5]
    steps = 3 * n_h

    def factors(q, act_on):
        buffer = lax.rem(q, 2)
        at = pl.ds(pl.multiple_of(lax.rem(q, n_h) * plan.rows, 16), plan.rows)

        def copies(lefts, rights):
            for i in range(2):
                for k, ((source, j), held) in enumerate(((lefts[i], left_v), (rights[i], right_v))):
                    act_on(
                        pltpu.make_async_copy(
                            source.at[j, at, :], held.at[buffer, i], p_sem.at[buffer, 2 * i + k]
                        )
                    )

        @pl.when(q < 2 * n_h)
        def _():
            j = lax.div(q, n_h)
            copies(((dgate, j), (dup, j)), ((rows, j), (rows, j)))

        @pl.when(q >= 2 * n_h)
        def _():
            copies(((act, 0), (act, 1)), ((grads, 0), (grads, 1)))

    def results(group, act_on):
        @pl.when(group < 2)
        def _():
            for i in range(2):
                act_on(pltpu.make_async_copy(made_v.at[i], outs[i].at[group], g_sem.at[i]))

        @pl.when(group == 2)
        def _():
            for i in range(2):
                act_on(pltpu.make_async_copy(made_v.at[i], outs[2].at[i], g_sem.at[i]))

    def product(q):
        buffer, turn, group = lax.rem(q, 2), lax.rem(q, n_h), lax.div(q, n_h)
        factors(q, lambda copy: copy.wait())

        @pl.when(q + 1 < steps)
        def _():
            factors(q + 1, lambda copy: copy.start())

        @pl.when((turn == 0) & (q > 0))
        def _():
            results(group - 1, lambda copy: copy.wait())

        @pl.when(turn == 0)
        def _():
            made_v[...] = jnp.zeros_like(made_v)

        for i in range(2):
            made_v[i] += contract_first(left_v[buffer, i], right_v[buffer, i])

        @pl.when(turn == n_h - 1)
        def _():
            results(group, lambda copy: copy.start())

    factors(0, lambda copy: copy.start())
    if plan.summed:
        load_sem, store_sem = refs[5:7]
        total = Sum(plan, *refs[7:])
        loads = [
            pltpu.make_async_copy(low.at[i], total.held.at[i], load_sem.at[i]) for i in range(4)
        ]
        stores = [
            pltpu.make_async_copy(total.whole.at[i], sums_out.at[i], store_sem.at[i])
            for i in range(4)
        ]
        for load in loads:
            load.start()
        total.few_v[0] = few[...]
        greet(plan)
        done = 0
        for slot in range(total.slots):
            total.slot(slot, lambda i: loads[i].wait(), lambda i: stores[i].start())
            if slot % 2 == 0 and done < steps:
                pl.loop(done, min(done + 2, steps))(product)
                done = min(done + 2, steps)
        few_out[...] = total.few_v[total.stages]
        total.finish()
        for store in stores:
            store.wait()
    else:
        pl.loop(0, steps)(product)
    results(2, lambda copy: copy.wait())


def sum_all(plan, dgate, dup, act, rows, grads, low, few):
    bf16, f32 = jnp.bfloat16, jnp.float32
    shape = jax.ShapeDtypeStruct
    vmem = pl.BlockSpec(memory_space=pltpu.VMEM)
    dma = pltpu.SemaphoreType.DMA
    args = [dgate, dup, act, rows, grads]
    in_specs, out_specs = [ANY] * 5, [ANY] * 3
    out_shape = [shape((2, plan.width, D), f32)] * 3
    scratch_shapes = [
        pltpu.VMEM((2, 2, plan.rows, plan.width), bf16),
        pltpu.VMEM((2, 2, plan.rows, D), bf16),
        pltpu.VMEM((2, plan.width, D), f32),
        dma((2, 4)),
        dma((2,)),
    ]
    params = {"vmem_limit_bytes": VMEM}
    if plan.summed:
        args += [low, few]
        in_specs += [ANY, vmem]
        out_specs += [ANY, vmem]
        out_shape += [shape((4, D, D), bf16), shape((Sum.few, D), f32)]
        scratch_shapes += [dma((4,)), dma((4,))] + Sum.scratch_shapes()
        params.update(collective_id=4, has_side_effects=True)
    out = pl.pallas_call(
        functools.partial(sum_body, plan),
        in_specs=in_specs,
        out_specs=out_specs,
        out_shape=out_shape,
        scratch_shapes=scratch_shapes,
        compiler_params=pltpu.CompilerParams(**params),
        name="sum_all",
    )(*args)
    if plan.summed:
        return out[:3], out[3], out[4]
    return out[:3], *lax.psum((low, few), ("expert", "hidden"))


def unattend_body(plan, n_r, *refs):
    (
        given,
        targets,
        grad_sent,
        hidden,
        grad_out,
        tokens,
        mixed,
        normed,
        query,
        key,
        value,
        soft,
        w_query,
        w_key,
        w_value,
        w_out,
        grad_gates,
        gates,
        routes,
        w_router,
        gains,
        roots,
        branch_out,
        back,
        land,
        low_out,
        tokens_out,
        few_out,
        lines_out,
        rows_v,
        stage,
        target_v,
        sum_v,
        total,
        grad_sent_v,
        hidden_v,
        grad_out_v,
        tokens_v,
        mixed_v,
        normed_v,
        heads_v,
        soft_v,
        weights_v,
        grad_hidden_v,
        branch_v,
        grad_heads_v,
        grads_v,
        low_v,
        wide_v,
        t_sem,
        in_sem,
        soft_sem,
        low_sem,
        out_sem,
        *sems,
    ) = refs
    f32, bf16 = jnp.float32, jnp.bfloat16
    ins = [
        (grad_sent, grad_sent_v),
        (hidden, hidden_v),
        (grad_out, grad_out_v),
        (mixed, mixed_v),
        (w_out, weights_v.at[3]),
        (query, heads_v.at[0]),
        (key, heads_v.at[1]),
        (value, heads_v.at[2]),
        (normed, normed_v),
        (w_query, weights_v.at[0]),
        (w_key, weights_v.at[1]),
        (w_value, weights_v.at[2]),
        (tokens, tokens_v),
    ]
    loads = [
        pltpu.make_async_copy(source, held, in_sem.at[i]) for i, (source, held) in enumerate(ins)
    ]
    targets_in = pltpu.make_async_copy(targets, target_v, t_sem.at[0])

    def soft_copy(pair):
        buffer = lax.rem(pair, 2)
        return pltpu.make_async_copy(
            soft.at[pl.ds(2 * pair, 2)], soft_v.at[buffer], soft_sem.at[buffer]
        )

    targets_in.start()
    for load in loads:
        load.start()
    soft_copy(0).start()
    greet(plan)
    give = ReturnHeld(plan, given, back, land, branch_out, stage, rows_v, sum_v, total, sems)
    turns = plan.n_h
    pl.loop(0, turns)(lambda turn: give.send(give.chunk_of(give.goal(turn))))
    targets_in.wait()

    def combine(turn):
        give.combine(turn, lambda at: target_v[at, 0])

    tile = 64

    def low_copy(i):
        return pltpu.make_async_copy(low_v.at[i % 2], low_out.at[i], low_sem.at[i % 2])

    for load in loads[:3]:
        load.wait()
    few_out[...] = jnp.zeros_like(few_out)
    mean = gates[0:1, :] * grad_gates[0:1, :] + gates[1:2, :] * grad_gates[1:2, :]
    experts = w_router.shape[0]
    numbers = lax.broadcasted_iota(jnp.int32, (experts, LEN), 0).astype(f32)
    grad_logits = jnp.zeros((experts, LEN), f32)
    for k in range(2):
        chosen = gates[k : k + 1, :] * (grad_gates[k : k + 1, :] - mean)
        grad_logits = grad_logits + jnp.where(numbers == routes[k : k + 1, :], chosen, 0.0)
    wide_v[...] = contract_first(grad_logits, w_router[...], precise)

    @pl.loop(0, LEN // tile)
    def _(i):
        at = pl.ds(pl.multiple_of(i * tile, 16), tile)
        rows, root = hidden_v[at, :], roots[at, 128:129]
        grad = wide_v[at, :] + grad_sent_v[at, :]
        near = rows * root
        few_out[experts + 1 : experts + 2, :] += jnp.sum(grad * near, axis=0, keepdims=True)
        scaled = grad * gains[1:2, :]
        pull = jnp.mean(scaled * rows, axis=1, keepdims=True) * (root * root * root)
        grad = grad_out_v[at, :].astype(f32) + root * scaled - rows * pull
        grad_hidden_v[at, :] = grad
        branch_v[at, :] = grad.astype(bf16)
        grad_sent_v[at, :] = near * gains[1:2, :]

    few_out[0:experts, :] = dot_high(grad_logits, grad_sent_v[...])
    for load in loads[3:5]:
        load.wait()
    low_v[1] = contract_first(mixed_v[...], branch_v[...]).astype(bf16)
    low_copy(3).start()
    mixed_v[...] = contract_last(branch_v[...], weights_v[3]).astype(bf16)
    for load in loads[5:8]:
        load.wait()

    def unmix_pair(pair):
        lanes = pl.ds(pl.multiple_of(pair * 2 * HEAD_DIM, 2 * HEAD_DIM), 2 * HEAD_DIM)
        soft_copy(pair).wait()

        @pl.when(pair + 1 < HEADS // 2)
        def _():
            soft_copy(pair + 1).start()

        both = [heads_v[k, :, lanes] for k in range(3)] + [mixed_v[:, lanes]]
        found = []
        for head in range(2):
            at = slice(head * HEAD_DIM, (head + 1) * HEAD_DIM)
            found.append(
                unmix_head(
                    *[item[:, at] for item in both], soft_v.at[lax.rem(pair, 2)], grads_v, head
                )
            )
        for k in range(3):
            grad_heads_v[k, :, lanes] = jnp.concatenate([found[0][k], found[1][k]], axis=1)
        lines_out[pair] = jnp.concatenate([found[0][3], found[1][3]], axis=0)

    pairs = HEADS // 2
    first, second = turns // 4, turns // 2
    pl.loop(0, pairs // 2)(unmix_pair)
    pl.loop(0, first)(combine)
    pl.loop(pairs // 2, pairs)(unmix_pair)
    pl.loop(first, second)(combine)
    for load in loads[8:]:
        load.wait()
    for k in range(3):
        if k == 1:
            low_copy(3).wait()
        if k == 2:
            low_copy(0).wait()
        low_v[k % 2] = contract_first(normed_v[...], grad_heads_v[k]).astype(bf16)
        low_copy(k).start()
    wide_v[...] = (
        contract_last(grad_heads_v[0], weights_v[0])
        + contract_last(grad_heads_v[1], weights_v[1])
        + contract_last(grad_heads_v[2], weights_v[2])
    )

    @pl.loop(0, LEN // tile)
    def _(i):
        at = pl.ds(pl.multiple_of(i * tile, 16), tile)
        rows, root = tokens_v[at, :].astype(f32), roots[at, 0:1]
        grad = wide_v[at, :]
        few_out[experts : experts + 1, :] += jnp.sum(grad * rows * root, axis=0, keepdims=True)
        scaled = grad * gains[0:1, :]
        pull = jnp.mean(scaled * rows, axis=1, keepdims=True) * (root * root * root)
        grad_hidden_v[at, :] = grad_hidden_v[at, :] + root * scaled - rows * pull

    tokens_copy = pltpu.make_async_copy(grad_hidden_v, tokens_out, out_sem.at[0])
    tokens_copy.start()
    pl.loop(second, turns)(combine)
    give.sent()
    give.finish()
    for i in (1, 2):
        low_copy(i).wait()
    tokens_copy.wait()


def unattend(
    plan,
    given,
    targets,
    grad_sent,
    hidden,
    grad_out,
    tokens,
    mixed,
    normed,
    query,
    key,
    value,
    soft,
    w_query,
    w_key,
    w_value,
    w_out,
    grad_gates,
    gates,
    routes,
    w_router,
    gains,
    roots,
):
    n_h, n_e = plan.n_h, plan.n_e
    bf16, f32 = jnp.bfloat16, jnp.float32
    shape = jax.ShapeDtypeStruct
    vmem = pl.BlockSpec(memory_space=pltpu.VMEM)
    dma = pltpu.SemaphoreType.DMA
    sems = Return.sem_shapes(plan)
    few = -(-(w_router.shape[0] + 3) // Sum.few) * Sum.few
    rows, wide = pltpu.VMEM((LEN, D), bf16), pltpu.VMEM((LEN, D), f32)
    out = pl.pallas_call(
        functools.partial(unattend_body, plan, len(sems)),
        in_specs=[ANY] * 16 + [vmem] * 6,
        out_specs=[ANY] * 5 + [vmem] * 2,
        out_shape=[
            shape((LEN, D), f32),
            shape((n_h, 2, plan.rows, D), bf16),
            shape((3, n_h, LEN, D), bf16),
            shape((4, D, D), bf16),
            shape((LEN, D), f32),
            shape((few, D), f32),
            shape((HEADS // 2, 2, 4 * NEAR), f32),
        ],
        scratch_shapes=[
            pltpu.VMEM((2, LEN, D), bf16),
            pltpu.VMEM((2, 2, plan.rows, D), bf16),
            pltpu.VMEM((n_h, n_e, 8, LEN), f32),
            rows,
            wide,
            wide,
            wide,
            rows,
            rows,
            rows,
            rows,
            pltpu.VMEM((3, LEN, D), bf16),
            pltpu.VMEM((2, 2, LEN, LEN), bf16),
            pltpu.VMEM((4, D, D), bf16),
            wide,
            rows,
            pltpu.VMEM((3, LEN, D), bf16),
            pltpu.VMEM((LEN, LEN), bf16),
            pltpu.VMEM((2, D, D), bf16),
            wide,
            dma((1,)),
            dma((13,)),
            dma((2,)),
            dma((2,)),
            dma((1,)),
        ]
        + sems,
        compiler_params=pltpu.CompilerParams(
            collective_id=3, has_side_effects=True, vmem_limit_bytes=VMEM
        ),
        name="unattend",
    )(
        given,
        targets,
        grad_sent,
        hidden,
        grad_out,
        tokens,
        mixed,
        normed,
        query,
        key,
        value,
        soft,
        w_query,
        w_key,
        w_value,
        w_out,
        grad_gates,
        gates,
        routes,
        w_router,
        gains,
        roots,
    )
    return out[0], out[3], out[4], out[5], out[6].reshape(HEADS, 4 * NEAR)


def per_device(
    n_e,
    n_h,
    tokens,
    gain_one,
    w_query,
    w_key,
    w_value,
    w_out,
    bias_table,
    gain_two,
    w_router,
    w_gate,
    w_up,
    w_down,
    routes,
    cotangent,
):
    experts_all = w_router.shape[1]
    plan = Plan(n_e, n_h, experts_all, w_gate.shape[2])
    both = ("expert", "hidden")

    def small(array):
        return jnp.pad(array.astype(jnp.float32), ((0, 8 - array.shape[0]), (0, 0)))

    targets = small(slot_targets(routes, experts_all, plan.capacity, plan.stride))
    gains, route_rows = small(jnp.stack([gain_one, gain_two])), small(routes.T)
    hot_bucket = offset_buckets()
    lines = jnp.dot(hot_bucket, bias_table, precision=precise).T
    (
        grads_in,
        targets_all,
        _,
        soft,
        mixed_rows,
        normed_one,
        query_rows,
        key_rows,
        value_rows,
        hidden,
        sent,
        gates,
        roots,
    ) = attend(
        plan,
        cotangent,
        targets,
        tokens,
        w_query,
        w_key,
        w_value,
        w_out,
        lines,
        gains,
        w_router.T,
        route_rows,
    )
    made = run_experts(
        plan, sent, gates, grads_in, targets_all, w_gate, w_up, w_down
    )
    grad_sent, grad_gates, rows_in, y_rows, gate_rows, up_rows, act_rows = made[:7]
    branch, low, tokens_grad, few, grad_lines = unattend(
        plan,
        y_rows,
        targets_all,
        grad_sent,
        hidden,
        cotangent,
        tokens,
        mixed_rows,
        normed_one,
        query_rows,
        key_rows,
        value_rows,
        soft,
        w_query,
        w_key,
        w_value,
        w_out,
        grad_gates,
        gates,
        route_rows,
        w_router.T,
        gains,
        roots,
    )
    block_out = (hidden + branch).astype(jnp.bfloat16)
    bias_table_grad = jnp.dot(grad_lines, hot_bucket, precision=precise).T
    last = jnp.pad(bias_table_grad.reshape(1, BUCKETS * HEADS), ((0, 0), (0, D - BUCKETS * HEADS)))
    few = lax.dynamic_update_slice(few, last, (experts_all + 2, 0))
    weight_grads, summed, few = sum_all(
        plan, gate_rows, up_rows, act_rows, rows_in, grads_in, low, few
    )
    summed = [summed[i].astype(jnp.float32) for i in range(4)]
    return (
        block_out,
        tokens_grad,
        few[experts_all],
        *summed,
        few[experts_all + 2, : BUCKETS * HEADS].reshape(BUCKETS, HEADS),
        few[experts_all + 1],
        few[:experts_all].T,
        jnp.swapaxes(weight_grads[0], 1, 2),
        jnp.swapaxes(weight_grads[1], 1, 2),
        weight_grads[2],
    )


def solution(mesh):
    in_specs = (
        P(("expert", "hidden"), None),
        P(),
        P(),
        P(),
        P(),
        P(),
        P(),
        P(),
        P(),
        P("expert", None, "hidden"),
        P("expert", None, "hidden"),
        P("expert", "hidden", None),
        P(("expert", "hidden"), None),
        P(("expert", "hidden"), None),
    )
    out_specs = (
        P(("expert", "hidden"), None),
        P(("expert", "hidden"), None),
        P(),
        P(),
        P(),
        P(),
        P(),
        P(),
        P(),
        P(),
        P("expert", None, "hidden"),
        P("expert", None, "hidden"),
        P("expert", "hidden", None),
    )
    return jax.shard_map(
        functools.partial(per_device, mesh.shape["expert"], mesh.shape["hidden"]),
        mesh=mesh, in_specs=in_specs, out_specs=out_specs, check_vma=False
    )
```

```python
import functools

import jax
import jax.numpy as jnp
from jax import lax
from jax.experimental import pallas as pl
from jax.experimental.pallas import tpu as pltpu
from jax.sharding import PartitionSpec as P

D = 1024
HEADS = 16
HEAD_DIM = 64
BUCKETS = 32
LEN = 512
MICRO = 2
MB_TOK = 256
VMEM = 62 * 1024 * 1024
MESH = pl.DeviceIdType.MESH


eps = 1e-06
precise = lax.Precision.HIGHEST
thresholds = (12, 16, 23, 32, 46, 64, 91)


def contract_last(matrix_a, matrix_b, mode=None):
    return lax.dot_general(
        matrix_a,
        matrix_b,
        (((1,), (1,)), ((), ())),
        precision=mode,
        preferred_element_type=jnp.float32,
    )


def contract_first(matrix_a, matrix_b, mode=None):
    return lax.dot_general(
        matrix_a,
        matrix_b,
        (((0,), (0,)), ((), ())),
        precision=mode,
        preferred_element_type=jnp.float32,
    )


def dot(matrix_a, matrix_b):
    return jnp.dot(matrix_a, matrix_b, preferred_element_type=jnp.float32)


def dot_high(matrix_a, matrix_b):
    return jnp.dot(matrix_a, matrix_b, precision=precise, preferred_element_type=jnp.float32)


def slot_targets(routes, experts_all, capacity, stride):
    pairs = 2 * MB_TOK
    flat = routes.reshape(-1, pairs)
    hits = (flat[:, :, None] == jnp.arange(experts_all, dtype=jnp.int32)).astype(jnp.bfloat16)
    lower = (
        jnp.arange(pairs, dtype=jnp.int32)[:, None] > jnp.arange(pairs, dtype=jnp.int32)[None, :]
    ).astype(jnp.bfloat16)
    earlier = jnp.einsum("pq,bqe->bpe", lower, hits, preferred_element_type=jnp.float32)
    rank = jnp.sum(earlier * hits.astype(jnp.float32), axis=-1).astype(jnp.int32)
    block = jnp.arange(flat.shape[0], dtype=jnp.int32)[:, None]
    target = flat * stride + block * capacity + rank
    return target.reshape(-1, 2).T


NEAR = 128


def offset_buckets():
    offset = jnp.arange(4 * NEAR, dtype=jnp.int32) - 2 * NEAR
    distance = jnp.abs(offset)
    far_bucket = 8 + sum(((distance >= threshold).astype(jnp.int32) for threshold in thresholds))
    bucket = jnp.where(distance < 8, distance, far_bucket) + 16 * (offset > 0).astype(jnp.int32)
    return (bucket[:, None] == jnp.arange(BUCKETS, dtype=jnp.int32)).astype(jnp.float32)


def bias_tiles(line):
    return pltpu.roll(
        jnp.broadcast_to(line, (NEAR, 4 * NEAR)), 0, 1, stride=1, stride_axis=0
    )


def mix_head(query, key, value, line, soft_ref, head):
    tiles = bias_tiles(line)
    blocks = LEN // NEAR
    outs = []
    for i in range(blocks):
        raw = contract_last(query[i * NEAR : (i + 1) * NEAR], key) * (HEAD_DIM**-0.5)
        parts = []
        for j in range(blocks):
            part = raw[:, j * NEAR : (j + 1) * NEAR]
            if abs(j - i) <= 1:
                parts.append(part + tiles[:, (j - i + 2) * NEAR : (j - i + 3) * NEAR])
            else:
                edge = 1 if j < i else 4 * NEAR - 1
                parts.append(part + line[:, edge : edge + 1])
        scores = jnp.concatenate(parts, axis=1)
        terms = jnp.exp(scores - jnp.max(scores, axis=1, keepdims=True))
        soft = (terms * (1.0 / jnp.sum(terms, axis=1, keepdims=True))).astype(jnp.bfloat16)
        soft_ref[head, i * NEAR : (i + 1) * NEAR, :] = soft
        outs.append(dot(soft, value))
    return jnp.concatenate(outs, axis=0).astype(jnp.bfloat16)


def unmix_head(query, key, value, grad_mixed, soft_ref, grads_v, head):
    blocks = LEN // NEAR
    near = [jnp.zeros((NEAR, NEAR), jnp.float32) for _ in range(3)]
    below = jnp.zeros((NEAR, NEAR), jnp.float32)
    above = jnp.zeros((NEAR, NEAR), jnp.float32)
    grad_query = []
    for i in range(blocks):
        at = slice(i * NEAR, (i + 1) * NEAR)
        soft = soft_ref[head, at, :].astype(jnp.float32)
        grad_soft = contract_last(grad_mixed[at], value)
        product = soft * grad_soft
        grad = product - soft * jnp.sum(product, axis=1, keepdims=True)
        low = grad.astype(jnp.bfloat16)
        grads_v[at, :] = low
        grad_query.append(dot(low, key))
        wide = low.astype(jnp.float32)
        for j in range(blocks):
            part = wide[:, j * NEAR : (j + 1) * NEAR]
            if abs(j - i) <= 1:
                near[j - i + 1] = near[j - i + 1] + part
            elif j < i:
                below = below + part
            else:
                above = above + part
    band = jnp.concatenate([jnp.zeros((NEAR, NEAR), jnp.float32)] + near, axis=1)
    eight = band[0:8]
    for i in range(8, NEAR, 8):
        eight = eight + pltpu.roll(band[i : i + 8], 4 * NEAR - i, 1)
    row = lax.broadcasted_iota(jnp.int32, (8, 4 * NEAR), 0)
    for bit in (1, 2, 4):
        eight = jnp.where(lax.rem(lax.div(row, bit), 2) == 1, pltpu.roll(eight, 4 * NEAR - bit, 1), eight)
    line = jnp.sum(eight, axis=0, keepdims=True)
    column = lax.broadcasted_iota(jnp.int32, (1, 4 * NEAR), 1)
    line = line + jnp.where(column == 1, jnp.sum(below), 0.0)
    line = line + jnp.where(column == 4 * NEAR - 1, jnp.sum(above), 0.0)
    scaling = HEAD_DIM**-0.5
    grad_query = (jnp.concatenate(grad_query, axis=0) * scaling).astype(jnp.bfloat16)
    grad_key = (contract_first(grads_v[...], query) * scaling).astype(jnp.bfloat16)
    grad_value = contract_first(soft_ref[head], grad_mixed).astype(jnp.bfloat16)
    return grad_query, grad_key, grad_value, line


class Plan:
    def __init__(self, n_e, n_h, experts_all, width):
        self.n_e, self.n_h, self.width = n_e, n_h, width
        self.capacity = 10 * MB_TOK // (4 * experts_all)
        self.stride = -(-MICRO * self.capacity // 16) * 16
        self.span = 2 * self.stride
        self.rows = n_e * self.stride
        self.total = n_h * self.rows
        self.relayed = n_e - 1 if (n_e, n_h) == (8, 4) else n_e
        self.summed = (n_e, n_h) == (8, 4)
        self.direct = n_h == 4

    def place(self):
        return lax.axis_index("expert"), lax.axis_index("hidden")

    def chunk(self, z, source):
        sign = 1 - 2 * lax.div(z, self.n_h // 2)
        return lax.rem(sign * (source - z) + self.n_h, self.n_h)

    def source(self, z, chunk):
        sign = 1 - 2 * lax.div(z, self.n_h // 2)
        return lax.rem(z + self.n_h + sign * chunk, self.n_h)


def across(here, mask):
    there, bit = here, 1
    while bit <= mask:
        if mask & bit:
            there = there + bit * (1 - 2 * lax.rem(lax.div(here, bit), 2))
        bit *= 2
    return there


def remote(src, dst, send_sem, recv_sem, device):
    return pltpu.make_async_remote_copy(
        src_ref=src,
        dst_ref=dst,
        send_sem=send_sem,
        recv_sem=recv_sem,
        device_id=device,
        device_id_type=MESH,
    )


def greet(plan):
    e, z = plan.place()
    barrier = pltpu.get_barrier_semaphore()
    for mask in range(1, plan.n_e):
        pl.semaphore_signal(barrier, inc=1, device_id=(across(e, mask), z), device_id_type=MESH)
    for shift in range(1, plan.n_h):
        pl.semaphore_signal(
            barrier, inc=1, device_id=(e, lax.rem(z + shift, plan.n_h)), device_id_type=MESH
        )
    pl.semaphore_wait(barrier, plan.n_e + plan.n_h - 2)


def slot_hits(plan, base, target):
    slots = lax.broadcasted_iota(jnp.int32, (plan.stride, LEN), 0).astype(jnp.float32) + base
    return jnp.where((slots == target[0:1, :]) | (slots == target[1:2, :]), 1.0, 0.0).astype(
        jnp.bfloat16
    )


def slot_base(plan, device, j):
    return (device * plan.span + j * plan.stride).astype(jnp.float32)


class Dispatch:
    def __init__(self, plan, rows, meta, land, out, meta_out, rows_v, meta_v, stage, sems):
        self.plan = plan
        self.rows, self.meta, self.land = rows, meta, land
        self.out, self.meta_out = out, meta_out
        self.rows_v, self.meta_v, self.stage = rows_v, meta_v, stage
        (
            self.z_send,
            self.z_recv,
            self.zm_send,
            self.zm_recv,
            self.a_send,
            self.a_recv,
            self.m_send,
            self.m_recv,
            self.r_send,
            self.r_recv,
            self.local,
        ) = sems

    @staticmethod
    def sem_shapes(plan):
        dma = pltpu.SemaphoreType.DMA
        n_h, n_e = plan.n_h, plan.n_e
        return [
            dma((n_h, 2)),
            dma((n_h,)),
            dma((n_h, 2)),
            dma((n_h,)),
            dma((2, n_e)),
            dma((n_h, n_e)),
            dma((n_h, n_e)),
            dma((n_h, n_e)),
            dma((n_h, 2)),
            dma((n_h,)),
            dma((3,)),
        ]

    def hop(self, source, way, own):
        e, z = self.plan.place()
        sems = [
            (self.z_send.at[source, (way + 1) // 2], self.z_recv.at[source]),
            (self.zm_send.at[source, (way + 1) // 2], self.zm_recv.at[source]),
        ]
        return (
            remote(self.meta_v.at[source], self.meta_v.at[source], *sems[1], (e, z + way)),
            remote(
                self.rows if own else self.land.at[source],
                self.land.at[source],
                *sems[0],
                (e, z + way),
            ),
        )

    def on_the_way(self, distance, act):
        n_h = self.plan.n_h
        _, z = self.plan.place()

        @pl.when(z + distance < n_h)
        def _():
            act(z + distance, z > 0, -1)

        @pl.when(z >= distance)
        def _():
            act(z - distance, z < n_h - 1, 1)

    def begin(self):
        _, z = self.plan.place()
        copy = pltpu.make_async_copy(self.meta, self.meta_v.at[z], self.local.at[1])
        copy.start()
        copy.wait()

        @pl.when(z > 0)
        def _():
            for copy in self.hop(z, -1, True):
                copy.start()

        @pl.when(z < self.plan.n_h - 1)
        def _():
            for copy in self.hop(z, 1, True):
                copy.start()

    def pass_on(self, distance):
        def act(source, forwarded, way):
            for copy in self.hop(source, way, False):
                copy.wait_recv()

            @pl.when(forwarded)
            def _():
                for copy in self.hop(source, way, False):
                    copy.start()

        self.on_the_way(distance, act)

    def in_plane(self, chunk, mask):
        plan = self.plan
        e, z = plan.place()
        buffer = lax.rem(chunk, 2)
        at = pl.multiple_of((chunk * plan.n_e + mask) * plan.stride, 16)
        return remote(
            self.stage.at[buffer, :, pl.ds(mask * plan.stride, plan.stride), :],
            self.out.at[:, pl.ds(at, plan.stride), :],
            self.a_send.at[buffer, mask],
            self.a_recv.at[chunk, mask],
            (across(e, mask), z),
        )

    def meta_copy(self, chunk, mask):
        e, z = self.plan.place()
        return remote(
            self.meta_v.at[self.plan.source(z, chunk)],
            self.meta_out.at[chunk, mask],
            self.m_send.at[chunk, mask],
            self.m_recv.at[chunk, mask],
            (across(e, mask), z),
        )

    def relay_copy(self, source, way):
        plan = self.plan
        e, z = plan.place()

        def at(place):
            chunk = plan.chunk(place, source)
            return pl.ds(
                pl.multiple_of((chunk * plan.n_e + plan.relayed) * plan.stride, 16), plan.stride
            )

        return remote(
            self.out.at[:, at(z), :],
            self.out.at[:, at(z + way), :],
            self.r_send.at[source, (way + 1) // 2],
            self.r_recv.at[source],
            (e, z + way),
        )

    def relay(self, distance):
        plan = self.plan
        if plan.relayed == plan.n_e:
            return
        _, z = plan.place()

        @pl.when(distance == 0)
        def _():
            self.in_plane(0, plan.relayed).wait_recv()

            @pl.when(z > 0)
            def _():
                self.relay_copy(z, -1).start()

            @pl.when(z < plan.n_h - 1)
            def _():
                self.relay_copy(z, 1).start()

        def act(source, forwarded, way):
            chunk = plan.chunk(z, source)
            at = pl.ds(
                pl.multiple_of((chunk * plan.n_e + plan.relayed) * plan.stride, 16), plan.stride
            )
            e, _ = plan.place()
            remote(
                self.out.at[:, at, :],
                self.out.at[:, at, :],
                self.r_send.at[source, 0],
                self.r_recv.at[source],
                (e, z - way),
            ).wait_recv()

            @pl.when(forwarded)
            def _():
                self.relay_copy(source, way).start()

        @pl.when(distance > 0)
        def _():
            self.on_the_way(distance, act)

    def chunk(self, chunk, target_of):
        plan = self.plan
        e, z = plan.place()
        buffer = lax.rem(chunk, 2)
        source = plan.source(z, chunk)

        @pl.when(chunk == 0)
        def _():
            copy = pltpu.make_async_copy(self.rows, self.rows_v.at[buffer], self.local.at[0])
            copy.start()
            copy.wait()

        @pl.when(chunk > 0)
        def _():
            self.pass_on(chunk)
            copy = pltpu.make_async_copy(
                self.land.at[source], self.rows_v.at[buffer], self.local.at[0]
            )
            copy.start()
            copy.wait()

        for mask in range(1, plan.n_e):
            self.meta_copy(chunk, mask).start()
        own_meta = pltpu.make_async_copy(
            self.meta_v.at[source], self.meta_out.at[chunk, 0], self.local.at[1]
        )
        own_meta.start()

        @pl.when(chunk >= 2)
        def _():
            self.wait_sent(chunk - 2)

        target = target_of(chunk)
        group = min(4, plan.n_e)
        for start in range(plan.n_e - group, -1, -group):
            for j in range(2):
                hot = jnp.concatenate(
                    [
                        slot_hits(plan, slot_base(plan, across(e, start + i), j), target)
                        for i in range(group)
                    ],
                    axis=0,
                )
                picked = dot(hot, self.rows_v[buffer]).astype(jnp.bfloat16)
                self.stage[
                    buffer, j, start * plan.stride : (start + group) * plan.stride, :
                ] = picked
            if start <= plan.relayed < start + group:

                @pl.when(chunk == 0)
                def _():
                    self.in_plane(chunk, plan.relayed).start()

            for mask in range(max(start, 1), min(start + group, plan.relayed)):
                self.in_plane(chunk, mask).start()
        at = pl.multiple_of(chunk * plan.rows, 16)
        own = pltpu.make_async_copy(
            self.stage.at[buffer, :, pl.ds(0, plan.stride), :],
            self.out.at[:, pl.ds(at, plan.stride), :],
            self.local.at[2],
        )
        own.start()
        own.wait()
        own_meta.wait()

    def wait_sent(self, chunk):
        for mask in range(1, self.plan.relayed):
            self.in_plane(chunk, mask).wait_send()
        if self.plan.relayed < self.plan.n_e:

            @pl.when(chunk == 0)
            def _():
                self.in_plane(chunk, self.plan.relayed).wait_send()

    def told(self, chunk):
        for mask in range(1, self.plan.n_e):
            self.meta_copy(chunk, mask).wait_recv()

    def arrived(self, chunk):
        for mask in range(1, self.plan.relayed):
            self.in_plane(chunk, mask).wait_recv()

    def finish(self):
        plan = self.plan
        for chunk in range(max(0, plan.n_h - 2), plan.n_h):
            self.wait_sent(chunk)
        _, z = plan.place()

        @pl.when(z > 0)
        def _():
            for copy in self.hop(z, -1, True):
                copy.wait_send()

        @pl.when(z < plan.n_h - 1)
        def _():
            for copy in self.hop(z, 1, True):
                copy.wait_send()

        def act(source, forwarded, way):
            @pl.when(forwarded)
            def _():
                for copy in self.hop(source, way, False):
                    copy.wait_send()

        for distance in range(1, plan.n_h):
            self.on_the_way(distance, act)
        for chunk in range(plan.n_h):
            for mask in range(1, plan.n_e):
                self.meta_copy(chunk, mask).wait_send()
        if plan.relayed < plan.n_e:

            @pl.when(z > 0)
            def _():
                self.relay_copy(z, -1).wait_send()

            @pl.when(z < plan.n_h - 1)
            def _():
                self.relay_copy(z, 1).wait_send()

            def passed(source, forwarded, way):
                @pl.when(forwarded)
                def _():
                    self.relay_copy(source, way).wait_send()

            for distance in range(1, plan.n_h):
                self.on_the_way(distance, passed)


def same(index, other, count):
    return 1 - lax.div(lax.rem(index - other + count, count) + count - 1, count)


class Return:
    own_first = True

    def __init__(self, plan, back, land, out, stage, rows_v, sum_v, total, slots_in, slots_v, sems):
        self.plan = plan
        self.back, self.land, self.out = back, land, out
        self.stage, self.rows_v, self.sum_v, self.total = stage, rows_v, sum_v, total
        self.slots_in, self.slots_v = slots_in, slots_v
        (
            self.b_send,
            self.b_recv,
            self.s_send,
            self.s_recv,
            self.local,
            self.own,
            self.r_send,
            self.r_recv,
        ) = sems

    @staticmethod
    def sem_shapes(plan):
        dma = pltpu.SemaphoreType.DMA
        n_h, n_e = plan.n_h, plan.n_e
        return [
            dma((n_h, n_e)),
            dma((n_h, n_e)),
            dma((n_h, 2)),
            dma((3, n_h, 2)),
            dma((2,)),
            dma((n_h,)),
            dma((n_h,)),
            dma((n_h,)),
        ]

    @staticmethod
    def slot_shapes(plan):
        return [
            pltpu.VMEM((plan.n_h, 2, plan.stride, D), jnp.bfloat16),
            pltpu.VMEM((2, plan.stride, D), jnp.bfloat16),
        ]

    def goal(self, turn):
        n_h = self.plan.n_h
        _, z = self.plan.place()
        found = 0
        for here in range(n_h):
            if self.plan.direct:
                order = ((2, 3, 1, 0), (3, 0, 2, 1), (0, 3, 1, 2), (1, 0, 2, 3))[here]
                for when, there in enumerate(order):
                    found = found + there * same(z, here, n_h) * same(turn, when, n_h)
                continue
            others = [there for there in range(n_h) if there != here]
            others.sort(key=lambda d: n_h - 1 - d + here if d > here else d + n_h - 1 - here)
            order = [here] + others if self.own_first else others + [here]
            for when, there in enumerate(order):
                found = found + there * same(z, here, n_h) * same(turn, when, n_h)
        return found

    def chunk_of(self, goal):
        _, z = self.plan.place()
        return self.plan.chunk(z, goal)

    def source(self, chunk, mask):
        raise NotImplementedError

    def in_plane(self, chunk, mask):
        plan = self.plan
        e, z = plan.place()
        return remote(
            self.source(chunk, mask),
            self.back.at[chunk, :, pl.ds(mask * plan.stride, plan.stride), :],
            self.b_send.at[chunk, mask],
            self.b_recv.at[chunk, mask],
            (across(e, mask), z),
        )

    def own_copy(self, chunk):
        plan = self.plan
        return pltpu.make_async_copy(
            self.source(chunk, 0),
            self.back.at[chunk, :, pl.ds(0, plan.stride), :],
            self.own.at[chunk],
        )

    def send(self, chunk, first=0, end=None):
        for mask in range(first, self.plan.relayed if end is None else end):
            if mask == 0:
                self.own_copy(chunk).start()
            else:
                self.in_plane(chunk, mask).start()

    def relay(self, chunk):
        plan = self.plan
        e, z = plan.place()
        return remote(
            self.source(chunk, plan.relayed),
            self.slots_in.at[z],
            self.r_send.at[chunk],
            self.r_recv.at[z],
            (e, plan.source(z, chunk)),
        )

    def relay_sum(self):
        plan = self.plan
        if plan.relayed == plan.n_e:
            return
        e, z = plan.place()
        copy = pltpu.make_async_copy(
            self.source(0, plan.relayed), self.slots_v, self.local.at[0]
        )
        copy.start()
        copy.wait()
        for j in range(2):
            total = self.slots_v[j].astype(jnp.float32)
            for distance in range(1, plan.n_h):
                other = lax.rem(z + distance, plan.n_h)
                if j == 0:
                    remote(
                        self.slots_v,
                        self.slots_in.at[other],
                        self.r_send.at[0],
                        self.r_recv.at[other],
                        (e, other),
                    ).wait_recv()
                total = total + self.slots_in[other, j].astype(jnp.float32)
            self.slots_v[j] = total.astype(jnp.bfloat16)
        self.relayed_copy().start()

    def relayed_copy(self):
        plan = self.plan
        e, z = plan.place()
        return remote(
            self.slots_v,
            self.back.at[0, :, pl.ds(plan.relayed * plan.stride, plan.stride), :],
            self.b_send.at[0, plan.relayed],
            self.b_recv.at[0, plan.relayed],
            (across(e, plan.relayed), z),
        )

    def wait_sent(self, chunk):
        plan = self.plan
        for mask in range(1, plan.relayed):
            self.in_plane(chunk, mask).wait_send()
        if plan.relayed < plan.n_e:
            if chunk == 0:
                self.relayed_copy().wait_send()
            else:
                self.relay(chunk).wait_send()

    def hop(self, turn, goal, way, half, far=False):
        e, z = self.plan.place()
        side = 2 if far else (1 - way) // 2
        return remote(
            self.rows_v.at[lax.rem(turn, 2), half, :],
            self.land.at[side, goal, half, :],
            self.s_send.at[turn, half.start // half.size],
            self.s_recv.at[side, goal, half.start // half.size],
            (e, goal if far else z + way),
        )

    def each_hop(self, turn, goal, way, half, act):
        last = self.plan.n_h - 1
        _, z = self.plan.place()
        if not self.plan.direct:
            act(self.hop(turn, goal, way, half))
            return
        far = (z == 0) & (goal == last) if way > 0 else (z == last) & (goal == 0)

        @pl.when(far)
        def _():
            act(self.hop(turn, goal, way, half, True))

        @pl.when(jnp.logical_not(far))
        def _():
            act(self.hop(turn, goal, way, half))

    def each_way(self, goal, act):
        _, z = self.plan.place()
        last = self.plan.n_h - 1
        below, above = z > 0, z < last
        if self.plan.direct:
            below = below & ((z > 1) | (goal < last))
            above = above & ((z < last - 1) | (goal > 0))

        @pl.when(goal > z)
        def _():
            act(1, below)

        @pl.when(goal < z)
        def _():
            act(-1, above)

    halves = (pl.ds(0, LEN // 2), pl.ds(LEN // 2, LEN // 2))

    def take(self, goal, way, half, far=False):
        side = 2 if far else (1 - way) // 2
        e, z = self.plan.place()
        remote(
            self.rows_v.at[0, half, :],
            self.land.at[side, goal, half, :],
            self.s_send.at[0, half.start // half.size],
            self.s_recv.at[side, goal, half.start // half.size],
            (e, self.plan.n_h - 1 - z if far else z - way),
        ).wait_recv()
        copy = pltpu.make_async_copy(
            self.land.at[side, goal, half, :], self.sum_v.at[half, :], self.local.at[1]
        )
        copy.start()
        copy.wait()
        return self.sum_v[half, :].astype(jnp.float32)

    def wait_hop(self, turn):
        goal = self.goal(turn)

        def act(way, _):
            for half in self.halves:
                self.each_hop(turn, goal, way, half, lambda copy: copy.wait_send())

        self.each_way(goal, act)

    def fetched(self, chunk, buffer):
        at = pl.ds(0, self.plan.relayed * self.plan.stride)
        return pltpu.make_async_copy(
            self.back.at[chunk, :, at, :], self.stage.at[buffer, :, at, :], self.local.at[0]
        )

    def fetch(self, goal, chunk, buffer):
        plan = self.plan
        for mask in range(1, plan.relayed):
            self.in_plane(chunk, mask).wait_recv()
        self.own_copy(chunk).wait()
        if plan.relayed < plan.n_e:

            @pl.when(chunk == 0)
            def _():
                self.relayed_copy().wait_recv()
                at = pl.ds(plan.relayed * plan.stride, plan.stride)
                copy = pltpu.make_async_copy(
                    self.back.at[0, :, at, :], self.stage.at[buffer, :, at, :], self.local.at[1]
                )
                copy.start()
                copy.wait()

        self.fetched(chunk, buffer).start()

    def combine(self, turn, target_of):
        plan = self.plan
        e, z = plan.place()
        goal = self.goal(turn)
        chunk = self.chunk_of(goal)
        target = target_of(chunk)
        buffer = lax.rem(turn, 2)
        self.fetch(goal, chunk, buffer)
        hot = [
            jnp.concatenate(
                [
                    slot_hits(plan, slot_base(plan, across(e, mask), j), target)
                    for mask in range(plan.relayed)
                ],
                axis=0,
            )
            for j in range(2)
        ]
        self.fetched(chunk, buffer).wait()

        @pl.when(turn >= 2)
        def _():
            self.wait_hop(turn - 2)

        count = plan.relayed * plan.stride
        part = contract_first(hot[0], self.stage[buffer, 0, :count, :]) + contract_first(
            hot[1], self.stage[buffer, 1, :count, :]
        )

        @pl.when(goal == z)
        def _():
            self.total[...] = part
            if plan.relayed < plan.n_e:
                for j in range(2):
                    base = slot_base(plan, across(e, plan.relayed), j)
                    self.total[...] += contract_first(
                        slot_hits(plan, base, target), self.stage[buffer, j, count:, :]
                    )

        @pl.when(goal != z)
        def _():
            self.rows_v[buffer] = part.astype(jnp.bfloat16)

        def act(way, more):
            for half in self.halves:

                @pl.when(more)
                def _():
                    so_far = self.take(goal, way, half)
                    self.rows_v[buffer, half, :] = (
                        self.rows_v[buffer, half, :].astype(jnp.float32) + so_far
                    ).astype(jnp.bfloat16)

                self.each_hop(turn, goal, way, half, lambda copy: copy.start())

        self.each_way(goal, act)

    def finish(self):
        plan = self.plan
        _, z = plan.place()
        for turn in range(plan.n_h - 2, plan.n_h):
            self.wait_hop(turn)

        @pl.when(z > 0)
        def _():
            for half in self.halves:
                self.total[half, :] += self.take(z, 1, half)

        @pl.when(z < plan.n_h - 1)
        def _():
            for half in self.halves:
                self.total[half, :] += self.take(z, -1, half)

        if plan.direct:

            @pl.when((z == 0) | (z == plan.n_h - 1))
            def _():
                for half in self.halves:
                    self.total[half, :] += self.take(z, 1, half, True)

        copy = pltpu.make_async_copy(self.total, self.out, self.local.at[0])
        copy.start()
        copy.wait()


class ReturnHeld(Return):
    own_first = False

    def __init__(self, plan, given, *rest):
        super().__init__(plan, *rest)
        self.given = given

    def source(self, chunk, mask):
        plan = self.plan
        at = pl.multiple_of((chunk * plan.n_e + mask) * plan.stride, 16)
        return self.given.at[:, pl.ds(at, plan.stride), :]

    def sent(self):
        for chunk in range(self.plan.n_h):
            self.wait_sent(chunk)


class ReturnMade(Return):
    def __init__(self, plan, made, *rest):
        super().__init__(plan, *rest)
        self.made = made
        self.ring = made.shape[0]

    def source(self, chunk, mask):
        plan = self.plan
        return self.made.at[
            lax.rem(chunk, self.ring), :, pl.ds(mask * plan.stride, plan.stride), :
        ]

    def free(self, chunk):
        if self.plan.n_h > self.ring:

            @pl.when(chunk >= self.ring)
            def _():
                self.wait_sent(chunk - self.ring)
                self.own_copy(chunk - self.ring).wait()

    def sent(self):
        for chunk in range(max(0, self.plan.n_h - self.ring), self.plan.n_h):
            self.wait_sent(chunk)


ANY = pl.BlockSpec(memory_space=pl.ANY)


def inverse_root(rows):
    return lax.rsqrt(jnp.mean(rows * rows, axis=1, keepdims=True) + eps)


def attend_body(plan, *refs):
    (
        grads,
        targets,
        tokens,
        w_query,
        w_key,
        w_value,
        w_out,
        lines,
        gains,
        w_router,
        routes,
        grads_out,
        targets_out,
        land,
        soft_out,
        mixed_out,
        normed_out,
        query_out,
        key_out,
        value_out,
        hidden_out,
        sent_out,
        gates_out,
        roots_out,
        rows_v,
        meta_v,
        stage,
        tokens_v,
        weights_v,
        normed_v,
        heads_v,
        soft_v,
        mixed_v,
        hidden_v,
        in_sem,
        soft_sem,
        out_sem,
        *sems,
    ) = refs
    loads = [
        pltpu.make_async_copy(given, held, in_sem.at[i])
        for i, (given, held) in enumerate(
            [(tokens, tokens_v)]
            + [
                (weight, weights_v.at[k])
                for k, weight in enumerate((w_query, w_key, w_value, w_out))
            ]
        )
    ]
    for load in loads:
        load.start()
    greet(plan)
    work = Dispatch(plan, grads, targets, land, grads_out, targets_out, rows_v, meta_v, stage, sems)
    work.begin()
    _, z = plan.place()
    stores = [
        pltpu.make_async_copy(held, out, out_sem.at[i])
        for i, (held, out) in enumerate(
            (
                (normed_v, normed_out),
                (heads_v.at[0], query_out),
                (heads_v.at[1], key_out),
                (heads_v.at[2], value_out),
                (mixed_v, mixed_out),
                (hidden_v, hidden_out),
                (normed_v, sent_out),
            )
        )
    ]

    def project():
        for load in loads:
            load.wait()
        rows = tokens_v[...].astype(jnp.float32)
        root = inverse_root(rows)
        roots_out[:, 0:128] = jnp.broadcast_to(root, (LEN, 128))
        normed_v[...] = (rows * root * gains[0:1, :]).astype(jnp.bfloat16)
        for k in range(3):
            heads_v[k] = dot(normed_v[...], weights_v[k]).astype(jnp.bfloat16)
        for store in stores[:4]:
            store.start()

    def soft_copy(pair):
        buffer = lax.rem(pair, 2)
        return pltpu.make_async_copy(
            soft_v.at[buffer], soft_out.at[pl.ds(2 * pair, 2)], soft_sem.at[buffer]
        )

    def mix_pair(pair):
        lanes = pl.ds(pl.multiple_of(pair * 2 * HEAD_DIM, 2 * HEAD_DIM), 2 * HEAD_DIM)
        both = [heads_v[k, :, lanes] for k in range(3)]

        @pl.when(pair >= 2)
        def _():
            soft_copy(pair - 2).wait()

        heads = []
        for head in range(2):
            at = slice(head * HEAD_DIM, (head + 1) * HEAD_DIM)
            heads.append(
                mix_head(
                    *[item[:, at] for item in both],
                    lines[pair, head : head + 1, :],
                    soft_v.at[lax.rem(pair, 2)],
                    head,
                )
            )
        mixed_v[:, lanes] = jnp.concatenate(heads, axis=1)
        soft_copy(pair).start()

    def route():
        stores[4].start()
        hidden = tokens_v[...].astype(jnp.float32) + dot(mixed_v[...], weights_v[3])
        hidden_v[...] = hidden
        stores[5].start()
        root = inverse_root(hidden)
        roots_out[:, 128:256] = jnp.broadcast_to(root, (LEN, 128))
        normed = hidden * root * gains[1:2, :]
        stores[0].wait()
        normed_v[...] = normed.astype(jnp.bfloat16)
        stores[6].start()
        logits = contract_last(w_router[...], normed, precise)
        experts = lax.broadcasted_iota(jnp.int32, logits.shape, 0).astype(jnp.float32)
        chosen = [
            jnp.sum(jnp.where(experts == routes[k : k + 1, :], logits, 0.0), axis=0, keepdims=True)
            for k in range(2)
        ]
        peak = jnp.maximum(chosen[0], chosen[1])
        terms = [jnp.exp(item - peak) for item in chosen]
        for k in range(2):
            gates_out[k : k + 1, :] = terms[k] / (terms[0] + terms[1])
        gates_out[2:8, :] = jnp.zeros((6, LEN), jnp.float32)

    pairs = HEADS // 2

    def mixed_by(chunk):
        n_h, found = plan.n_h, 0
        for when in range(1, n_h + 1):
            share = (0, 0, 6, 8, 8)[when] if n_h == 4 else pairs * when // n_h
            found = found + same(chunk, when, n_h + 1) * share
        return found

    @pl.loop(0, plan.n_h)
    def _(chunk):
        work.chunk(chunk, lambda at: meta_v[plan.source(z, at)])
        pl.when(chunk == 0)(project)
        pl.when(chunk > 0)(lambda: work.relay(chunk - 1))
        pl.loop(mixed_by(chunk), mixed_by(chunk + 1))(mix_pair)

    work.relay(plan.n_h - 1)
    soft_copy(pairs - 2).wait()
    soft_copy(pairs - 1).wait()
    route()
    for store in stores[1:]:
        store.wait()
    for chunk in range(plan.n_h):
        work.told(chunk)
        work.arrived(chunk)
    work.finish()


def attend(
    plan,
    grads,
    targets,
    tokens,
    w_query,
    w_key,
    w_value,
    w_out,
    lines,
    gains,
    w_router,
    routes,
):
    n_h, n_e = plan.n_h, plan.n_e
    bf16, f32 = jnp.bfloat16, jnp.float32
    shape = jax.ShapeDtypeStruct
    vmem = pl.BlockSpec(memory_space=pltpu.VMEM)
    rows = shape((LEN, D), bf16)
    return pl.pallas_call(
        functools.partial(attend_body, plan),
        in_specs=[ANY] * 7 + [vmem] * 4,
        out_specs=[ANY] * 11 + [vmem] * 2,
        out_shape=[
            shape((2, plan.total, D), bf16),
            shape((n_h, n_e, 8, LEN), f32),
            shape((n_h, LEN, D), bf16),
            shape((HEADS, LEN, LEN), bf16),
            rows,
            rows,
            rows,
            rows,
            rows,
            shape((LEN, D), f32),
            rows,
            shape((8, LEN), f32),
            shape((LEN, 256), f32),
        ],
        scratch_shapes=[
            pltpu.VMEM((2, LEN, D), bf16),
            pltpu.VMEM((n_h, 8, LEN), f32),
            pltpu.VMEM((2, 2, plan.rows, D), bf16),
            pltpu.VMEM((LEN, D), bf16),
            pltpu.VMEM((4, D, D), bf16),
            pltpu.VMEM((LEN, D), bf16),
            pltpu.VMEM((3, LEN, D), bf16),
            pltpu.VMEM((2, 2, LEN, LEN), bf16),
            pltpu.VMEM((LEN, D), bf16),
            pltpu.VMEM((LEN, D), f32),
            pltpu.SemaphoreType.DMA((5,)),
            pltpu.SemaphoreType.DMA((2,)),
            pltpu.SemaphoreType.DMA((7,)),
        ]
        + Dispatch.sem_shapes(plan),
        compiler_params=pltpu.CompilerParams(
            collective_id=1, has_side_effects=True, vmem_limit_bytes=VMEM
        ),
        name="attend",
    )(
        grads,
        targets,
        tokens,
        w_query,
        w_key,
        w_value,
        w_out,
        lines.reshape(HEADS // 2, 2, 4 * NEAR),
        gains,
        w_router,
        routes,
    )


def expert_body(plan, halves, n_d, *refs):
    (
        sent,
        gates,
        grads,
        targets,
        w_gate,
        w_up,
        w_down,
        total_out,
        gg_out,
        rows_out,
        y_out,
        dgate_out,
        dup_out,
        act_out,
        meta_out,
        land,
        back,
        land_back,
        rows_v,
        meta_v,
        stage,
        wg_v,
        wu_v,
        wd_v,
        target_v,
        gate_v,
        x_v,
        g_v,
        dx_v,
        y_v,
        dgate_v,
        dup_v,
        act_v,
        gg_v,
        gg_back,
        gg_part,
        gg_land,
        column_v,
        dots_v,
        sum_v,
        total,
        slots_in,
        slots_v,
        w_sem,
        t_sem,
        x_sem,
        o_sem,
        gg_send,
        gg_recv,
        ggs_send,
        ggs_recv,
        y_sem,
        *sems,
    ) = refs
    n_e, n_h = plan.n_e, plan.n_h
    e, z = plan.place()
    loads = [
        pltpu.make_async_copy(source, held, w_sem.at[i])
        for i, (source, held) in enumerate(((w_gate, wg_v), (w_up, wu_v), (w_down, wd_v)))
    ]
    for load in loads:
        load.start()
    targets_in = pltpu.make_async_copy(targets, target_v, t_sem.at[0])
    targets_in.start()
    greet(plan)
    work = Dispatch(
        plan, sent, gates, land, rows_out, meta_out, rows_v, meta_v, stage, sems[:n_d]
    )
    give = ReturnMade(
        plan,
        dx_v,
        back,
        land_back,
        total_out,
        stage,
        rows_v,
        sum_v,
        total,
        slots_in,
        slots_v,
        sems[n_d:],
    )
    work.begin()
    targets_in.wait()
    ahead = min(3, n_h)

    @pl.loop(0, ahead)
    def _(chunk):
        work.chunk(chunk, lambda at: target_v[at, 0])
        pl.when(chunk > 0)(lambda: work.relay(chunk - 1))

    for load in loads:
        load.wait()

    def gg_copy(chunk, mask):
        return remote(
            gg_v.at[chunk, mask],
            gg_back.at[chunk, mask],
            gg_send.at[chunk, mask],
            gg_recv.at[chunk, mask],
            (across(e, mask), z),
        )

    def gg_along(chunk):
        return remote(
            gg_part.at[chunk],
            gg_land.at[z],
            ggs_send.at[chunk],
            ggs_recv.at[z],
            (e, plan.source(z, chunk)),
        )

    def gg_from(distance):
        other = lax.rem(z + distance, n_h)
        return other, remote(
            gg_part.at[0], gg_land.at[other], ggs_send.at[0], ggs_recv.at[other], (e, other)
        )

    def outs(chunk, j):
        at = pl.multiple_of(chunk * plan.rows, 16)
        return [
            pltpu.make_async_copy(held.at[j], out.at[j, pl.ds(at, plan.rows), :], o_sem.at[i, j])
            for i, (held, out) in enumerate(
                ((dgate_v, dgate_out), (dup_v, dup_out), (act_v, act_out))
            )
        ]

    all_held = n_h <= dx_v.shape[0]
    masks = n_e // halves
    piece = masks * plan.stride

    def own_slots(j):
        slots = lax.broadcasted_iota(jnp.int32, (plan.stride, LEN), 0).astype(jnp.float32)
        return slots + slot_base(plan, e, j)

    def weigh(chunk, mask):
        aim, weight = target_v[chunk, mask], gate_v[mask]
        at = pl.ds(pl.multiple_of(mask * plan.stride, 16), plan.stride)
        for j in range(2):
            hit = jnp.where(own_slots(j) == aim[0:1, :], weight[0:1, :], 0.0)
            hit = hit + jnp.where(own_slots(j) == aim[1:2, :], weight[1:2, :], 0.0)
            column_v[j, at, :] = jnp.broadcast_to(
                jnp.sum(hit, axis=1, keepdims=True), (plan.stride, 128)
            )

    def spread(chunk, mask):
        aim = target_v[chunk, mask]
        at = pl.ds(pl.multiple_of(mask * plan.stride, 16), plan.stride)
        for k in range(2):
            line = jnp.zeros((1, LEN), jnp.float32)
            for j in range(2):
                hit = own_slots(j) == aim[k : k + 1, :]
                line = line + jnp.sum(
                    jnp.where(hit, dots_v[chunk, j, at, 0:1], 0.0), axis=0, keepdims=True
                )
            gg_v[chunk, mask, k : k + 1, :] = line

    def y_copy(chunk):
        at = pl.ds(pl.multiple_of(chunk * plan.rows, 16), plan.rows)
        return pltpu.make_async_copy(y_v, y_out.at[:, at, :], y_sem.at[1])

    def make_y(chunk):
        at = pl.ds(pl.multiple_of(chunk * plan.rows, 16), plan.rows)
        kept = pltpu.make_async_copy(act_out.at[:, at, :], act_v, y_sem.at[0])
        kept.start()

        @pl.when(chunk > 0)
        def _():
            y_copy(chunk - 1).wait()

        kept.wait()

        @pl.loop(0, 2)
        def _(j):
            y_v[j] = dot(act_v[j], wd_v[j]).astype(jnp.bfloat16)

        y_copy(chunk).start()

    def step(chunk, index):
        j, half = lax.div(index, halves), lax.rem(index, halves)
        at = pl.ds(pl.multiple_of(half * piece, 16), piece)
        gate_pre = contract_last(x_v[j, at, :], wg_v[j])
        up_pre = contract_last(x_v[j, at, :], wu_v[j])
        raw = contract_last(g_v[j, at, :], wd_v[j])
        gate = column_v[j, at, 0:1]
        square = gate_pre * gate_pre
        tanh = jnp.tanh(gate_pre * (0.7978845608028654 + 0.035677408136300125 * square))
        side = 0.5 + 0.5 * tanh
        gelu = gate_pre * side
        slope = side + gelu * (1.0 - side) * (1.5957691216057308 + 0.21406444881780075 * square)
        act = gelu * up_pre
        dots_v[chunk, j, at, :] = jnp.broadcast_to(
            jnp.sum(act * raw, axis=1, keepdims=True), (piece, 128)
        )
        grad_act = gate * raw
        grad_gate = (grad_act * up_pre * slope).astype(jnp.bfloat16)
        grad_up = (grad_act * gelu).astype(jnp.bfloat16)
        dgate_v[j, at, :] = grad_gate
        dup_v[j, at, :] = grad_up
        act_v[j, at, :] = (act * gate).astype(jnp.bfloat16)
        dx_v[lax.rem(chunk, dx_v.shape[0]), j, at, :] = (
            dot(grad_gate, wg_v[j]) + dot(grad_up, wu_v[j])
        ).astype(jnp.bfloat16)

    split = n_e - n_e // 4

    def now(chunk):
        if plan.direct:
            return chunk > 1
        return (chunk < 1) | (not all_held)

    gg_v[...] = jnp.zeros_like(gg_v)

    @pl.loop(0, n_h)
    def _(chunk):
        at = pl.multiple_of(chunk * plan.rows, 16)
        ins = [
            pltpu.make_async_copy(source.at[:, pl.ds(at, plan.rows), :], held, x_sem.at[i])
            for i, (source, held) in enumerate(((rows_out, x_v), (grads, g_v)))
        ]
        ins[1].start()
        work.told(chunk)
        gate_in = pltpu.make_async_copy(meta_out.at[chunk], gate_v, t_sem.at[0])
        gate_in.start()
        gate_in.wait()
        pl.loop(0, n_e)(lambda mask: weigh(chunk, mask))
        give.free(chunk)

        @pl.when(chunk > 0)
        def _():
            for j in range(2):
                for copy in outs(chunk - 1, j):
                    copy.wait()

        work.arrived(chunk)
        ins[0].start()
        for copy in ins:
            copy.wait()
        pl.loop(0, 2 * halves)(lambda index: step(chunk, index))
        for j in range(2):
            for copy in outs(chunk, j):
                copy.start()

        @pl.when(chunk + ahead < n_h)
        def _():
            work.chunk(chunk + ahead, lambda at: target_v[at, 0])

        pl.when(chunk + ahead <= n_h)(lambda: work.relay(chunk + ahead - 1))
        pl.loop(0, n_e)(lambda mask: spread(chunk, mask))
        for mask in range(1, n_e):
            gg_copy(chunk, mask).start()

        if plan.relayed < n_e:
            pl.when(chunk > 0)(lambda: give.relay(chunk).start())

        @pl.when(now(chunk))
        def _():
            give.send(chunk)

        if plan.direct:
            pl.when(chunk == 0)(lambda: give.send(0, 0, split))


    if plan.direct:
        give.send(1)
        give.send(0, split, plan.relayed)
        give.relay_sum()
    elif all_held:
        pl.loop(1, n_h)(lambda turn: give.send(give.chunk_of(give.goal(turn))))
    for j in range(2):
        for copy in outs(n_h - 1, j):
            copy.wait()
    make_y(0)
    work.finish()

    @pl.loop(0, n_h)
    def _(turn):
        chunk = give.chunk_of(give.goal(turn))
        part = gg_v[chunk, 0]
        for mask in range(1, n_e):
            gg_copy(chunk, mask).wait_recv()
            part = part + gg_back[chunk, mask]
        gg_part[chunk] = part

        @pl.when(chunk > 0)
        def _():
            gg_along(chunk).start()

        give.combine(turn, lambda at: target_v[at, 0])
        pl.when(turn + 1 < n_h)(lambda: make_y(turn + 1))

    y_copy(n_h - 1).wait()
    give.sent()
    for chunk in range(n_h):
        for mask in range(1, n_e):
            gg_copy(chunk, mask).wait_send()
    sum_gg = gg_part[0]
    for distance in range(1, n_h):
        other, arrival = gg_from(distance)
        arrival.wait_recv()
        sum_gg = sum_gg + gg_land[other]
    gg_out[...] = sum_gg
    for chunk in range(1, n_h):
        gg_along(chunk).wait_send()
    give.finish()


def run_experts(plan, sent, gates, grads, targets, w_gate, w_up, w_down):
    n_h, n_e, width = plan.n_h, plan.n_e, plan.width
    bf16, f32 = jnp.bfloat16, jnp.float32
    shape = jax.ShapeDtypeStruct
    dma = pltpu.SemaphoreType.DMA
    ring = min(4, n_h)
    d_sems, r_sems = Dispatch.sem_shapes(plan), Return.sem_shapes(plan)
    halves = 2 if plan.rows <= 640 else 4
    return pl.pallas_call(
        functools.partial(expert_body, plan, halves, len(d_sems)),
        in_specs=[ANY] * 7,
        out_specs=[ANY, pl.BlockSpec(memory_space=pltpu.VMEM)] + [ANY] * 9,
        out_shape=[
            shape((LEN, D), f32),
            shape((8, LEN), f32),
            shape((2, plan.total, D), bf16),
            shape((2, plan.total, D), bf16),
            shape((2, plan.total, width), bf16),
            shape((2, plan.total, width), bf16),
            shape((2, plan.total, width), bf16),
            shape((n_h, n_e, 8, LEN), f32),
            shape((n_h, LEN, D), bf16),
            shape((n_h, 2, plan.rows, D), bf16),
            shape((3, n_h, LEN, D), bf16),
        ],
        scratch_shapes=[
            pltpu.VMEM((2, LEN, D), bf16),
            pltpu.VMEM((n_h, 8, LEN), f32),
            pltpu.VMEM((2, 2, plan.rows, D), bf16),
            pltpu.VMEM((2, width, D), bf16),
            pltpu.VMEM((2, width, D), bf16),
            pltpu.VMEM((2, width, D), bf16),
            pltpu.VMEM((n_h, n_e, 8, LEN), f32),
            pltpu.VMEM((n_e, 8, LEN), f32),
            pltpu.VMEM((2, plan.rows, D), bf16),
            pltpu.VMEM((2, plan.rows, D), bf16),
            pltpu.VMEM((ring, 2, plan.rows, D), bf16),
            pltpu.VMEM((2, plan.rows, D), bf16),
            pltpu.VMEM((2, plan.rows, width), bf16),
            pltpu.VMEM((2, plan.rows, width), bf16),
            pltpu.VMEM((2, plan.rows, width), bf16),
            pltpu.VMEM((n_h, n_e, 8, LEN), f32),
            pltpu.VMEM((n_h, n_e, 8, LEN), f32),
            pltpu.VMEM((n_h, 8, LEN), f32),
            pltpu.VMEM((n_h, 8, LEN), f32),
            pltpu.VMEM((2, plan.rows, 128), f32),
            pltpu.VMEM((n_h, 2, plan.rows, 128), f32),
            pltpu.VMEM((LEN, D), bf16),
            pltpu.VMEM((LEN, D), f32),
            *Return.slot_shapes(plan),
            dma((3,)),
            dma((1,)),
            dma((2,)),
            dma((3, 2)),
            dma((n_h, n_e)),
            dma((n_h, n_e)),
            dma((n_h,)),
            dma((n_h,)),
            dma((2,)),
        ]
        + d_sems
        + r_sems,
        compiler_params=pltpu.CompilerParams(
            collective_id=2, has_side_effects=True, vmem_limit_bytes=VMEM
        ),
        name="run_experts",
    )(sent, gates, grads, targets, jnp.swapaxes(w_gate, 1, 2), jnp.swapaxes(w_up, 1, 2), w_down)


class Sum:
    pieces, stages, few = 4, 5, 32

    def __init__(self, plan, held, whole, few_v, few_in, *rest):
        self.plan = plan
        self.held, self.whole, self.few_v, self.few_in = held, whole, few_v, few_in
        self.landed, (self.send, self.recv, self.f_send, self.f_recv) = rest[:5], rest[5:]

    @classmethod
    def scratch_shapes(cls):
        dma = pltpu.SemaphoreType.DMA
        bf16, f32 = jnp.bfloat16, jnp.float32
        rows = (D // 2, D // 4, D // 8, D // 16, D // 32)
        return (
            [
                pltpu.VMEM((cls.pieces, D, D), bf16),
                pltpu.VMEM((cls.pieces, D, D), bf16),
                pltpu.VMEM((cls.stages + 1, cls.few, D), f32),
                pltpu.VMEM((cls.stages, cls.few, D), f32),
            ]
            + [pltpu.VMEM((cls.pieces, count, D), bf16) for count in rows]
            + [
                dma((2 * cls.stages, cls.pieces, 2)),
                dma((2 * cls.stages, cls.pieces, 2)),
                dma((cls.stages,)),
                dma((cls.stages,)),
            ]
        )

    def partner(self, bit):
        e, z = self.plan.place()
        if bit < 3:
            return (across(e, 1 << bit), z)
        return (e, across(z, 1 << (bit - 3)))

    def parts(self, stage):
        e, z = self.plan.place()
        place = [lax.rem(lax.div(e, 1 << k), 2) for k in range(3)]
        place += [lax.rem(lax.div(z, 1 << k), 2) for k in range(2)]
        base, count = place[0] * (D // 2), D // 2
        if stage == 1:
            return [(self.partner(0), base, D // 2 - base, count)]
        out = []
        for part, order in enumerate(((1, 2, 3, 4), (2, 1, 3, 4))):
            at, count = base + part * (D // 4), D // 4
            for bit in order[: stage - 1]:
                count //= 2
                keep, give = at + place[bit] * count, at + (1 - place[bit]) * count
                at = keep
            out.append((self.partner(bit), keep, give, count))
        return out

    def copies(self, stage, piece):
        halving = stage <= self.stages
        out = []
        parts = self.parts(stage if halving else 2 * self.stages + 1 - stage)
        for part, (device, keep, give, count) in enumerate(parts):
            here = pl.ds(pl.multiple_of(give if halving else keep, 16), count)
            there = (
                self.landed[stage - 1].at[piece, part * count : (part + 1) * count, :]
                if halving
                else self.whole.at[piece, here, :]
            )
            out.append(
                remote(
                    (self.held if halving else self.whole).at[piece, here, :],
                    there,
                    self.send.at[stage - 1, piece, part],
                    self.recv.at[stage - 1, piece, part],
                    device,
                )
            )
        return out

    def few_copy(self, stage):
        return remote(
            self.few_v.at[stage - 1],
            self.few_in.at[stage - 1],
            self.f_send.at[stage - 1],
            self.f_recv.at[stage - 1],
            self.partner(stage - 1),
        )

    def add(self, stage, piece):
        for part, (_, keep, _, count) in enumerate(self.parts(stage)):
            tile = min(count, 64)

            @pl.loop(0, count // tile)
            def _(i):
                at = pl.ds(pl.multiple_of(keep + i * tile, 16), tile)
                come = pl.ds(pl.multiple_of(part * count + i * tile, 16), tile)
                total = self.held[piece, at, :].astype(jnp.float32) + self.landed[stage - 1][
                    piece, come, :
                ].astype(jnp.float32)
                into = self.whole if stage == self.stages else self.held
                into[piece, at, :] = total.astype(jnp.bfloat16)

    slots = pieces + 2 * stages

    def slot(self, slot, ready, done):
        for piece in range(self.pieces):
            stage = slot - piece + 1
            if stage == 1:
                ready(piece)
            if 2 <= stage <= 2 * self.stages + 1:
                for copy in self.copies(stage - 1, piece):
                    copy.wait_recv()
                if stage - 1 <= self.stages:
                    self.add(stage - 1, piece)
            if 1 <= stage <= 2 * self.stages:
                for copy in self.copies(stage, piece):
                    copy.start()
            if stage == 2 * self.stages + 1:
                done(piece)
        stage = slot + 1
        if 2 <= stage <= self.stages + 1:
            self.few_copy(stage - 1).wait_recv()
            self.few_v[stage - 1] = self.few_v[stage - 2] + self.few_in[stage - 2]
        if stage <= self.stages:
            self.few_copy(stage).start()

    def finish(self):
        for stage in range(1, 2 * self.stages + 1):
            for piece in range(self.pieces):
                for copy in self.copies(stage, piece):
                    copy.wait_send()
        for stage in range(1, self.stages + 1):
            self.few_copy(stage).wait_send()


def sum_body(plan, *refs):
    n_h = plan.n_h
    dgate, dup, act, rows, grads = refs[:5]
    refs = refs[5:]
    if plan.summed:
        low, few = refs[:2]
        refs = refs[2:]
    outs, refs = refs[:3], refs[3:]
    if plan.summed:
        sums_out, few_out = refs[:2]
        refs = refs[2:]
    left_v, right_v, made_v, p_sem, g_sem = refs[:5]
    steps = 3 * n_h

    def factors(q, act_on):
        buffer = lax.rem(q, 2)
        at = pl.ds(pl.multiple_of(lax.rem(q, n_h) * plan.rows, 16), plan.rows)

        def copies(lefts, rights):
            for i in range(2):
                for k, ((source, j), held) in enumerate(((lefts[i], left_v), (rights[i], right_v))):
                    act_on(
                        pltpu.make_async_copy(
                            source.at[j, at, :], held.at[buffer, i], p_sem.at[buffer, 2 * i + k]
                        )
                    )

        @pl.when(q < 2 * n_h)
        def _():
            j = lax.div(q, n_h)
            copies(((dgate, j), (dup, j)), ((rows, j), (rows, j)))

        @pl.when(q >= 2 * n_h)
        def _():
            copies(((act, 0), (act, 1)), ((grads, 0), (grads, 1)))

    def results(group, act_on):
        @pl.when(group < 2)
        def _():
            for i in range(2):
                act_on(pltpu.make_async_copy(made_v.at[i], outs[i].at[group], g_sem.at[i]))

        @pl.when(group == 2)
        def _():
            for i in range(2):
                act_on(pltpu.make_async_copy(made_v.at[i], outs[2].at[i], g_sem.at[i]))

    def product(q):
        buffer, turn, group = lax.rem(q, 2), lax.rem(q, n_h), lax.div(q, n_h)
        factors(q, lambda copy: copy.wait())

        @pl.when(q + 1 < steps)
        def _():
            factors(q + 1, lambda copy: copy.start())

        @pl.when((turn == 0) & (q > 0))
        def _():
            results(group - 1, lambda copy: copy.wait())

        @pl.when(turn == 0)
        def _():
            made_v[...] = jnp.zeros_like(made_v)

        for i in range(2):
            made_v[i] += contract_first(left_v[buffer, i], right_v[buffer, i])

        @pl.when(turn == n_h - 1)
        def _():
            results(group, lambda copy: copy.start())

    factors(0, lambda copy: copy.start())
    if plan.summed:
        load_sem, store_sem = refs[5:7]
        total = Sum(plan, *refs[7:])
        loads = [
            pltpu.make_async_copy(low.at[i], total.held.at[i], load_sem.at[i]) for i in range(4)
        ]
        stores = [
            pltpu.make_async_copy(total.whole.at[i], sums_out.at[i], store_sem.at[i])
            for i in range(4)
        ]
        for load in loads:
            load.start()
        total.few_v[0] = few[...]
        greet(plan)
        done = 0
        for slot in range(total.slots):
            total.slot(slot, lambda i: loads[i].wait(), lambda i: stores[i].start())
            if slot % 2 == 0 and done < steps:
                pl.loop(done, min(done + 2, steps))(product)
                done = min(done + 2, steps)
        few_out[...] = total.few_v[total.stages]
        total.finish()
        for store in stores:
            store.wait()
    else:
        pl.loop(0, steps)(product)
    results(2, lambda copy: copy.wait())


def sum_all(plan, dgate, dup, act, rows, grads, low, few):
    bf16, f32 = jnp.bfloat16, jnp.float32
    shape = jax.ShapeDtypeStruct
    vmem = pl.BlockSpec(memory_space=pltpu.VMEM)
    dma = pltpu.SemaphoreType.DMA
    args = [dgate, dup, act, rows, grads]
    in_specs, out_specs = [ANY] * 5, [ANY] * 3
    out_shape = [shape((2, plan.width, D), f32)] * 3
    scratch_shapes = [
        pltpu.VMEM((2, 2, plan.rows, plan.width), bf16),
        pltpu.VMEM((2, 2, plan.rows, D), bf16),
        pltpu.VMEM((2, plan.width, D), f32),
        dma((2, 4)),
        dma((2,)),
    ]
    params = {"vmem_limit_bytes": VMEM}
    if plan.summed:
        args += [low, few]
        in_specs += [ANY, vmem]
        out_specs += [ANY, vmem]
        out_shape += [shape((4, D, D), bf16), shape((Sum.few, D), f32)]
        scratch_shapes += [dma((4,)), dma((4,))] + Sum.scratch_shapes()
        params.update(collective_id=4, has_side_effects=True)
    out = pl.pallas_call(
        functools.partial(sum_body, plan),
        in_specs=in_specs,
        out_specs=out_specs,
        out_shape=out_shape,
        scratch_shapes=scratch_shapes,
        compiler_params=pltpu.CompilerParams(**params),
        name="sum_all",
    )(*args)
    if plan.summed:
        return out[:3], out[3], out[4]
    return out[:3], *lax.psum((low, few), ("expert", "hidden"))


def unattend_body(plan, n_r, *refs):
    (
        given,
        targets,
        grad_sent,
        hidden,
        grad_out,
        tokens,
        mixed,
        normed,
        query,
        key,
        value,
        soft,
        w_query,
        w_key,
        w_value,
        w_out,
        grad_gates,
        gates,
        routes,
        w_router,
        gains,
        roots,
        branch_out,
        back,
        land,
        low_out,
        tokens_out,
        few_out,
        lines_out,
        rows_v,
        stage,
        target_v,
        sum_v,
        total,
        slots_in,
        slots_v,
        grad_sent_v,
        hidden_v,
        grad_out_v,
        tokens_v,
        mixed_v,
        normed_v,
        heads_v,
        soft_v,
        weights_v,
        grad_hidden_v,
        branch_v,
        grad_heads_v,
        grads_v,
        low_v,
        wide_v,
        t_sem,
        in_sem,
        soft_sem,
        low_sem,
        out_sem,
        *sems,
    ) = refs
    f32, bf16 = jnp.float32, jnp.bfloat16
    ins = [
        (grad_sent, grad_sent_v),
        (hidden, hidden_v),
        (grad_out, grad_out_v),
        (mixed, mixed_v),
        (w_out, weights_v.at[3]),
        (query, heads_v.at[0]),
        (key, heads_v.at[1]),
        (value, heads_v.at[2]),
        (normed, normed_v),
        (w_query, weights_v.at[0]),
        (w_key, weights_v.at[1]),
        (w_value, weights_v.at[2]),
        (tokens, tokens_v),
    ]
    loads = [
        pltpu.make_async_copy(source, held, in_sem.at[i]) for i, (source, held) in enumerate(ins)
    ]
    targets_in = pltpu.make_async_copy(targets, target_v, t_sem.at[0])

    def soft_copy(pair):
        buffer = lax.rem(pair, 2)
        return pltpu.make_async_copy(
            soft.at[pl.ds(2 * pair, 2)], soft_v.at[buffer], soft_sem.at[buffer]
        )

    targets_in.start()
    for load in loads:
        load.start()
    soft_copy(0).start()
    greet(plan)
    give = ReturnHeld(
        plan, given, back, land, branch_out, stage, rows_v, sum_v, total, slots_in, slots_v, sems
    )
    turns = plan.n_h
    if plan.relayed < plan.n_e:
        pl.loop(1, turns)(lambda chunk: give.relay(chunk).start())
    pl.loop(0, turns)(lambda turn: give.send(give.chunk_of(give.goal(turn))))
    targets_in.wait()

    def combine(turn):
        give.combine(turn, lambda at: target_v[at, 0])

    tile = 64

    def low_copy(i):
        return pltpu.make_async_copy(low_v.at[i % 2], low_out.at[i], low_sem.at[i % 2])

    for load in loads[:3]:
        load.wait()
    few_out[...] = jnp.zeros_like(few_out)
    mean = gates[0:1, :] * grad_gates[0:1, :] + gates[1:2, :] * grad_gates[1:2, :]
    experts = w_router.shape[0]
    numbers = lax.broadcasted_iota(jnp.int32, (experts, LEN), 0).astype(f32)
    grad_logits = jnp.zeros((experts, LEN), f32)
    for k in range(2):
        chosen = gates[k : k + 1, :] * (grad_gates[k : k + 1, :] - mean)
        grad_logits = grad_logits + jnp.where(numbers == routes[k : k + 1, :], chosen, 0.0)
    wide_v[...] = contract_first(grad_logits, w_router[...], precise)

    @pl.loop(0, LEN // tile)
    def _(i):
        at = pl.ds(pl.multiple_of(i * tile, 16), tile)
        rows, root = hidden_v[at, :], roots[at, 128:129]
        grad = wide_v[at, :] + grad_sent_v[at, :]
        near = rows * root
        few_out[experts + 1 : experts + 2, :] += jnp.sum(grad * near, axis=0, keepdims=True)
        scaled = grad * gains[1:2, :]
        pull = jnp.mean(scaled * rows, axis=1, keepdims=True) * (root * root * root)
        grad = grad_out_v[at, :].astype(f32) + root * scaled - rows * pull
        grad_hidden_v[at, :] = grad
        branch_v[at, :] = grad.astype(bf16)
        grad_sent_v[at, :] = near * gains[1:2, :]

    few_out[0:experts, :] = dot_high(grad_logits, grad_sent_v[...])
    for load in loads[3:5]:
        load.wait()
    low_v[1] = contract_first(mixed_v[...], branch_v[...]).astype(bf16)
    low_copy(3).start()
    give.relay_sum()
    mixed_v[...] = contract_last(branch_v[...], weights_v[3]).astype(bf16)
    for load in loads[5:8]:
        load.wait()

    def unmix_pair(pair):
        lanes = pl.ds(pl.multiple_of(pair * 2 * HEAD_DIM, 2 * HEAD_DIM), 2 * HEAD_DIM)
        soft_copy(pair).wait()

        @pl.when(pair + 1 < HEADS // 2)
        def _():
            soft_copy(pair + 1).start()

        both = [heads_v[k, :, lanes] for k in range(3)] + [mixed_v[:, lanes]]
        found = []
        for head in range(2):
            at = slice(head * HEAD_DIM, (head + 1) * HEAD_DIM)
            found.append(
                unmix_head(
                    *[item[:, at] for item in both], soft_v.at[lax.rem(pair, 2)], grads_v, head
                )
            )
        for k in range(3):
            grad_heads_v[k, :, lanes] = jnp.concatenate([found[0][k], found[1][k]], axis=1)
        lines_out[pair] = jnp.concatenate([found[0][3], found[1][3]], axis=0)

    pairs = HEADS // 2
    first, second = turns // 4, turns // 2
    pl.loop(0, pairs // 2)(unmix_pair)
    pl.loop(0, first)(combine)
    pl.loop(pairs // 2, pairs)(unmix_pair)
    pl.loop(first, second)(combine)
    for load in loads[8:]:
        load.wait()
    for k in range(3):
        if k == 1:
            low_copy(3).wait()
        if k == 2:
            low_copy(0).wait()
        low_v[k % 2] = contract_first(normed_v[...], grad_heads_v[k]).astype(bf16)
        low_copy(k).start()
    wide_v[...] = (
        contract_last(grad_heads_v[0], weights_v[0])
        + contract_last(grad_heads_v[1], weights_v[1])
        + contract_last(grad_heads_v[2], weights_v[2])
    )

    @pl.loop(0, LEN // tile)
    def _(i):
        at = pl.ds(pl.multiple_of(i * tile, 16), tile)
        rows, root = tokens_v[at, :].astype(f32), roots[at, 0:1]
        grad = wide_v[at, :]
        few_out[experts : experts + 1, :] += jnp.sum(grad * rows * root, axis=0, keepdims=True)
        scaled = grad * gains[0:1, :]
        pull = jnp.mean(scaled * rows, axis=1, keepdims=True) * (root * root * root)
        grad_hidden_v[at, :] = grad_hidden_v[at, :] + root * scaled - rows * pull

    tokens_copy = pltpu.make_async_copy(grad_hidden_v, tokens_out, out_sem.at[0])
    tokens_copy.start()
    pl.loop(second, turns)(combine)
    give.sent()
    give.finish()
    for i in (1, 2):
        low_copy(i).wait()
    tokens_copy.wait()


def unattend(
    plan,
    given,
    targets,
    grad_sent,
    hidden,
    grad_out,
    tokens,
    mixed,
    normed,
    query,
    key,
    value,
    soft,
    w_query,
    w_key,
    w_value,
    w_out,
    grad_gates,
    gates,
    routes,
    w_router,
    gains,
    roots,
):
    n_h, n_e = plan.n_h, plan.n_e
    bf16, f32 = jnp.bfloat16, jnp.float32
    shape = jax.ShapeDtypeStruct
    vmem = pl.BlockSpec(memory_space=pltpu.VMEM)
    dma = pltpu.SemaphoreType.DMA
    sems = Return.sem_shapes(plan)
    few = -(-(w_router.shape[0] + 3) // Sum.few) * Sum.few
    rows, wide = pltpu.VMEM((LEN, D), bf16), pltpu.VMEM((LEN, D), f32)
    out = pl.pallas_call(
        functools.partial(unattend_body, plan, len(sems)),
        in_specs=[ANY] * 16 + [vmem] * 6,
        out_specs=[ANY] * 5 + [vmem] * 2,
        out_shape=[
            shape((LEN, D), f32),
            shape((n_h, 2, plan.rows, D), bf16),
            shape((3, n_h, LEN, D), bf16),
            shape((4, D, D), bf16),
            shape((LEN, D), f32),
            shape((few, D), f32),
            shape((HEADS // 2, 2, 4 * NEAR), f32),
        ],
        scratch_shapes=[
            pltpu.VMEM((2, LEN, D), bf16),
            pltpu.VMEM((2, 2, plan.rows, D), bf16),
            pltpu.VMEM((n_h, n_e, 8, LEN), f32),
            rows,
            wide,
            *Return.slot_shapes(plan),
            wide,
            wide,
            rows,
            rows,
            rows,
            rows,
            pltpu.VMEM((3, LEN, D), bf16),
            pltpu.VMEM((2, 2, LEN, LEN), bf16),
            pltpu.VMEM((4, D, D), bf16),
            wide,
            rows,
            pltpu.VMEM((3, LEN, D), bf16),
            pltpu.VMEM((LEN, LEN), bf16),
            pltpu.VMEM((2, D, D), bf16),
            wide,
            dma((1,)),
            dma((13,)),
            dma((2,)),
            dma((2,)),
            dma((1,)),
        ]
        + sems,
        compiler_params=pltpu.CompilerParams(
            collective_id=3, has_side_effects=True, vmem_limit_bytes=VMEM
        ),
        name="unattend",
    )(
        given,
        targets,
        grad_sent,
        hidden,
        grad_out,
        tokens,
        mixed,
        normed,
        query,
        key,
        value,
        soft,
        w_query,
        w_key,
        w_value,
        w_out,
        grad_gates,
        gates,
        routes,
        w_router,
        gains,
        roots,
    )
    return out[0], out[3], out[4], out[5], out[6].reshape(HEADS, 4 * NEAR)


def per_device(
    n_e,
    n_h,
    tokens,
    gain_one,
    w_query,
    w_key,
    w_value,
    w_out,
    bias_table,
    gain_two,
    w_router,
    w_gate,
    w_up,
    w_down,
    routes,
    cotangent,
):
    experts_all = w_router.shape[1]
    plan = Plan(n_e, n_h, experts_all, w_gate.shape[2])
    both = ("expert", "hidden")

    def small(array):
        return jnp.pad(array.astype(jnp.float32), ((0, 8 - array.shape[0]), (0, 0)))

    targets = small(slot_targets(routes, experts_all, plan.capacity, plan.stride))
    gains, route_rows = small(jnp.stack([gain_one, gain_two])), small(routes.T)
    hot_bucket = offset_buckets()
    lines = jnp.dot(hot_bucket, bias_table, precision=precise).T
    (
        grads_in,
        targets_all,
        _,
        soft,
        mixed_rows,
        normed_one,
        query_rows,
        key_rows,
        value_rows,
        hidden,
        sent,
        gates,
        roots,
    ) = attend(
        plan,
        cotangent,
        targets,
        tokens,
        w_query,
        w_key,
        w_value,
        w_out,
        lines,
        gains,
        w_router.T,
        route_rows,
    )
    made = run_experts(
        plan, sent, gates, grads_in, targets_all, w_gate, w_up, w_down
    )
    grad_sent, grad_gates, rows_in, y_rows, gate_rows, up_rows, act_rows = made[:7]
    branch, low, tokens_grad, few, grad_lines = unattend(
        plan,
        y_rows,
        targets_all,
        grad_sent,
        hidden,
        cotangent,
        tokens,
        mixed_rows,
        normed_one,
        query_rows,
        key_rows,
        value_rows,
        soft,
        w_query,
        w_key,
        w_value,
        w_out,
        grad_gates,
        gates,
        route_rows,
        w_router.T,
        gains,
        roots,
    )
    block_out = (hidden + branch).astype(jnp.bfloat16)
    bias_table_grad = jnp.dot(grad_lines, hot_bucket, precision=precise).T
    last = jnp.pad(bias_table_grad.reshape(1, BUCKETS * HEADS), ((0, 0), (0, D - BUCKETS * HEADS)))
    few = lax.dynamic_update_slice(few, last, (experts_all + 2, 0))
    weight_grads, summed, few = sum_all(
        plan, gate_rows, up_rows, act_rows, rows_in, grads_in, low, few
    )
    summed = [summed[i].astype(jnp.float32) for i in range(4)]
    return (
        block_out,
        tokens_grad,
        few[experts_all],
        *summed,
        few[experts_all + 2, : BUCKETS * HEADS].reshape(BUCKETS, HEADS),
        few[experts_all + 1],
        few[:experts_all].T,
        jnp.swapaxes(weight_grads[0], 1, 2),
        jnp.swapaxes(weight_grads[1], 1, 2),
        weight_grads[2],
    )


def solution(mesh):
    in_specs = (
        P(("expert", "hidden"), None),
        P(),
        P(),
        P(),
        P(),
        P(),
        P(),
        P(),
        P(),
        P("expert", None, "hidden"),
        P("expert", None, "hidden"),
        P("expert", "hidden", None),
        P(("expert", "hidden"), None),
        P(("expert", "hidden"), None),
    )
    out_specs = (
        P(("expert", "hidden"), None),
        P(("expert", "hidden"), None),
        P(),
        P(),
        P(),
        P(),
        P(),
        P(),
        P(),
        P(),
        P("expert", None, "hidden"),
        P("expert", None, "hidden"),
        P("expert", "hidden", None),
    )
    return jax.shard_map(
        functools.partial(per_device, mesh.shape["expert"], mesh.shape["hidden"]),
        mesh=mesh, in_specs=in_specs, out_specs=out_specs, check_vma=False
    )
```

```python
import functools

import jax
import jax.numpy as jnp
from jax import lax
from jax.experimental import pallas as pl
from jax.experimental.pallas import tpu as pltpu
from jax.sharding import PartitionSpec as P

D = 1024
HEADS = 16
HEAD_DIM = 64
BUCKETS = 32
LEN = 512
MICRO = 2
MB_TOK = 256
VMEM = 62 * 1024 * 1024
MESH = pl.DeviceIdType.MESH


eps = 1e-06
precise = lax.Precision.HIGHEST
thresholds = (12, 16, 23, 32, 46, 64, 91)


def contract_last(matrix_a, matrix_b, mode=None):
    return lax.dot_general(
        matrix_a,
        matrix_b,
        (((1,), (1,)), ((), ())),
        precision=mode,
        preferred_element_type=jnp.float32,
    )


def contract_first(matrix_a, matrix_b, mode=None):
    return lax.dot_general(
        matrix_a,
        matrix_b,
        (((0,), (0,)), ((), ())),
        precision=mode,
        preferred_element_type=jnp.float32,
    )


def dot(matrix_a, matrix_b):
    return jnp.dot(matrix_a, matrix_b, preferred_element_type=jnp.float32)


def slot_targets(routes, experts_all, capacity, stride):
    pairs = 2 * MB_TOK
    flat = routes.reshape(-1, pairs)
    hits = (flat[:, :, None] == jnp.arange(experts_all, dtype=jnp.int32)).astype(jnp.bfloat16)
    lower = (
        jnp.arange(pairs, dtype=jnp.int32)[:, None] > jnp.arange(pairs, dtype=jnp.int32)[None, :]
    ).astype(jnp.bfloat16)
    earlier = jnp.einsum("pq,bqe->bpe", lower, hits, preferred_element_type=jnp.float32)
    rank = jnp.sum(earlier * hits.astype(jnp.float32), axis=-1).astype(jnp.int32)
    block = jnp.arange(flat.shape[0], dtype=jnp.int32)[:, None]
    target = flat * stride + block * capacity + rank
    return target.reshape(-1, 2).T


NEAR = 128


def offset_buckets():
    offset = jnp.arange(4 * NEAR, dtype=jnp.int32) - 2 * NEAR
    distance = jnp.abs(offset)
    far_bucket = 8 + sum(((distance >= threshold).astype(jnp.int32) for threshold in thresholds))
    bucket = jnp.where(distance < 8, distance, far_bucket) + 16 * (offset > 0).astype(jnp.int32)
    return (bucket[:, None] == jnp.arange(BUCKETS, dtype=jnp.int32)).astype(jnp.float32)


def bias_tiles(line):
    return pltpu.roll(
        jnp.broadcast_to(line, (NEAR, 4 * NEAR)), 0, 1, stride=1, stride_axis=0
    )


def mix_head(query, key, value, line, soft_ref, head):
    tiles = bias_tiles(line)
    blocks = LEN // NEAR
    outs = []
    for i in range(blocks):
        raw = contract_last(query[i * NEAR : (i + 1) * NEAR], key) * (HEAD_DIM**-0.5)
        parts = []
        for j in range(blocks):
            part = raw[:, j * NEAR : (j + 1) * NEAR]
            if abs(j - i) <= 1:
                parts.append(part + tiles[:, (j - i + 2) * NEAR : (j - i + 3) * NEAR])
            else:
                edge = 1 if j < i else 4 * NEAR - 1
                parts.append(part + line[:, edge : edge + 1])
        scores = jnp.concatenate(parts, axis=1)
        terms = jnp.exp(scores - jnp.max(scores, axis=1, keepdims=True))
        soft = (terms * (1.0 / jnp.sum(terms, axis=1, keepdims=True))).astype(jnp.bfloat16)
        soft_ref[head, i * NEAR : (i + 1) * NEAR, :] = soft
        outs.append(dot(soft, value))
    return jnp.concatenate(outs, axis=0).astype(jnp.bfloat16)


def unmix_head(query, key, value, grad_mixed, soft_ref, grads_v, head):
    blocks = LEN // NEAR
    near = [jnp.zeros((NEAR, NEAR), jnp.float32) for _ in range(3)]
    below = jnp.zeros((NEAR, NEAR), jnp.float32)
    above = jnp.zeros((NEAR, NEAR), jnp.float32)
    grad_query = []
    for i in range(blocks):
        at = slice(i * NEAR, (i + 1) * NEAR)
        soft = soft_ref[head, at, :].astype(jnp.float32)
        grad_soft = contract_last(grad_mixed[at], value)
        product = soft * grad_soft
        grad = product - soft * jnp.sum(product, axis=1, keepdims=True)
        low = grad.astype(jnp.bfloat16)
        grads_v[at, :] = low
        grad_query.append(dot(low, key))
        wide = low.astype(jnp.float32)
        for j in range(blocks):
            part = wide[:, j * NEAR : (j + 1) * NEAR]
            if abs(j - i) <= 1:
                near[j - i + 1] = near[j - i + 1] + part
            elif j < i:
                below = below + part
            else:
                above = above + part
    band = jnp.concatenate([jnp.zeros((NEAR, NEAR), jnp.float32)] + near, axis=1)
    eight = band[0:8]
    for i in range(8, NEAR, 8):
        eight = eight + pltpu.roll(band[i : i + 8], 4 * NEAR - i, 1)
    row = lax.broadcasted_iota(jnp.int32, (8, 4 * NEAR), 0)
    for bit in (1, 2, 4):
        eight = jnp.where(lax.rem(lax.div(row, bit), 2) == 1, pltpu.roll(eight, 4 * NEAR - bit, 1), eight)
    line = jnp.sum(eight, axis=0, keepdims=True)
    column = lax.broadcasted_iota(jnp.int32, (1, 4 * NEAR), 1)
    line = line + jnp.where(column == 1, jnp.sum(below), 0.0)
    line = line + jnp.where(column == 4 * NEAR - 1, jnp.sum(above), 0.0)
    scaling = HEAD_DIM**-0.5
    grad_query = (jnp.concatenate(grad_query, axis=0) * scaling).astype(jnp.bfloat16)
    grad_key = (contract_first(grads_v[...], query) * scaling).astype(jnp.bfloat16)
    grad_value = contract_first(soft_ref[head], grad_mixed).astype(jnp.bfloat16)
    return grad_query, grad_key, grad_value, line


class Plan:
    def __init__(self, n_e, n_h, experts_all, width):
        self.n_e, self.n_h, self.width = n_e, n_h, width
        self.capacity = 10 * MB_TOK // (4 * experts_all)
        self.stride = -(-MICRO * self.capacity // 16) * 16
        self.span = 2 * self.stride
        self.rows = n_e * self.stride
        self.total = n_h * self.rows
        self.relayed = n_e - 1 if (n_e, n_h) == (8, 4) else n_e
        self.summed = (n_e, n_h) == (8, 4)
        self.direct = n_h == 4

    def place(self):
        return lax.axis_index("expert"), lax.axis_index("hidden")

    def chunk(self, z, source):
        sign = 1 - 2 * lax.div(z, self.n_h // 2)
        return lax.rem(sign * (source - z) + self.n_h, self.n_h)

    def source(self, z, chunk):
        sign = 1 - 2 * lax.div(z, self.n_h // 2)
        return lax.rem(z + self.n_h + sign * chunk, self.n_h)


def across(here, mask):
    there, bit = here, 1
    while bit <= mask:
        if mask & bit:
            there = there + bit * (1 - 2 * lax.rem(lax.div(here, bit), 2))
        bit *= 2
    return there


def remote(src, dst, send_sem, recv_sem, device):
    return pltpu.make_async_remote_copy(
        src_ref=src,
        dst_ref=dst,
        send_sem=send_sem,
        recv_sem=recv_sem,
        device_id=device,
        device_id_type=MESH,
    )


def greet(plan):
    e, z = plan.place()
    barrier = pltpu.get_barrier_semaphore()
    for mask in range(1, plan.n_e):
        pl.semaphore_signal(barrier, inc=1, device_id=(across(e, mask), z), device_id_type=MESH)
    for shift in range(1, plan.n_h):
        pl.semaphore_signal(
            barrier, inc=1, device_id=(e, lax.rem(z + shift, plan.n_h)), device_id_type=MESH
        )
    pl.semaphore_wait(barrier, plan.n_e + plan.n_h - 2)


def slot_hits(plan, base, target):
    slots = lax.broadcasted_iota(jnp.int32, (plan.stride, LEN), 0).astype(jnp.float32) + base
    return jnp.where((slots == target[0:1, :]) | (slots == target[1:2, :]), 1.0, 0.0).astype(
        jnp.bfloat16
    )


def slot_base(plan, device, j):
    return (device * plan.span + j * plan.stride).astype(jnp.float32)


class Dispatch:
    def __init__(self, plan, rows, meta, land, out, meta_out, rows_v, meta_v, stage, sems):
        self.plan = plan
        self.rows, self.meta, self.land = rows, meta, land
        self.out, self.meta_out = out, meta_out
        self.rows_v, self.meta_v, self.stage = rows_v, meta_v, stage
        (
            self.z_send,
            self.z_recv,
            self.zm_send,
            self.zm_recv,
            self.a_send,
            self.a_recv,
            self.m_send,
            self.m_recv,
            self.r_send,
            self.r_recv,
            self.local,
        ) = sems

    @staticmethod
    def sem_shapes(plan):
        dma = pltpu.SemaphoreType.DMA
        n_h, n_e = plan.n_h, plan.n_e
        return [
            dma((n_h, 2)),
            dma((n_h,)),
            dma((n_h, 2)),
            dma((n_h,)),
            dma((2, n_e)),
            dma((n_h, n_e)),
            dma((n_h, n_e)),
            dma((n_h, n_e)),
            dma((n_h, 2)),
            dma((n_h,)),
            dma((3,)),
        ]

    def hop(self, source, way, own):
        e, z = self.plan.place()
        sems = [
            (self.z_send.at[source, (way + 1) // 2], self.z_recv.at[source]),
            (self.zm_send.at[source, (way + 1) // 2], self.zm_recv.at[source]),
        ]
        return (
            remote(self.meta_v.at[source], self.meta_v.at[source], *sems[1], (e, z + way)),
            remote(
                self.rows if own else self.land.at[source],
                self.land.at[source],
                *sems[0],
                (e, z + way),
            ),
        )

    def on_the_way(self, distance, act):
        n_h = self.plan.n_h
        _, z = self.plan.place()

        @pl.when(z + distance < n_h)
        def _():
            act(z + distance, z > 0, -1)

        @pl.when(z >= distance)
        def _():
            act(z - distance, z < n_h - 1, 1)

    def begin(self):
        _, z = self.plan.place()
        copy = pltpu.make_async_copy(self.meta, self.meta_v.at[z], self.local.at[1])
        copy.start()
        copy.wait()

        @pl.when(z > 0)
        def _():
            for copy in self.hop(z, -1, True):
                copy.start()

        @pl.when(z < self.plan.n_h - 1)
        def _():
            for copy in self.hop(z, 1, True):
                copy.start()

    def pass_on(self, distance):
        def act(source, forwarded, way):
            for copy in self.hop(source, way, False):
                copy.wait_recv()

            @pl.when(forwarded)
            def _():
                for copy in self.hop(source, way, False):
                    copy.start()

        self.on_the_way(distance, act)

    def in_plane(self, chunk, mask):
        plan = self.plan
        e, z = plan.place()
        buffer = lax.rem(chunk, 2)
        at = pl.multiple_of((chunk * plan.n_e + mask) * plan.stride, 16)
        return remote(
            self.stage.at[buffer, :, pl.ds(mask * plan.stride, plan.stride), :],
            self.out.at[:, pl.ds(at, plan.stride), :],
            self.a_send.at[buffer, mask],
            self.a_recv.at[chunk, mask],
            (across(e, mask), z),
        )

    def meta_copy(self, chunk, mask):
        e, z = self.plan.place()
        return remote(
            self.meta_v.at[self.plan.source(z, chunk)],
            self.meta_out.at[chunk, mask],
            self.m_send.at[chunk, mask],
            self.m_recv.at[chunk, mask],
            (across(e, mask), z),
        )

    def relay_copy(self, source, way):
        plan = self.plan
        e, z = plan.place()

        def at(place):
            chunk = plan.chunk(place, source)
            return pl.ds(
                pl.multiple_of((chunk * plan.n_e + plan.relayed) * plan.stride, 16), plan.stride
            )

        return remote(
            self.out.at[:, at(z), :],
            self.out.at[:, at(z + way), :],
            self.r_send.at[source, (way + 1) // 2],
            self.r_recv.at[source],
            (e, z + way),
        )

    def relay(self, distance):
        plan = self.plan
        if plan.relayed == plan.n_e:
            return
        _, z = plan.place()

        @pl.when(distance == 0)
        def _():
            self.in_plane(0, plan.relayed).wait_recv()

            @pl.when(z > 0)
            def _():
                self.relay_copy(z, -1).start()

            @pl.when(z < plan.n_h - 1)
            def _():
                self.relay_copy(z, 1).start()

        def act(source, forwarded, way):
            chunk = plan.chunk(z, source)
            at = pl.ds(
                pl.multiple_of((chunk * plan.n_e + plan.relayed) * plan.stride, 16), plan.stride
            )
            e, _ = plan.place()
            remote(
                self.out.at[:, at, :],
                self.out.at[:, at, :],
                self.r_send.at[source, 0],
                self.r_recv.at[source],
                (e, z - way),
            ).wait_recv()

            @pl.when(forwarded)
            def _():
                self.relay_copy(source, way).start()

        @pl.when(distance > 0)
        def _():
            self.on_the_way(distance, act)

    def chunk(self, chunk, target_of):
        plan = self.plan
        e, z = plan.place()
        buffer = lax.rem(chunk, 2)
        source = plan.source(z, chunk)

        @pl.when(chunk == 0)
        def _():
            copy = pltpu.make_async_copy(self.rows, self.rows_v.at[buffer], self.local.at[0])
            copy.start()
            copy.wait()

        @pl.when(chunk > 0)
        def _():
            self.pass_on(chunk)
            copy = pltpu.make_async_copy(
                self.land.at[source], self.rows_v.at[buffer], self.local.at[0]
            )
            copy.start()
            copy.wait()

        for mask in range(1, plan.n_e):
            self.meta_copy(chunk, mask).start()
        own_meta = pltpu.make_async_copy(
            self.meta_v.at[source], self.meta_out.at[chunk, 0], self.local.at[1]
        )
        own_meta.start()

        @pl.when(chunk >= 2)
        def _():
            self.wait_sent(chunk - 2)

        target = target_of(chunk)
        group = min(4, plan.n_e)
        for start in range(plan.n_e - group, -1, -group):
            for j in range(2):
                hot = jnp.concatenate(
                    [
                        slot_hits(plan, slot_base(plan, across(e, start + i), j), target)
                        for i in range(group)
                    ],
                    axis=0,
                )
                picked = dot(hot, self.rows_v[buffer]).astype(jnp.bfloat16)
                self.stage[
                    buffer, j, start * plan.stride : (start + group) * plan.stride, :
                ] = picked
            if start <= plan.relayed < start + group:

                @pl.when(chunk == 0)
                def _():
                    self.in_plane(chunk, plan.relayed).start()

            for mask in range(max(start, 1), min(start + group, plan.relayed)):
                self.in_plane(chunk, mask).start()
        at = pl.multiple_of(chunk * plan.rows, 16)
        own = pltpu.make_async_copy(
            self.stage.at[buffer, :, pl.ds(0, plan.stride), :],
            self.out.at[:, pl.ds(at, plan.stride), :],
            self.local.at[2],
        )
        own.start()
        own.wait()
        own_meta.wait()

    def wait_sent(self, chunk):
        for mask in range(1, self.plan.relayed):
            self.in_plane(chunk, mask).wait_send()
        if self.plan.relayed < self.plan.n_e:

            @pl.when(chunk == 0)
            def _():
                self.in_plane(chunk, self.plan.relayed).wait_send()

    def told(self, chunk):
        for mask in range(1, self.plan.n_e):
            self.meta_copy(chunk, mask).wait_recv()

    def arrived(self, chunk):
        for mask in range(1, self.plan.relayed):
            self.in_plane(chunk, mask).wait_recv()

    def finish(self):
        plan = self.plan
        for chunk in range(max(0, plan.n_h - 2), plan.n_h):
            self.wait_sent(chunk)
        _, z = plan.place()

        @pl.when(z > 0)
        def _():
            for copy in self.hop(z, -1, True):
                copy.wait_send()

        @pl.when(z < plan.n_h - 1)
        def _():
            for copy in self.hop(z, 1, True):
                copy.wait_send()

        def act(source, forwarded, way):
            @pl.when(forwarded)
            def _():
                for copy in self.hop(source, way, False):
                    copy.wait_send()

        for distance in range(1, plan.n_h):
            self.on_the_way(distance, act)
        for chunk in range(plan.n_h):
            for mask in range(1, plan.n_e):
                self.meta_copy(chunk, mask).wait_send()
        if plan.relayed < plan.n_e:

            @pl.when(z > 0)
            def _():
                self.relay_copy(z, -1).wait_send()

            @pl.when(z < plan.n_h - 1)
            def _():
                self.relay_copy(z, 1).wait_send()

            def passed(source, forwarded, way):
                @pl.when(forwarded)
                def _():
                    self.relay_copy(source, way).wait_send()

            for distance in range(1, plan.n_h):
                self.on_the_way(distance, passed)


def same(index, other, count):
    return 1 - lax.div(lax.rem(index - other + count, count) + count - 1, count)


class Return:
    own_first = True

    def __init__(self, plan, back, land, out, stage, rows_v, sum_v, total, slots_in, slots_v, sems):
        self.plan = plan
        self.back, self.land, self.out = back, land, out
        self.stage, self.rows_v, self.sum_v, self.total = stage, rows_v, sum_v, total
        self.slots_in, self.slots_v = slots_in, slots_v
        (
            self.b_send,
            self.b_recv,
            self.s_send,
            self.s_recv,
            self.local,
            self.own,
            self.r_send,
            self.r_recv,
        ) = sems

    @staticmethod
    def sem_shapes(plan):
        dma = pltpu.SemaphoreType.DMA
        n_h, n_e = plan.n_h, plan.n_e
        return [
            dma((n_h, n_e)),
            dma((n_h, n_e)),
            dma((n_h, 2)),
            dma((3, n_h, 2)),
            dma((2,)),
            dma((n_h,)),
            dma((n_h,)),
            dma((n_h,)),
        ]

    @staticmethod
    def slot_shapes(plan):
        return [
            pltpu.VMEM((plan.n_h, 2, plan.stride, D), jnp.bfloat16),
            pltpu.VMEM((2, plan.stride, D), jnp.bfloat16),
        ]

    def goal(self, turn):
        n_h = self.plan.n_h
        _, z = self.plan.place()
        found = 0
        for here in range(n_h):
            if self.plan.direct:
                order = ((2, 3, 1, 0), (3, 0, 2, 1), (0, 3, 1, 2), (1, 0, 2, 3))[here]
                for when, there in enumerate(order):
                    found = found + there * same(z, here, n_h) * same(turn, when, n_h)
                continue
            others = [there for there in range(n_h) if there != here]
            others.sort(key=lambda d: n_h - 1 - d + here if d > here else d + n_h - 1 - here)
            order = [here] + others if self.own_first else others + [here]
            for when, there in enumerate(order):
                found = found + there * same(z, here, n_h) * same(turn, when, n_h)
        return found

    def chunk_of(self, goal):
        _, z = self.plan.place()
        return self.plan.chunk(z, goal)

    def source(self, chunk, mask):
        raise NotImplementedError

    def in_plane(self, chunk, mask):
        plan = self.plan
        e, z = plan.place()
        return remote(
            self.source(chunk, mask),
            self.back.at[chunk, :, pl.ds(mask * plan.stride, plan.stride), :],
            self.b_send.at[chunk, mask],
            self.b_recv.at[chunk, mask],
            (across(e, mask), z),
        )

    def own_copy(self, chunk):
        plan = self.plan
        return pltpu.make_async_copy(
            self.source(chunk, 0),
            self.back.at[chunk, :, pl.ds(0, plan.stride), :],
            self.own.at[chunk],
        )

    def send(self, chunk, first=0, end=None):
        for mask in range(first, self.plan.relayed if end is None else end):
            if mask == 0:
                self.own_copy(chunk).start()
            else:
                self.in_plane(chunk, mask).start()

    def relay(self, chunk):
        plan = self.plan
        e, z = plan.place()
        return remote(
            self.source(chunk, plan.relayed),
            self.slots_in.at[z],
            self.r_send.at[chunk],
            self.r_recv.at[z],
            (e, plan.source(z, chunk)),
        )

    def relay_sum(self):
        plan = self.plan
        if plan.relayed == plan.n_e:
            return
        e, z = plan.place()
        copy = pltpu.make_async_copy(
            self.source(0, plan.relayed), self.slots_v, self.local.at[0]
        )
        copy.start()
        copy.wait()
        for j in range(2):
            total = self.slots_v[j].astype(jnp.float32)
            for distance in range(1, plan.n_h):
                other = lax.rem(z + distance, plan.n_h)
                if j == 0:
                    remote(
                        self.slots_v,
                        self.slots_in.at[other],
                        self.r_send.at[0],
                        self.r_recv.at[other],
                        (e, other),
                    ).wait_recv()
                total = total + self.slots_in[other, j].astype(jnp.float32)
            self.slots_v[j] = total.astype(jnp.bfloat16)
        self.relayed_copy().start()

    def relayed_copy(self):
        plan = self.plan
        e, z = plan.place()
        return remote(
            self.slots_v,
            self.back.at[0, :, pl.ds(plan.relayed * plan.stride, plan.stride), :],
            self.b_send.at[0, plan.relayed],
            self.b_recv.at[0, plan.relayed],
            (across(e, plan.relayed), z),
        )

    def wait_sent(self, chunk):
        plan = self.plan
        for mask in range(1, plan.relayed):
            self.in_plane(chunk, mask).wait_send()
        if plan.relayed < plan.n_e:
            if chunk == 0:
                self.relayed_copy().wait_send()
            else:
                self.relay(chunk).wait_send()

    def hop(self, turn, goal, way, half, far=False):
        e, z = self.plan.place()
        side = 2 if far else (1 - way) // 2
        return remote(
            self.rows_v.at[lax.rem(turn, 2), half, :],
            self.land.at[side, goal, half, :],
            self.s_send.at[turn, half.start // half.size],
            self.s_recv.at[side, goal, half.start // half.size],
            (e, goal if far else z + way),
        )

    def each_hop(self, turn, goal, way, half, act):
        last = self.plan.n_h - 1
        _, z = self.plan.place()
        if not self.plan.direct:
            act(self.hop(turn, goal, way, half))
            return
        far = (z == 0) & (goal == last) if way > 0 else (z == last) & (goal == 0)

        @pl.when(far)
        def _():
            act(self.hop(turn, goal, way, half, True))

        @pl.when(jnp.logical_not(far))
        def _():
            act(self.hop(turn, goal, way, half))

    def each_way(self, goal, act):
        _, z = self.plan.place()
        last = self.plan.n_h - 1
        below, above = z > 0, z < last
        if self.plan.direct:
            below = below & ((z > 1) | (goal < last))
            above = above & ((z < last - 1) | (goal > 0))

        @pl.when(goal > z)
        def _():
            act(1, below)

        @pl.when(goal < z)
        def _():
            act(-1, above)

    halves = (pl.ds(0, LEN // 2), pl.ds(LEN // 2, LEN // 2))

    def take(self, goal, way, half, far=False):
        side = 2 if far else (1 - way) // 2
        e, z = self.plan.place()
        remote(
            self.rows_v.at[0, half, :],
            self.land.at[side, goal, half, :],
            self.s_send.at[0, half.start // half.size],
            self.s_recv.at[side, goal, half.start // half.size],
            (e, self.plan.n_h - 1 - z if far else z - way),
        ).wait_recv()
        copy = pltpu.make_async_copy(
            self.land.at[side, goal, half, :], self.sum_v.at[half, :], self.local.at[1]
        )
        copy.start()
        copy.wait()
        return self.sum_v[half, :].astype(jnp.float32)

    def wait_hop(self, turn):
        goal = self.goal(turn)

        def act(way, _):
            for half in self.halves:
                self.each_hop(turn, goal, way, half, lambda copy: copy.wait_send())

        self.each_way(goal, act)

    def fetched(self, chunk, buffer):
        at = pl.ds(0, self.plan.relayed * self.plan.stride)
        return pltpu.make_async_copy(
            self.back.at[chunk, :, at, :], self.stage.at[buffer, :, at, :], self.local.at[0]
        )

    def fetch(self, goal, chunk, buffer):
        plan = self.plan
        for mask in range(1, plan.relayed):
            self.in_plane(chunk, mask).wait_recv()
        self.own_copy(chunk).wait()
        if plan.relayed < plan.n_e:

            @pl.when(chunk == 0)
            def _():
                self.relayed_copy().wait_recv()
                at = pl.ds(plan.relayed * plan.stride, plan.stride)
                copy = pltpu.make_async_copy(
                    self.back.at[0, :, at, :], self.stage.at[buffer, :, at, :], self.local.at[1]
                )
                copy.start()
                copy.wait()

        self.fetched(chunk, buffer).start()

    def combine(self, turn, target_of):
        plan = self.plan
        e, z = plan.place()
        goal = self.goal(turn)
        chunk = self.chunk_of(goal)
        target = target_of(chunk)
        buffer = lax.rem(turn, 2)
        self.fetch(goal, chunk, buffer)
        hot = [
            jnp.concatenate(
                [
                    slot_hits(plan, slot_base(plan, across(e, mask), j), target)
                    for mask in range(plan.relayed)
                ],
                axis=0,
            )
            for j in range(2)
        ]
        self.fetched(chunk, buffer).wait()

        @pl.when(turn >= 2)
        def _():
            self.wait_hop(turn - 2)

        count = plan.relayed * plan.stride
        part = contract_first(hot[0], self.stage[buffer, 0, :count, :]) + contract_first(
            hot[1], self.stage[buffer, 1, :count, :]
        )

        @pl.when(goal == z)
        def _():
            self.total[...] = part
            if plan.relayed < plan.n_e:
                for j in range(2):
                    base = slot_base(plan, across(e, plan.relayed), j)
                    self.total[...] += contract_first(
                        slot_hits(plan, base, target), self.stage[buffer, j, count:, :]
                    )

        @pl.when(goal != z)
        def _():
            self.rows_v[buffer] = part.astype(jnp.bfloat16)

        def act(way, more):
            for half in self.halves:

                @pl.when(more)
                def _():
                    so_far = self.take(goal, way, half)
                    self.rows_v[buffer, half, :] = (
                        self.rows_v[buffer, half, :].astype(jnp.float32) + so_far
                    ).astype(jnp.bfloat16)

                self.each_hop(turn, goal, way, half, lambda copy: copy.start())

        self.each_way(goal, act)

    def finish(self, base=None):
        plan = self.plan
        _, z = plan.place()
        for turn in range(plan.n_h - 2, plan.n_h):
            self.wait_hop(turn)

        @pl.when(z > 0)
        def _():
            for half in self.halves:
                self.total[half, :] += self.take(z, 1, half)

        @pl.when(z < plan.n_h - 1)
        def _():
            for half in self.halves:
                self.total[half, :] += self.take(z, -1, half)

        if plan.direct:

            @pl.when((z == 0) | (z == plan.n_h - 1))
            def _():
                for half in self.halves:
                    self.total[half, :] += self.take(z, 1, half, True)

        if base is None:
            copy = pltpu.make_async_copy(self.total, self.out, self.local.at[0])
        else:
            self.rows_v[0] = (self.total[...] + base[...]).astype(jnp.bfloat16)
            copy = pltpu.make_async_copy(self.rows_v.at[0], self.out, self.local.at[0])
        copy.start()
        copy.wait()


class ReturnHeld(Return):
    own_first = False

    def __init__(self, plan, given, *rest):
        super().__init__(plan, *rest)
        self.given = given

    def source(self, chunk, mask):
        plan = self.plan
        at = pl.multiple_of((chunk * plan.n_e + mask) * plan.stride, 16)
        return self.given.at[:, pl.ds(at, plan.stride), :]

    def sent(self):
        for chunk in range(self.plan.n_h):
            self.wait_sent(chunk)


class ReturnMade(Return):
    def __init__(self, plan, made, *rest):
        super().__init__(plan, *rest)
        self.made = made
        self.ring = made.shape[0]

    def source(self, chunk, mask):
        plan = self.plan
        return self.made.at[
            lax.rem(chunk, self.ring), :, pl.ds(mask * plan.stride, plan.stride), :
        ]

    def free(self, chunk):
        if self.plan.n_h > self.ring:

            @pl.when(chunk >= self.ring)
            def _():
                self.wait_sent(chunk - self.ring)
                self.own_copy(chunk - self.ring).wait()

    def sent(self):
        for chunk in range(max(0, self.plan.n_h - self.ring), self.plan.n_h):
            self.wait_sent(chunk)


ANY = pl.BlockSpec(memory_space=pl.ANY)


def inverse_root(rows):
    return lax.rsqrt(jnp.mean(rows * rows, axis=1, keepdims=True) + eps)


def attend_body(plan, *refs):
    (
        grads,
        targets,
        tokens,
        w_query,
        w_key,
        w_value,
        w_out,
        lines,
        gains,
        w_router,
        routes,
        grads_out,
        targets_out,
        land,
        soft_out,
        mixed_out,
        normed_out,
        query_out,
        key_out,
        value_out,
        hidden_out,
        sent_out,
        gates_out,
        roots_out,
        rows_v,
        meta_v,
        stage,
        tokens_v,
        weights_v,
        normed_v,
        heads_v,
        soft_v,
        mixed_v,
        hidden_v,
        in_sem,
        soft_sem,
        out_sem,
        *sems,
    ) = refs
    loads = [
        pltpu.make_async_copy(given, held, in_sem.at[i])
        for i, (given, held) in enumerate(
            [(tokens, tokens_v)]
            + [
                (weight, weights_v.at[k])
                for k, weight in enumerate((w_query, w_key, w_value, w_out))
            ]
        )
    ]
    for load in loads:
        load.start()
    greet(plan)
    work = Dispatch(plan, grads, targets, land, grads_out, targets_out, rows_v, meta_v, stage, sems)
    work.begin()
    _, z = plan.place()
    stores = [
        pltpu.make_async_copy(held, out, out_sem.at[i])
        for i, (held, out) in enumerate(
            (
                (normed_v, normed_out),
                (heads_v.at[0], query_out),
                (heads_v.at[1], key_out),
                (heads_v.at[2], value_out),
                (mixed_v, mixed_out),
                (hidden_v, hidden_out),
                (normed_v, sent_out),
            )
        )
    ]

    def project():
        for load in loads:
            load.wait()
        rows = tokens_v[...].astype(jnp.float32)
        root = inverse_root(rows)
        roots_out[:, 0:128] = jnp.broadcast_to(root, (LEN, 128))
        normed_v[...] = (rows * root * gains[0:1, :]).astype(jnp.bfloat16)
        for k in range(3):
            heads_v[k] = dot(normed_v[...], weights_v[k]).astype(jnp.bfloat16)
        for store in stores[:4]:
            store.start()

    def soft_copy(pair):
        buffer = lax.rem(pair, 2)
        return pltpu.make_async_copy(
            soft_v.at[buffer], soft_out.at[pl.ds(2 * pair, 2)], soft_sem.at[buffer]
        )

    def mix_pair(pair):
        lanes = pl.ds(pl.multiple_of(pair * 2 * HEAD_DIM, 2 * HEAD_DIM), 2 * HEAD_DIM)
        both = [heads_v[k, :, lanes] for k in range(3)]

        @pl.when(pair >= 2)
        def _():
            soft_copy(pair - 2).wait()

        heads = []
        for head in range(2):
            at = slice(head * HEAD_DIM, (head + 1) * HEAD_DIM)
            heads.append(
                mix_head(
                    *[item[:, at] for item in both],
                    lines[pair, head : head + 1, :],
                    soft_v.at[lax.rem(pair, 2)],
                    head,
                )
            )
        mixed_v[:, lanes] = jnp.concatenate(heads, axis=1)
        soft_copy(pair).start()

    def route():
        stores[4].start()
        hidden = tokens_v[...].astype(jnp.float32) + dot(mixed_v[...], weights_v[3])
        hidden_v[...] = hidden
        stores[5].start()
        root = inverse_root(hidden)
        roots_out[:, 128:256] = jnp.broadcast_to(root, (LEN, 128))
        normed = hidden * root * gains[1:2, :]
        stores[0].wait()
        normed_v[...] = normed.astype(jnp.bfloat16)
        stores[6].start()
        logits = contract_last(w_router[...], normed, precise)
        experts = lax.broadcasted_iota(jnp.int32, logits.shape, 0).astype(jnp.float32)
        chosen = [
            jnp.sum(jnp.where(experts == routes[k : k + 1, :], logits, 0.0), axis=0, keepdims=True)
            for k in range(2)
        ]
        peak = jnp.maximum(chosen[0], chosen[1])
        terms = [jnp.exp(item - peak) for item in chosen]
        for k in range(2):
            gates_out[k : k + 1, :] = terms[k] / (terms[0] + terms[1])
        gates_out[2:8, :] = jnp.zeros((6, LEN), jnp.float32)

    pairs = HEADS // 2

    def mixed_by(chunk):
        n_h, found = plan.n_h, 0
        for when in range(1, n_h + 1):
            share = (0, 0, 6, 8, 8)[when] if n_h == 4 else pairs * when // n_h
            found = found + same(chunk, when, n_h + 1) * share
        return found

    @pl.loop(0, plan.n_h)
    def _(chunk):
        work.chunk(chunk, lambda at: meta_v[plan.source(z, at)])
        pl.when(chunk == 0)(project)
        pl.when(chunk > 0)(lambda: work.relay(chunk - 1))
        pl.loop(mixed_by(chunk), mixed_by(chunk + 1))(mix_pair)

    work.relay(plan.n_h - 1)
    soft_copy(pairs - 2).wait()
    soft_copy(pairs - 1).wait()
    route()
    for store in stores[1:]:
        store.wait()
    for chunk in range(plan.n_h):
        work.told(chunk)
        work.arrived(chunk)
    work.finish()


def attend(
    plan,
    grads,
    targets,
    tokens,
    w_query,
    w_key,
    w_value,
    w_out,
    lines,
    gains,
    w_router,
    routes,
):
    n_h, n_e = plan.n_h, plan.n_e
    bf16, f32 = jnp.bfloat16, jnp.float32
    shape = jax.ShapeDtypeStruct
    vmem = pl.BlockSpec(memory_space=pltpu.VMEM)
    rows = shape((LEN, D), bf16)
    return pl.pallas_call(
        functools.partial(attend_body, plan),
        in_specs=[ANY] * 7 + [vmem] * 4,
        out_specs=[ANY] * 11 + [vmem] * 2,
        out_shape=[
            shape((2, plan.total, D), bf16),
            shape((n_h, n_e, 8, LEN), f32),
            shape((n_h, LEN, D), bf16),
            shape((HEADS, LEN, LEN), bf16),
            rows,
            rows,
            rows,
            rows,
            rows,
            shape((LEN, D), f32),
            rows,
            shape((8, LEN), f32),
            shape((LEN, 256), f32),
        ],
        scratch_shapes=[
            pltpu.VMEM((2, LEN, D), bf16),
            pltpu.VMEM((n_h, 8, LEN), f32),
            pltpu.VMEM((2, 2, plan.rows, D), bf16),
            pltpu.VMEM((LEN, D), bf16),
            pltpu.VMEM((4, D, D), bf16),
            pltpu.VMEM((LEN, D), bf16),
            pltpu.VMEM((3, LEN, D), bf16),
            pltpu.VMEM((2, 2, LEN, LEN), bf16),
            pltpu.VMEM((LEN, D), bf16),
            pltpu.VMEM((LEN, D), f32),
            pltpu.SemaphoreType.DMA((5,)),
            pltpu.SemaphoreType.DMA((2,)),
            pltpu.SemaphoreType.DMA((7,)),
        ]
        + Dispatch.sem_shapes(plan),
        compiler_params=pltpu.CompilerParams(
            collective_id=1, has_side_effects=True, vmem_limit_bytes=VMEM
        ),
        name="attend",
    )(
        grads,
        targets,
        tokens,
        w_query,
        w_key,
        w_value,
        w_out,
        lines.reshape(HEADS // 2, 2, 4 * NEAR),
        gains,
        w_router,
        routes,
    )


def expert_body(plan, halves, n_d, *refs):
    (
        sent,
        gates,
        grads,
        targets,
        w_gate,
        w_up,
        w_down,
        total_out,
        gg_out,
        rows_out,
        y_out,
        dgate_out,
        dup_out,
        act_out,
        meta_out,
        land,
        back,
        land_back,
        rows_v,
        meta_v,
        stage,
        wg_v,
        wu_v,
        wd_v,
        target_v,
        gate_v,
        x_v,
        g_v,
        dx_v,
        y_v,
        dgate_v,
        dup_v,
        act_v,
        gg_v,
        gg_back,
        gg_part,
        gg_land,
        column_v,
        dots_v,
        sum_v,
        total,
        slots_in,
        slots_v,
        w_sem,
        t_sem,
        x_sem,
        o_sem,
        gg_send,
        gg_recv,
        ggs_send,
        ggs_recv,
        y_sem,
        *sems,
    ) = refs
    n_e, n_h = plan.n_e, plan.n_h
    e, z = plan.place()
    loads = [
        pltpu.make_async_copy(source, held, w_sem.at[i])
        for i, (source, held) in enumerate(((w_gate, wg_v), (w_up, wu_v), (w_down, wd_v)))
    ]
    for load in loads:
        load.start()
    targets_in = pltpu.make_async_copy(targets, target_v, t_sem.at[0])
    targets_in.start()
    greet(plan)
    work = Dispatch(
        plan, sent, gates, land, rows_out, meta_out, rows_v, meta_v, stage, sems[:n_d]
    )
    give = ReturnMade(
        plan,
        dx_v,
        back,
        land_back,
        total_out,
        stage,
        rows_v,
        sum_v,
        total,
        slots_in,
        slots_v,
        sems[n_d:],
    )
    work.begin()
    targets_in.wait()
    ahead = min(3, n_h)

    @pl.loop(0, ahead)
    def _(chunk):
        work.chunk(chunk, lambda at: target_v[at, 0])
        pl.when(chunk > 0)(lambda: work.relay(chunk - 1))

    for load in loads:
        load.wait()

    def gg_copy(chunk, mask):
        return remote(
            gg_v.at[chunk, mask],
            gg_back.at[chunk, mask],
            gg_send.at[chunk, mask],
            gg_recv.at[chunk, mask],
            (across(e, mask), z),
        )

    def gg_along(chunk):
        return remote(
            gg_part.at[chunk],
            gg_land.at[z],
            ggs_send.at[chunk],
            ggs_recv.at[z],
            (e, plan.source(z, chunk)),
        )

    def gg_from(distance):
        other = lax.rem(z + distance, n_h)
        return other, remote(
            gg_part.at[0], gg_land.at[other], ggs_send.at[0], ggs_recv.at[other], (e, other)
        )

    def outs(chunk, j):
        at = pl.multiple_of(chunk * plan.rows, 16)
        return [
            pltpu.make_async_copy(held.at[j], out.at[j, pl.ds(at, plan.rows), :], o_sem.at[i, j])
            for i, (held, out) in enumerate(
                ((dgate_v, dgate_out), (dup_v, dup_out), (act_v, act_out))
            )
        ]

    all_held = n_h <= dx_v.shape[0]
    masks = n_e // halves
    piece = masks * plan.stride

    def own_slots(j):
        slots = lax.broadcasted_iota(jnp.int32, (plan.stride, LEN), 0).astype(jnp.float32)
        return slots + slot_base(plan, e, j)

    def weigh(chunk, mask):
        aim, weight = target_v[chunk, mask], gate_v[mask]
        at = pl.ds(pl.multiple_of(mask * plan.stride, 16), plan.stride)
        for j in range(2):
            hit = jnp.where(own_slots(j) == aim[0:1, :], weight[0:1, :], 0.0)
            hit = hit + jnp.where(own_slots(j) == aim[1:2, :], weight[1:2, :], 0.0)
            column_v[j, at, :] = jnp.broadcast_to(
                jnp.sum(hit, axis=1, keepdims=True), (plan.stride, 128)
            )

    def spread(chunk, mask):
        aim = target_v[chunk, mask]
        at = pl.ds(pl.multiple_of(mask * plan.stride, 16), plan.stride)
        for k in range(2):
            line = jnp.zeros((1, LEN), jnp.float32)
            for j in range(2):
                hit = own_slots(j) == aim[k : k + 1, :]
                line = line + jnp.sum(
                    jnp.where(hit, dots_v[chunk, j, at, 0:1], 0.0), axis=0, keepdims=True
                )
            gg_v[chunk, mask, k : k + 1, :] = line

    def y_copy(chunk):
        at = pl.ds(pl.multiple_of(chunk * plan.rows, 16), plan.rows)
        return pltpu.make_async_copy(y_v, y_out.at[:, at, :], y_sem.at[1])

    def make_y(chunk):
        at = pl.ds(pl.multiple_of(chunk * plan.rows, 16), plan.rows)
        kept = pltpu.make_async_copy(act_out.at[:, at, :], act_v, y_sem.at[0])
        kept.start()

        @pl.when(chunk > 0)
        def _():
            y_copy(chunk - 1).wait()

        kept.wait()

        @pl.loop(0, 2)
        def _(j):
            y_v[j] = dot(act_v[j], wd_v[j]).astype(jnp.bfloat16)

        y_copy(chunk).start()

    def step(chunk, index):
        j, half = lax.div(index, halves), lax.rem(index, halves)
        at = pl.ds(pl.multiple_of(half * piece, 16), piece)
        gate_pre = contract_last(x_v[j, at, :], wg_v[j])
        up_pre = contract_last(x_v[j, at, :], wu_v[j])
        raw = contract_last(g_v[j, at, :], wd_v[j])
        gate = column_v[j, at, 0:1]
        square = gate_pre * gate_pre
        tanh = jnp.tanh(gate_pre * (0.7978845608028654 + 0.035677408136300125 * square))
        side = 0.5 + 0.5 * tanh
        gelu = gate_pre * side
        slope = side + gelu * (1.0 - side) * (1.5957691216057308 + 0.21406444881780075 * square)
        act = gelu * up_pre
        dots_v[chunk, j, at, :] = jnp.broadcast_to(
            jnp.sum(act * raw, axis=1, keepdims=True), (piece, 128)
        )
        grad_act = gate * raw
        grad_gate = (grad_act * up_pre * slope).astype(jnp.bfloat16)
        grad_up = (grad_act * gelu).astype(jnp.bfloat16)
        dgate_v[j, at, :] = grad_gate
        dup_v[j, at, :] = grad_up
        act_v[j, at, :] = (act * gate).astype(jnp.bfloat16)
        dx_v[lax.rem(chunk, dx_v.shape[0]), j, at, :] = (
            dot(grad_gate, wg_v[j]) + dot(grad_up, wu_v[j])
        ).astype(jnp.bfloat16)

    split = n_e - n_e // 4

    def now(chunk):
        if plan.direct:
            return chunk > 1
        return (chunk < 1) | (not all_held)

    gg_v[...] = jnp.zeros_like(gg_v)

    @pl.loop(0, n_h)
    def _(chunk):
        at = pl.multiple_of(chunk * plan.rows, 16)
        ins = [
            pltpu.make_async_copy(source.at[:, pl.ds(at, plan.rows), :], held, x_sem.at[i])
            for i, (source, held) in enumerate(((rows_out, x_v), (grads, g_v)))
        ]
        ins[1].start()
        work.told(chunk)
        gate_in = pltpu.make_async_copy(meta_out.at[chunk], gate_v, t_sem.at[0])
        gate_in.start()
        gate_in.wait()
        pl.loop(0, n_e)(lambda mask: weigh(chunk, mask))
        give.free(chunk)

        @pl.when(chunk > 0)
        def _():
            for j in range(2):
                for copy in outs(chunk - 1, j):
                    copy.wait()

        work.arrived(chunk)
        ins[0].start()
        for copy in ins:
            copy.wait()
        pl.loop(0, 2 * halves)(lambda index: step(chunk, index))
        for j in range(2):
            for copy in outs(chunk, j):
                copy.start()

        @pl.when(chunk + ahead < n_h)
        def _():
            work.chunk(chunk + ahead, lambda at: target_v[at, 0])

        pl.when(chunk + ahead <= n_h)(lambda: work.relay(chunk + ahead - 1))
        pl.loop(0, n_e)(lambda mask: spread(chunk, mask))
        for mask in range(1, n_e):
            gg_copy(chunk, mask).start()

        if plan.relayed < n_e:
            pl.when(chunk > 0)(lambda: give.relay(chunk).start())

        @pl.when(now(chunk))
        def _():
            give.send(chunk)

        if plan.direct:
            pl.when(chunk == 0)(lambda: give.send(0, 0, split))


    if plan.direct:
        give.send(1)
        give.send(0, split, plan.relayed)
        give.relay_sum()
    elif all_held:
        pl.loop(1, n_h)(lambda turn: give.send(give.chunk_of(give.goal(turn))))
    for j in range(2):
        for copy in outs(n_h - 1, j):
            copy.wait()
    make_y(0)
    work.finish()

    @pl.loop(0, n_h)
    def _(turn):
        chunk = give.chunk_of(give.goal(turn))
        part = gg_v[chunk, 0]
        for mask in range(1, n_e):
            gg_copy(chunk, mask).wait_recv()
            part = part + gg_back[chunk, mask]
        gg_part[chunk] = part

        @pl.when(chunk > 0)
        def _():
            gg_along(chunk).start()

        give.combine(turn, lambda at: target_v[at, 0])
        pl.when(turn + 1 < n_h)(lambda: make_y(turn + 1))

    y_copy(n_h - 1).wait()
    give.sent()
    for chunk in range(n_h):
        for mask in range(1, n_e):
            gg_copy(chunk, mask).wait_send()
    sum_gg = gg_part[0]
    for distance in range(1, n_h):
        other, arrival = gg_from(distance)
        arrival.wait_recv()
        sum_gg = sum_gg + gg_land[other]
    gg_out[...] = sum_gg
    for chunk in range(1, n_h):
        gg_along(chunk).wait_send()
    give.finish()


def run_experts(plan, sent, gates, grads, targets, w_gate, w_up, w_down):
    n_h, n_e, width = plan.n_h, plan.n_e, plan.width
    bf16, f32 = jnp.bfloat16, jnp.float32
    shape = jax.ShapeDtypeStruct
    dma = pltpu.SemaphoreType.DMA
    ring = min(4, n_h)
    d_sems, r_sems = Dispatch.sem_shapes(plan), Return.sem_shapes(plan)
    halves = 2 if plan.rows <= 640 else 4
    return pl.pallas_call(
        functools.partial(expert_body, plan, halves, len(d_sems)),
        in_specs=[ANY] * 7,
        out_specs=[ANY, pl.BlockSpec(memory_space=pltpu.VMEM)] + [ANY] * 9,
        out_shape=[
            shape((LEN, D), f32),
            shape((8, LEN), f32),
            shape((2, plan.total, D), bf16),
            shape((2, plan.total, D), bf16),
            shape((2, plan.total, width), bf16),
            shape((2, plan.total, width), bf16),
            shape((2, plan.total, width), bf16),
            shape((n_h, n_e, 8, LEN), f32),
            shape((n_h, LEN, D), bf16),
            shape((n_h, 2, plan.rows, D), bf16),
            shape((3, n_h, LEN, D), bf16),
        ],
        scratch_shapes=[
            pltpu.VMEM((2, LEN, D), bf16),
            pltpu.VMEM((n_h, 8, LEN), f32),
            pltpu.VMEM((2, 2, plan.rows, D), bf16),
            pltpu.VMEM((2, width, D), bf16),
            pltpu.VMEM((2, width, D), bf16),
            pltpu.VMEM((2, width, D), bf16),
            pltpu.VMEM((n_h, n_e, 8, LEN), f32),
            pltpu.VMEM((n_e, 8, LEN), f32),
            pltpu.VMEM((2, plan.rows, D), bf16),
            pltpu.VMEM((2, plan.rows, D), bf16),
            pltpu.VMEM((ring, 2, plan.rows, D), bf16),
            pltpu.VMEM((2, plan.rows, D), bf16),
            pltpu.VMEM((2, plan.rows, width), bf16),
            pltpu.VMEM((2, plan.rows, width), bf16),
            pltpu.VMEM((2, plan.rows, width), bf16),
            pltpu.VMEM((n_h, n_e, 8, LEN), f32),
            pltpu.VMEM((n_h, n_e, 8, LEN), f32),
            pltpu.VMEM((n_h, 8, LEN), f32),
            pltpu.VMEM((n_h, 8, LEN), f32),
            pltpu.VMEM((2, plan.rows, 128), f32),
            pltpu.VMEM((n_h, 2, plan.rows, 128), f32),
            pltpu.VMEM((LEN, D), bf16),
            pltpu.VMEM((LEN, D), f32),
            *Return.slot_shapes(plan),
            dma((3,)),
            dma((1,)),
            dma((2,)),
            dma((3, 2)),
            dma((n_h, n_e)),
            dma((n_h, n_e)),
            dma((n_h,)),
            dma((n_h,)),
            dma((2,)),
        ]
        + d_sems
        + r_sems,
        compiler_params=pltpu.CompilerParams(
            collective_id=2, has_side_effects=True, vmem_limit_bytes=VMEM
        ),
        name="run_experts",
    )(sent, gates, grads, targets, jnp.swapaxes(w_gate, 1, 2), jnp.swapaxes(w_up, 1, 2), w_down)


class Sum:
    pieces, stages, few = 4, 5, 32

    def __init__(self, plan, held, whole, few_v, few_in, *rest):
        self.plan = plan
        self.held, self.whole, self.few_v, self.few_in = held, whole, few_v, few_in
        self.landed, (self.send, self.recv, self.f_send, self.f_recv) = rest[:5], rest[5:]

    @classmethod
    def scratch_shapes(cls):
        dma = pltpu.SemaphoreType.DMA
        bf16, f32 = jnp.bfloat16, jnp.float32
        rows = (D // 2, D // 4, D // 8, D // 16, D // 32)
        return (
            [
                pltpu.VMEM((cls.pieces, D, D), bf16),
                pltpu.VMEM((cls.pieces, D, D), bf16),
                pltpu.VMEM((cls.stages + 1, cls.few, D), f32),
                pltpu.VMEM((cls.stages, cls.few, D), f32),
            ]
            + [pltpu.VMEM((cls.pieces, count, D), bf16) for count in rows]
            + [
                dma((2 * cls.stages, cls.pieces, 2)),
                dma((2 * cls.stages, cls.pieces, 2)),
                dma((cls.stages,)),
                dma((cls.stages,)),
            ]
        )

    def partner(self, bit):
        e, z = self.plan.place()
        if bit < 3:
            return (across(e, 1 << bit), z)
        return (e, across(z, 1 << (bit - 3)))

    def parts(self, stage):
        e, z = self.plan.place()
        place = [lax.rem(lax.div(e, 1 << k), 2) for k in range(3)]
        place += [lax.rem(lax.div(z, 1 << k), 2) for k in range(2)]
        base, count = place[0] * (D // 2), D // 2
        if stage == 1:
            return [(self.partner(0), base, D // 2 - base, count)]
        out = []
        for part, order in enumerate(((1, 2, 3, 4), (2, 1, 3, 4))):
            at, count = base + part * (D // 4), D // 4
            for bit in order[: stage - 1]:
                count //= 2
                keep, give = at + place[bit] * count, at + (1 - place[bit]) * count
                at = keep
            out.append((self.partner(bit), keep, give, count))
        return out

    def copies(self, stage, piece):
        halving = stage <= self.stages
        out = []
        parts = self.parts(stage if halving else 2 * self.stages + 1 - stage)
        for part, (device, keep, give, count) in enumerate(parts):
            here = pl.ds(pl.multiple_of(give if halving else keep, 16), count)
            there = (
                self.landed[stage - 1].at[piece, part * count : (part + 1) * count, :]
                if halving
                else self.whole.at[piece, here, :]
            )
            out.append(
                remote(
                    (self.held if halving else self.whole).at[piece, here, :],
                    there,
                    self.send.at[stage - 1, piece, part],
                    self.recv.at[stage - 1, piece, part],
                    device,
                )
            )
        return out

    def few_copy(self, stage):
        return remote(
            self.few_v.at[stage - 1],
            self.few_in.at[stage - 1],
            self.f_send.at[stage - 1],
            self.f_recv.at[stage - 1],
            self.partner(stage - 1),
        )

    def add(self, stage, piece):
        for part, (_, keep, _, count) in enumerate(self.parts(stage)):
            tile = min(count, 64)

            @pl.loop(0, count // tile)
            def _(i):
                at = pl.ds(pl.multiple_of(keep + i * tile, 16), tile)
                come = pl.ds(pl.multiple_of(part * count + i * tile, 16), tile)
                total = self.held[piece, at, :].astype(jnp.float32) + self.landed[stage - 1][
                    piece, come, :
                ].astype(jnp.float32)
                into = self.whole if stage == self.stages else self.held
                into[piece, at, :] = total.astype(jnp.bfloat16)

    slots = pieces + 2 * stages

    def slot(self, slot, ready, done):
        for piece in range(self.pieces):
            stage = slot - piece + 1
            if stage == 1:
                ready(piece)
            if 2 <= stage <= 2 * self.stages + 1:
                for copy in self.copies(stage - 1, piece):
                    copy.wait_recv()
                if stage - 1 <= self.stages:
                    self.add(stage - 1, piece)
            if 1 <= stage <= 2 * self.stages:
                for copy in self.copies(stage, piece):
                    copy.start()
            if stage == 2 * self.stages + 1:
                done(piece)
        stage = slot + 1
        if 2 <= stage <= self.stages + 1:
            self.few_copy(stage - 1).wait_recv()
            self.few_v[stage - 1] = self.few_v[stage - 2] + self.few_in[stage - 2]
        if stage <= self.stages:
            self.few_copy(stage).start()

    def finish(self):
        for stage in range(1, 2 * self.stages + 1):
            for piece in range(self.pieces):
                for copy in self.copies(stage, piece):
                    copy.wait_send()
        for stage in range(1, self.stages + 1):
            self.few_copy(stage).wait_send()


def sum_body(plan, *refs):
    n_h = plan.n_h
    dgate, dup, act, rows, grads = refs[:5]
    refs = refs[5:]
    if plan.summed:
        low, few = refs[:2]
        refs = refs[2:]
    outs, refs = refs[:3], refs[3:]
    if plan.summed:
        sums_out, few_out = refs[:2]
        refs = refs[2:]
    left_v, right_v, made_v, p_sem, g_sem = refs[:5]
    steps = 3 * n_h

    def factors(q, act_on):
        buffer = lax.rem(q, 2)
        at = pl.ds(pl.multiple_of(lax.rem(q, n_h) * plan.rows, 16), plan.rows)

        def copies(lefts, rights):
            for i in range(2):
                for k, ((source, j), held) in enumerate(((lefts[i], left_v), (rights[i], right_v))):
                    act_on(
                        pltpu.make_async_copy(
                            source.at[j, at, :], held.at[buffer, i], p_sem.at[buffer, 2 * i + k]
                        )
                    )

        @pl.when(q < 2 * n_h)
        def _():
            j = lax.div(q, n_h)
            copies(((dgate, j), (dup, j)), ((rows, j), (rows, j)))

        @pl.when(q >= 2 * n_h)
        def _():
            copies(((act, 0), (act, 1)), ((grads, 0), (grads, 1)))

    def results(group, act_on):
        @pl.when(group < 2)
        def _():
            for i in range(2):
                act_on(pltpu.make_async_copy(made_v.at[i], outs[i].at[group], g_sem.at[i]))

        @pl.when(group == 2)
        def _():
            for i in range(2):
                act_on(pltpu.make_async_copy(made_v.at[i], outs[2].at[i], g_sem.at[i]))

    def product(q):
        buffer, turn, group = lax.rem(q, 2), lax.rem(q, n_h), lax.div(q, n_h)
        factors(q, lambda copy: copy.wait())

        @pl.when(q + 1 < steps)
        def _():
            factors(q + 1, lambda copy: copy.start())

        @pl.when((turn == 0) & (q > 0))
        def _():
            results(group - 1, lambda copy: copy.wait())

        @pl.when(turn == 0)
        def _():
            made_v[...] = jnp.zeros_like(made_v)

        for i in range(2):
            made_v[i] += contract_first(left_v[buffer, i], right_v[buffer, i])

        @pl.when(turn == n_h - 1)
        def _():
            results(group, lambda copy: copy.start())

    factors(0, lambda copy: copy.start())
    if plan.summed:
        load_sem, store_sem = refs[5:7]
        total = Sum(plan, *refs[7:])
        loads = [
            pltpu.make_async_copy(low.at[i], total.held.at[i], load_sem.at[i]) for i in range(4)
        ]
        stores = [
            pltpu.make_async_copy(total.whole.at[i], sums_out.at[i], store_sem.at[i])
            for i in range(4)
        ]
        for load in loads:
            load.start()
        total.few_v[0] = few[...]
        greet(plan)
        done = 0
        for slot in range(total.slots):
            total.slot(slot, lambda i: loads[i].wait(), lambda i: stores[i].start())
            if slot % 2 == 0 and done < steps:
                pl.loop(done, min(done + 2, steps))(product)
                done = min(done + 2, steps)
        few_out[...] = total.few_v[total.stages]
        total.finish()
        for store in stores:
            store.wait()
    else:
        pl.loop(0, steps)(product)
    results(2, lambda copy: copy.wait())


def sum_all(plan, dgate, dup, act, rows, grads, low, few):
    bf16, f32 = jnp.bfloat16, jnp.float32
    shape = jax.ShapeDtypeStruct
    vmem = pl.BlockSpec(memory_space=pltpu.VMEM)
    dma = pltpu.SemaphoreType.DMA
    args = [dgate, dup, act, rows, grads]
    in_specs, out_specs = [ANY] * 5, [ANY] * 3
    out_shape = [shape((2, plan.width, D), f32)] * 3
    scratch_shapes = [
        pltpu.VMEM((2, 2, plan.rows, plan.width), bf16),
        pltpu.VMEM((2, 2, plan.rows, D), bf16),
        pltpu.VMEM((2, plan.width, D), f32),
        dma((2, 4)),
        dma((2,)),
    ]
    params = {"vmem_limit_bytes": VMEM}
    if plan.summed:
        args += [low, few]
        in_specs += [ANY, vmem]
        out_specs += [ANY, vmem]
        out_shape += [shape((4, D, D), bf16), shape((Sum.few, D), f32)]
        scratch_shapes += [dma((4,)), dma((4,))] + Sum.scratch_shapes()
        params.update(collective_id=4, has_side_effects=True)
    out = pl.pallas_call(
        functools.partial(sum_body, plan),
        in_specs=in_specs,
        out_specs=out_specs,
        out_shape=out_shape,
        scratch_shapes=scratch_shapes,
        compiler_params=pltpu.CompilerParams(**params),
        name="sum_all",
    )(*args)
    if plan.summed:
        return out[:3], out[3], out[4]
    return out[:3], *lax.psum((low, few), ("expert", "hidden"))


def two_parts(array):
    high = array.astype(jnp.bfloat16)
    return high, (array - high.astype(jnp.float32)).astype(jnp.bfloat16)


def unattend_body(plan, n_r, *refs):
    (
        given,
        targets,
        grad_sent,
        hidden,
        grad_out,
        tokens,
        mixed,
        normed,
        query,
        key,
        value,
        soft,
        w_query,
        w_key,
        w_value,
        w_out,
        grad_gates,
        gates,
        routes,
        w_router,
        gains,
        roots,
        branch_out,
        back,
        land,
        low_out,
        tokens_out,
        few_out,
        lines_out,
        rows_v,
        stage,
        target_v,
        sum_v,
        total,
        slots_in,
        slots_v,
        grad_sent_v,
        hidden_v,
        grad_out_v,
        tokens_v,
        mixed_v,
        normed_v,
        heads_v,
        soft_v,
        weights_v,
        grad_hidden_v,
        branch_v,
        grad_heads_v,
        grads_v,
        low_v,
        wide_v,
        t_sem,
        in_sem,
        soft_sem,
        low_sem,
        out_sem,
        *sems,
    ) = refs
    f32, bf16 = jnp.float32, jnp.bfloat16
    ins = [
        (grad_sent, grad_sent_v),
        (hidden, hidden_v),
        (grad_out, grad_out_v),
        (mixed, mixed_v),
        (w_out, weights_v.at[3]),
        (query, heads_v.at[0]),
        (key, heads_v.at[1]),
        (value, heads_v.at[2]),
        (normed, normed_v),
        (w_query, weights_v.at[0]),
        (w_key, weights_v.at[1]),
        (w_value, weights_v.at[2]),
        (tokens, tokens_v),
    ]
    loads = [
        pltpu.make_async_copy(source, held, in_sem.at[i]) for i, (source, held) in enumerate(ins)
    ]
    targets_in = pltpu.make_async_copy(targets, target_v, t_sem.at[0])

    def soft_copy(pair):
        buffer = lax.rem(pair, 2)
        return pltpu.make_async_copy(
            soft.at[pl.ds(2 * pair, 2)], soft_v.at[buffer], soft_sem.at[buffer]
        )

    targets_in.start()
    for load in loads:
        load.start()
    soft_copy(0).start()
    greet(plan)
    give = ReturnHeld(
        plan, given, back, land, branch_out, stage, rows_v, sum_v, total, slots_in, slots_v, sems
    )
    turns = plan.n_h
    if plan.relayed < plan.n_e:
        pl.loop(1, turns)(lambda chunk: give.relay(chunk).start())
    pl.loop(0, turns)(lambda turn: give.send(give.chunk_of(give.goal(turn))))
    targets_in.wait()

    def combine(turn):
        give.combine(turn, lambda at: target_v[at, 0])

    tile = 64

    def low_copy(i):
        return pltpu.make_async_copy(low_v.at[i % 2], low_out.at[i], low_sem.at[i % 2])

    for load in loads[:3]:
        load.wait()
    few_out[...] = jnp.zeros_like(few_out)
    mean = gates[0:1, :] * grad_gates[0:1, :] + gates[1:2, :] * grad_gates[1:2, :]
    experts = w_router.shape[0]
    numbers = lax.broadcasted_iota(jnp.int32, (experts, LEN), 0).astype(f32)
    grad_logits = jnp.zeros((experts, LEN), f32)
    for k in range(2):
        chosen = gates[k : k + 1, :] * (grad_gates[k : k + 1, :] - mean)
        grad_logits = grad_logits + jnp.where(numbers == routes[k : k + 1, :], chosen, 0.0)
    high, rest = two_parts(grad_logits)
    wide_v[...] = contract_first(
        jnp.concatenate([high, high, rest], axis=0),
        jnp.concatenate([*two_parts(w_router[...]), w_router[...].astype(bf16)], axis=0),
    )

    @pl.loop(0, LEN // tile)
    def _(i):
        at = pl.ds(pl.multiple_of(i * tile, 16), tile)
        rows, root = hidden_v[at, :], roots[at, 128:129]
        grad = wide_v[at, :] + grad_sent_v[at, :]
        near = rows * root
        few_out[experts + 1 : experts + 2, :] += jnp.sum(grad * near, axis=0, keepdims=True)
        scaled = grad * gains[1:2, :]
        pull = jnp.mean(scaled * rows, axis=1, keepdims=True) * (root * root * root)
        grad = grad_out_v[at, :].astype(f32) + root * scaled - rows * pull
        grad_hidden_v[at, :] = grad
        branch_v[at, :] = grad.astype(bf16)
        grad_sent_v[at, :] = near * gains[1:2, :]

    normed_high, normed_rest = two_parts(grad_sent_v[...])
    few_out[0:experts, :] = dot(high, normed_high) + dot(rest, normed_high) + dot(high, normed_rest)
    for load in loads[3:5]:
        load.wait()
    low_v[1] = contract_first(mixed_v[...], branch_v[...]).astype(bf16)
    low_copy(3).start()
    mixed_v[...] = contract_last(branch_v[...], weights_v[3]).astype(bf16)
    for load in loads[5:8]:
        load.wait()

    def unmix_pair(pair):
        lanes = pl.ds(pl.multiple_of(pair * 2 * HEAD_DIM, 2 * HEAD_DIM), 2 * HEAD_DIM)
        soft_copy(pair).wait()

        @pl.when(pair + 1 < HEADS // 2)
        def _():
            soft_copy(pair + 1).start()

        both = [heads_v[k, :, lanes] for k in range(3)] + [mixed_v[:, lanes]]
        found = []
        for head in range(2):
            at = slice(head * HEAD_DIM, (head + 1) * HEAD_DIM)
            found.append(
                unmix_head(
                    *[item[:, at] for item in both], soft_v.at[lax.rem(pair, 2)], grads_v, head
                )
            )
        for k in range(3):
            grad_heads_v[k, :, lanes] = jnp.concatenate([found[0][k], found[1][k]], axis=1)
        lines_out[pair] = jnp.concatenate([found[0][3], found[1][3]], axis=0)

    pairs = HEADS // 2
    first, second = turns // 4, turns // 2
    pl.loop(0, pairs // 2)(unmix_pair)
    pl.loop(0, first)(combine)
    pl.loop(pairs // 2, pairs)(unmix_pair)
    give.relay_sum()
    pl.loop(first, second)(combine)
    for load in loads[8:]:
        load.wait()
    for k in range(3):
        if k == 1:
            low_copy(3).wait()
        if k == 2:
            low_copy(0).wait()
        low_v[k % 2] = contract_first(normed_v[...], grad_heads_v[k]).astype(bf16)
        low_copy(k).start()
    pl.loop(second, turns - 1)(combine)
    wide_v[...] = (
        contract_last(grad_heads_v[0], weights_v[0])
        + contract_last(grad_heads_v[1], weights_v[1])
        + contract_last(grad_heads_v[2], weights_v[2])
    )

    @pl.loop(0, LEN // tile)
    def _(i):
        at = pl.ds(pl.multiple_of(i * tile, 16), tile)
        rows, root = tokens_v[at, :].astype(f32), roots[at, 0:1]
        grad = wide_v[at, :]
        few_out[experts : experts + 1, :] += jnp.sum(grad * rows * root, axis=0, keepdims=True)
        scaled = grad * gains[0:1, :]
        pull = jnp.mean(scaled * rows, axis=1, keepdims=True) * (root * root * root)
        grad_hidden_v[at, :] = grad_hidden_v[at, :] + root * scaled - rows * pull

    tokens_copy = pltpu.make_async_copy(grad_hidden_v, tokens_out, out_sem.at[0])
    tokens_copy.start()
    combine(turns - 1)
    give.sent()
    give.finish(hidden_v)
    for i in (1, 2):
        low_copy(i).wait()
    tokens_copy.wait()


def unattend(
    plan,
    given,
    targets,
    grad_sent,
    hidden,
    grad_out,
    tokens,
    mixed,
    normed,
    query,
    key,
    value,
    soft,
    w_query,
    w_key,
    w_value,
    w_out,
    grad_gates,
    gates,
    routes,
    w_router,
    gains,
    roots,
):
    n_h, n_e = plan.n_h, plan.n_e
    bf16, f32 = jnp.bfloat16, jnp.float32
    shape = jax.ShapeDtypeStruct
    vmem = pl.BlockSpec(memory_space=pltpu.VMEM)
    dma = pltpu.SemaphoreType.DMA
    sems = Return.sem_shapes(plan)
    few = -(-(w_router.shape[0] + 3) // Sum.few) * Sum.few
    rows, wide = pltpu.VMEM((LEN, D), bf16), pltpu.VMEM((LEN, D), f32)
    out = pl.pallas_call(
        functools.partial(unattend_body, plan, len(sems)),
        in_specs=[ANY] * 16 + [vmem] * 6,
        out_specs=[ANY] * 5 + [vmem] * 2,
        out_shape=[
            shape((LEN, D), bf16),
            shape((n_h, 2, plan.rows, D), bf16),
            shape((3, n_h, LEN, D), bf16),
            shape((4, D, D), bf16),
            shape((LEN, D), f32),
            shape((few, D), f32),
            shape((HEADS // 2, 2, 4 * NEAR), f32),
        ],
        scratch_shapes=[
            pltpu.VMEM((2, LEN, D), bf16),
            pltpu.VMEM((2, 2, plan.rows, D), bf16),
            pltpu.VMEM((n_h, n_e, 8, LEN), f32),
            rows,
            wide,
            *Return.slot_shapes(plan),
            wide,
            wide,
            rows,
            rows,
            rows,
            rows,
            pltpu.VMEM((3, LEN, D), bf16),
            pltpu.VMEM((2, 2, LEN, LEN), bf16),
            pltpu.VMEM((4, D, D), bf16),
            wide,
            rows,
            pltpu.VMEM((3, LEN, D), bf16),
            pltpu.VMEM((LEN, LEN), bf16),
            pltpu.VMEM((2, D, D), bf16),
            wide,
            dma((1,)),
            dma((13,)),
            dma((2,)),
            dma((2,)),
            dma((1,)),
        ]
        + sems,
        compiler_params=pltpu.CompilerParams(
            collective_id=3, has_side_effects=True, vmem_limit_bytes=VMEM
        ),
        name="unattend",
    )(
        given,
        targets,
        grad_sent,
        hidden,
        grad_out,
        tokens,
        mixed,
        normed,
        query,
        key,
        value,
        soft,
        w_query,
        w_key,
        w_value,
        w_out,
        grad_gates,
        gates,
        routes,
        w_router,
        gains,
        roots,
    )
    return out[0], out[3], out[4], out[5], out[6].reshape(HEADS, 4 * NEAR)


def per_device(
    n_e,
    n_h,
    tokens,
    gain_one,
    w_query,
    w_key,
    w_value,
    w_out,
    bias_table,
    gain_two,
    w_router,
    w_gate,
    w_up,
    w_down,
    routes,
    cotangent,
):
    experts_all = w_router.shape[1]
    plan = Plan(n_e, n_h, experts_all, w_gate.shape[2])
    both = ("expert", "hidden")

    def small(array):
        return jnp.pad(array.astype(jnp.float32), ((0, 8 - array.shape[0]), (0, 0)))

    targets = small(slot_targets(routes, experts_all, plan.capacity, plan.stride))
    gains, route_rows = small(jnp.stack([gain_one, gain_two])), small(routes.T)
    hot_bucket = offset_buckets()
    lines = jnp.dot(hot_bucket, bias_table, precision=precise).T
    (
        grads_in,
        targets_all,
        _,
        soft,
        mixed_rows,
        normed_one,
        query_rows,
        key_rows,
        value_rows,
        hidden,
        sent,
        gates,
        roots,
    ) = attend(
        plan,
        cotangent,
        targets,
        tokens,
        w_query,
        w_key,
        w_value,
        w_out,
        lines,
        gains,
        w_router.T,
        route_rows,
    )
    made = run_experts(
        plan, sent, gates, grads_in, targets_all, w_gate, w_up, w_down
    )
    grad_sent, grad_gates, rows_in, y_rows, gate_rows, up_rows, act_rows = made[:7]
    block_out, low, tokens_grad, few, grad_lines = unattend(
        plan,
        y_rows,
        targets_all,
        grad_sent,
        hidden,
        cotangent,
        tokens,
        mixed_rows,
        normed_one,
        query_rows,
        key_rows,
        value_rows,
        soft,
        w_query,
        w_key,
        w_value,
        w_out,
        grad_gates,
        gates,
        route_rows,
        w_router.T,
        gains,
        roots,
    )
    bias_table_grad = jnp.dot(grad_lines, hot_bucket, precision=precise).T
    last = jnp.pad(bias_table_grad.reshape(1, BUCKETS * HEADS), ((0, 0), (0, D - BUCKETS * HEADS)))
    few = lax.dynamic_update_slice(few, last, (experts_all + 2, 0))
    weight_grads, summed, few = sum_all(
        plan, gate_rows, up_rows, act_rows, rows_in, grads_in, low, few
    )
    summed = [summed[i].astype(jnp.float32) for i in range(4)]
    return (
        block_out,
        tokens_grad,
        few[experts_all],
        *summed,
        few[experts_all + 2, : BUCKETS * HEADS].reshape(BUCKETS, HEADS),
        few[experts_all + 1],
        few[:experts_all].T,
        jnp.swapaxes(weight_grads[0], 1, 2),
        jnp.swapaxes(weight_grads[1], 1, 2),
        weight_grads[2],
    )


def solution(mesh):
    in_specs = (
        P(("expert", "hidden"), None),
        P(),
        P(),
        P(),
        P(),
        P(),
        P(),
        P(),
        P(),
        P("expert", None, "hidden"),
        P("expert", None, "hidden"),
        P("expert", "hidden", None),
        P(("expert", "hidden"), None),
        P(("expert", "hidden"), None),
    )
    out_specs = (
        P(("expert", "hidden"), None),
        P(("expert", "hidden"), None),
        P(),
        P(),
        P(),
        P(),
        P(),
        P(),
        P(),
        P(),
        P("expert", None, "hidden"),
        P("expert", None, "hidden"),
        P("expert", "hidden", None),
    )
    return jax.shard_map(
        functools.partial(per_device, mesh.shape["expert"], mesh.shape["hidden"]),
        mesh=mesh, in_specs=in_specs, out_specs=out_specs, check_vma=False
    )
```
